32 devices in a mesh: fsdp: 2 (over x), ctx: 4 (over y, core), tensor: 4 (over z).
Axes of the slice: x: 2, y: 2, z: 4, core: 2. Of those that a mesh axis runs over, the one named last changes fastest.
Arguments:
- prompt_in: bfloat16 [8, 2048, 1088], P(('fsdp', 'tensor'), 'ctx'), may hold values from -6 to 6
- cont_in: bfloat16 [8, 1536, 1088], P(('fsdp', 'tensor'), 'ctx'), may hold values from -6 to 6
- cont_seg: int32 [8, 1536], P(('fsdp', 'tensor')), may hold values from 0 to 4, never falling along the last dimension, each value on 1 to 384 neighbouring positions
- ln1_gain: float32 [1088], replicated, may hold values from 0.1 to 1.9
- ln1_bias: float32 [1088], replicated, may hold values from -3 to 3
- w_qkv: float32 [1088, 3264], P('fsdp'), may hold values from -0.1875 to 0.1875
- qv_bias: float32 [2, 1088], replicated, may hold values from -3 to 3
- w_out: float32 [1088, 1088], P('fsdp'), may hold values from -1.5 to 1.5
- out_bias: float32 [1088], replicated, may hold values from -3 to 3
- ln2_gain: float32 [1088], replicated, may hold values from 0.1 to 1.9
- ln2_bias: float32 [1088], replicated, may hold values from -3 to 3
- w_fc: float32 [1088, 4352], P('fsdp', 'tensor'), may hold values from -0.1875 to 0.1875
- fc_bias: float32 [4352], P('tensor'), may hold values from -3 to 3
- w_proj: float32 [4352, 1088], P('tensor', 'fsdp'), may hold values from -0.09375 to 0.09375
- proj_bias: float32 [1088], replicated, may hold values from -3 to 3
- prompt_cot: bfloat16 [8, 2048, 1088], P(('fsdp', 'tensor'), 'ctx'), may hold values from -6 to 6
- cont_cot: bfloat16 [8, 1536, 1088], P(('fsdp', 'tensor'), 'ctx'), may hold values from -6 to 6
Outputs:
- prompt_out: bfloat16 [8, 2048, 1088], P(('fsdp', 'tensor'), 'ctx')
- cont_out: bfloat16 [8, 1536, 1088], P(('fsdp', 'tensor'), 'ctx')
- prompt_grad: bfloat16 [8, 2048, 1088], P(('fsdp', 'tensor'), 'ctx')
- cont_grad: bfloat16 [8, 1536, 1088], P(('fsdp', 'tensor'), 'ctx')
- grad_ln1_gain: float32 [1088], replicated
- grad_ln1_bias: float32 [1088], replicated
- grad_w_qkv: float32 [1088, 3264], P('fsdp')
- grad_qv_bias: float32 [2, 1088], replicated
- grad_w_out: float32 [1088, 1088], P('fsdp')
- grad_out_bias: float32 [1088], replicated
- grad_ln2_gain: float32 [1088], replicated
- grad_ln2_bias: float32 [1088], replicated
- grad_w_fc: float32 [1088, 4352], P('fsdp', 'tensor')
- grad_fc_bias: float32 [4352], P('tensor')
- grad_w_proj: float32 [4352, 1088], P('tensor', 'fsdp')
- grad_proj_bias: float32 [1088], replicated
The draws below stay inside these ranges and needn't reach their ends.
Inputs may be any that keep to these rules, and one draw needn't show every extreme that they name: `cont_seg`: in each group the numbers never fall along the tokens; each continuation is 1 to 384 consecutive tokens, one exactly 384.
All inputs are finite; a program needn't handle non-finite values.
Results may differ from the reference program's by a relative error of at most 0.012.
The reference program's roundings to bfloat16 on the way count: a program that leaves them out, or rounds other values in their place, can miss the bound.
Values may be sent and summed in bfloat16 or wider, within the bound.
A program may use at most 320 MiB of HBM per device.

```python
import math
import jax
import jax.numpy as jnp
import numpy as np
from jax import lax

D = 1088
HEADS = 17
HEAD = 64
FF = 4352
PROMPT = 2048
CONT_LEN = 384
CONT_TOKENS = 1536
CONTS = 5
GROUPS = 8


def shard_levels(rng, dims, split, least, high):
    gain = 1.0
    for axis_at, parts in split:
        steps = jax.random.uniform(jax.random.fold_in(jax.random.fold_in(rng, 6), axis_at), (parts,), jnp.float32, least / len(split), high / len(split))
        gain = gain * jnp.repeat(jnp.exp(steps), dims[axis_at] // parts).reshape((-1,) + (1,) * (len(dims) - 1 - axis_at))
    return gain


def profile(number_of, total, bound, skew):
    weights = [(1 << 20) // math.isqrt(rank ** skew) + 1 for rank in range(2, number_of + 1)]
    spare, holding = total - bound - (number_of - 1), [1] * (number_of - 1)
    while spare > 0:
        movable = [i for i in range(number_of - 1) if holding[i] < bound]
        mass, budget = sum([weights[i] for i in movable]), spare
        for i in movable:
            more = min(bound - holding[i], max(1, budget * weights[i] // mass), spare)
            holding[i] = holding[i] + more
            spare = spare - more
    return np.array([bound] + holding)


def ragged(own_key, number_of, total, bound, slope):
    if number_of == 2:
        one = jax.random.randint(own_key, (), max(1, total - bound), min(bound, total - 1) + 1)
        return jnp.stack([one, total - one])
    sizes = jnp.asarray(profile(number_of, total, bound, slope), jnp.int32)
    twos = (number_of - 1) // 2
    giver, taker = sizes[1:1 + 2 * twos:2], sizes[2:2 + 2 * twos:2]
    slack = jnp.minimum(giver - 1, bound - taker)
    shifted = jax.random.randint(jax.random.fold_in(own_key, 1), (twos,), 0, 1 << 20) % (slack + 1)
    sizes = sizes.at[1:1 + 2 * twos:2].set(giver - shifted).at[2:2 + 2 * twos:2].set(taker + shifted)
    return sizes[jax.random.permutation(jax.random.fold_in(own_key, 2), number_of)]


def normal_values(stream_key, dims, deviation, bound, pieces=(), kind=jnp.bfloat16):
    entries = deviation * jax.random.normal(stream_key, dims, jnp.float32)
    if pieces:
        entries = entries * shard_levels(stream_key, dims, pieces, -0.22, 0.18)
    return jnp.clip(entries, -bound, bound).astype(kind)


def setup_inputs(seed: int = 0) -> dict:
    key_list = jax.random.split(jax.random.key(seed), 18)
    return {
        "prompt_in": normal_values(key_list[0], (GROUPS, PROMPT, D), 1.0, 6.0, ((0, 8), (1, 4))),
        "cont_in": normal_values(key_list[1], (GROUPS, CONT_TOKENS, D), 1.0, 6.0, ((0, 8), (1, 4))),
        "cont_seg": jax.vmap(lambda own: jnp.searchsorted(jnp.cumsum(ragged(own, CONTS, CONT_TOKENS, CONT_LEN, 0)), jnp.arange(CONT_TOKENS), side="right"))(jax.random.split(key_list[2], GROUPS)).reshape((GROUPS, CONT_TOKENS)).astype(jnp.int32),
        "ln1_gain": jnp.clip(1.0 + 0.18 * jax.random.normal(key_list[3], (D,), jnp.float32), 0.1, 1.9),
        "ln1_bias": normal_values(key_list[4], (D,), 0.5, 3.0, (), jnp.float32),
        "w_qkv": normal_values(key_list[5], (D, 3 * D), D ** -0.5, 0.1875, ((0, 2),), jnp.float32),
        "qv_bias": normal_values(key_list[6], (2, D), 0.5, 3.0, (), jnp.float32),
        "w_out": normal_values(key_list[7], (D, D), (max(D // 64, 1)) ** -0.5, 1.5, ((0, 2),), jnp.float32),
        "out_bias": normal_values(key_list[8], (D,), 0.5, 3.0, (), jnp.float32),
        "ln2_gain": jnp.clip(1.0 + 0.18 * jax.random.normal(key_list[9], (D,), jnp.float32), 0.1, 1.9),
        "ln2_bias": normal_values(key_list[10], (D,), 0.5, 3.0, (), jnp.float32),
        "w_fc": normal_values(key_list[11], (D, FF), D ** -0.5, 0.1875, ((0, 2), (1, 4)), jnp.float32),
        "fc_bias": normal_values(key_list[12], (FF,), 0.5, 3.0, ((0, 4),), jnp.float32),
        "w_proj": normal_values(key_list[13], (FF, D), FF ** -0.5, 0.09375, ((0, 4), (1, 2)), jnp.float32),
        "proj_bias": normal_values(key_list[14], (D,), 0.5, 3.0, (), jnp.float32),
        "prompt_cot": normal_values(key_list[15], (GROUPS, PROMPT, D), 1.0, 6.0, ((0, 8), (1, 4))),
        "cont_cot": normal_values(key_list[16], (GROUPS, CONT_TOKENS, D), 1.0, 6.0, ((0, 8), (1, 4))),
    }


@jax.custom_vjp
def low(v):
    return lax.optimization_barrier(v.astype(jnp.bfloat16)).astype(jnp.float32)

@jax.custom_vjp
def low_back(v):
    return v

def low_keep(v):
    return (low(v), None)

def low_pass(kept, grad):
    return (grad,)

def back_keep(v):
    return (v, None)

def back_low(kept, grad):
    return (low(grad),)
low.defvjp(low_keep, low_pass)
low_back.defvjp(back_keep, back_low)

def matmul(left_op, right_op):
    return jnp.dot(left_op, right_op, precision=lax.Precision.HIGHEST)

def layer_norm(values, norm_gain, norm_bias):
    average = lax.optimization_barrier(jnp.mean(values, axis=-1, keepdims=True))
    centred = values - average
    variance = lax.optimization_barrier(jnp.mean(centred * centred, axis=-1, keepdims=True))
    return centred * lax.rsqrt(variance + 1e-05) * norm_gain + norm_bias

def to_heads(values):
    return jnp.swapaxes(values.reshape(values.shape[0], HEADS, HEAD), 0, 1)

def allowed_pairs(labels):
    length_all = PROMPT + CONT_TOKENS
    places = jnp.arange(length_all, dtype=jnp.int32)
    numbers = jnp.concatenate([jnp.full((PROMPT,), -1, jnp.int32), labels.astype(jnp.int32)])
    key_prompt = places[None, :] < PROMPT
    query_cont = places[:, None] >= PROMPT
    causal = places[None, :] <= places[:, None]
    same_seq = numbers[:, None] == numbers[None, :]
    return key_prompt & (query_cont | causal) | same_seq & causal & jnp.logical_not(key_prompt)

def group_forward(inputs, labels, params):
    ln1_gain, ln1_bias, w_qkv, qv_bias, w_out, out_bias, ln2_gain, ln2_bias, w_fc, fc_bias, w_proj, proj_bias = params
    length_all = inputs.shape[0]
    allowed = allowed_pairs(labels)
    normed = low(layer_norm(inputs, ln1_gain, ln1_bias))
    projected = matmul(normed, low(w_qkv))
    queries = low(low_back(projected[:, :D] + qv_bias[0]))
    keys = low(low_back(projected[:, D:2 * D]))
    values = low(low_back(projected[:, 2 * D:] + qv_bias[1]))

    def one_head(operands):
        query_head, key_head, value_head = operands
        scores = low_back(matmul(query_head, key_head.T) * 0.125)
        scores = jnp.where(allowed, scores, -1e+30)
        probability = jax.nn.softmax(scores, axis=-1)
        return matmul(low(probability), value_head)
    heads_out = lax.map(jax.checkpoint(one_head), (to_heads(queries), to_heads(keys), to_heads(values)))
    attended = low(low_back(jnp.swapaxes(heads_out, 0, 1).reshape(length_all, D)))
    hidden = inputs + low_back(matmul(attended, low(w_out))) + out_bias
    mlp_in = low(layer_norm(hidden, ln2_gain, ln2_bias))
    pre_act = low_back(matmul(mlp_in, low(w_fc)) + fc_bias)
    activated = low(jax.nn.gelu(pre_act, approximate=True))
    return hidden + matmul(activated, low(w_proj)) + proj_bias

def reference(prompt_in, cont_in, cont_seg, ln1_gain, ln1_bias, w_qkv, qv_bias, w_out, out_bias, ln2_gain, ln2_bias, w_fc, fc_bias, w_proj, proj_bias, prompt_cot, cont_cot):
    inputs = jnp.concatenate([prompt_in, cont_in], axis=1).astype(jnp.float32)
    cotangent = jnp.concatenate([prompt_cot, cont_cot], axis=1).astype(jnp.float32)
    params = tuple((item.astype(jnp.float32) for item in (ln1_gain, ln1_bias, w_qkv, qv_bias, w_out, out_bias, ln2_gain, ln2_bias, w_fc, fc_bias, w_proj, proj_bias)))
    checked = jax.checkpoint(group_forward)

    def forward(weights_all, rows_all):
        return lax.map(lambda operands: checked(operands[0], operands[1], weights_all), (rows_all, cont_seg))
    result, pullback = jax.vjp(forward, params, inputs)
    gradients, grad_inputs = pullback(cotangent)
    return (result[:, :PROMPT].astype(jnp.bfloat16), result[:, PROMPT:].astype(jnp.bfloat16), grad_inputs[:, :PROMPT].astype(jnp.bfloat16), grad_inputs[:, PROMPT:].astype(jnp.bfloat16), gradients[0], gradients[1], gradients[2], gradients[3], gradients[4], gradients[5], gradients[6], gradients[7], gradients[8], gradients[9], gradients[10], gradients[11])
```

```python
import functools

import jax
import jax.numpy as jnp
from jax import lax
from jax.experimental import pallas as pl
from jax.experimental.pallas import tpu as pltpu
from jax.sharding import PartitionSpec as P

HEADS = 17
HEAD = 64


def passed_along(value, axis, steps):
    count = lax.axis_size(axis)
    leading, last = (max(0, -steps), min(count, count - steps))
    return lax.ppermute(value, axis, [(source, source + steps) for source in range(leading, last)])


def layer_norm(values, norm_gain, norm_bias):
    average = jnp.mean(values, axis=-1, keepdims=True)
    centred = values - average
    variance = jnp.mean(centred * centred, axis=-1, keepdims=True)
    return centred * lax.rsqrt(variance + 1e-05) * norm_gain + norm_bias


def gelu_tanh(values):
    return jax.nn.gelu(values, approximate=True)


def inner_first(left_op, right_op):
    return lax.dot_general(
        left_op, right_op, (((0,), (0,)), ((), ())), preferred_element_type=jnp.float32
    )


def inner_last(left_op, right_op):
    return lax.dot_general(
        left_op, right_op, (((1,), (1,)), ((), ())), preferred_element_type=jnp.float32
    )


def to_heads(values):
    return jnp.swapaxes(values.reshape(values.shape[0], HEADS, HEAD), 0, 1)


def from_heads(values):
    return jnp.swapaxes(values, 0, 1).reshape(values.shape[1], values.shape[0] * values.shape[2])


def fetch_prompt(rows_kv):
    return lax.all_gather(rows_kv, "ctx", axis=0, tiled=True)


def local_rows(
    prompt_in,
    cont_in,
    cont_seg,
    ln1_gain,
    ln1_bias,
    w_qkv,
    qv_bias,
    w_out,
    out_bias,
    ln2_gain,
    ln2_bias,
    w_fc,
    fc_bias,
    w_proj,
    proj_bias,
    prompt_cot,
    cont_cot,
):
    model_width = prompt_in.shape[2]
    prompt_rows = prompt_in.shape[1]
    cont_rows = cont_in.shape[1]
    row_count = prompt_rows + cont_rows
    ctx_count = lax.axis_size("ctx")
    ctx_place = lax.axis_index("ctx")
    prompt_total = prompt_rows * ctx_count
    qkv_full, out_full = (
        lax.all_gather(w_qkv.astype(jnp.bfloat16), "fsdp", axis=0, tiled=True),
        lax.all_gather(w_out.astype(jnp.bfloat16), "fsdp", axis=0, tiled=True),
    )
    fc_full, proj_full = (
        lax.all_gather(w_fc.astype(jnp.bfloat16), "fsdp", axis=0, tiled=True),
        lax.all_gather(w_proj.astype(jnp.bfloat16), "fsdp", axis=1, tiled=True),
    )
    row_ids = jnp.arange(row_count, dtype=jnp.int32)
    labels_all = cont_seg[0]
    own_labels = lax.dynamic_slice_in_dim(labels_all, ctx_place * cont_rows, cont_rows)
    earlier_labels = lax.dynamic_slice_in_dim(
        labels_all, jnp.maximum(ctx_place - 1, 0) * cont_rows, cont_rows
    )
    query_labels = jnp.concatenate([jnp.full((prompt_rows,), -1, jnp.int32), own_labels])
    query_prompt = ctx_place * prompt_rows + row_ids
    query_cont = ctx_place * cont_rows + row_ids - prompt_rows
    is_cont = row_ids >= prompt_rows
    prompt_ids = jnp.arange(prompt_total, dtype=jnp.int32)
    near_ids = (ctx_place - 1) * cont_rows + jnp.arange(2 * cont_rows, dtype=jnp.int32)
    near_labels = jnp.concatenate([earlier_labels, own_labels])
    allowed_far = is_cont[:, None] | (prompt_ids[None, :] <= query_prompt[:, None])
    allowed_near = (
        (query_labels[:, None] == near_labels[None, :])
        & (near_ids[None, :] <= query_cont[:, None])
        & (near_ids[None, :] >= 0)
    )
    allowed = jnp.concatenate([allowed_far, allowed_near], 1)
    inputs = jnp.concatenate([prompt_in[0], cont_in[0]], 0).astype(jnp.float32)
    normed, norm1_back = jax.vjp(layer_norm, inputs, ln1_gain, ln1_bias)
    normed_low = normed.astype(jnp.bfloat16)
    projected = jnp.dot(normed_low, qkv_full, preferred_element_type=jnp.float32)
    queries = (projected[:, :model_width] + qv_bias[0]).astype(jnp.bfloat16)
    key_value = jnp.concatenate(
        [projected[:, model_width : 2 * model_width], projected[:, 2 * model_width :] + qv_bias[1]],
        1,
    ).astype(jnp.bfloat16)
    own_cont_kv = key_value[prompt_rows:]
    earlier_kv = passed_along(own_cont_kv, "ctx", 1)
    prompt_kv = fetch_prompt(key_value[:prompt_rows])
    keys_all = jnp.concatenate([prompt_kv, earlier_kv, own_cont_kv], 0)
    query_heads = to_heads(queries)
    key_heads = to_heads(keys_all[:, :model_width])
    value_heads = to_heads(keys_all[:, model_width:])

    def head_forward(operands):
        query_head, key_head, value_head = operands
        scores = inner_last(query_head, key_head) * 0.125
        scores = jnp.where(allowed, scores, -1e30)
        row_max = jnp.max(scores, axis=1, keepdims=True)
        exponent = jnp.exp(scores - row_max)
        row_total = jnp.sum(exponent, axis=1, keepdims=True)
        probability = (exponent / row_total).astype(jnp.bfloat16)
        head_out = jnp.dot(probability, value_head, preferred_element_type=jnp.float32)
        return (head_out.astype(jnp.bfloat16), (row_max + jnp.log(row_total))[:, 0])

    heads_out, logsum = lax.map(head_forward, (query_heads, key_heads, value_heads))
    attended = from_heads(heads_out)
    hidden = inputs + jnp.dot(attended, out_full, preferred_element_type=jnp.float32) + out_bias
    mlp_in, norm2_back = jax.vjp(layer_norm, hidden, ln2_gain, ln2_bias)
    mlp_low = mlp_in.astype(jnp.bfloat16)
    mlp_rows = lax.all_gather(mlp_low, "tensor", axis=0, tiled=True)
    pre_act = jnp.dot(mlp_rows, fc_full, preferred_element_type=jnp.float32) + fc_bias
    activated, gelu_back = jax.vjp(gelu_tanh, pre_act)
    act_low = activated.astype(jnp.bfloat16)
    partial_out = jnp.dot(act_low, proj_full, preferred_element_type=jnp.float32)
    mlp_out = lax.psum_scatter(
        partial_out.astype(jnp.bfloat16), "tensor", scatter_dimension=0, tiled=True
    ).astype(jnp.float32)
    layer_out = (hidden + mlp_out + proj_bias).astype(jnp.bfloat16)
    grad_layer = jnp.concatenate([prompt_cot[0], cont_cot[0]], 0)
    grad_float = grad_layer.astype(jnp.float32)
    grad_proj_bias = jnp.sum(grad_float, axis=0)
    grad_rows = lax.all_gather(grad_layer, "tensor", axis=0, tiled=True)
    grad_w_proj = inner_first(act_low, grad_rows)
    grad_act = inner_last(grad_rows, proj_full)
    grad_pre = gelu_back(grad_act)[0].astype(jnp.bfloat16)
    grad_fc_bias = jnp.sum(grad_pre.astype(jnp.float32), axis=0)
    grad_w_fc = inner_first(mlp_rows, grad_pre)
    grad_mlp_part = inner_last(grad_pre, fc_full)
    grad_mlp_in = lax.psum_scatter(grad_mlp_part, "tensor", scatter_dimension=0, tiled=True)
    grad_hidden_norm, grad_ln2_gain, grad_ln2_bias = norm2_back(grad_mlp_in)
    grad_hidden = grad_float + grad_hidden_norm
    grad_out_bias = jnp.sum(grad_hidden, axis=0)
    grad_branch = grad_hidden.astype(jnp.bfloat16)
    grad_w_out = inner_first(attended, grad_branch)
    grad_attended = inner_last(grad_branch, out_full).astype(jnp.bfloat16)
    prompt_again = fetch_prompt(key_value[:prompt_rows])
    keys_back = jnp.concatenate([prompt_again, earlier_kv, own_cont_kv], 0)
    key_back_heads = to_heads(keys_back[:, :model_width])
    value_back_heads = to_heads(keys_back[:, model_width:])

    def head_backward(operands):
        query_head, key_head, value_head, grad_head, logsum_head = operands
        scores = inner_last(query_head, key_head) * 0.125
        scores = jnp.where(allowed, scores, -1e30)
        probability = jnp.exp(scores - logsum_head[:, None])
        prob_low = probability.astype(jnp.bfloat16)
        grad_prob = inner_last(grad_head, value_head)
        centre = jnp.sum(probability * grad_prob, axis=1, keepdims=True)
        grad_scores = (probability * (grad_prob - centre)).astype(jnp.bfloat16)
        grad_query = jnp.dot(grad_scores, key_head, preferred_element_type=jnp.float32) * 0.125
        grad_key = inner_first(grad_scores, query_head) * 0.125
        grad_value = inner_first(prob_low, grad_head)
        return (grad_query, grad_key, grad_value)

    head_operands = (query_heads, key_back_heads, value_back_heads, to_heads(grad_attended), logsum)
    grad_q_heads, grad_k_heads, grad_v_heads = lax.map(head_backward, head_operands)
    grad_queries = from_heads(grad_q_heads).astype(jnp.bfloat16)
    grad_kv = jnp.concatenate([from_heads(grad_k_heads), from_heads(grad_v_heads)], 1)
    prompt_grad_kv = lax.psum_scatter(
        grad_kv[:prompt_total], "ctx", scatter_dimension=0, tiled=True
    )
    from_later = passed_along(
        grad_kv[prompt_total : prompt_total + cont_rows].astype(jnp.bfloat16), "ctx", -1
    ).astype(jnp.float32)
    cont_grad_kv = grad_kv[prompt_total + cont_rows :] + from_later
    grad_kv_rows = jnp.concatenate([prompt_grad_kv, cont_grad_kv], 0).astype(jnp.bfloat16)
    grad_projected = jnp.concatenate([grad_queries, grad_kv_rows], 1)
    grad_qv_bias = jnp.stack(
        [
            jnp.sum(grad_queries.astype(jnp.float32), axis=0),
            jnp.sum(grad_kv_rows[:, model_width:].astype(jnp.float32), axis=0),
        ]
    )
    grad_w_qkv = inner_first(normed_low, grad_projected)
    grad_normed = inner_last(grad_projected, qkv_full)
    grad_inputs_norm, grad_ln1_gain, grad_ln1_bias = norm1_back(grad_normed)
    grad_inputs = (grad_hidden + grad_inputs_norm).astype(jnp.bfloat16)
    shard_qkv, shard_out = (
        lax.psum_scatter(
            grad_w_qkv.astype(jnp.bfloat16), "fsdp", scatter_dimension=0, tiled=True
        ).astype(jnp.float32),
        lax.psum_scatter(
            grad_w_out.astype(jnp.bfloat16), "fsdp", scatter_dimension=0, tiled=True
        ).astype(jnp.float32),
    )
    sum_qkv, sum_out = lax.psum((shard_qkv, shard_out), ("ctx", "tensor"))
    sum_fc, sum_proj, sum_fc_bias = lax.psum(
        (grad_w_fc, grad_w_proj, grad_fc_bias), ("fsdp", "ctx")
    )
    fsdp_place = lax.axis_index("fsdp")
    fsdp_rows = w_fc.shape[0]
    own_fc = lax.dynamic_slice_in_dim(sum_fc, fsdp_place * fsdp_rows, fsdp_rows, 0)
    own_proj = lax.dynamic_slice_in_dim(sum_proj, fsdp_place * fsdp_rows, fsdp_rows, 1)
    small_sums = lax.psum(
        (
            grad_ln1_gain,
            grad_ln1_bias,
            grad_qv_bias,
            grad_out_bias,
            grad_ln2_gain,
            grad_ln2_bias,
            grad_proj_bias,
        ),
        ("fsdp", "ctx", "tensor"),
    )
    return (
        layer_out[:prompt_rows][None],
        layer_out[prompt_rows:][None],
        grad_inputs[:prompt_rows][None],
        grad_inputs[prompt_rows:][None],
        small_sums[0],
        small_sums[1],
        sum_qkv,
        small_sums[2],
        sum_out,
        small_sums[3],
        small_sums[4],
        small_sums[5],
        own_fc,
        sum_fc_bias,
        own_proj,
        small_sums[6],
    )


PAIRS = 2
TILE = 2 * HEAD
BF16 = jnp.bfloat16
F32 = jnp.float32
LOG2E = 1.4426950408889634
SCALE2 = 0.125 * LOG2E
NN = (((1,), (0,)), ((), ()))
NT = (((1,), (1,)), ((), ()))
TN = (((0,), (0,)), ((), ()))


def dot(left_op, right_op, dims=NN):
    return lax.dot_general(left_op, right_op, dims, preferred_element_type=F32)


def swap(value, axis, bit):
    count = lax.axis_size(axis)
    return lax.ppermute(value, axis, [(place, place ^ bit) for place in range(count)])


def turn(value, axis, steps):
    count = lax.axis_size(axis)
    return lax.ppermute(value, axis, [(place, (place + steps) % count) for place in range(count)])


def canonical(by_distance, place):
    low, high = place % 2 == 1, place >= 2
    a, b, c, d = by_distance
    a, b, c, d = (
        jnp.where(low, b, a),
        jnp.where(low, a, b),
        jnp.where(low, d, c),
        jnp.where(low, c, d),
    )
    return [
        jnp.where(high, c, a),
        jnp.where(high, d, b),
        jnp.where(high, a, c),
        jnp.where(high, b, d),
    ]


def in_order(own, other, place):
    first = place == 0
    return jnp.where(first, own, other), jnp.where(first, other, own)


def project_kernel(
    place_ref, x_ref, w_ref, gain_ref, bias_ref, col_bias_ref, *refs
):
    norm_ref, q_ref, k_ref, v_ref, kt_ref, vt_ref = refs[-6:]
    values = x_ref[...].astype(F32)
    average = jnp.mean(values, axis=1, keepdims=True)
    centred = values - average
    variance = jnp.mean(centred * centred, axis=1, keepdims=True)
    normed = (centred * lax.rsqrt(variance + 1e-05) * gain_ref[...] + bias_ref[...]).astype(BF16)
    norm_ref[0] = normed
    tiles = q_ref.shape[0]
    width = tiles * TILE
    for part, out_ref, flip_ref in ((0, q_ref, None), (1, k_ref, kt_ref), (2, v_ref, vt_ref)):
        cols = slice(part * width, (part + 1) * width)
        out = (dot(normed, w_ref[:, cols]) + col_bias_ref[:, cols]).astype(BF16)
        for tile in range(tiles):
            piece = out[:, tile * TILE : (tile + 1) * TILE]
            out_ref[tile, 0] = piece
            if flip_ref is not None:
                flip_ref[tile, 0] = piece.T


def project(place, rows, w_own, gain, bias, col_bias, before, count):
    row_count, width = rows.shape
    tiles = w_own.shape[1] // (3 * TILE)
    full = lambda *shape: pl.BlockSpec(shape, lambda i, p: (0,) * len(shape))
    tall = pl.BlockSpec((tiles, 1, row_count, TILE), lambda i, p: (0, p[0], 0, 0))
    flat = pl.BlockSpec((tiles, 1, TILE, row_count), lambda i, p: (0, p[0], 0, 0))
    tall_shape = jax.ShapeDtypeStruct((tiles, count, row_count, TILE), BF16)
    flat_shape = jax.ShapeDtypeStruct((tiles, count, TILE, row_count), BF16)
    operands = (rows, w_own, gain[None], bias[None], col_bias[None])
    aliases = {}
    if before is not None:
        aliases = {1 + len(operands) + i: i for i in range(len(before))}
        operands = operands + tuple(before)
    return pl.pallas_call(
        project_kernel,
        grid_spec=pltpu.PrefetchScalarGridSpec(
            num_scalar_prefetch=1,
            grid=(1,),
            in_specs=[
                full(row_count, width),
                full(*w_own.shape),
                full(1, width),
                full(1, width),
                full(1, w_own.shape[1]),
            ]
            + [pl.BlockSpec(memory_space=pl.ANY)] * len(aliases),
            out_specs=[
                pl.BlockSpec((1, row_count, width), lambda i, p: (p[0], 0, 0)),
                tall,
                tall,
                tall,
                flat,
                flat,
            ],
        ),
        out_shape=[
            jax.ShapeDtypeStruct((count, row_count, width), BF16),
            tall_shape,
            tall_shape,
            tall_shape,
            flat_shape,
            flat_shape,
        ],
        input_output_aliases=aliases,
        compiler_params=pltpu.CompilerParams(vmem_limit_bytes=48 << 20),
        cost_estimate=pl.CostEstimate(
            flops=2 * row_count * width * w_own.shape[1], bytes_accessed=12 << 20, transcendentals=0
        ),
        name="project",
    )(place.reshape(1), *operands)


def halves(values):
    lane = lax.broadcasted_iota(jnp.int32, values.shape, 1)
    zero = jnp.zeros_like(values)
    return [jnp.where(lane < HEAD, values, zero), jnp.where(lane >= HEAD, values, zero)]


def own_mask(rows):
    key_at = lax.broadcasted_iota(jnp.int32, (rows, rows), 0)
    query_at = lax.broadcasted_iota(jnp.int32, (rows, rows), 1)
    return key_at <= query_at


def attend_kernel(
    prompt_rows, items_ref, q_ref, k_ref, vt_ref, seg_col_ref, seg_row_ref, o_ref, lse_ref, acc
):
    item = items_ref[pl.program_id(0)]
    count, row_count = k_ref.shape[1], k_ref.shape[2]
    cont_rows = row_count - prompt_rows

    def part(queries, block, start, size, mask, before):
        keys = k_ref[0, block, pl.ds(start, size), :]
        scores = [dot(keys, query, NT) for query in queries]
        if mask is not None:
            scores = [jnp.where(mask, score, -1e30) for score in scores]
        tops = [jnp.max(score, axis=0, keepdims=True) for score in scores]
        if before is not None:
            tops = [jnp.maximum(top, state[0]) for top, state in zip(tops, before)]
        exps = [jnp.exp2(score * SCALE2 - top * SCALE2) for score, top in zip(scores, tops)]
        totals = [jnp.sum(exp, axis=0, keepdims=True) for exp in exps]
        after = []
        for head in range(2):
            rows = slice(head * HEAD, (head + 1) * HEAD)
            cols = slice(0, queries[head].shape[0])
            out = dot(vt_ref[0, block, rows, pl.ds(start, size)], exps[head].astype(BF16))
            total = totals[head]
            if before is None:
                acc[rows, cols] = out
            else:
                shrink = jnp.exp2((before[head][0] - tops[head]) * SCALE2)
                total = total + before[head][1] * shrink
                acc[rows, cols] = acc[rows, cols] * shrink + out
            after.append((tops[head], total))
        return after

    def finish(block, start, size, states):
        for head in range(2):
            rows = slice(head * HEAD, (head + 1) * HEAD)
            top, total = states[head]
            acc[rows, :size] = acc[rows, :size] / total
            lse_ref[0, block, head : head + 1, pl.ds(start, size)] = top * SCALE2 + jnp.log2(total)
        o_ref[0, block, pl.ds(start, size), :] = acc[:, :size].T.astype(BF16)

    def over_prompt(queries, blocks, states):
        return lax.fori_loop(
            0, blocks, lambda c, states: part(queries, c, 0, prompt_rows, None, states), states
        )

    @pl.when(item < count)
    def _():
        queries = halves(q_ref[0, item, :prompt_rows, :])
        states = part(queries, item, 0, prompt_rows, own_mask(prompt_rows), None)
        finish(item, 0, prompt_rows, over_prompt(queries, item, states))

    @pl.when(item >= count)
    def _():
        block = item - count
        before = jnp.maximum(block - 1, 0)
        labels = seg_row_ref[block]
        queries = halves(q_ref[0, block, prompt_rows:, :])
        own = own_mask(cont_rows) & (seg_col_ref[block] == labels)
        near = (seg_col_ref[before] == labels) & (block > 0)
        states = part(queries, block, prompt_rows, cont_rows, own, None)
        states = part(queries, before, prompt_rows, cont_rows, near, states)
        finish(block, prompt_rows, cont_rows, over_prompt(queries, count, states))


def attend(pair, items, q, k, vt, seg_col, seg_row, prompt_rows):
    _, count, row_count, _ = q.shape
    cont_rows = row_count - prompt_rows
    pick = lambda i, s: (pair, 0, 0, 0)
    first = lambda i, s: (0, 0, 0, 0)
    labels = lambda i, s: (0, 0, 0)
    pairs = items.shape[0] * row_count // 2 * count * row_count // 2
    return pl.pallas_call(
        functools.partial(attend_kernel, prompt_rows),
        grid_spec=pltpu.PrefetchScalarGridSpec(
            num_scalar_prefetch=1,
            grid=(items.shape[0],),
            in_specs=[
                pl.BlockSpec((1, count, row_count, TILE), pick),
                pl.BlockSpec((1, count, row_count, TILE), pick),
                pl.BlockSpec((1, count, TILE, row_count), pick),
                pl.BlockSpec((count, cont_rows, 1), labels),
                pl.BlockSpec((count, 1, cont_rows), labels),
            ],
            out_specs=[
                pl.BlockSpec((1, count, row_count, TILE), first),
                pl.BlockSpec((1, count, 2, row_count), first),
            ],
            scratch_shapes=[pltpu.VMEM((TILE, max(prompt_rows, cont_rows)), F32)],
        ),
        out_shape=[
            jax.ShapeDtypeStruct((1, count, row_count, TILE), BF16),
            jax.ShapeDtypeStruct((1, count, 2, row_count), F32),
        ],
        compiler_params=pltpu.CompilerParams(vmem_limit_bytes=48 << 20),
        cost_estimate=pl.CostEstimate(
            flops=4 * 4 * TILE * pairs, bytes_accessed=6 << 20, transcendentals=2 * pairs
        ),
        name="attend",
    )(items, q, k, vt, seg_col, seg_row)


def attend_back_kernel(
    prompt_rows,
    items_ref,
    q_ref,
    k_ref,
    v_ref,
    kt_ref,
    do_ref,
    o_ref,
    lse_ref,
    seg_col_ref,
    seg_row_ref,
    dq_ref,
    dk_ref,
    dv_ref,
    dk_acc,
    dv_acc,
    dq_acc,
):
    step = pl.program_id(0)
    item = items_ref[step]
    count, row_count = k_ref.shape[1], k_ref.shape[2]
    cont_rows = row_count - prompt_rows

    @pl.when(step == 0)
    def _():
        dk_acc[...] = jnp.zeros_like(dk_acc)
        dv_acc[...] = jnp.zeros_like(dv_acc)
        dq_ref[...] = jnp.zeros_like(dq_ref)

    def part(given, block, start, size, mask, first):
        rows = pl.ds(start, size)
        for head in range(2):
            query, grad, lse, centre = (entry[head] for entry in given)
            cols = slice(0, query.shape[0])
            own = slice(head * HEAD, (head + 1) * HEAD)
            scores = dot(k_ref[0, block, rows, :], query, NT)
            if mask is not None:
                scores = jnp.where(mask, scores, -1e30)
            probability = jnp.exp2(scores * SCALE2 - lse)
            grad_probability = dot(v_ref[0, block, rows, :], grad, NT)
            grad_scores = (probability * (grad_probability - centre)).astype(BF16)
            dv_acc[block, rows, :] += dot(probability.astype(BF16), grad)
            dk_acc[block, rows, :] += dot(grad_scores, query)
            out = dot(kt_ref[0, block, own, rows], grad_scores)
            if first:
                dq_acc[own, cols] = out
            else:
                dq_acc[own, cols] += out

    def setup(block, start, size):
        rows = pl.ds(start, size)
        grad = do_ref[0, block, rows, :]
        product = (grad.astype(F32) * o_ref[0, block, rows, :].astype(F32)).T
        centres = [
            jnp.sum(product[head * HEAD : (head + 1) * HEAD], axis=0, keepdims=True)
            for head in range(2)
        ]
        lses = [lse_ref[0, block, head : head + 1, rows] for head in range(2)]
        return halves(q_ref[0, block, rows, :]), halves(grad), lses, centres

    def finish(block, start, size):
        dq_ref[0, block, pl.ds(start, size), :] = (dq_acc[:, :size].T * 0.125).astype(BF16)

    @pl.when(item < count)
    def _():
        given = setup(item, 0, prompt_rows)
        part(given, item, 0, prompt_rows, own_mask(prompt_rows), True)

        @pl.loop(0, item)
        def _(c):
            part(given, c, 0, prompt_rows, None, False)

        finish(item, 0, prompt_rows)

    @pl.when(item >= count)
    def _():
        block = item - count
        before = jnp.maximum(block - 1, 0)
        labels = seg_row_ref[block]
        own = own_mask(cont_rows) & (seg_col_ref[block] == labels)
        near = (seg_col_ref[before] == labels) & (block > 0)
        given = setup(block, prompt_rows, cont_rows)
        part(given, block, prompt_rows, cont_rows, own, True)
        part(given, before, prompt_rows, cont_rows, near, False)

        @pl.loop(0, count)
        def _(c):
            part(given, c, 0, prompt_rows, None, False)

        finish(block, prompt_rows, cont_rows)

    @pl.when(step == pl.num_programs(0) - 1)
    def _():
        dk_ref[0] = (dk_acc[...] * 0.125).astype(BF16)
        dv_ref[0] = dv_acc[...].astype(BF16)


def attend_back(pair, items, q, k, v, kt, do, o, lse, seg_col, seg_row, prompt_rows):
    _, count, row_count, _ = q.shape
    cont_rows = row_count - prompt_rows
    pick = lambda i, s: (pair, 0, 0, 0)
    first = lambda i, s: (0, 0, 0, 0)
    labels = lambda i, s: (0, 0, 0)
    tall = pl.BlockSpec((1, count, row_count, TILE), pick)
    own = pl.BlockSpec((1, count, row_count, TILE), first)
    pairs = items.shape[0] * row_count // 2 * count * row_count // 2
    return pl.pallas_call(
        functools.partial(attend_back_kernel, prompt_rows),
        grid_spec=pltpu.PrefetchScalarGridSpec(
            num_scalar_prefetch=1,
            grid=(items.shape[0],),
            in_specs=[
                tall,
                tall,
                tall,
                pl.BlockSpec((1, count, TILE, row_count), pick),
                own,
                own,
                pl.BlockSpec((1, count, 2, row_count), first),
                pl.BlockSpec((count, cont_rows, 1), labels),
                pl.BlockSpec((count, 1, cont_rows), labels),
            ],
            out_specs=[own] * 3,
            scratch_shapes=[
                pltpu.VMEM((count, row_count, TILE), F32),
                pltpu.VMEM((count, row_count, TILE), F32),
                pltpu.VMEM((TILE, max(prompt_rows, cont_rows)), F32),
            ],
        ),
        out_shape=[jax.ShapeDtypeStruct((1, count, row_count, TILE), BF16)] * 3,
        compiler_params=pltpu.CompilerParams(vmem_limit_bytes=56 << 20),
        cost_estimate=pl.CostEstimate(
            flops=10 * 4 * TILE * pairs, bytes_accessed=9 << 20, transcendentals=2 * pairs
        ),
        name="attend_back",
    )(items, q, k, v, kt, do, o, lse, seg_col, seg_row)


GELU_RATE = 0.7978845608028654


def gelu_both(values):
    square = values * values
    bent = jnp.tanh(GELU_RATE * (values + 0.044715 * square * values))
    half = 0.5 * (1.0 + bent)
    slope = half + 0.5 * values * (1.0 - bent * bent) * (GELU_RATE * (1.0 + 0.134145 * square))
    return values * half, slope


def mlp_kernel(
    x_ref,
    g_ref,
    xt_ref,
    gt_ref,
    b_ref,
    wf_ref,
    wp_ref,
    out_ref,
    gm_ref,
    gwf_ref,
    gwp_ref,
    gb_ref,
    act_s,
    gp_s,
):
    hidden, width = wf_ref.shape[2], x_ref.shape[1]

    def over(total, body):
        whole = total // 256

        @pl.loop(0, whole)
        def _(i):
            body(pl.ds(pl.multiple_of(i * 256, 256), 256))

        if total % 256:
            body(pl.ds(whole * 256, total % 256))

    def up(cols):
        pre_act = dot(x_ref[...], wf_ref[0, :, cols]) + b_ref[0, :, cols]
        grad_act = dot(g_ref[...], wp_ref[0, :, cols])
        activated, slope = gelu_both(pre_act)
        grad_pre = (grad_act * slope).astype(BF16)
        act_s[:, cols] = activated.astype(BF16)
        gp_s[:, cols] = grad_pre
        gb_ref[0, :, cols] = jnp.sum(grad_pre.astype(F32), axis=0, keepdims=True)

    def weights(cols):
        gwf_ref[0, :, cols] = dot(xt_ref[...], gp_s[:, cols]).astype(BF16)
        gwp_ref[0, :, cols] = dot(gt_ref[...], act_s[:, cols]).astype(BF16)

    over(hidden, up)
    over(hidden, weights)

    @pl.when(pl.program_id(0) == 0)
    def _():
        def down(rows):
            out_ref[:, rows] = dot(act_s[...], wp_ref[0, rows, :], NT)
            gm_ref[:, rows] = dot(gp_s[...], wf_ref[0, rows, :], NT)

        over(width, down)

    @pl.when(pl.program_id(0) > 0)
    def _():
        def down(rows):
            out_ref[:, rows] += dot(act_s[...], wp_ref[0, rows, :], NT)
            gm_ref[:, rows] += dot(gp_s[...], wf_ref[0, rows, :], NT)

        over(width, down)


def mlp(x, g, xt, gt, bias, wf, wp):
    rows, width = x.shape
    parts, _, hidden = wf.shape
    full = lambda *shape: pl.BlockSpec(shape, lambda k: (0, 0))
    each = lambda *shape: pl.BlockSpec((1,) + shape, lambda k: (k, 0, 0))
    return pl.pallas_call(
        mlp_kernel,
        grid=(parts,),
        in_specs=[
            full(rows, width),
            full(rows, width),
            full(width, rows),
            full(width, rows),
            each(1, hidden),
            each(width, hidden),
            each(width, hidden),
        ],
        out_specs=[
            full(rows, width),
            full(rows, width),
            each(width, hidden),
            each(width, hidden),
            each(1, hidden),
        ],
        out_shape=[
            jax.ShapeDtypeStruct((rows, width), F32),
            jax.ShapeDtypeStruct((rows, width), F32),
            jax.ShapeDtypeStruct(wf.shape, BF16),
            jax.ShapeDtypeStruct(wf.shape, BF16),
            jax.ShapeDtypeStruct((parts, 1, hidden), F32),
        ],
        scratch_shapes=[pltpu.VMEM((rows, hidden), BF16)] * 2,
        compiler_params=pltpu.CompilerParams(vmem_limit_bytes=60 << 20),
        cost_estimate=pl.CostEstimate(
            flops=12 * rows * width * hidden * parts,
            bytes_accessed=60 << 20,
            transcendentals=rows * hidden * parts,
        ),
        name="mlp",
    )(x, g, xt, gt, bias, wf, wp)


def project_back_kernel(place_ref, *refs):
    grads, (w_ref, norm_ref, gn_ref, gw_ref, sum_ref, acc) = refs[:-6], refs[-6:]
    step = pl.program_id(0)
    joined = jnp.concatenate([ref[0, 0] for ref in grads], axis=1)
    gn_ref[0] = dot(joined, w_ref[...], NT).astype(BF16)
    sums = jnp.sum(joined.astype(F32), axis=0, keepdims=True)
    normed = norm_ref[0].T

    @pl.when(step == 0)
    def _():
        acc[...] = dot(normed, joined)
        sum_ref[...] = sums

    @pl.when(step > 0)
    def _():
        acc[...] += dot(normed, joined)
        sum_ref[...] += sums

    @pl.when(step == pl.num_programs(0) - 1)
    def _():
        gw_ref[...] = acc[...].astype(BF16)


def project_back(place, grads, w_own, normed):
    count, row_count, width = normed.shape
    cols = w_own.shape[1]
    full = lambda *shape: pl.BlockSpec(shape, lambda i, p: (0, 0))
    return pl.pallas_call(
        project_back_kernel,
        grid_spec=pltpu.PrefetchScalarGridSpec(
            num_scalar_prefetch=1,
            grid=(count,),
            in_specs=[
                pl.BlockSpec((1, 1, row_count, TILE), lambda i, p: (0, (count - 1 - i) ^ p[0], 0, 0))
            ]
            * len(grads)
            + [
                full(width, cols),
                pl.BlockSpec((1, row_count, width), lambda i, p: ((count - 1 - i) ^ p[0], 0, 0)),
            ],
            out_specs=[
                pl.BlockSpec((1, row_count, width), lambda i, p: (count - 1 - i, 0, 0)),
                full(width, cols),
                full(1, cols),
            ],
            scratch_shapes=[pltpu.VMEM((width, cols), F32)],
        ),
        out_shape=[
            jax.ShapeDtypeStruct((count, row_count, width), BF16),
            jax.ShapeDtypeStruct((width, cols), BF16),
            jax.ShapeDtypeStruct((1, cols), F32),
        ],
        compiler_params=pltpu.CompilerParams(vmem_limit_bytes=56 << 20),
        cost_estimate=pl.CostEstimate(
            flops=4 * count * row_count * width * cols,
            bytes_accessed=30 << 20,
            transcendentals=0,
        ),
        name="project_back",
    )(place.reshape(1), *grads, w_own, normed)


def own_columns(matrix, place):
    width = matrix.shape[1] // 3
    own = 2 * PAIRS * HEAD
    blank = jnp.zeros((matrix.shape[0], TILE - HEAD), matrix.dtype)
    pieces = []
    for part in range(3):
        whole = matrix[:, part * width : (part + 1) * width]
        pieces += [
            lax.dynamic_slice_in_dim(whole, place * own, own, 1),
            whole[:, width - HEAD :],
            blank,
        ]
    return jnp.concatenate(pieces, axis=1)


def local_heads(
    prompt_in,
    cont_in,
    cont_seg,
    ln1_gain,
    ln1_bias,
    w_qkv,
    qv_bias,
    w_out,
    out_bias,
    ln2_gain,
    ln2_bias,
    w_fc,
    fc_bias,
    w_proj,
    proj_bias,
    prompt_cot,
    cont_cot,
):
    width = prompt_in.shape[2]
    prompt_rows, cont_rows = prompt_in.shape[1], cont_in.shape[1]
    row_count = prompt_rows + cont_rows
    count = lax.axis_size("ctx")
    place = lax.axis_index("ctx")
    core = place % 2
    fsdp = lax.axis_index("fsdp")
    tensor = lax.axis_index("tensor")
    tensors = lax.axis_size("tensor")
    own_width = 2 * PAIRS * HEAD
    half = w_fc.shape[0]
    quarter = half // 2

    w_mine = own_columns(w_qkv, place).astype(BF16)
    w_own = jnp.concatenate(in_order(w_mine, swap(w_mine, "fsdp", 1), fsdp), axis=0)
    zero_bias = jnp.zeros_like(qv_bias[0])
    col_bias = own_columns(jnp.concatenate([qv_bias[0], zero_bias, qv_bias[1]])[None], place)[0]

    rows_own = jnp.concatenate([prompt_in[0], cont_in[0]], axis=0)
    rows_across = swap(rows_own, "ctx", 2)
    rows_beside = swap(rows_own, "ctx", 1)
    rows_corner = swap(rows_across, "ctx", 1)
    made = None
    for distance, rows in enumerate((rows_own, rows_beside, rows_across, rows_corner)):
        made = project(place ^ distance, rows, w_own, ln1_gain, ln1_bias, col_bias, made, count)
    normed, q, k, v, kt, vt = made

    fc_mine = lax.dynamic_slice_in_dim(w_fc, core * quarter, quarter, 0).astype(BF16)
    proj_mine = lax.dynamic_slice_in_dim(w_proj, core * quarter, quarter, 1).astype(BF16).T
    fc_parts = [jnp.stack(in_order(fc_mine, swap(fc_mine, "fsdp", 1), fsdp))]
    proj_parts = [proj_mine]
    for _ in range(tensors - 1):
        fc_parts.append(turn(fc_parts[-1], "tensor", 1))
        proj_parts.append(turn(proj_parts[-1], "tensor", 1))
    fc_half = jnp.stack(fc_parts)
    proj_stack = jnp.stack(proj_parts)
    proj_half = jnp.stack(in_order(proj_stack, swap(proj_stack, "fsdp", 1), fsdp), axis=1)
    fc_all = jnp.stack(in_order(fc_half, swap(fc_half, "ctx", 1), core), axis=2)
    proj_all = jnp.stack(in_order(proj_half, swap(proj_half, "ctx", 1), core), axis=2)
    fc_all = fc_all.reshape(tensors, width, w_fc.shape[1])
    proj_all = proj_all.reshape(tensors, width, w_fc.shape[1])
    fc_bias_parts = [fc_bias[None]]
    for _ in range(tensors - 1):
        fc_bias_parts.append(turn(fc_bias_parts[-1], "tensor", 1))
    fc_bias_all = jnp.stack(fc_bias_parts)
    out_mine = w_out.astype(BF16)
    out_full = jnp.concatenate(in_order(out_mine, swap(out_mine, "fsdp", 1), fsdp), axis=0)

    labels = cont_seg[0].reshape(count, cont_rows)
    seg_col, seg_row = labels[:, :, None], labels[:, None, :]
    every = jnp.arange(2 * count, dtype=jnp.int32)
    mine = jnp.stack([place, place + count]).astype(jnp.int32)
    heads_out, lses, returned = [], [], [[] for _ in range(count)]
    for pair in range(PAIRS + 1):
        out, lse = attend(
            pair, every if pair < PAIRS else mine, q, k, vt, seg_col, seg_row, prompt_rows
        )
        heads_out.append(out)
        lses.append(lse)
        if pair < PAIRS:
            for distance in range(count):
                piece = lax.dynamic_index_in_dim(out[0], place ^ distance, 0, False)
                returned[distance].append(swap(piece, "ctx", distance) if distance else piece)
        else:
            last_out = lax.dynamic_index_in_dim(out[0], place, 0, False)[:, :HEAD]
    attended = jnp.concatenate(
        canonical([jnp.concatenate(entry, axis=1) for entry in returned], place) + [last_out],
        axis=1,
    )

    inputs = rows_own.astype(F32)
    hidden = inputs + dot(attended, out_full) + out_bias
    mlp_in, norm2_back = jax.vjp(layer_norm, hidden, ln2_gain, ln2_bias)
    mlp_low = mlp_in.astype(BF16)
    grad_layer = jnp.concatenate([prompt_cot[0], cont_cot[0]], axis=0)
    grad_float = grad_layer.astype(F32)
    mlp_out, grad_mlp_in, grad_fc, grad_proj, grad_fc_bias = mlp(
        mlp_low, grad_layer, mlp_low.T, grad_layer.T, fc_bias_all, fc_all, proj_all
    )
    layer_out = (hidden + mlp_out + proj_bias).astype(BF16)
    grad_proj_bias = jnp.sum(grad_float, axis=0)
    grad_hidden_norm, grad_ln2_gain, grad_ln2_bias = norm2_back(grad_mlp_in)
    grad_hidden = grad_float + grad_hidden_norm
    grad_out_bias = jnp.sum(grad_hidden, axis=0)
    grad_branch = grad_hidden.astype(BF16)
    grad_attended = dot(grad_branch, out_full, NT).astype(BF16)
    grad_w_out = dot(attended, grad_branch, TN).astype(BF16)

    split = (tensors, 2, 2, quarter, w_fc.shape[1])

    def over_cores(grad):
        grad = grad.reshape(split)
        other = lax.dynamic_index_in_dim(grad, 1 - core, 2, False)
        return lax.dynamic_index_in_dim(grad, core, 2, False).astype(F32) + swap(
            other, "ctx", 1
        ).astype(F32)

    def over_tensor(parts):
        total = parts[tensors - 1]
        for distance in range(tensors - 2, -1, -1):
            total = parts[distance] + turn(total.astype(BF16), "tensor", -1).astype(F32)
        return total

    def over_fsdp(grad, axis):
        other = lax.dynamic_index_in_dim(grad, 1 - fsdp, axis, False).astype(BF16)
        return lax.dynamic_index_in_dim(grad, fsdp, axis, False) + swap(other, "fsdp", 1).astype(F32)

    fc_sum = over_fsdp(over_tensor(over_cores(grad_fc)), 0)
    proj_sum = over_tensor(over_fsdp(over_cores(grad_proj), 1))
    both = jnp.stack([fc_sum, proj_sum]).astype(BF16)
    both = both.astype(F32) + swap(both, "ctx", 2).astype(F32)
    both = jnp.concatenate(in_order(both, swap(both, "ctx", 1), core), axis=1)
    own_fc, own_proj = both[0], both[1].T

    grads = []
    for pair in range(PAIRS + 1):
        if pair < PAIRS:
            pieces = []
            for distance in range(count):
                start = (place ^ distance) * own_width + pair * TILE
                piece = lax.dynamic_slice_in_dim(grad_attended, start, TILE, 1)
                pieces.append(swap(piece, "ctx", distance) if distance else piece)
            grad_heads = jnp.stack(canonical(pieces, place))[None]
            items = every
        else:
            last = jnp.pad(grad_attended[:, width - HEAD :], ((0, 0), (0, TILE - HEAD)))
            grad_heads = jnp.broadcast_to(last[None, None], (1, count) + last.shape)
            items = mine
        grads.append(
            attend_back(
                pair,
                items,
                q,
                k,
                v,
                kt,
                grad_heads,
                heads_out[pair],
                lses[pair],
                seg_col,
                seg_row,
                prompt_rows,
            )
        )
    ordered = [grads[pair][part] for part in range(3) for pair in range(PAIRS + 1)]
    grad_normed, grad_own, col_sums = project_back(place, ordered, w_own, normed)
    from_core = swap(grad_normed[1::2], "ctx", 1)
    summed = grad_normed[0::2].astype(F32) + from_core.astype(F32)
    grad_norm_rows = summed[0] + swap(summed[1].astype(BF16), "ctx", 2).astype(F32)
    _, norm1_back = jax.vjp(layer_norm, inputs, ln1_gain, ln1_bias)
    grad_inputs_norm, grad_ln1_gain, grad_ln1_bias = norm1_back(grad_norm_rows)
    grad_inputs = (grad_hidden + grad_inputs_norm).astype(BF16)

    def shard(grad):
        other = lax.dynamic_slice_in_dim(grad, (1 - fsdp) * half, half, 0)
        mine = lax.dynamic_slice_in_dim(grad, fsdp * half, half, 0)
        return (mine.astype(F32) + swap(other, "fsdp", 1).astype(F32)).astype(BF16)

    sum_out = lax.psum(shard(grad_w_out), ("ctx", "tensor")).astype(F32)
    grad_own = lax.psum(shard(grad_own), "tensor")
    step_width = grad_own.shape[1] // 3
    own_part = jnp.concatenate(
        [grad_own[:, i * step_width : i * step_width + own_width] for i in range(3)], axis=1
    )
    last_part = jnp.concatenate(
        [grad_own[:, i * step_width + own_width :][:, :HEAD] for i in range(3)], axis=1
    )
    across = swap(own_part, "ctx", 2)
    beside = swap(jnp.stack([own_part, across]), "ctx", 1)
    by_place = canonical([own_part, beside[0], across, beside[1]], place)
    last_part = lax.psum(last_part.astype(F32), "ctx")
    columns = []
    for i in range(3):
        columns += [entry[:, i * own_width : (i + 1) * own_width].astype(F32) for entry in by_place]
        columns.append(last_part[:, i * HEAD : (i + 1) * HEAD])
    sum_qkv = jnp.concatenate(columns, axis=1)

    def spread(sums):
        full = lax.dynamic_update_slice_in_dim(
            jnp.zeros((width,), F32), sums[:own_width], place * own_width, 0
        )
        return full.at[width - HEAD :].set(sums[own_width : own_width + HEAD])

    grad_q_bias = spread(col_sums[0, :step_width])
    grad_v_bias = spread(col_sums[0, 2 * step_width :])
    fc_bias_sums = jnp.zeros((tensors, w_fc.shape[1]), F32)
    for distance in range(tensors):
        fc_bias_sums = lax.dynamic_update_slice_in_dim(
            fc_bias_sums, grad_fc_bias[distance], (tensor - distance) % tensors, 0
        )
    vectors = lax.psum(
        jnp.concatenate(
            [
                grad_ln1_gain,
                grad_ln1_bias,
                grad_q_bias,
                grad_v_bias,
                grad_out_bias,
                grad_ln2_gain,
                grad_ln2_bias,
                grad_proj_bias,
                fc_bias_sums.reshape(-1),
            ]
        ),
        ("fsdp", "ctx", "tensor"),
    )
    vector = [vectors[i * width : (i + 1) * width] for i in range(8)]
    fc_bias_sum = lax.dynamic_slice_in_dim(
        vectors, 8 * width + tensor * w_fc.shape[1], w_fc.shape[1], 0
    )
    return (
        layer_out[:prompt_rows][None],
        layer_out[prompt_rows:][None],
        grad_inputs[:prompt_rows][None],
        grad_inputs[prompt_rows:][None],
        vector[0],
        vector[1],
        sum_qkv,
        jnp.stack([vector[2], vector[3]]),
        sum_out,
        vector[4],
        vector[5],
        vector[6],
        own_fc,
        fc_bias_sum,
        own_proj,
        vector[7],
    )


def solution(mesh):
    placed = (
        P(("fsdp", "tensor"), "ctx", None),
        P(("fsdp", "tensor"), "ctx", None),
        P(("fsdp", "tensor"), None),
        P(),
        P(),
        P("fsdp", None),
        P(),
        P("fsdp", None),
        P(),
        P(),
        P(),
        P("fsdp", "tensor"),
        P("tensor"),
        P("tensor", "fsdp"),
        P(),
        P(("fsdp", "tensor"), "ctx", None),
        P(("fsdp", "tensor"), "ctx", None),
    )
    by_heads = HEADS // mesh.shape["ctx"] == PAIRS * 2 and HEADS % mesh.shape["ctx"] == 1
    return jax.shard_map(
        local_heads if by_heads else local_rows,
        mesh=mesh,
        in_specs=placed,
        out_specs=(
            P(("fsdp", "tensor"), "ctx", None),
            P(("fsdp", "tensor"), "ctx", None),
            P(("fsdp", "tensor"), "ctx", None),
            P(("fsdp", "tensor"), "ctx", None),
            P(),
            P(),
            P("fsdp", None),
            P(),
            P("fsdp", None),
            P(),
            P(),
            P(),
            P("fsdp", "tensor"),
            P("tensor"),
            P("tensor", "fsdp"),
            P(),
        ),
        check_vma=False,
    )
```

```python
import functools

import jax
import jax.numpy as jnp
from jax import lax
from jax.experimental import pallas as pl
from jax.experimental.pallas import tpu as pltpu
from jax.sharding import PartitionSpec as P

HEADS = 17
HEAD = 64


def passed_along(value, axis, steps):
    count = lax.axis_size(axis)
    leading, last = (max(0, -steps), min(count, count - steps))
    return lax.ppermute(value, axis, [(source, source + steps) for source in range(leading, last)])


def layer_norm(values, norm_gain, norm_bias):
    average = jnp.mean(values, axis=-1, keepdims=True)
    centred = values - average
    variance = jnp.mean(centred * centred, axis=-1, keepdims=True)
    return centred * lax.rsqrt(variance + 1e-05) * norm_gain + norm_bias


def gelu_tanh(values):
    return jax.nn.gelu(values, approximate=True)


def inner_first(left_op, right_op):
    return lax.dot_general(
        left_op, right_op, (((0,), (0,)), ((), ())), preferred_element_type=jnp.float32
    )


def inner_last(left_op, right_op):
    return lax.dot_general(
        left_op, right_op, (((1,), (1,)), ((), ())), preferred_element_type=jnp.float32
    )


def to_heads(values):
    return jnp.swapaxes(values.reshape(values.shape[0], HEADS, HEAD), 0, 1)


def from_heads(values):
    return jnp.swapaxes(values, 0, 1).reshape(values.shape[1], values.shape[0] * values.shape[2])


def fetch_prompt(rows_kv):
    return lax.all_gather(rows_kv, "ctx", axis=0, tiled=True)


def local_rows(
    prompt_in,
    cont_in,
    cont_seg,
    ln1_gain,
    ln1_bias,
    w_qkv,
    qv_bias,
    w_out,
    out_bias,
    ln2_gain,
    ln2_bias,
    w_fc,
    fc_bias,
    w_proj,
    proj_bias,
    prompt_cot,
    cont_cot,
):
    model_width = prompt_in.shape[2]
    prompt_rows = prompt_in.shape[1]
    cont_rows = cont_in.shape[1]
    row_count = prompt_rows + cont_rows
    ctx_count = lax.axis_size("ctx")
    ctx_place = lax.axis_index("ctx")
    prompt_total = prompt_rows * ctx_count
    qkv_full, out_full = (
        lax.all_gather(w_qkv.astype(jnp.bfloat16), "fsdp", axis=0, tiled=True),
        lax.all_gather(w_out.astype(jnp.bfloat16), "fsdp", axis=0, tiled=True),
    )
    fc_full, proj_full = (
        lax.all_gather(w_fc.astype(jnp.bfloat16), "fsdp", axis=0, tiled=True),
        lax.all_gather(w_proj.astype(jnp.bfloat16), "fsdp", axis=1, tiled=True),
    )
    row_ids = jnp.arange(row_count, dtype=jnp.int32)
    labels_all = cont_seg[0]
    own_labels = lax.dynamic_slice_in_dim(labels_all, ctx_place * cont_rows, cont_rows)
    earlier_labels = lax.dynamic_slice_in_dim(
        labels_all, jnp.maximum(ctx_place - 1, 0) * cont_rows, cont_rows
    )
    query_labels = jnp.concatenate([jnp.full((prompt_rows,), -1, jnp.int32), own_labels])
    query_prompt = ctx_place * prompt_rows + row_ids
    query_cont = ctx_place * cont_rows + row_ids - prompt_rows
    is_cont = row_ids >= prompt_rows
    prompt_ids = jnp.arange(prompt_total, dtype=jnp.int32)
    near_ids = (ctx_place - 1) * cont_rows + jnp.arange(2 * cont_rows, dtype=jnp.int32)
    near_labels = jnp.concatenate([earlier_labels, own_labels])
    allowed_far = is_cont[:, None] | (prompt_ids[None, :] <= query_prompt[:, None])
    allowed_near = (
        (query_labels[:, None] == near_labels[None, :])
        & (near_ids[None, :] <= query_cont[:, None])
        & (near_ids[None, :] >= 0)
    )
    allowed = jnp.concatenate([allowed_far, allowed_near], 1)
    inputs = jnp.concatenate([prompt_in[0], cont_in[0]], 0).astype(jnp.float32)
    normed, norm1_back = jax.vjp(layer_norm, inputs, ln1_gain, ln1_bias)
    normed_low = normed.astype(jnp.bfloat16)
    projected = jnp.dot(normed_low, qkv_full, preferred_element_type=jnp.float32)
    queries = (projected[:, :model_width] + qv_bias[0]).astype(jnp.bfloat16)
    key_value = jnp.concatenate(
        [projected[:, model_width : 2 * model_width], projected[:, 2 * model_width :] + qv_bias[1]],
        1,
    ).astype(jnp.bfloat16)
    own_cont_kv = key_value[prompt_rows:]
    earlier_kv = passed_along(own_cont_kv, "ctx", 1)
    prompt_kv = fetch_prompt(key_value[:prompt_rows])
    keys_all = jnp.concatenate([prompt_kv, earlier_kv, own_cont_kv], 0)
    query_heads = to_heads(queries)
    key_heads = to_heads(keys_all[:, :model_width])
    value_heads = to_heads(keys_all[:, model_width:])

    def head_forward(operands):
        query_head, key_head, value_head = operands
        scores = inner_last(query_head, key_head) * 0.125
        scores = jnp.where(allowed, scores, -1e30)
        row_max = jnp.max(scores, axis=1, keepdims=True)
        exponent = jnp.exp(scores - row_max)
        row_total = jnp.sum(exponent, axis=1, keepdims=True)
        probability = (exponent / row_total).astype(jnp.bfloat16)
        head_out = jnp.dot(probability, value_head, preferred_element_type=jnp.float32)
        return (head_out.astype(jnp.bfloat16), (row_max + jnp.log(row_total))[:, 0])

    heads_out, logsum = lax.map(head_forward, (query_heads, key_heads, value_heads))
    attended = from_heads(heads_out)
    hidden = inputs + jnp.dot(attended, out_full, preferred_element_type=jnp.float32) + out_bias
    mlp_in, norm2_back = jax.vjp(layer_norm, hidden, ln2_gain, ln2_bias)
    mlp_low = mlp_in.astype(jnp.bfloat16)
    mlp_rows = lax.all_gather(mlp_low, "tensor", axis=0, tiled=True)
    pre_act = jnp.dot(mlp_rows, fc_full, preferred_element_type=jnp.float32) + fc_bias
    activated, gelu_back = jax.vjp(gelu_tanh, pre_act)
    act_low = activated.astype(jnp.bfloat16)
    partial_out = jnp.dot(act_low, proj_full, preferred_element_type=jnp.float32)
    mlp_out = lax.psum_scatter(
        partial_out.astype(jnp.bfloat16), "tensor", scatter_dimension=0, tiled=True
    ).astype(jnp.float32)
    layer_out = (hidden + mlp_out + proj_bias).astype(jnp.bfloat16)
    grad_layer = jnp.concatenate([prompt_cot[0], cont_cot[0]], 0)
    grad_float = grad_layer.astype(jnp.float32)
    grad_proj_bias = jnp.sum(grad_float, axis=0)
    grad_rows = lax.all_gather(grad_layer, "tensor", axis=0, tiled=True)
    grad_w_proj = inner_first(act_low, grad_rows)
    grad_act = inner_last(grad_rows, proj_full)
    grad_pre = gelu_back(grad_act)[0].astype(jnp.bfloat16)
    grad_fc_bias = jnp.sum(grad_pre.astype(jnp.float32), axis=0)
    grad_w_fc = inner_first(mlp_rows, grad_pre)
    grad_mlp_part = inner_last(grad_pre, fc_full)
    grad_mlp_in = lax.psum_scatter(grad_mlp_part, "tensor", scatter_dimension=0, tiled=True)
    grad_hidden_norm, grad_ln2_gain, grad_ln2_bias = norm2_back(grad_mlp_in)
    grad_hidden = grad_float + grad_hidden_norm
    grad_out_bias = jnp.sum(grad_hidden, axis=0)
    grad_branch = grad_hidden.astype(jnp.bfloat16)
    grad_w_out = inner_first(attended, grad_branch)
    grad_attended = inner_last(grad_branch, out_full).astype(jnp.bfloat16)
    prompt_again = fetch_prompt(key_value[:prompt_rows])
    keys_back = jnp.concatenate([prompt_again, earlier_kv, own_cont_kv], 0)
    key_back_heads = to_heads(keys_back[:, :model_width])
    value_back_heads = to_heads(keys_back[:, model_width:])

    def head_backward(operands):
        query_head, key_head, value_head, grad_head, logsum_head = operands
        scores = inner_last(query_head, key_head) * 0.125
        scores = jnp.where(allowed, scores, -1e30)
        probability = jnp.exp(scores - logsum_head[:, None])
        prob_low = probability.astype(jnp.bfloat16)
        grad_prob = inner_last(grad_head, value_head)
        centre = jnp.sum(probability * grad_prob, axis=1, keepdims=True)
        grad_scores = (probability * (grad_prob - centre)).astype(jnp.bfloat16)
        grad_query = jnp.dot(grad_scores, key_head, preferred_element_type=jnp.float32) * 0.125
        grad_key = inner_first(grad_scores, query_head) * 0.125
        grad_value = inner_first(prob_low, grad_head)
        return (grad_query, grad_key, grad_value)

    head_operands = (query_heads, key_back_heads, value_back_heads, to_heads(grad_attended), logsum)
    grad_q_heads, grad_k_heads, grad_v_heads = lax.map(head_backward, head_operands)
    grad_queries = from_heads(grad_q_heads).astype(jnp.bfloat16)
    grad_kv = jnp.concatenate([from_heads(grad_k_heads), from_heads(grad_v_heads)], 1)
    prompt_grad_kv = lax.psum_scatter(
        grad_kv[:prompt_total], "ctx", scatter_dimension=0, tiled=True
    )
    from_later = passed_along(
        grad_kv[prompt_total : prompt_total + cont_rows].astype(jnp.bfloat16), "ctx", -1
    ).astype(jnp.float32)
    cont_grad_kv = grad_kv[prompt_total + cont_rows :] + from_later
    grad_kv_rows = jnp.concatenate([prompt_grad_kv, cont_grad_kv], 0).astype(jnp.bfloat16)
    grad_projected = jnp.concatenate([grad_queries, grad_kv_rows], 1)
    grad_qv_bias = jnp.stack(
        [
            jnp.sum(grad_queries.astype(jnp.float32), axis=0),
            jnp.sum(grad_kv_rows[:, model_width:].astype(jnp.float32), axis=0),
        ]
    )
    grad_w_qkv = inner_first(normed_low, grad_projected)
    grad_normed = inner_last(grad_projected, qkv_full)
    grad_inputs_norm, grad_ln1_gain, grad_ln1_bias = norm1_back(grad_normed)
    grad_inputs = (grad_hidden + grad_inputs_norm).astype(jnp.bfloat16)
    shard_qkv, shard_out = (
        lax.psum_scatter(
            grad_w_qkv.astype(jnp.bfloat16), "fsdp", scatter_dimension=0, tiled=True
        ).astype(jnp.float32),
        lax.psum_scatter(
            grad_w_out.astype(jnp.bfloat16), "fsdp", scatter_dimension=0, tiled=True
        ).astype(jnp.float32),
    )
    sum_qkv, sum_out = lax.psum((shard_qkv, shard_out), ("ctx", "tensor"))
    sum_fc, sum_proj, sum_fc_bias = lax.psum(
        (grad_w_fc, grad_w_proj, grad_fc_bias), ("fsdp", "ctx")
    )
    fsdp_place = lax.axis_index("fsdp")
    fsdp_rows = w_fc.shape[0]
    own_fc = lax.dynamic_slice_in_dim(sum_fc, fsdp_place * fsdp_rows, fsdp_rows, 0)
    own_proj = lax.dynamic_slice_in_dim(sum_proj, fsdp_place * fsdp_rows, fsdp_rows, 1)
    small_sums = lax.psum(
        (
            grad_ln1_gain,
            grad_ln1_bias,
            grad_qv_bias,
            grad_out_bias,
            grad_ln2_gain,
            grad_ln2_bias,
            grad_proj_bias,
        ),
        ("fsdp", "ctx", "tensor"),
    )
    return (
        layer_out[:prompt_rows][None],
        layer_out[prompt_rows:][None],
        grad_inputs[:prompt_rows][None],
        grad_inputs[prompt_rows:][None],
        small_sums[0],
        small_sums[1],
        sum_qkv,
        small_sums[2],
        sum_out,
        small_sums[3],
        small_sums[4],
        small_sums[5],
        own_fc,
        sum_fc_bias,
        own_proj,
        small_sums[6],
    )


PAIRS = 2
TILE = 2 * HEAD
BF16 = jnp.bfloat16
F32 = jnp.float32
LOG2E = 1.4426950408889634
SCALE2 = 0.125 * LOG2E
HINT = 0.2
NN = (((1,), (0,)), ((), ()))
NT = (((1,), (1,)), ((), ()))
TN = (((0,), (0,)), ((), ()))


def dot(left_op, right_op, dims=NN):
    return lax.dot_general(left_op, right_op, dims, preferred_element_type=F32)


def swap(value, axis, bit):
    count = lax.axis_size(axis)
    return lax.ppermute(value, axis, [(place, place ^ bit) for place in range(count)])


def turn(value, axis, steps):
    count = lax.axis_size(axis)
    return lax.ppermute(value, axis, [(place, (place + steps) % count) for place in range(count)])


def halves(values, heads=2):
    lane = lax.broadcasted_iota(jnp.int32, values.shape, 1)
    zero = jnp.zeros_like(values)
    return [jnp.where((lane < HEAD) == (head == 0), values, zero) for head in range(heads)]


ANYWHERE = pl.BlockSpec(memory_space=pl.ANY)


def blocks(*shape):
    return pl.BlockSpec(shape, lambda i, *_: (0,) * len(shape))


def shape_of(*shape, kind=BF16):
    return jax.ShapeDtypeStruct(shape, kind)


def launch(
    kernel, name, scalars, grid, operands, in_specs, outs, scratch=(), limit=48, flops=0, traffic=16, exps=0, after=(), carry=(), aliases=None
):
    out_specs, out_shapes = [out[0] for out in outs], [out[1] for out in outs]
    given = len(scalars) + len(operands)
    tied = given + len(after) + len(carry)

    def body(*refs):
        made = refs[tied : tied + len(outs)]
        kernel(*refs[:given], *made, *refs[tied + len(outs) + len(carry) :])

    links = {len(scalars) + here: there for here, there in (aliases or {}).items()}
    links.update({given + len(after) + i: len(outs) + i for i in range(len(carry))})
    out = pl.pallas_call(
        body,
        grid_spec=pltpu.PrefetchScalarGridSpec(
            num_scalar_prefetch=len(scalars),
            grid=grid,
            in_specs=list(in_specs) + [ANYWHERE] * (len(after) + len(carry)),
            out_specs=out_specs + [ANYWHERE] * len(carry),
            scratch_shapes=list(scratch),
        ),
        out_shape=out_shapes + [shape_of(*entry.shape, kind=entry.dtype) for entry in carry],
        input_output_aliases=links,
        compiler_params=pltpu.CompilerParams(vmem_limit_bytes=limit << 20),
        cost_estimate=pl.CostEstimate(
            flops=int(flops * HINT),
            bytes_accessed=int(traffic * HINT * (1 << 20)),
            transcendentals=int(exps * HINT),
        ),
        name=name,
    )(*scalars, *operands, *after, *carry)
    return (out[: len(outs)], *out[len(outs) :]) if carry else out


def behind(arrays, token):
    out = launch(
        lambda *refs: None, "behind", (), (1,), (), (), (), after=(token,), carry=tuple(arrays)
    )
    return out[1:]


def whole_out(*shape, kind=BF16):
    return blocks(*shape), shape_of(*shape, kind=kind)


def pack_kernel(place_ref, prompt_ref, cont_ref, w_ref, rows_ref, out_ref):
    prompt_rows, width = prompt_ref.shape[1], prompt_ref.shape[2]
    rows_ref[:prompt_rows, :width] = prompt_ref[0]
    rows_ref[prompt_rows:, :width] = cont_ref[0]
    rows_ref[:, width:] = jnp.zeros((rows_ref.shape[0], rows_ref.shape[1] - width), BF16)
    place = place_ref[0]
    own = 2 * PAIRS * HEAD
    step = out_ref.shape[1] // 3
    for part in range(3):
        for at in range((width - HEAD) // own):

            @pl.when(place == at)
            def _():
                cols = slice(part * width + at * own, part * width + (at + 1) * own)
                out_ref[:, part * step : part * step + own] = w_ref[:, cols].astype(BF16)

        last = w_ref[:, (part + 1) * width - HEAD : (part + 1) * width].astype(BF16)
        out_ref[:, part * step + own : (part + 1) * step] = jnp.concatenate(
            [last, jnp.zeros((last.shape[0], step - own - HEAD), BF16)], axis=1
        )


def pack(place, prompt_in, cont_in, w_qkv, padded):
    rows = prompt_in.shape[1] + cont_in.shape[1]
    operands = (prompt_in, cont_in, w_qkv)
    return launch(
        pack_kernel,
        "pack",
        (place,),
        (1,),
        operands,
        [blocks(*entry.shape) for entry in operands],
        [whole_out(rows, padded), whole_out(w_qkv.shape[0], 3 * (PAIRS + 1) * TILE)],
    )


def pack_more_kernel(
    core_ref, fc_ref, proj_ref, bias_ref, prompt_ref, cont_ref, mine_ref, *refs
):
    copy_refs, (g_ref, gt_ref) = refs[:-2], refs[-2:]
    quarter = fc_ref.shape[0] // 2
    prompt_rows = prompt_ref.shape[1]
    start = pl.multiple_of(core_ref[0] * quarter, quarter)
    mine_ref[:quarter] = fc_ref[pl.ds(start, quarter), :].astype(BF16)
    for core in range(2):

        @pl.when(core_ref[0] == core)
        def _():
            mine_ref[quarter : 2 * quarter] = (
                proj_ref[:, core * quarter : (core + 1) * quarter].T.astype(BF16)
            )

    bias = bias_ref[...]
    pieces = []
    for _ in range(3):
        piece = bias.astype(BF16)
        pieces.append(piece)
        bias = bias - piece.astype(F32)
    spare = mine_ref.shape[0] - 2 * quarter
    pieces.append(jnp.zeros((spare - 3, bias.shape[1]), BF16))
    mine_ref[2 * quarter :] = jnp.concatenate(pieces, axis=0)
    for ref in copy_refs:
        ref[...] = mine_ref[...]
    g_ref[:prompt_rows] = prompt_ref[0]
    g_ref[prompt_rows:] = cont_ref[0]
    gt_ref[:, :prompt_rows] = prompt_ref[0].T
    gt_ref[:, prompt_rows:] = cont_ref[0].T


def pack_more(core, w_fc, w_proj, fc_bias, prompt_cot, cont_cot, after):
    rows, width = prompt_cot.shape[1] + cont_cot.shape[1], prompt_cot.shape[2]
    operands = (w_fc, w_proj, fc_bias[None], prompt_cot, cont_cot)
    return launch(
        pack_more_kernel,
        "pack_more",
        (core,),
        (1,),
        operands,
        [blocks(*entry.shape) for entry in operands],
        [
            *[whole_out(w_fc.shape[0] + 16, w_fc.shape[1])] * 4,
            whole_out(rows, width),
            whole_out(width, rows),
        ],
        after=after,
    )


def in_order(own, other, place):
    first = place == 0
    return jnp.where(first, own, other), jnp.where(first, other, own)


def project_kernel(
    place_ref, x_ref, w_ref, gain_ref, bias_ref, col_bias_ref, *refs
):
    norm_ref, q_ref, k_ref, v_ref, kt_ref, vt_ref = refs[-6:]
    values = x_ref[:, : w_ref.shape[0]].astype(F32)
    average = jnp.mean(values, axis=1, keepdims=True)
    centred = values - average
    variance = jnp.mean(centred * centred, axis=1, keepdims=True)
    normed = (centred * lax.rsqrt(variance + 1e-05) * gain_ref[...] + bias_ref[...]).astype(BF16)
    norm_ref[0, : w_ref.shape[0]] = normed.T
    extra = norm_ref.shape[1] - w_ref.shape[0]
    at_row = lax.broadcasted_iota(jnp.int32, (extra, normed.shape[0]), 0)
    norm_ref[0, w_ref.shape[0] :] = jnp.where(at_row == 0, 1.0, 0.0).astype(BF16)
    tiles = q_ref.shape[0]
    width = tiles * TILE
    for part, out_ref, flip_ref in ((0, q_ref, None), (1, k_ref, kt_ref), (2, v_ref, vt_ref)):
        cols = slice(part * width, (part + 1) * width)
        out = (dot(normed, w_ref[:, cols]) + col_bias_ref[:, cols]).astype(BF16)
        for tile in range(tiles):
            piece = out[:, tile * TILE : (tile + 1) * TILE]
            out_ref[tile, 0] = piece
            if flip_ref is not None:
                flip_ref[tile, 0] = piece.T


def project(place, rows, w_own, gain, bias, col_bias, before, count, after=(), carry=()):
    row_count, width = rows.shape[0], w_own.shape[0]
    tiles = w_own.shape[1] // (3 * TILE)
    tall = (
        pl.BlockSpec((tiles, 1, row_count, TILE), lambda i, p: (0, p[0], 0, 0)),
        shape_of(tiles, count, row_count, TILE),
    )
    flat = (
        pl.BlockSpec((tiles, 1, TILE, row_count), lambda i, p: (0, p[0], 0, 0)),
        shape_of(tiles, count, TILE, row_count),
    )
    operands = (rows, w_own, gain[None], bias[None], col_bias[None])
    before = tuple(before or ())
    return launch(
        lambda *refs: project_kernel(*refs[:6], *refs[-6:]),
        "project",
        (place,),
        (1,),
        operands + before,
        [blocks(*entry.shape) for entry in operands] + [ANYWHERE] * len(before),
        [
            (
                pl.BlockSpec((1, width + 16, row_count), lambda i, p: (p[0], 0, 0)),
                shape_of(count, width + 16, row_count),
            ),
            tall,
            tall,
            tall,
            flat,
            flat,
        ],
        aliases={len(operands) + i: i for i in range(len(before))},
        flops=2 * row_count * width * w_own.shape[1],
        after=after,
        carry=carry,
    )


def own_mask(rows):
    key_at = lax.broadcasted_iota(jnp.int32, (rows, rows), 0)
    query_at = lax.broadcasted_iota(jnp.int32, (rows, rows), 1)
    return key_at <= query_at


def attend_kernel(
    heads, spans, prompt_rows, place_ref, q_ref, k_ref, vt_ref, seg_col_ref, seg_row_ref, *refs
):
    o_refs, lse_ref, acc = refs[:spans], refs[-2], refs[-1]
    step = pl.program_id(0)
    distance = step % spans
    block = place_ref[0] ^ distance
    count, row_count = k_ref.shape[1], k_ref.shape[2]
    cont_rows = row_count - prompt_rows

    def part(queries, at, start, size, mask, before):
        keys = k_ref[0, at, pl.ds(start, size), :]
        scores = [dot(keys, query, NT) for query in queries]
        if mask is not None:
            scores = [jnp.where(mask, score, -1e30) for score in scores]
        tops = [jnp.max(score, axis=0, keepdims=True) for score in scores]
        if before is not None:
            tops = [jnp.maximum(top, state[0]) for top, state in zip(tops, before)]
        exps = [jnp.exp2(score * SCALE2 - top * SCALE2) for score, top in zip(scores, tops)]
        totals = [jnp.sum(exp, axis=0, keepdims=True) for exp in exps]
        after = []
        for head in range(heads):
            rows = slice(head * HEAD, (head + 1) * HEAD)
            cols = slice(0, queries[head].shape[0])
            out = dot(vt_ref[0, at, rows, pl.ds(start, size)], exps[head].astype(BF16))
            total = totals[head]
            if before is None:
                acc[rows, cols] = out
            else:
                shrink = jnp.exp2((before[head][0] - tops[head]) * SCALE2)
                total = total + before[head][1] * shrink
                acc[rows, cols] = acc[rows, cols] * shrink + out
            after.append((tops[head], total))
        return after

    def finish(start, size, states):
        for head in range(heads):
            rows = slice(head * HEAD, (head + 1) * HEAD)
            top, total = states[head]
            acc[rows, :size] = acc[rows, :size] / total
            lse_ref[0, block, head : head + 1, pl.ds(start, size)] = top * SCALE2 + jnp.log2(total)
        if heads == 1:
            acc[HEAD:, :size] = jnp.zeros((TILE - HEAD, size), F32)
        out = acc[:, :size].T.astype(BF16)
        for at in range(spans):

            @pl.when(distance == at)
            def _():
                o_refs[at][pl.ds(start, size), :] = out

    def over_prompt(queries, total, states):
        return lax.fori_loop(
            0, total, lambda c, states: part(queries, c, 0, prompt_rows, None, states), states
        )

    @pl.when(step >= spans)
    def _():
        queries = halves(q_ref[0, block, :prompt_rows, :], heads)
        states = part(queries, block, 0, prompt_rows, own_mask(prompt_rows), None)
        finish(0, prompt_rows, over_prompt(queries, block, states))

    @pl.when(step < spans)
    def _():
        before = jnp.maximum(block - 1, 0)
        labels = seg_row_ref[block]
        queries = halves(q_ref[0, block, prompt_rows:, :], heads)
        own = own_mask(cont_rows) & (seg_col_ref[block] == labels)
        near = (seg_col_ref[before] == labels) & (block > 0)
        states = part(queries, block, prompt_rows, cont_rows, own, None)
        states = part(queries, before, prompt_rows, cont_rows, near, states)
        finish(prompt_rows, cont_rows, over_prompt(queries, count, states))


def attend(pair, heads, spans, place, q, k, vt, seg_col, seg_row, prompt_rows, after=(), carry=()):
    _, count, row_count, _ = q.shape
    cont_rows = row_count - prompt_rows
    pick = lambda i, s: (pair, 0, 0, 0)
    pairs = spans * (prompt_rows + 2 * cont_rows) * prompt_rows * count // 2
    return launch(
        functools.partial(attend_kernel, heads, spans, prompt_rows),
        "attend",
        (place,),
        (2 * spans,),
        (q, k, vt, seg_col, seg_row),
        [
            pl.BlockSpec((1, count, row_count, TILE), pick),
            pl.BlockSpec((1, count, row_count, TILE), pick),
            pl.BlockSpec((1, count, TILE, row_count), pick),
            blocks(count, cont_rows, 1),
            blocks(count, 1, cont_rows),
        ],
        [whole_out(row_count, TILE)] * spans + [whole_out(1, count, 2, row_count, kind=F32)],
        scratch=[pltpu.VMEM((TILE, max(prompt_rows, cont_rows)), F32)],
        flops=4 * heads * TILE * pairs,
        exps=heads * pairs,
        after=after,
        carry=carry,
    )


def attend_back_kernel(
    heads,
    spans,
    prompt_rows,
    place_ref,
    q_ref,
    k_ref,
    v_ref,
    kt_ref,
    lse_ref,
    seg_col_ref,
    seg_row_ref,
    *refs,
):
    do_refs, o_refs, refs = refs[:spans], refs[spans : 2 * spans], refs[2 * spans :]
    dq_ref, dk_ref, dv_ref, dk_acc, dv_acc, dq_acc, do_s, o_s = refs
    step = pl.program_id(0)
    distance = step % spans
    block = place_ref[0] ^ distance
    count, row_count = k_ref.shape[1], k_ref.shape[2]
    cont_rows = row_count - prompt_rows

    @pl.when(step == 0)
    def _():
        dk_acc[...] = jnp.zeros_like(dk_acc)
        dv_acc[...] = jnp.zeros_like(dv_acc)
        if spans < count:
            dq_ref[...] = jnp.zeros_like(dq_ref)

    def part(given, at, start, size, mask, first):
        rows = pl.ds(start, size)
        for head in range(heads):
            query, grad, lse, centre = (entry[head] for entry in given)
            cols = slice(0, query.shape[0])
            own = slice(head * HEAD, (head + 1) * HEAD)
            scores = dot(k_ref[0, at, rows, :], query, NT)
            if mask is not None:
                scores = jnp.where(mask, scores, -1e30)
            probability = jnp.exp2(scores * SCALE2 - lse)
            grad_probability = dot(v_ref[0, at, rows, :], grad, NT)
            grad_scores = (probability * (grad_probability - centre)).astype(BF16)
            dv_acc[at, rows, :] += dot(probability.astype(BF16), grad)
            dk_acc[at, rows, :] += dot(grad_scores, query)
            out = dot(kt_ref[0, at, own, rows], grad_scores)
            if first:
                dq_acc[own, cols] = out
            else:
                dq_acc[own, cols] += out

    def setup(start, size):
        rows = pl.ds(start, size)
        for at in range(spans):

            @pl.when(distance == at)
            def _():
                do_s[:size] = do_refs[at][rows, :]
                o_s[:size] = o_refs[at][rows, :]

        grad = do_s[:size]
        product = (grad.astype(F32) * o_s[:size].astype(F32)).T
        centres = [
            jnp.sum(product[head * HEAD : (head + 1) * HEAD], axis=0, keepdims=True)
            for head in range(heads)
        ]
        lses = [lse_ref[0, block, head : head + 1, rows] for head in range(heads)]
        return halves(q_ref[0, block, rows, :], heads), halves(grad, heads), lses, centres

    def finish(start, size):
        if heads == 1:
            dq_acc[HEAD:, :size] = jnp.zeros((TILE - HEAD, size), F32)
        dq_ref[0, block, pl.ds(start, size), :] = (dq_acc[:, :size].T * 0.125).astype(BF16)

    @pl.when(step >= spans)
    def _():
        given = setup(0, prompt_rows)
        part(given, block, 0, prompt_rows, own_mask(prompt_rows), True)

        @pl.loop(0, block)
        def _(c):
            part(given, c, 0, prompt_rows, None, False)

        finish(0, prompt_rows)

    @pl.when(step < spans)
    def _():
        before = jnp.maximum(block - 1, 0)
        labels = seg_row_ref[block]
        own = own_mask(cont_rows) & (seg_col_ref[block] == labels)
        near = (seg_col_ref[before] == labels) & (block > 0)
        given = setup(prompt_rows, cont_rows)
        part(given, block, prompt_rows, cont_rows, own, True)
        part(given, before, prompt_rows, cont_rows, near, False)

        @pl.loop(0, count)
        def _(c):
            part(given, c, 0, prompt_rows, None, False)

        finish(prompt_rows, cont_rows)

    @pl.when(step == pl.num_programs(0) - 1)
    def _():
        dk_ref[0] = (dk_acc[...] * 0.125).astype(BF16)
        dv_ref[0] = dv_acc[...].astype(BF16)


def attend_back(
    pair, tile, heads, place, q, k, v, kt, lse, seg_col, seg_row, grads, outs, prompt_rows, after=(), carry=()
):
    _, count, row_count, _ = q.shape
    spans = len(grads)
    cont_rows = row_count - prompt_rows
    pick = lambda i, s: (pair, 0, 0, 0)
    tall = pl.BlockSpec((1, count, row_count, TILE), pick)
    most = max(prompt_rows, cont_rows)
    pairs = spans * (prompt_rows + 2 * cont_rows) * prompt_rows * count // 2
    return launch(
        functools.partial(attend_back_kernel, heads, spans, prompt_rows),
        "attend_back",
        (place,),
        (2 * spans,),
        (q, k, v, kt, lse, seg_col, seg_row, *grads, *outs),
        [
            tall,
            tall,
            tall,
            pl.BlockSpec((1, count, TILE, row_count), pick),
            blocks(1, count, 2, row_count),
            blocks(count, cont_rows, 1),
            blocks(count, 1, cont_rows),
        ]
        + [pl.BlockSpec((row_count, TILE), lambda i, s: (0, tile))] * spans
        + [blocks(row_count, TILE)] * spans,
        [whole_out(1, count, row_count, TILE)] * 3,
        scratch=[
            pltpu.VMEM((count, row_count, TILE), F32),
            pltpu.VMEM((count, row_count, TILE), F32),
            pltpu.VMEM((TILE, most), F32),
            pltpu.VMEM((most, TILE), BF16),
            pltpu.VMEM((most, TILE), BF16),
        ],
        limit=56,
        flops=10 * heads * TILE * pairs,
        exps=heads * pairs,
        after=after,
        carry=carry,
    )


def normalize(values):
    average = jnp.mean(values, axis=1, keepdims=True)
    centred = values - average
    variance = jnp.mean(centred * centred, axis=1, keepdims=True)
    rate = lax.rsqrt(variance + 1e-05)
    return centred * rate, rate


def normalize_back(unit, rate, grad):
    shift = jnp.mean(grad, axis=1, keepdims=True)
    along = jnp.mean(grad * unit, axis=1, keepdims=True)
    return rate * (grad - shift - unit * along)


def merge_kernel(places, place_ref, x_ref, w_ref, out_bias_ref, gain_ref, bias_ref, *refs):
    pieces, last_ref, (hidden_ref, low_ref, flip_ref) = refs[:-4], refs[-4], refs[-3:]
    own = 2 * PAIRS * HEAD
    width = hidden_ref.shape[1]
    total = x_ref[:, :width].astype(F32) + out_bias_ref[...]
    for distance in range(places):
        start = pl.multiple_of((place_ref[0] ^ distance) * own, own)
        joined = jnp.concatenate(
            [ref[...] for ref in pieces[distance * PAIRS : (distance + 1) * PAIRS]], axis=1
        )
        total = total + dot(joined, w_ref[pl.ds(start, own), :])
    total = total + dot(last_ref[:, :HEAD], w_ref[width - HEAD :, :])
    hidden_ref[...] = total
    unit, _ = normalize(total)
    low = (unit * gain_ref[...] + bias_ref[...]).astype(BF16)
    low_ref[...] = low
    flip_ref[...] = low.T


def merge(place, rows, w_out, out_bias, gain, bias, pieces, last, after=(), carry=()):
    row_count, width = rows.shape[0], w_out.shape[1]
    size = 128
    by_row = lambda cols: pl.BlockSpec((size, cols), lambda i, p: (i, 0))
    return launch(
        functools.partial(merge_kernel, len(pieces) // PAIRS),
        "merge",
        (place,),
        (row_count // size,),
        (rows, w_out, out_bias[None], gain[None], bias[None], *pieces, last),
        [by_row(rows.shape[1]), blocks(*w_out.shape)]
        + [blocks(1, width)] * 3
        + [by_row(TILE)] * (len(pieces) + 1),
        [
            (by_row(width), shape_of(row_count, width, kind=F32)),
            (by_row(width), shape_of(row_count, width)),
            (
                pl.BlockSpec((width, size), lambda i, p: (0, i)),
                shape_of(width, row_count),
            ),
        ],
        flops=2 * row_count * width * width,
        after=after,
        carry=carry,
    )


def bend_kernel(
    places,
    prompt_steps,
    place_ref,
    mlp_ref,
    gm_ref,
    hidden_ref,
    g_ref,
    w_ref,
    gain_ref,
    proj_bias_ref,
    *refs,
):
    pieces, last_ref, refs = refs[: places * PAIRS], refs[places * PAIRS], refs[places * PAIRS + 1 :]
    prompt_ref, cont_ref, gh_ref = refs[:3]
    ga_refs, (ga_last_ref, *gw_refs, sums_ref, acc) = refs[3 : 3 + places], refs[3 + places :]
    step = pl.program_id(0)
    own = 2 * PAIRS * HEAD
    width = hidden_ref.shape[1]
    hidden = hidden_ref[...]
    layer_out = (hidden + mlp_ref[...] + proj_bias_ref[...]).astype(BF16)

    @pl.when(step < prompt_steps)
    def _():
        prompt_ref[0] = layer_out

    @pl.when(step >= prompt_steps)
    def _():
        cont_ref[0] = layer_out

    unit, rate = normalize(hidden)
    grad_in = gm_ref[...]
    grad_layer = g_ref[...].astype(F32)
    grad_hidden = grad_layer + normalize_back(unit, rate, grad_in * gain_ref[...])
    gh_ref[...] = grad_hidden
    branch = grad_hidden.astype(BF16)
    sums = [grad_hidden, grad_in * unit, grad_in, grad_layer]
    sums = jnp.concatenate([jnp.sum(entry, axis=0, keepdims=True) for entry in sums], axis=0)

    @pl.when(step == 0)
    def _():
        acc[...] = jnp.zeros_like(acc)
        sums_ref[...] = sums

    @pl.when(step > 0)
    def _():
        sums_ref[...] += sums

    for distance in range(places):
        start = pl.multiple_of((place_ref[0] ^ distance) * own, own)
        rows = pl.ds(start, own)
        ga_refs[distance][...] = dot(branch, w_ref[rows, :], NT).astype(BF16)
        joined = jnp.concatenate(
            [ref[...] for ref in pieces[distance * PAIRS : (distance + 1) * PAIRS]], axis=1
        )
        acc[rows, :] += dot(joined.T, branch)
    last = dot(branch, w_ref[width - HEAD :, :], NT).astype(BF16)
    ga_last_ref[...] = jnp.concatenate([last, jnp.zeros_like(last)], axis=1)
    acc[width - HEAD :, :] += dot(last_ref[:, :HEAD].T, branch)

    @pl.when(step == pl.num_programs(0) - 1)
    def _():
        quarter = width // 4
        core, fsdp = place_ref[0] % 2, place_ref[1]
        for beside, ref in enumerate(gw_refs):
            for away in range(2):
                start = ((fsdp ^ away) * 2 + (core ^ beside)) * quarter
                ref[away] = acc[pl.ds(pl.multiple_of(start, 16), quarter), :].astype(BF16)


def bend(place, mlp_out, gm, hidden, g, w_out, gain, proj_bias, pieces, last, prompt_rows, after=(), carry=()):
    row_count, width = hidden.shape
    size = 128
    places = len(pieces) // PAIRS
    prompt_steps = prompt_rows // size
    own = 2 * PAIRS * HEAD
    by_row = lambda cols: pl.BlockSpec((size, cols), lambda i, p: (i, 0))
    return launch(
        functools.partial(bend_kernel, places, prompt_steps),
        "bend",
        (place,),
        (row_count // size,),
        (mlp_out, gm, hidden, g, w_out, gain[None], proj_bias[None], *pieces, last),
        [by_row(width)] * 4
        + [blocks(*w_out.shape)]
        + [blocks(1, width)] * 2
        + [by_row(TILE)] * (len(pieces) + 1),
        [
            (
                pl.BlockSpec((1, size, width), lambda i, p: (0, jnp.minimum(i, prompt_steps - 1), 0)),
                shape_of(1, prompt_rows, width),
            ),
            (
                pl.BlockSpec((1, size, width), lambda i, p: (0, jnp.maximum(i - prompt_steps, 0), 0)),
                shape_of(1, row_count - prompt_rows, width),
            ),
            (by_row(width), shape_of(row_count, width, kind=F32)),
        ]
        + [(by_row(own), shape_of(row_count, own))] * places
        + [
            (by_row(TILE), shape_of(row_count, TILE)),
            whole_out(2, width // 4, width),
            whole_out(2, width // 4, width),
            whole_out(4, width, kind=F32),
        ],
        scratch=[pltpu.VMEM((width, width), F32)],
        flops=4 * row_count * width * width,
        traffic=30,
        after=after,
        carry=carry,
    )


GELU_RATE = 0.7978845608028654


def gelu_both(values):
    square = values * values
    bent = jnp.tanh(GELU_RATE * (values + 0.044715 * square * values))
    half = 0.5 * (1.0 + bent)
    slope = half + 0.5 * values * (1.0 - bent * bent) * (GELU_RATE * (1.0 + 0.134145 * square))
    return values * half, slope


def mlp_kernel(
    parts,
    first,
    spot_ref,
    x_ref,
    g_ref,
    xt_ref,
    gt_ref,
    *refs,
):
    own, far, beside = refs[:parts], refs[parts : 2 * parts], refs[2 * parts : 3 * parts]
    before_refs = refs[3 * parts : 3 * parts + 2]
    refs = refs[3 * parts + (0 if first else 2) :]
    out_ref, gm_ref, keep_f, send_f, keep_p, send_p, gb_ref = refs[:7]
    wf_s, wp_s, bias_s, biases, act_s, gp_s, wide, sems = refs[7:]
    step = pl.program_id(0)
    core, fsdp = spot_ref[0], spot_ref[1]
    slot = step % 2
    _, width, hidden = wf_s.shape
    quarter = width // 4

    def spot(away, across):
        start = ((fsdp ^ away) * 2 + (core ^ across)) * quarter
        return pl.ds(pl.multiple_of(start, 16), quarter)

    def loads(at, to):
        moves = [(own[at].at[pl.ds(2 * quarter, 16)], bias_s.at[to])]
        for away, local in enumerate((own[at], far[at])):
            for across, source in enumerate((local, beside[at].at[away])):
                for weight, target in enumerate((wf_s, wp_s)):
                    moves.append(
                        (
                            source.at[pl.ds(weight * quarter, quarter)],
                            target.at[to, spot(away, across)],
                        )
                    )
        return [
            pltpu.make_async_copy(source, target, sems.at[to, i])
            for i, (source, target) in enumerate(moves)
        ]

    @pl.when(step == 0)
    def _():
        for part in range(parts):
            for copy in loads(part, part):
                copy.start()

    for part in range(parts):

        @pl.when(step == part)
        def _():
            for copy in loads(part, part):
                copy.wait()

    bias = jnp.sum(bias_s[slot, :3, :].astype(F32), axis=0, keepdims=True)
    biases[...] = bias

    def over(total, body):
        whole = total // 256

        @pl.loop(0, whole)
        def _(i):
            body(pl.multiple_of(i * 256, 256), 256)

        if total % 256:
            body(whole * 256, total % 256)

    def up(start, size):
        cols = pl.ds(start, size)
        pre_act = dot(x_ref[...], wf_s[slot, :, cols]) + biases[:, cols]
        grad_act = dot(g_ref[...], wp_s[slot, :, cols])
        activated, slope = gelu_both(pre_act)
        grad_pre = (grad_act * slope).astype(BF16)
        act_s[:, cols] = activated.astype(BF16)
        gp_s[:, cols] = grad_pre
        gb_ref[0, :, cols] = jnp.sum(grad_pre.astype(F32), axis=0, keepdims=True)

    def weights(start, size):
        cols = pl.ds(start, size)
        for left, right, keep, send, by_part in (
            (xt_ref, gp_s, keep_f, send_f, True),
            (gt_ref, act_s, keep_p, send_p, False),
        ):
            wide[:, :size] = dot(left[...], right[:, cols]).astype(BF16)
            for far in range(2):
                for beside, to in enumerate((keep, send)):
                    piece = wide[spot(far, beside), :size]
                    if by_part:
                        to[0, far, :, cols] = piece
                    else:
                        to[far, 0, :, cols] = piece

    over(hidden, up)
    over(hidden, weights)

    if first:

        @pl.when(step == 0)
        def _():
            out_ref[...] = jnp.zeros_like(out_ref)
            gm_ref[...] = jnp.zeros_like(gm_ref)

    else:

        @pl.when(step == 0)
        def _():
            out_ref[...] = before_refs[0][...]
            gm_ref[...] = before_refs[1][...]

    def down(start, size):
        rows = pl.ds(start, size)
        out_ref[:, rows] += dot(act_s[...], wp_s[slot, rows, :], NT)
        gm_ref[:, rows] += dot(gp_s[...], wf_s[slot, rows, :], NT)

    over(width, down)


def mlp(spot, x, g, xt, gt, own, far, beside, before=(), after=(), carry=()):
    rows, width = x.shape
    hidden = own[0].shape[1]
    parts, quarter = len(own), width // 4
    once = pl.Buffered(buffer_count=1)
    whole = lambda *shape: pl.BlockSpec(shape, lambda k, s: (0,) * len(shape), pipeline_mode=once)
    by_part = pl.BlockSpec((1, 2, quarter, hidden), lambda k, s: (k, 0, 0, 0))
    by_far = pl.BlockSpec((2, 1, quarter, hidden), lambda k, s: (0, k, 0, 0))
    total = (whole(rows, width), shape_of(rows, width, kind=F32))
    by_part = (by_part, shape_of(parts, 2, quarter, hidden))
    by_far = (by_far, shape_of(2, parts, quarter, hidden))
    return launch(
        functools.partial(mlp_kernel, parts, not before),
        "mlp",
        (spot,),
        (parts,),
        (x, g, xt, gt, *own, *far, *beside, *before),
        [
            whole(rows, width),
            whole(rows, width),
            whole(width, rows),
            whole(width, rows),
        ]
        + [ANYWHERE] * (3 * parts)
        + [whole(rows, width)] * len(before),
        [
            total,
            total,
            by_part,
            by_part,
            by_far,
            by_far,
            (
                pl.BlockSpec((1, 1, hidden), lambda k, s: (k, 0, 0)),
                shape_of(parts, 1, hidden, kind=F32),
            ),
        ],
        scratch=[
            pltpu.VMEM((2, width, hidden), BF16),
            pltpu.VMEM((2, width, hidden), BF16),
            pltpu.VMEM((2, 16, hidden), BF16),
            pltpu.VMEM((1, hidden), F32),
            pltpu.VMEM((rows, hidden), BF16),
            pltpu.VMEM((rows, hidden), BF16),
            pltpu.VMEM((width, 256), BF16),
            pltpu.SemaphoreType.DMA((2, 9)),
        ],
        limit=62,
        flops=12 * rows * width * hidden * parts,
        traffic=40,
        exps=rows * hidden * parts,
        after=after,
        carry=carry,
    )


def tail_kernel(prompt_rows, *refs):
    grads, refs = refs[:9], refs[9:]
    w_ref, norm_ref, rows_ref, gh_ref, keep_ref, come_ref, gain_ref, given_ref = refs[:8]
    prompt_ref, cont_ref, qkv_ref, wo_ref, vec_ref = refs[8:13]
    (
        norms,
        rows_s,
        gh_s,
        joined,
        hold,
        core_out,
        core_in,
        chip_out,
        chip_in,
        acc,
        keep,
        far_out,
        far_in,
        sums,
        sums_in,
        ring_in,
        ring_all,
        whole,
        near_in,
        left_out,
        left_in,
        vec_out,
        vec_in,
        wo_near,
        wo_sum,
        wo_ring,
        wo_chip,
        wo_all,
        wo_core,
        local_sem,
        send_sem,
        recv_sem,
    ) = refs[13:]
    place = lax.axis_index("ctx")
    fsdp = lax.axis_index("fsdp")
    tensor = lax.axis_index("tensor")
    tensors = lax.axis_size("tensor")
    count, row_count = grads[0].shape[1], grads[0].shape[2]
    width = w_ref.shape[0]
    half = width // 2
    own = acc.shape[1]
    shard = ring_in.shape[2]
    chunk = 128
    beside, across, far = {"ctx": place ^ 1}, {"ctx": place ^ 2}, {"fsdp": 1 - fsdp}
    others = [{"tensor": lax.rem(tensor + k, tensors)} for k in range(1, tensors)]

    barrier = pltpu.get_barrier_semaphore()
    for partner in (beside, across, far, *others):
        pl.semaphore_signal(barrier, inc=1, device_id=partner, device_id_type=pl.DeviceIdType.MESH)

    loads = [pltpu.make_async_copy(norm_ref, norms, local_sem.at[0])]
    loads.append(pltpu.make_async_copy(keep_ref, wo_core.at[0], local_sem.at[1]))
    loads.append(pltpu.make_async_copy(come_ref, wo_near, local_sem.at[2]))
    for load in loads:
        load.start()
    sent, used = [], []

    def push(source, target, partner):
        at = len(used)
        used.append(at)
        copy = pltpu.make_async_remote_copy(
            src_ref=source,
            dst_ref=target,
            send_sem=send_sem.at[at],
            recv_sem=recv_sem.at[at],
            device_id=partner,
            device_id_type=pl.DeviceIdType.MESH,
        )
        copy.start()
        sent.append(copy)
        return copy

    quarter, part_rows = wo_sum.shape[0], wo_ring.shape[1]

    def part_start(owner):
        return pl.multiple_of(jnp.minimum(owner * part_rows, quarter - part_rows), 16)

    def rows_grad(distance, out):
        block = place ^ distance
        for i, ref in enumerate(grads):
            joined[:, i * TILE : (i + 1) * TILE] = ref[0, block]

        @pl.loop(0, width // 256)
        def _(i):
            cols = pl.ds(pl.multiple_of(i * 256, 256), 256)
            out[:, cols] = dot(joined[...], w_ref[cols, :], NT).astype(out.dtype)

        if width % 256:
            cols = pl.ds(width // 256 * 256, width % 256)
            out[:, cols] = dot(joined[...], w_ref[cols, :], NT).astype(out.dtype)

    rows_grad(3, core_out)
    pl.semaphore_wait(barrier, 3 + len(others))
    to_core = push(core_out, core_in.at[0], beside)
    loads[1].wait()
    loads[2].wait()
    wo_sum[...] = (wo_core[0].astype(F32) + wo_near[...].astype(F32)).astype(BF16)
    wo_to_ring = [
        push(wo_sum.at[pl.ds(part_start(other["tensor"]), part_rows)], wo_ring.at[k], other)
        for k, other in enumerate(others)
    ]
    rows_grad(2, hold)
    to_core.wait_recv()

    @pl.loop(0, row_count // chunk)
    def _(i):
        rows = pl.ds(pl.multiple_of(i * chunk, chunk), chunk)
        chip_out[rows, :] = (hold[rows, :] + core_in[0, rows, :].astype(F32)).astype(BF16)

    to_chip = push(chip_out, chip_in, across)

    loads[0].wait()
    to_far = [None] * 4

    def weights(part):
        @pl.loop(0, count)
        def _(block):
            if part < 3:
                pieces = [grads[3 * part + pair][0, block] for pair in range(PAIRS)]
            else:
                pieces = [grads[3 * i + PAIRS][0, block][:, :HEAD] for i in range(3)]
                pieces.append(jnp.zeros((row_count, own - 3 * HEAD), BF16))
            piece = dot(norms[block], jnp.concatenate(pieces, axis=1))

            @pl.when(block == 0)
            def _():
                acc[...] = piece

            @pl.when(block > 0)
            def _():
                acc[...] += piece

        sums[part] = acc[width : width + 8, :]
        keep[part] = acc[pl.ds(pl.multiple_of(fsdp * half, 16), half), :]
        far_out[part] = acc[pl.ds(pl.multiple_of((1 - fsdp) * half, 16), half), :].astype(BF16)
        to_far[part] = push(far_out.at[part], far_in.at[part], far)

    def joined_far(part):
        to_far[part].wait_recv()
        return keep[part] + far_in[part].astype(F32)

    def start_of(owner):
        return pl.multiple_of(jnp.minimum(owner * shard, half - shard), 16)

    to_ring, to_all, to_near = [None] * 4, [None] * 4, [None] * 4

    def ring(part, total):
        sums_in[part] = total.astype(BF16)
        to_ring[part] = [
            push(
                sums_in.at[part, pl.ds(start_of(other["tensor"]), shard)],
                ring_in.at[part, k],
                other,
            )
            for k, other in enumerate(others)
        ]

    def spread(part):
        total = sums_in[part, pl.ds(start_of(tensor), shard), :].astype(F32)
        for k, copy in enumerate(to_ring[part]):
            copy.wait_recv()
            total = total + ring_in[part, k].astype(F32)
        ring_all[part, tensor] = total.astype(BF16)
        to_all[part] = [
            push(ring_all.at[part, tensor], ring_all.at[part, tensor], other) for other in others
        ]

    def gather(part):
        for copy in to_all[part]:
            copy.wait_recv()
        for owner in range(tensors - 1):
            whole[part, owner * shard : (owner + 1) * shard] = ring_all[part, owner]
        rest = (tensors - 1) * shard
        whole[part, rest:] = ring_all[part, tensors - 1, tensors * shard - half :]
        if part < 3:
            to_near[part] = [
                push(whole.at[part], near_in.at[part, 0], beside),
                push(whole.at[part], near_in.at[part, 1], across),
            ]

    weights(3)
    to_core.wait_send()
    sent.remove(to_core)
    rows_grad(1, core_out)
    to_core_2 = push(core_out, core_in.at[1], beside)
    left_out[0] = joined_far(3).astype(BF16)
    to_left = push(left_out.at[0], left_in.at[0], beside)
    weights(0)
    to_left.wait_recv()
    left_out[1] = (left_out[0].astype(F32) + left_in[0].astype(F32)).astype(BF16)
    to_left = push(left_out.at[1], left_in.at[1], across)
    ring(0, joined_far(0))
    weights(1)
    wo_total = wo_sum[pl.ds(part_start(tensor), part_rows), :].astype(F32)
    for k, copy in enumerate(wo_to_ring):
        copy.wait_recv()
        wo_total = wo_total + wo_ring[k].astype(F32)
    wo_chip[0] = wo_total.astype(BF16)
    wo_to_chip = push(wo_chip.at[0], wo_chip.at[1], across)
    ring(1, joined_far(1))
    weights(2)
    spread(0)
    rows_grad(0, hold)
    ring(2, joined_far(2))
    to_left.wait_recv()
    ring(3, left_out[1].astype(F32) + left_in[1].astype(F32))
    to_core_2.wait_recv()
    wo_to_chip.wait_recv()
    wo_all[tensor] = (wo_chip[0].astype(F32) + wo_chip[1].astype(F32)).astype(BF16)
    wo_to_all = [push(wo_all.at[tensor], wo_all.at[tensor], other) for other in others]
    spread(1)
    gather(0)
    to_chip.wait_recv()

    vec_out[0, :8] = jnp.zeros((8, vec_out.shape[2]), F32)
    vec_out[0, 8:] = given_ref[...]
    chunks = row_count // chunk

    def chunk_rows(i):
        return pl.ds(pl.multiple_of(i * chunk, chunk), chunk)

    def row_loads(i):
        slot = i % 2
        return [
            pltpu.make_async_copy(gh_ref.at[chunk_rows(i)], gh_s.at[slot], local_sem.at[3 + slot]),
            pltpu.make_async_copy(rows_ref.at[chunk_rows(i)], rows_s.at[slot], local_sem.at[5 + slot]),
        ]

    for load in row_loads(0):
        load.start()

    @pl.loop(0, chunks)
    def _(i):
        @pl.when(i + 1 < chunks)
        def _():
            for load in row_loads(i + 1):
                load.start()

        for load in row_loads(i):
            load.wait()

        rows = chunk_rows(i)
        unit, rate = normalize(rows_s[i % 2, :, :width].astype(F32))
        grad = hold[rows, :] + core_in[1, rows, :].astype(F32) + chip_in[rows, :].astype(F32)
        back = normalize_back(unit, rate, grad * gain_ref[...])
        out = (gh_s[i % 2] + back).astype(BF16)

        @pl.when(i < prompt_rows // chunk)
        def _():
            prompt_ref[0, rows, :] = out

        @pl.when(i >= prompt_rows // chunk)
        def _():
            cont_ref[0, chunk_rows(i - prompt_rows // chunk), :] = out

        vec_out[0, 0:1, :width] += jnp.sum(grad * unit, axis=0, keepdims=True)
        vec_out[0, 1:2, :width] += jnp.sum(grad, axis=0, keepdims=True)

    spread(2)
    for row, part in ((2, 0), (3, 2)):
        cols = pl.ds(pl.multiple_of(place * own, own), own)
        vec_out[0, row : row + 1, cols] = sums[part, 0:1, :]
        left = slice(part * HEAD, (part + 1) * HEAD)
        vec_out[0, row : row + 1, width - HEAD : width] = sums[3, 0:1, left]
    spread(3)
    gather(1)

    def forward(part):
        to_near[part][1].wait_recv()
        return push(near_in.at[part, 1], near_in.at[part, 2], beside)

    def store(part, passed):
        to_near[part][0].wait_recv()
        passed.wait_recv()
        sources = [whole.at[part]] + [near_in.at[part, i] for i in range(3)]
        for distance, source in enumerate(sources):
            for block in range(count):

                @pl.when(place ^ distance == block)
                def _():
                    start = part * width + block * own
                    qkv_ref[:, start : start + own] = source[...]

    partners = (beside, across, far, {"tensor": tensor ^ 1}, {"tensor": tensor ^ 2})

    def exchange(level):
        return push(vec_out.at[level], vec_in.at[level], partners[level])

    def add(level, copy):
        copy.wait_recv()
        vec_out[level + 1] = vec_out[level] + vec_in[level]

    add(0, exchange(0))
    passed_0 = forward(0)
    step = exchange(1)
    gather(2)
    add(1, step)
    step = exchange(2)
    gather(3)
    store(0, passed_0)
    add(2, step)
    for copy in wo_to_all:
        copy.wait_recv()
    for owner in range(tensors - 1):
        wo_core[0, owner * part_rows : (owner + 1) * part_rows] = wo_all[owner]
    rest = (tensors - 1) * part_rows
    wo_core[0, rest:] = wo_all[tensors - 1, tensors * part_rows - quarter :]
    wo_to_core = push(wo_core.at[0], wo_core.at[1], beside)
    step = exchange(3)
    passed_1 = forward(1)
    for part in range(3):
        cols = slice((part + 1) * width - HEAD, (part + 1) * width)
        qkv_ref[:, cols] = whole[3, :, part * HEAD : (part + 1) * HEAD]
    add(3, step)
    step = exchange(4)
    store(1, passed_1)
    passed_2 = forward(2)
    add(4, step)
    vec_ref[...] = vec_out[5]
    wo_to_core.wait_recv()
    core = place % 2
    for away in range(2):
        wo_ref[pl.ds(pl.multiple_of((core ^ away) * quarter, 16), quarter), :] = wo_core[away]
    store(2, passed_2)
    for copy in sent:
        copy.wait_send()


def tail(
    grads, w_own, normed, rows, grad_hidden, gain, vectors, out_keep, out_come, prompt_rows, after=()
):
    count, depth, row_count = normed.shape
    width, cols = w_own.shape
    half, own = width // 2, 2 * PAIRS * HEAD
    tensors = lax.axis_size("tensor")
    shard = -(-half // tensors // 16) * 16
    padded = rows.shape[1]
    in_vmem = pl.BlockSpec(memory_space=pltpu.VMEM)
    vmem = lambda *shape, kind=BF16: pltpu.VMEM(shape, kind)
    copies = 4 + 4 * 2 * (tensors - 1) + 3 + 3 * 3 + 2 + 5 + 2 * (tensors - 1) + 2
    given = len(grads) + 8
    quarter = width // 4
    part_rows = -(-quarter // tensors // 16) * 16

    def body(*refs):
        tail_kernel(prompt_rows, *refs[:given], *refs[given + len(after) :])

    return pl.pallas_call(
        body,
        in_specs=[in_vmem] * (len(grads) + 1) + [ANYWHERE] * 5 + [in_vmem] * 2 + [ANYWHERE] * len(after),
        out_specs=[in_vmem] * 5,
        out_shape=[
            shape_of(1, prompt_rows, width),
            shape_of(1, row_count - prompt_rows, width),
            shape_of(half, 3 * width),
            shape_of(half, width),
            shape_of(16, padded, kind=F32),
        ],
        scratch_shapes=[
            vmem(*normed.shape),
            vmem(2, TILE, padded),
            vmem(2, TILE, width, kind=F32),
            vmem(row_count, cols),
            vmem(row_count, width, kind=F32),
            vmem(row_count, width),
            vmem(2, row_count, width),
            vmem(row_count, width),
            vmem(row_count, width),
            vmem(depth, own, kind=F32),
            vmem(4, half, own, kind=F32),
            vmem(4, half, own),
            vmem(4, half, own),
            vmem(4, 8, own, kind=F32),
            vmem(4, half, own),
            vmem(4, tensors - 1, shard, own),
            vmem(4, tensors, shard, own),
            vmem(4, half, own),
            vmem(3, 3, half, own),
            vmem(2, half, own),
            vmem(2, half, own),
            vmem(6, 16, padded, kind=F32),
            vmem(5, 16, padded, kind=F32),
            vmem(quarter, width),
            vmem(quarter, width),
            vmem(tensors - 1, part_rows, width),
            vmem(2, part_rows, width),
            vmem(tensors, part_rows, width),
            vmem(2, quarter, width),
            pltpu.SemaphoreType.DMA((7,)),
            pltpu.SemaphoreType.DMA((copies,)),
            pltpu.SemaphoreType.DMA((copies,)),
        ],
        compiler_params=pltpu.CompilerParams(
            vmem_limit_bytes=62 << 20, collective_id=1, has_side_effects=True
        ),
        cost_estimate=pl.CostEstimate(
            flops=4 * count * row_count * width * cols, bytes_accessed=30 << 20, transcendentals=0
        ),
        name="tail",
    )(*grads, w_own, normed, rows, grad_hidden, out_keep, out_come, gain[None], vectors, *after)


def join_kernel(spot_ref, *refs):
    firsts, lasts, (keep_o, come_o) = refs[:4], refs[4:8], refs[8:10]
    out_f, sum_f, out_p, sum_p, out_o, sum_o, total = refs[10:]
    step = pl.program_id(0)
    eighth = out_f.shape[2]
    chip = spot_ref[4] // 2
    sums_o = (keep_o[...].astype(F32) + come_o[...].astype(F32)).astype(BF16)
    sum_o[...] = sums_o[0]
    out_o[...] = sums_o[1]
    for entries, here in ((firsts, step < 2), (lasts, step >= 2)):
        keep_f, come_f, keep_p, come_p = entries

        @pl.when(here)
        def _():
            for at in range(2):
                total[...] = keep_f[0, at].astype(F32) + come_f[0, at].astype(F32)
                for target, away in ((sum_f, 0), (out_f, 1)):
                    rows = pl.ds(pl.multiple_of((chip ^ away) * eighth, 8), eighth)
                    target[0, at] = total[rows, :].astype(BF16)
            for target, at in ((sum_p, 0), (out_p, 1)):
                target[0] = (keep_p[at, 0].astype(F32) + come_p[at, 0].astype(F32)).astype(BF16)


def join(spot, firsts, lasts, outs, after=()):
    _, _, quarter, hidden = firsts[0].shape
    specs = []
    for part in (lambda k: jnp.minimum(k, 1), lambda k: jnp.maximum(k - 2, 0)):
        by_part = pl.BlockSpec((1, 2, quarter, hidden), lambda k, s, part=part: (part(k), 0, 0, 0))
        by_far = pl.BlockSpec((2, 1, quarter, hidden), lambda k, s, part=part: (0, part(k), 0, 0))
        specs += [by_part, by_part, by_far, by_far]
    eighth = quarter // 2
    fc = pl.BlockSpec((1, 2, eighth, hidden), lambda k, s: (k, 0, 0, 0))
    proj = pl.BlockSpec((1, quarter, hidden), lambda k, s: (k, 0, 0))
    return launch(
        join_kernel,
        "join",
        (spot,),
        (4,),
        (*firsts, *lasts, *outs),
        specs + [blocks(*entry.shape) for entry in outs],
        [
            (fc, shape_of(4, 2, eighth, hidden)),
            (fc, shape_of(4, 2, eighth, hidden)),
            (proj, shape_of(4, quarter, hidden)),
            (proj, shape_of(4, quarter, hidden)),
            whole_out(*outs[0].shape[1:]),
            whole_out(*outs[0].shape[1:]),
        ],
        scratch=[pltpu.VMEM((quarter, hidden), F32)],
        traffic=30,
        after=after,
    )


def own_columns(matrix, place):
    width = matrix.shape[1] // 3
    own = 2 * PAIRS * HEAD
    blank = jnp.zeros((matrix.shape[0], TILE - HEAD), matrix.dtype)
    pieces = []
    for part in range(3):
        whole = matrix[:, part * width : (part + 1) * width]
        pieces += [
            lax.dynamic_slice_in_dim(whole, place * own, own, 1),
            whole[:, width - HEAD :],
            blank,
        ]
    return jnp.concatenate(pieces, axis=1)


def local_heads(
    prompt_in,
    cont_in,
    cont_seg,
    ln1_gain,
    ln1_bias,
    w_qkv,
    qv_bias,
    w_out,
    out_bias,
    ln2_gain,
    ln2_bias,
    w_fc,
    fc_bias,
    w_proj,
    proj_bias,
    prompt_cot,
    cont_cot,
):
    width = prompt_in.shape[2]
    prompt_rows, cont_rows = prompt_in.shape[1], cont_in.shape[1]
    row_count = prompt_rows + cont_rows
    count = lax.axis_size("ctx")
    place = lax.axis_index("ctx")
    core, chip = place % 2, place // 2
    fsdp = lax.axis_index("fsdp")
    tensor = lax.axis_index("tensor")
    tensors = lax.axis_size("tensor")
    own_width = 2 * PAIRS * HEAD
    half, hidden_units = w_fc.shape
    quarter = half // 2
    eighth = quarter // 2
    padded = (width + TILE - 1) // TILE * TILE
    at = place.reshape(1)
    spot = jnp.stack([core, fsdp, tensor, jnp.int32(tensors), place])

    rows_own, w_mine = pack(at, prompt_in, cont_in, w_qkv, padded)
    rows_across = swap(rows_own, "ctx", 2)
    rows_beside = swap(rows_own, "ctx", 1)
    w_far = swap(w_mine, "fsdp", 1)
    zero_bias = jnp.zeros_like(qv_bias[0])
    col_bias = own_columns(jnp.concatenate([qv_bias[0], zero_bias, qv_bias[1]])[None], place)[0]

    mine, for_far, for_two, for_three, grad_layer, grad_flip = pack_more(
        core.reshape(1), w_fc, w_proj, fc_bias, prompt_cot, cont_cot, (rows_own,)
    )
    out_mine = w_out.astype(BF16)
    one_away = turn(mine, "tensor", 1)

    w_own = jnp.concatenate(in_order(w_mine, w_far, fsdp), axis=0)
    step_in = functools.partial(
        project, w_own=w_own, gain=ln1_gain, bias=ln1_bias, col_bias=col_bias, count=count
    )
    made = step_in(at, rows_own, before=None, after=(mine,))
    made, for_far, out_mine = step_in(
        at ^ 1, rows_beside, before=made, carry=(for_far, out_mine)
    )
    near_far, out_far = swap(for_far, "fsdp", 1), swap(out_mine, "fsdp", 1)
    (rows_across,) = behind((rows_across,), made[1])
    rows_corner = swap(rows_across, "ctx", 1)
    made = step_in(at ^ 2, rows_across, before=made, after=(one_away,))
    made, for_two = step_in(at ^ 3, rows_corner, before=made, carry=(for_two,))
    two_away, one_far = turn(for_two, "tensor", 2), swap(one_away, "fsdp", 1)
    normed, q, k, v, kt, vt = made

    labels = cont_seg[0].reshape(count, cont_rows)
    seg_col, seg_row = labels[:, :, None], labels[:, None, :]
    near = (q, k, vt, seg_col, seg_row, prompt_rows)
    heads_out, lses = [], []
    returned = [[] for _ in range(count)]

    def send_back(outs, lse):
        heads_out.append(outs)
        lses.append(lse)
        for distance, out in enumerate(outs):
            returned[distance].append(swap(out, "ctx", distance) if distance else out)

    (*outs, lse), for_three = attend(0, 2, count, at, *near, carry=(for_three,))
    three_away = turn(for_three, "tensor", 3)
    send_back(outs, lse)
    *outs, lse = attend(1, 2, count, at, *near, after=(outs[0],))
    send_back(outs, lse)
    (two_away,) = behind((two_away,), outs[0])
    two_far = swap(two_away, "fsdp", 1)
    last_out, lse = attend(PAIRS, 1, 1, at, *near, after=(outs[0], two_away))
    lses.append(lse)
    near_far, one_far = behind((near_far, one_far), last_out)
    beside_first = (
        swap(jnp.stack([mine, near_far]), "ctx", 1),
        swap(jnp.stack([one_away, one_far]), "ctx", 1),
    )
    out_full = jnp.concatenate(in_order(out_mine, out_far, fsdp), axis=0)
    pieces = [piece for entry in returned for piece in entry]
    (hidden, mlp_low, mlp_flip), three_away, two_far = merge(
        at,
        rows_own,
        out_full,
        out_bias,
        ln2_gain,
        ln2_bias,
        pieces,
        last_out,
        carry=(three_away, two_far),
    )
    three_far = swap(three_away, "fsdp", 1)
    beside_two = swap(jnp.stack([two_away, two_far]), "ctx", 1)

    given = (spot, mlp_low, grad_layer, mlp_flip, grad_flip)
    mlp_out, grad_mlp_in, *grads_first, bias_first = mlp(
        *given, (mine, one_away), (near_far, one_far), beside_first
    )
    (three_far,) = behind((three_far,), bias_first)
    beside_last = (beside_two, swap(jnp.stack([three_away, three_far]), "ctx", 1))
    come_first = [swap(grads_first[1], "ctx", 1), swap(grads_first[3], "ctx", 1)]
    mlp_out, grad_mlp_in, *grads_last, bias_last = mlp(
        *given,
        (two_away, three_away),
        (two_far, three_far),
        beside_last,
        before=(mlp_out, grad_mlp_in),
    )
    come_last = [swap(grads_last[1], "ctx", 1), swap(grads_last[3], "ctx", 1)]
    grad_fc_bias = jnp.concatenate([bias_first, bias_last], axis=0)
    prompt_out, cont_out, grad_hidden, *rest = bend(
        jnp.stack([place, fsdp]),
        mlp_out,
        grad_mlp_in,
        hidden,
        grad_layer,
        out_full,
        ln2_gain,
        proj_bias,
        pieces,
        last_out,
        prompt_rows,
    )
    grads_own, (grad_last, out_keep, out_send, sums2) = rest[:count], rest[count:]
    grads_all = [grads_own[0]] + [swap(grads_own[k], "ctx", k) for k in range(1, count)]

    def added(left, right):
        return left.astype(F32) + right.astype(F32)

    def over_tensor(parts, token):
        come = [turn(parts[k], "tensor", -k) for k in range(1, tensors)]
        total = parts[0].astype(F32)
        for part in behind(come, token):
            total = total + part.astype(F32)
        return total

    def back(pair, tile, heads, grads, outs, after=()):
        return attend_back(
            pair, tile, heads, at, q, k, v, kt, lses[pair], seg_col, seg_row, grads, outs, prompt_rows, after
        )

    grads_left = back(PAIRS, 0, 1, [grad_last], [last_out])
    out_f, sum_f, out_p, sum_p, out_o, sum_o = join(
        spot,
        (grads_first[0], come_first[0], grads_first[2], come_first[1]),
        (grads_last[0], come_last[0], grads_last[2], come_last[1]),
        (out_keep, swap(out_send, "ctx", 1)),
        (grads_left[0], *grads_all[1:]),
    )
    grads_pair = [back(0, 0, 2, grads_all, heads_out[0], (out_f, out_p))]
    come_o = swap(out_o, "fsdp", 1)
    come_f, come_p = swap(out_f, "ctx", 2), swap(out_p, "fsdp", 1)
    come_f, come_p = behind((come_f, come_p), grads_pair[0][0])
    sum_f = added(sum_f, come_f).astype(BF16)
    sum_p = added(sum_p, come_p).astype(BF16)
    out_f, sum_f = sum_f[:, 1], sum_f[:, 0]
    grads_pair.append(back(1, 1, 2, grads_all, heads_out[1], (out_f, sum_p, grads_pair[0][0])))
    (come_f,) = behind((swap(out_f, "fsdp", 1),), grads_pair[1][0])
    sum_f = added(sum_f, come_f).astype(BF16)
    sum_p = over_tensor(sum_p, grads_pair[1][0]).astype(BF16)
    ordered = [entry[part] for part in range(3) for entry in (*grads_pair, grads_left)]
    vectors = jnp.concatenate([sums2, jnp.zeros((tensors, hidden_units), F32)], axis=0)
    for distance in range(tensors):
        vectors = lax.dynamic_update_slice(
            vectors, grad_fc_bias[distance], (4 + (tensor - distance) % tensors, 0)
        )
    vectors = jnp.pad(vectors, ((0, 0), (0, padded - width)))
    prompt_grad, cont_grad, sum_qkv, sum_out, late = tail(
        ordered,
        w_own,
        normed,
        rows_own,
        grad_hidden,
        ln1_gain,
        vectors,
        sum_o,
        come_o,
        prompt_rows,
        (sum_f, sum_p),
    )
    sum_f = over_tensor(sum_f, late).astype(BF16)
    (come_p,) = behind((swap(sum_p, "ctx", 2),), late)
    sum_p = added(sum_p, come_p).astype(BF16)
    far_f = swap(sum_f, "ctx", 2)
    sum_f = jnp.concatenate(in_order(sum_f, far_f, chip), axis=0)
    both = jnp.stack([sum_f, sum_p])
    both = jnp.concatenate(in_order(both, swap(both, "ctx", 1), core), axis=1).astype(F32)
    own_fc, own_proj = both[0], both[1].T


    fc_bias_sum = lax.dynamic_index_in_dim(late, 12 + tensor, 0, False)[:hidden_units]
    return (
        prompt_out,
        cont_out,
        prompt_grad,
        cont_grad,
        late[0, :width],
        late[1, :width],
        sum_qkv.astype(F32),
        late[2:4, :width],
        sum_out.astype(F32),
        late[8, :width],
        late[9, :width],
        late[10, :width],
        own_fc,
        fc_bias_sum,
        own_proj,
        late[11, :width],
    )


def solution(mesh):
    placed = (
        P(("fsdp", "tensor"), "ctx", None),
        P(("fsdp", "tensor"), "ctx", None),
        P(("fsdp", "tensor"), None),
        P(),
        P(),
        P("fsdp", None),
        P(),
        P("fsdp", None),
        P(),
        P(),
        P(),
        P("fsdp", "tensor"),
        P("tensor"),
        P("tensor", "fsdp"),
        P(),
        P(("fsdp", "tensor"), "ctx", None),
        P(("fsdp", "tensor"), "ctx", None),
    )
    by_heads = HEADS // mesh.shape["ctx"] == PAIRS * 2 and HEADS % mesh.shape["ctx"] == 1
    return jax.shard_map(
        local_heads if by_heads else local_rows,
        mesh=mesh,
        in_specs=placed,
        out_specs=(
            P(("fsdp", "tensor"), "ctx", None),
            P(("fsdp", "tensor"), "ctx", None),
            P(("fsdp", "tensor"), "ctx", None),
            P(("fsdp", "tensor"), "ctx", None),
            P(),
            P(),
            P("fsdp", None),
            P(),
            P("fsdp", None),
            P(),
            P(),
            P(),
            P("fsdp", "tensor"),
            P("tensor"),
            P("tensor", "fsdp"),
            P(),
        ),
        check_vma=False,
    )
```

```python
import functools

import jax
import jax.numpy as jnp
from jax import lax
from jax.experimental import pallas as pl
from jax.experimental.pallas import tpu as pltpu
from jax.sharding import PartitionSpec as P

HEADS = 17
HEAD = 64


def passed_along(value, axis, steps):
    count = lax.axis_size(axis)
    leading, last = (max(0, -steps), min(count, count - steps))
    return lax.ppermute(value, axis, [(source, source + steps) for source in range(leading, last)])


def layer_norm(values, norm_gain, norm_bias):
    average = jnp.mean(values, axis=-1, keepdims=True)
    centred = values - average
    variance = jnp.mean(centred * centred, axis=-1, keepdims=True)
    return centred * lax.rsqrt(variance + 1e-05) * norm_gain + norm_bias


def gelu_tanh(values):
    return jax.nn.gelu(values, approximate=True)


def inner_first(left_op, right_op):
    return lax.dot_general(
        left_op, right_op, (((0,), (0,)), ((), ())), preferred_element_type=jnp.float32
    )


def inner_last(left_op, right_op):
    return lax.dot_general(
        left_op, right_op, (((1,), (1,)), ((), ())), preferred_element_type=jnp.float32
    )


def to_heads(values):
    return jnp.swapaxes(values.reshape(values.shape[0], HEADS, HEAD), 0, 1)


def from_heads(values):
    return jnp.swapaxes(values, 0, 1).reshape(values.shape[1], values.shape[0] * values.shape[2])


def fetch_prompt(rows_kv):
    return lax.all_gather(rows_kv, "ctx", axis=0, tiled=True)


def local_rows(
    prompt_in,
    cont_in,
    cont_seg,
    ln1_gain,
    ln1_bias,
    w_qkv,
    qv_bias,
    w_out,
    out_bias,
    ln2_gain,
    ln2_bias,
    w_fc,
    fc_bias,
    w_proj,
    proj_bias,
    prompt_cot,
    cont_cot,
):
    model_width = prompt_in.shape[2]
    prompt_rows = prompt_in.shape[1]
    cont_rows = cont_in.shape[1]
    row_count = prompt_rows + cont_rows
    ctx_count = lax.axis_size("ctx")
    ctx_place = lax.axis_index("ctx")
    prompt_total = prompt_rows * ctx_count
    qkv_full, out_full = (
        lax.all_gather(w_qkv.astype(jnp.bfloat16), "fsdp", axis=0, tiled=True),
        lax.all_gather(w_out.astype(jnp.bfloat16), "fsdp", axis=0, tiled=True),
    )
    fc_full, proj_full = (
        lax.all_gather(w_fc.astype(jnp.bfloat16), "fsdp", axis=0, tiled=True),
        lax.all_gather(w_proj.astype(jnp.bfloat16), "fsdp", axis=1, tiled=True),
    )
    row_ids = jnp.arange(row_count, dtype=jnp.int32)
    labels_all = cont_seg[0]
    own_labels = lax.dynamic_slice_in_dim(labels_all, ctx_place * cont_rows, cont_rows)
    earlier_labels = lax.dynamic_slice_in_dim(
        labels_all, jnp.maximum(ctx_place - 1, 0) * cont_rows, cont_rows
    )
    query_labels = jnp.concatenate([jnp.full((prompt_rows,), -1, jnp.int32), own_labels])
    query_prompt = ctx_place * prompt_rows + row_ids
    query_cont = ctx_place * cont_rows + row_ids - prompt_rows
    is_cont = row_ids >= prompt_rows
    prompt_ids = jnp.arange(prompt_total, dtype=jnp.int32)
    near_ids = (ctx_place - 1) * cont_rows + jnp.arange(2 * cont_rows, dtype=jnp.int32)
    near_labels = jnp.concatenate([earlier_labels, own_labels])
    allowed_far = is_cont[:, None] | (prompt_ids[None, :] <= query_prompt[:, None])
    allowed_near = (
        (query_labels[:, None] == near_labels[None, :])
        & (near_ids[None, :] <= query_cont[:, None])
        & (near_ids[None, :] >= 0)
    )
    allowed = jnp.concatenate([allowed_far, allowed_near], 1)
    inputs = jnp.concatenate([prompt_in[0], cont_in[0]], 0).astype(jnp.float32)
    normed, norm1_back = jax.vjp(layer_norm, inputs, ln1_gain, ln1_bias)
    normed_low = normed.astype(jnp.bfloat16)
    projected = jnp.dot(normed_low, qkv_full, preferred_element_type=jnp.float32)
    queries = (projected[:, :model_width] + qv_bias[0]).astype(jnp.bfloat16)
    key_value = jnp.concatenate(
        [projected[:, model_width : 2 * model_width], projected[:, 2 * model_width :] + qv_bias[1]],
        1,
    ).astype(jnp.bfloat16)
    own_cont_kv = key_value[prompt_rows:]
    earlier_kv = passed_along(own_cont_kv, "ctx", 1)
    prompt_kv = fetch_prompt(key_value[:prompt_rows])
    keys_all = jnp.concatenate([prompt_kv, earlier_kv, own_cont_kv], 0)
    query_heads = to_heads(queries)
    key_heads = to_heads(keys_all[:, :model_width])
    value_heads = to_heads(keys_all[:, model_width:])

    def head_forward(operands):
        query_head, key_head, value_head = operands
        scores = inner_last(query_head, key_head) * 0.125
        scores = jnp.where(allowed, scores, -1e30)
        row_max = jnp.max(scores, axis=1, keepdims=True)
        exponent = jnp.exp(scores - row_max)
        row_total = jnp.sum(exponent, axis=1, keepdims=True)
        probability = (exponent / row_total).astype(jnp.bfloat16)
        head_out = jnp.dot(probability, value_head, preferred_element_type=jnp.float32)
        return (head_out.astype(jnp.bfloat16), (row_max + jnp.log(row_total))[:, 0])

    heads_out, logsum = lax.map(head_forward, (query_heads, key_heads, value_heads))
    attended = from_heads(heads_out)
    hidden = inputs + jnp.dot(attended, out_full, preferred_element_type=jnp.float32) + out_bias
    mlp_in, norm2_back = jax.vjp(layer_norm, hidden, ln2_gain, ln2_bias)
    mlp_low = mlp_in.astype(jnp.bfloat16)
    mlp_rows = lax.all_gather(mlp_low, "tensor", axis=0, tiled=True)
    pre_act = jnp.dot(mlp_rows, fc_full, preferred_element_type=jnp.float32) + fc_bias
    activated, gelu_back = jax.vjp(gelu_tanh, pre_act)
    act_low = activated.astype(jnp.bfloat16)
    partial_out = jnp.dot(act_low, proj_full, preferred_element_type=jnp.float32)
    mlp_out = lax.psum_scatter(
        partial_out.astype(jnp.bfloat16), "tensor", scatter_dimension=0, tiled=True
    ).astype(jnp.float32)
    layer_out = (hidden + mlp_out + proj_bias).astype(jnp.bfloat16)
    grad_layer = jnp.concatenate([prompt_cot[0], cont_cot[0]], 0)
    grad_float = grad_layer.astype(jnp.float32)
    grad_proj_bias = jnp.sum(grad_float, axis=0)
    grad_rows = lax.all_gather(grad_layer, "tensor", axis=0, tiled=True)
    grad_w_proj = inner_first(act_low, grad_rows)
    grad_act = inner_last(grad_rows, proj_full)
    grad_pre = gelu_back(grad_act)[0].astype(jnp.bfloat16)
    grad_fc_bias = jnp.sum(grad_pre.astype(jnp.float32), axis=0)
    grad_w_fc = inner_first(mlp_rows, grad_pre)
    grad_mlp_part = inner_last(grad_pre, fc_full)
    grad_mlp_in = lax.psum_scatter(grad_mlp_part, "tensor", scatter_dimension=0, tiled=True)
    grad_hidden_norm, grad_ln2_gain, grad_ln2_bias = norm2_back(grad_mlp_in)
    grad_hidden = grad_float + grad_hidden_norm
    grad_out_bias = jnp.sum(grad_hidden, axis=0)
    grad_branch = grad_hidden.astype(jnp.bfloat16)
    grad_w_out = inner_first(attended, grad_branch)
    grad_attended = inner_last(grad_branch, out_full).astype(jnp.bfloat16)
    prompt_again = fetch_prompt(key_value[:prompt_rows])
    keys_back = jnp.concatenate([prompt_again, earlier_kv, own_cont_kv], 0)
    key_back_heads = to_heads(keys_back[:, :model_width])
    value_back_heads = to_heads(keys_back[:, model_width:])

    def head_backward(operands):
        query_head, key_head, value_head, grad_head, logsum_head = operands
        scores = inner_last(query_head, key_head) * 0.125
        scores = jnp.where(allowed, scores, -1e30)
        probability = jnp.exp(scores - logsum_head[:, None])
        prob_low = probability.astype(jnp.bfloat16)
        grad_prob = inner_last(grad_head, value_head)
        centre = jnp.sum(probability * grad_prob, axis=1, keepdims=True)
        grad_scores = (probability * (grad_prob - centre)).astype(jnp.bfloat16)
        grad_query = jnp.dot(grad_scores, key_head, preferred_element_type=jnp.float32) * 0.125
        grad_key = inner_first(grad_scores, query_head) * 0.125
        grad_value = inner_first(prob_low, grad_head)
        return (grad_query, grad_key, grad_value)

    head_operands = (query_heads, key_back_heads, value_back_heads, to_heads(grad_attended), logsum)
    grad_q_heads, grad_k_heads, grad_v_heads = lax.map(head_backward, head_operands)
    grad_queries = from_heads(grad_q_heads).astype(jnp.bfloat16)
    grad_kv = jnp.concatenate([from_heads(grad_k_heads), from_heads(grad_v_heads)], 1)
    prompt_grad_kv = lax.psum_scatter(
        grad_kv[:prompt_total], "ctx", scatter_dimension=0, tiled=True
    )
    from_later = passed_along(
        grad_kv[prompt_total : prompt_total + cont_rows].astype(jnp.bfloat16), "ctx", -1
    ).astype(jnp.float32)
    cont_grad_kv = grad_kv[prompt_total + cont_rows :] + from_later
    grad_kv_rows = jnp.concatenate([prompt_grad_kv, cont_grad_kv], 0).astype(jnp.bfloat16)
    grad_projected = jnp.concatenate([grad_queries, grad_kv_rows], 1)
    grad_qv_bias = jnp.stack(
        [
            jnp.sum(grad_queries.astype(jnp.float32), axis=0),
            jnp.sum(grad_kv_rows[:, model_width:].astype(jnp.float32), axis=0),
        ]
    )
    grad_w_qkv = inner_first(normed_low, grad_projected)
    grad_normed = inner_last(grad_projected, qkv_full)
    grad_inputs_norm, grad_ln1_gain, grad_ln1_bias = norm1_back(grad_normed)
    grad_inputs = (grad_hidden + grad_inputs_norm).astype(jnp.bfloat16)
    shard_qkv, shard_out = (
        lax.psum_scatter(
            grad_w_qkv.astype(jnp.bfloat16), "fsdp", scatter_dimension=0, tiled=True
        ).astype(jnp.float32),
        lax.psum_scatter(
            grad_w_out.astype(jnp.bfloat16), "fsdp", scatter_dimension=0, tiled=True
        ).astype(jnp.float32),
    )
    sum_qkv, sum_out = lax.psum((shard_qkv, shard_out), ("ctx", "tensor"))
    sum_fc, sum_proj, sum_fc_bias = lax.psum(
        (grad_w_fc, grad_w_proj, grad_fc_bias), ("fsdp", "ctx")
    )
    fsdp_place = lax.axis_index("fsdp")
    fsdp_rows = w_fc.shape[0]
    own_fc = lax.dynamic_slice_in_dim(sum_fc, fsdp_place * fsdp_rows, fsdp_rows, 0)
    own_proj = lax.dynamic_slice_in_dim(sum_proj, fsdp_place * fsdp_rows, fsdp_rows, 1)
    small_sums = lax.psum(
        (
            grad_ln1_gain,
            grad_ln1_bias,
            grad_qv_bias,
            grad_out_bias,
            grad_ln2_gain,
            grad_ln2_bias,
            grad_proj_bias,
        ),
        ("fsdp", "ctx", "tensor"),
    )
    return (
        layer_out[:prompt_rows][None],
        layer_out[prompt_rows:][None],
        grad_inputs[:prompt_rows][None],
        grad_inputs[prompt_rows:][None],
        small_sums[0],
        small_sums[1],
        sum_qkv,
        small_sums[2],
        sum_out,
        small_sums[3],
        small_sums[4],
        small_sums[5],
        own_fc,
        sum_fc_bias,
        own_proj,
        small_sums[6],
    )


PAIRS = 2
TILE = 2 * HEAD
BF16 = jnp.bfloat16
F32 = jnp.float32
LOG2E = 1.4426950408889634
SCALE2 = 0.125 * LOG2E
HINT = 0.2
NN = (((1,), (0,)), ((), ()))
NT = (((1,), (1,)), ((), ()))
TN = (((0,), (0,)), ((), ()))


def dot(left_op, right_op, dims=NN):
    return lax.dot_general(left_op, right_op, dims, preferred_element_type=F32)


def swap(value, axis, bit):
    count = lax.axis_size(axis)
    return lax.ppermute(value, axis, [(place, place ^ bit) for place in range(count)])


def turn(value, axis, steps):
    count = lax.axis_size(axis)
    return lax.ppermute(value, axis, [(place, (place + steps) % count) for place in range(count)])


def halves(values, heads=2):
    lane = lax.broadcasted_iota(jnp.int32, values.shape, 1)
    zero = jnp.zeros_like(values)
    return [jnp.where((lane < HEAD) == (head == 0), values, zero) for head in range(heads)]


ANYWHERE = pl.BlockSpec(memory_space=pl.ANY)


def blocks(*shape):
    return pl.BlockSpec(shape, lambda i, *_: (0,) * len(shape))


def shape_of(*shape, kind=BF16):
    return jax.ShapeDtypeStruct(shape, kind)


def launch(
    kernel, name, scalars, grid, operands, in_specs, outs, scratch=(), limit=48, flops=0, traffic=16, exps=0, after=(), carry=(), aliases=None
):
    out_specs, out_shapes = [out[0] for out in outs], [out[1] for out in outs]
    given = len(scalars) + len(operands)
    tied = given + len(after) + len(carry)

    def body(*refs):
        made = refs[tied : tied + len(outs)]
        kernel(*refs[:given], *made, *refs[tied + len(outs) + len(carry) :])

    links = {len(scalars) + here: there for here, there in (aliases or {}).items()}
    links.update({given + len(after) + i: len(outs) + i for i in range(len(carry))})
    out = pl.pallas_call(
        body,
        grid_spec=pltpu.PrefetchScalarGridSpec(
            num_scalar_prefetch=len(scalars),
            grid=grid,
            in_specs=list(in_specs) + [ANYWHERE] * (len(after) + len(carry)),
            out_specs=out_specs + [ANYWHERE] * len(carry),
            scratch_shapes=list(scratch),
        ),
        out_shape=out_shapes + [shape_of(*entry.shape, kind=entry.dtype) for entry in carry],
        input_output_aliases=links,
        compiler_params=pltpu.CompilerParams(vmem_limit_bytes=limit << 20),
        cost_estimate=pl.CostEstimate(
            flops=int(flops * HINT),
            bytes_accessed=int(traffic * HINT * (1 << 20)),
            transcendentals=int(exps * HINT),
        ),
        name=name,
    )(*scalars, *operands, *after, *carry)
    return (out[: len(outs)], *out[len(outs) :]) if carry else out


def behind(arrays, token):
    out = launch(
        lambda *refs: None, "behind", (), (1,), (), (), (), after=(token,), carry=tuple(arrays)
    )
    return out[1:]


def whole_out(*shape, kind=BF16):
    return blocks(*shape), shape_of(*shape, kind=kind)


def in_order(own, other, place):
    first = place == 0
    return jnp.where(first, own, other), jnp.where(first, other, own)


def open_kernel(*refs):
    prompt_ref, cont_ref, w_ref, fc_ref, proj_ref, wo_ref, gp_ref, gc_ref = refs[:8]
    fc_bias_ref, gain_ref, bias_ref, col_bias_ref = refs[8:12]
    norm_ref, q_ref, k_ref, v_ref, kt_ref, vt_ref = refs[12:18]
    w_own_ref, rows_ref, g_ref, gt_ref, mine_ref, one_ref, three_ref, far_ref, out_ref = refs[18:27]
    (
        rows_t,
        w_s,
        w_own,
        w_out,
        fc_s,
        proj_s,
        mine_s,
        g_t,
        normed,
        norms,
        tall_s,
        flat_s,
        turned,
        wo_f,
        wo_s,
        local_sem,
        send_sem,
        recv_sem,
        out_sem,
    ) = refs[27:]
    place = lax.axis_index("ctx")
    fsdp = lax.axis_index("fsdp")
    tensor = lax.axis_index("tensor")
    tensors = lax.axis_size("tensor")
    core = place % 2
    width, row_count = rows_t.shape[1], rows_t.shape[2]
    prompt_rows = prompt_ref.shape[1]
    half, quarter = width // 2, width // 4
    own = 2 * PAIRS * HEAD
    beside, across, far = {"ctx": place ^ 1}, {"ctx": place ^ 2}, {"fsdp": 1 - fsdp}
    others = [{"tensor": lax.rem(tensor + k, tensors)} for k in range(1, tensors)]

    barrier = pltpu.get_barrier_semaphore()
    for partner in (beside, across, far, *others):
        pl.semaphore_signal(barrier, inc=1, device_id=partner, device_id_type=pl.DeviceIdType.MESH)

    def load(source, target, at):
        copy = pltpu.make_async_copy(source, target, local_sem.at[at])
        copy.start()
        return copy

    def spans(ref):
        return ref.at[:, :prompt_rows], ref.at[:, prompt_rows:]

    own_prompt, own_cont = spans(rows_t.at[0])
    load_rows = [load(prompt_ref, own_prompt, 0), load(cont_ref, own_cont, 1)]
    load_w = load(w_ref, w_s, 2)
    mine_rows = pl.ds(pl.multiple_of(core * quarter, 16), quarter)
    load_mine = [load(fc_ref.at[mine_rows], fc_s, 3), load(proj_ref.at[mine_rows], proj_s, 4)]
    g_prompt, g_cont = spans(g_t)
    load_g = [load(gp_ref, g_prompt, 5), load(gc_ref, g_cont, 6)]
    load_wo = load(wo_ref, wo_f, 7)
    sent, used = [], []

    def push(source, target, partner):
        at = len(used)
        used.append(at)
        copy = pltpu.make_async_remote_copy(
            src_ref=source,
            dst_ref=target,
            send_sem=send_sem.at[at],
            recv_sem=recv_sem.at[at],
            device_id=partner,
            device_id_type=pl.DeviceIdType.MESH,
        )
        copy.start()
        sent.append(copy)
        return copy

    for copy in load_rows:
        copy.wait()
    pl.semaphore_wait(barrier, 3 + len(others))
    to_chip = [
        push(source, target, across) for source, target in zip(spans(rows_t.at[0]), spans(rows_t.at[2]))
    ]
    to_core = push(rows_t.at[0], rows_t.at[1], beside)

    load_w.wait()
    step = w_own.shape[1] // 3
    for part in range(3):
        for at in range((width - HEAD) // own):

            @pl.when(place == at)
            def _():
                start = part * width + at * own
                w_out[:, part * step : part * step + own] = w_s[:, start : start + own].astype(BF16)

        last = w_s[:, (part + 1) * width - HEAD : (part + 1) * width].astype(BF16)
        w_out[:, part * step + own : (part + 1) * step] = jnp.concatenate(
            [last, jnp.zeros((half, step - own - HEAD), BF16)], axis=1
        )
    mine_half = pl.ds(pl.multiple_of(fsdp * half, 16), half)
    to_far = push(w_out, w_own.at[mine_half], far)
    w_own[mine_half, :] = w_out[...]

    for copy in load_mine:
        copy.wait()
    mine_s[:quarter] = fc_s[...].astype(BF16)
    mine_s[quarter : 2 * quarter] = proj_s[...].astype(BF16)
    bias = fc_bias_ref[...]
    pieces = []
    for _ in range(3):
        piece = bias.astype(BF16)
        pieces.append(piece)
        bias = bias - piece.astype(F32)
    pieces.append(jnp.zeros((mine_s.shape[0] - 2 * quarter - 3, width), BF16))
    mine_s[2 * quarter :] = jnp.concatenate(pieces, axis=0)
    to_one = push(mine_s, one_ref, others[0])
    to_near = push(mine_s, far_ref, far)
    to_three = push(mine_s, three_ref, others[2])
    outs, put_at = [], []

    def put(source, target):
        copy = pltpu.make_async_copy(source, target, out_sem.at[len(put_at)])
        put_at.append(len(put_at))
        copy.start()
        outs.append(copy)
        return copy

    def take(copies):
        for copy in copies:
            copy.wait()
        outs[:] = [copy for copy in outs if all(copy is not done for done in copies)]

    put(mine_s, mine_ref)

    def out_rows(away):
        return pl.ds(pl.multiple_of((fsdp ^ away) * half + core * quarter, 16), quarter)

    load_wo.wait()
    wo_s[...] = wo_f[...].astype(BF16)
    put(wo_s, out_ref.at[mine_half])
    to_out = push(wo_s.at[mine_rows], out_ref.at[out_rows(0)], far)
    chunk = 128

    def over_rows(body):
        @pl.loop(0, row_count // chunk)
        def _(i):
            body(pl.ds(pl.multiple_of(i * chunk, chunk), chunk))

    for copy in load_g:
        copy.wait()
    put(g_t, gt_ref)

    def turn_rows(source, target):
        def body(rows):
            target[rows, :] = source[:, rows].T

        over_rows(body)

    turn_rows(g_t, turned.at[0])
    put(turned.at[0], g_ref)
    turn_rows(rows_t.at[0], turned.at[1])
    put(turned.at[1], rows_ref)

    extra = norms.shape[1] - width
    at_row = lax.broadcasted_iota(jnp.int32, (extra, row_count), 0)
    ones = jnp.where(at_row == 0, 1.0, 0.0).astype(BF16)
    norms[0, width:] = ones
    norms[1, width:] = ones

    def normalise(distance, slot):
        def body(rows):
            values = rows_t[distance, :, rows].astype(F32)
            average = jnp.mean(values, axis=0, keepdims=True)
            centred = values - average
            variance = jnp.mean(centred * centred, axis=0, keepdims=True)
            low = centred * lax.rsqrt(variance + 1e-05) * gain_ref[...] + bias_ref[...]
            low = low.astype(BF16)
            norms[slot, :width, rows] = low
            normed[rows, :] = low.T

        over_rows(body)

    def project(distance, slot):
        block = place ^ distance
        made = [put(norms.at[slot], norm_ref.at[block])]
        tiles = step // TILE
        for part, (out, flip) in enumerate(((q_ref, None), (k_ref, kt_ref), (v_ref, vt_ref))):
            cols = slice(part * step, (part + 1) * step)
            value = (dot(normed[...], w_own[:, cols]) + col_bias_ref[:, cols]).astype(BF16)
            for tile in range(tiles):
                piece = value[:, tile * TILE : (tile + 1) * TILE]
                tall_s[slot, :, (part * tiles + tile) * TILE : (part * tiles + tile + 1) * TILE] = piece
                if flip is not None:
                    flat_s[slot, part - 1, tile] = piece.T
            for tile in range(tiles):
                lanes = slice((part * tiles + tile) * TILE, (part * tiles + tile + 1) * TILE)
                made.append(put(tall_s.at[slot, :, lanes], out.at[tile, block]))
                if flip is not None:
                    made.append(put(flat_s.at[slot, part - 1, tile], flip.at[tile, block]))
        return made

    normalise(0, 0)
    to_far.wait_recv()
    put(w_own, w_own_ref)
    first = project(0, 0)
    to_core.wait_recv()
    normalise(1, 1)
    second = project(1, 1)
    to_corner = []
    for copy, source, target in zip(to_chip, spans(rows_t.at[2]), spans(rows_t.at[3])):
        copy.wait_recv()
        to_corner.append(push(source, target, beside))
    take(first)
    normalise(2, 0)
    project(2, 0)
    for copy in to_corner:
        copy.wait_recv()
    take(second)
    normalise(3, 1)
    project(3, 1)
    to_out.wait_recv()
    to_out_beside = push(out_ref.at[out_rows(1)], out_ref.at[out_rows(1)], beside)
    for copy in outs:
        copy.wait()
    for copy in (to_one, to_near, to_three, to_out_beside):
        copy.wait_recv()
    for copy in sent:
        copy.wait_send()


def open_up(
    prompt_in, cont_in, w_qkv, w_fc, w_proj, w_out, fc_bias, prompt_cot, cont_cot, gain, bias, col_bias, count
):
    prompt_rows, width = prompt_in.shape[1:]
    row_count = prompt_rows + cont_in.shape[1]
    half, quarter = width // 2, width // 4
    tiles = PAIRS + 1
    cols = 3 * tiles * TILE
    in_vmem = pl.BlockSpec(memory_space=pltpu.VMEM)
    vmem = lambda *shape, kind=BF16: pltpu.VMEM(shape, kind)
    tall, flat = (tiles, count, row_count, TILE), (tiles, count, TILE, row_count)
    mine = (2 * quarter + 16, w_fc.shape[1])
    outs = [
        (count, width + 16, row_count),
        tall,
        tall,
        tall,
        flat,
        flat,
        (width, cols),
        (row_count, width),
        (row_count, width),
        (width, row_count),
        mine,
        mine,
        mine,
        mine,
        (width, width),
    ]
    copies = 2 + 1 + 1 + 3 + 2 + 2
    return pl.pallas_call(
        open_kernel,
        in_specs=[ANYWHERE] * 8 + [in_vmem] * 4,
        out_specs=[ANYWHERE] * len(outs),
        out_shape=[shape_of(*out) for out in outs],
        scratch_shapes=[
            vmem(4, width, row_count),
            vmem(*w_qkv.shape, kind=F32),
            vmem(width, cols),
            vmem(half, cols),
            vmem(quarter, w_fc.shape[1], kind=F32),
            vmem(quarter, w_fc.shape[1], kind=F32),
            vmem(*mine),
            vmem(width, row_count),
            vmem(row_count, width),
            vmem(2, width + 16, row_count),
            vmem(2, row_count, cols),
            vmem(2, 2, tiles, TILE, row_count),
            vmem(2, row_count, width),
            vmem(half, width, kind=F32),
            vmem(half, width),
            pltpu.SemaphoreType.DMA((8,)),
            pltpu.SemaphoreType.DMA((copies,)),
            pltpu.SemaphoreType.DMA((copies,)),
            pltpu.SemaphoreType.DMA((80,)),
        ],
        compiler_params=pltpu.CompilerParams(
            vmem_limit_bytes=60 << 20, collective_id=2, has_side_effects=True
        ),
        cost_estimate=pl.CostEstimate(
            flops=2 * count * row_count * width * cols, bytes_accessed=40 << 20, transcendentals=0
        ),
        name="open",
    )(
        prompt_in[0].T,
        cont_in[0].T,
        w_qkv,
        w_fc,
        w_proj.T,
        w_out,
        prompt_cot[0].T,
        cont_cot[0].T,
        fc_bias[None],
        gain[:, None],
        bias[:, None],
        col_bias[None],
    )


def own_mask(rows):
    key_at = lax.broadcasted_iota(jnp.int32, (rows, rows), 0)
    query_at = lax.broadcasted_iota(jnp.int32, (rows, rows), 1)
    return key_at <= query_at


def attend_kernel(prompt_rows, q_ref, k_ref, vt_ref, seg_col_ref, seg_row_ref, *refs):
    mine_ref, near_ref, one_ref, three_ref = refs[:4]
    lse_ref, outs_ref, pieces_ref, last_ref, two_ref, one_far_ref, three_far_ref = refs[4:11]
    beside_refs, (acc, o_s, send_sem, recv_sem, out_sem) = refs[11:17], refs[17:]
    step = pl.program_id(0)
    place = lax.axis_index("ctx")
    fsdp = lax.axis_index("fsdp")
    tensor = lax.axis_index("tensor")
    tensors = lax.axis_size("tensor")
    count, row_count = k_ref.shape[1], k_ref.shape[2]
    cont_rows = row_count - prompt_rows
    per_pair = 2 * count
    steps = PAIRS * per_pair
    beside, far = {"ctx": place ^ 1}, {"fsdp": 1 - fsdp}
    after, before = lax.rem(tensor + 1, tensors), lax.rem(tensor + tensors - 1, tensors)
    distance = jnp.where(step < steps, count - 1 - step % per_pair // 2, 0)
    block = place ^ distance

    def copy_to(at, source, target, partner):
        return pltpu.make_async_remote_copy(
            src_ref=source,
            dst_ref=target,
            send_sem=send_sem.at[at],
            recv_sem=recv_sem.at[at],
            device_id=partner,
            device_id_type=pl.DeviceIdType.MESH,
        )

    b_mine, b_near, b_one, b_one_far, b_three, b_three_far = beside_refs
    returns = {}
    for pair in range(PAIRS):
        for away in range(1, count):
            returns[pair, away] = copy_to(
                pair * (count - 1) + away - 1,
                o_s.at[pair, away],
                pieces_ref.at[pair, away - 1],
                {"ctx": place ^ away},
            )
    base = PAIRS * (count - 1)
    early = [
        copy_to(base, one_ref, one_far_ref, far),
        copy_to(base + 1, one_ref, two_ref, {"tensor": after}),
        copy_to(base + 2, mine_ref, b_mine, beside),
        copy_to(base + 3, near_ref, b_near, beside),
        copy_to(base + 4, one_ref, b_one, beside),
        copy_to(base + 5, three_ref, b_three, beside),
        copy_to(base + 6, three_ref, three_far_ref, far),
    ]
    late = [
        copy_to(base + 7, one_far_ref, b_one_far, beside),
        copy_to(base + 8, three_far_ref, b_three_far, beside),
    ]

    @pl.when(step == 0)
    def _():
        barrier = pltpu.get_barrier_semaphore()
        partners = [{"ctx": place ^ away} for away in range(1, count)]
        partners += [far, {"tensor": after}, {"tensor": before}]
        for partner in partners:
            pl.semaphore_signal(
                barrier, inc=1, device_id=partner, device_id_type=pl.DeviceIdType.MESH
            )
        pl.semaphore_wait(barrier, len(partners))
        for copy in early:
            copy.start()

    @pl.when(step == per_pair + 2)
    def _():
        early[0].wait_recv()
        late[0].start()

    @pl.when(step == steps)
    def _():
        early[6].wait_recv()
        late[1].start()

    def part(queries, at, start, size, mask, states):
        keys = k_ref[0, at, pl.ds(start, size), :]
        scores = [dot(keys, query, NT) for query in queries]
        if mask is not None:
            scores = [jnp.where(mask, score, -1e30) for score in scores]
        tops = [jnp.max(score, axis=0, keepdims=True) for score in scores]
        if states is not None:
            tops = [jnp.maximum(top, state[0]) for top, state in zip(tops, states)]
        exps = [jnp.exp2(score * SCALE2 - top * SCALE2) for score, top in zip(scores, tops)]
        totals = [jnp.sum(exp, axis=0, keepdims=True) for exp in exps]
        made = []
        for head in range(len(queries)):
            rows = slice(head * HEAD, (head + 1) * HEAD)
            cols = slice(0, queries[head].shape[0])
            out = dot(vt_ref[0, at, rows, pl.ds(start, size)], exps[head].astype(BF16))
            total = totals[head]
            if states is None:
                acc[rows, cols] = out
            else:
                shrink = jnp.exp2((states[head][0] - tops[head]) * SCALE2)
                total = total + states[head][1] * shrink
                acc[rows, cols] = acc[rows, cols] * shrink + out
            made.append((tops[head], total))
        return made

    def finish(start, size, states):
        for head, (top, total) in enumerate(states):
            rows = slice(head * HEAD, (head + 1) * HEAD)
            acc[rows, :size] = acc[rows, :size] / total
            lse_ref[0, block, head : head + 1, pl.ds(start, size)] = top * SCALE2 + jnp.log2(total)
        if len(states) == 1:
            acc[HEAD:, :size] = jnp.zeros((TILE - HEAD, size), F32)
        pair = step // per_pair
        o_s[pair, distance, pl.ds(start, size), :] = acc[:, :size].T.astype(BF16)

    def over_prompt(queries, total, states):
        return lax.fori_loop(
            0, total, lambda c, states: part(queries, c, 0, prompt_rows, None, states), states
        )

    for heads, here in ((2, step < steps), (1, step >= steps)):

        @pl.when(here & (step % 2 == 1))
        def _():
            queries = halves(q_ref[0, block, :prompt_rows, :], heads)
            states = part(queries, block, 0, prompt_rows, own_mask(prompt_rows), None)
            finish(0, prompt_rows, over_prompt(queries, block, states))

        @pl.when(here & (step % 2 == 0))
        def _():
            previous = jnp.maximum(block - 1, 0)
            labels = seg_row_ref[block]
            queries = halves(q_ref[0, block, prompt_rows:, :], heads)
            own = own_mask(cont_rows) & (seg_col_ref[block] == labels)
            near = (seg_col_ref[previous] == labels) & (block > 0)
            states = part(queries, block, prompt_rows, cont_rows, own, None)
            states = part(queries, previous, prompt_rows, cont_rows, near, states)
            finish(prompt_rows, cont_rows, over_prompt(queries, count, states))

    for pair in range(PAIRS):
        for away in range(1, count):

            @pl.when(step == pair * per_pair + 2 * (count - 1 - away) + 1)
            def _():
                returns[pair, away].start()

    @pl.when(step == steps + 1)
    def _():
        stores = [
            pltpu.make_async_copy(o_s.at[pl.ds(0, PAIRS)], outs_ref, out_sem.at[0]),
            pltpu.make_async_copy(o_s.at[PAIRS, 0], last_ref, out_sem.at[1]),
        ]
        for store in stores:
            store.start()
        for copy in early[1:6] + late + list(returns.values()):
            copy.wait_recv()
        for copy in early + late + list(returns.values()):
            copy.wait_send()
        for store in stores:
            store.wait()


def attend(q, k, vt, seg_col, seg_row, prompt_rows, weights):
    groups, count, row_count, _ = q.shape
    cont_rows = row_count - prompt_rows
    pair = lambda i: (jnp.minimum(i // (2 * count), PAIRS), 0, 0, 0)
    pairs = groups * count * (prompt_rows + 2 * cont_rows) * prompt_rows * count // 2
    mine = weights[0].shape
    copies = PAIRS * (count - 1) + 9
    outs = [
        (pl.BlockSpec((1, count, 2, row_count), pair), shape_of(groups, count, 2, row_count, kind=F32)),
        (ANYWHERE, shape_of(PAIRS, count, row_count, TILE)),
        (ANYWHERE, shape_of(PAIRS, count - 1, row_count, TILE)),
        (ANYWHERE, shape_of(row_count, TILE)),
    ] + [(ANYWHERE, shape_of(*mine))] * 9
    return pl.pallas_call(
        functools.partial(attend_kernel, prompt_rows),
        grid=(PAIRS * 2 * count + 2,),
        in_specs=[
            pl.BlockSpec((1, count, row_count, TILE), pair),
            pl.BlockSpec((1, count, row_count, TILE), pair),
            pl.BlockSpec((1, count, TILE, row_count), pair),
            pl.BlockSpec((count, cont_rows, 1), lambda i: (0, 0, 0)),
            pl.BlockSpec((count, 1, cont_rows), lambda i: (0, 0, 0)),
        ]
        + [ANYWHERE] * len(weights),
        out_specs=[out[0] for out in outs],
        out_shape=[out[1] for out in outs],
        scratch_shapes=[
            pltpu.VMEM((TILE, max(prompt_rows, cont_rows)), F32),
            pltpu.VMEM((groups, count, row_count, TILE), BF16),
            pltpu.SemaphoreType.DMA((copies,)),
            pltpu.SemaphoreType.DMA((copies,)),
            pltpu.SemaphoreType.DMA((2,)),
        ],
        compiler_params=pltpu.CompilerParams(
            vmem_limit_bytes=56 << 20, collective_id=3, has_side_effects=True
        ),
        cost_estimate=pl.CostEstimate(
            flops=8 * TILE * pairs, bytes_accessed=20 << 20, transcendentals=2 * pairs
        ),
        name="attend",
    )(q, k, vt, seg_col, seg_row, *weights)


def attend_back_kernel(
    heads,
    spans,
    prompt_rows,
    place_ref,
    q_ref,
    k_ref,
    v_ref,
    kt_ref,
    lse_ref,
    seg_col_ref,
    seg_row_ref,
    *refs,
):
    do_refs, o_refs, refs = refs[:spans], refs[spans : 2 * spans], refs[2 * spans :]
    dq_ref, dk_ref, dv_ref, dk_acc, dv_acc, dq_acc, do_s, o_s = refs
    step = pl.program_id(0)
    distance = step % spans
    block = place_ref[0] ^ distance
    count, row_count = k_ref.shape[1], k_ref.shape[2]
    cont_rows = row_count - prompt_rows

    @pl.when(step == 0)
    def _():
        dk_acc[...] = jnp.zeros_like(dk_acc)
        dv_acc[...] = jnp.zeros_like(dv_acc)
        if spans < count:
            dq_ref[...] = jnp.zeros_like(dq_ref)

    def part(given, at, start, size, mask, first):
        rows = pl.ds(start, size)
        for head in range(heads):
            query, grad, lse, centre = (entry[head] for entry in given)
            cols = slice(0, query.shape[0])
            own = slice(head * HEAD, (head + 1) * HEAD)
            scores = dot(k_ref[0, at, rows, :], query, NT)
            if mask is not None:
                scores = jnp.where(mask, scores, -1e30)
            probability = jnp.exp2(scores * SCALE2 - lse)
            grad_probability = dot(v_ref[0, at, rows, :], grad, NT)
            grad_scores = (probability * (grad_probability - centre)).astype(BF16)
            dv_acc[at, rows, :] += dot(probability.astype(BF16), grad)
            dk_acc[at, rows, :] += dot(grad_scores, query)
            out = dot(kt_ref[0, at, own, rows], grad_scores)
            if first:
                dq_acc[own, cols] = out
            else:
                dq_acc[own, cols] += out

    def setup(start, size):
        rows = pl.ds(start, size)
        for at in range(spans):

            @pl.when(distance == at)
            def _():
                do_s[:size] = do_refs[at][rows, :]
                o_s[:size] = o_refs[at][0, 0, rows, :]

        grad = do_s[:size]
        product = (grad.astype(F32) * o_s[:size].astype(F32)).T
        centres = [
            jnp.sum(product[head * HEAD : (head + 1) * HEAD], axis=0, keepdims=True)
            for head in range(heads)
        ]
        lses = [lse_ref[0, block, head : head + 1, rows] for head in range(heads)]
        return halves(q_ref[0, block, rows, :], heads), halves(grad, heads), lses, centres

    def finish(start, size):
        if heads == 1:
            dq_acc[HEAD:, :size] = jnp.zeros((TILE - HEAD, size), F32)
        dq_ref[0, block, pl.ds(start, size), :] = (dq_acc[:, :size].T * 0.125).astype(BF16)

    @pl.when(step >= spans)
    def _():
        given = setup(0, prompt_rows)
        part(given, block, 0, prompt_rows, own_mask(prompt_rows), True)

        @pl.loop(0, block)
        def _(c):
            part(given, c, 0, prompt_rows, None, False)

        finish(0, prompt_rows)

    @pl.when(step < spans)
    def _():
        before = jnp.maximum(block - 1, 0)
        labels = seg_row_ref[block]
        own = own_mask(cont_rows) & (seg_col_ref[block] == labels)
        near = (seg_col_ref[before] == labels) & (block > 0)
        given = setup(prompt_rows, cont_rows)
        part(given, block, prompt_rows, cont_rows, own, True)
        part(given, before, prompt_rows, cont_rows, near, False)

        @pl.loop(0, count)
        def _(c):
            part(given, c, 0, prompt_rows, None, False)

        finish(prompt_rows, cont_rows)

    @pl.when(step == pl.num_programs(0) - 1)
    def _():
        dk_ref[0] = (dk_acc[...] * 0.125).astype(BF16)
        dv_ref[0] = dv_acc[...].astype(BF16)


def attend_back(
    pair, tile, heads, place, q, k, v, kt, lse, seg_col, seg_row, grads, outs, prompt_rows, after=(), carry=()
):
    _, count, row_count, _ = q.shape
    spans = len(grads)
    cont_rows = row_count - prompt_rows
    pick = lambda i, s: (pair, 0, 0, 0)
    tall = pl.BlockSpec((1, count, row_count, TILE), pick)
    most = max(prompt_rows, cont_rows)
    pairs = spans * (prompt_rows + 2 * cont_rows) * prompt_rows * count // 2
    return launch(
        functools.partial(attend_back_kernel, heads, spans, prompt_rows),
        "attend_back",
        (place,),
        (2 * spans,),
        (q, k, v, kt, lse, seg_col, seg_row, *grads, *[outs] * spans),
        [
            tall,
            tall,
            tall,
            pl.BlockSpec((1, count, TILE, row_count), pick),
            pl.BlockSpec((1, count, 2, row_count), pick),
            blocks(count, cont_rows, 1),
            blocks(count, 1, cont_rows),
        ]
        + [pl.BlockSpec((row_count, TILE), lambda i, s: (0, tile))] * spans
        + [
            pl.BlockSpec((1, 1, row_count, TILE), lambda i, s, away=away: (tile, away, 0, 0))
            for away in range(spans)
        ],
        [whole_out(1, count, row_count, TILE)] * 3,
        scratch=[
            pltpu.VMEM((count, row_count, TILE), F32),
            pltpu.VMEM((count, row_count, TILE), F32),
            pltpu.VMEM((TILE, most), F32),
            pltpu.VMEM((most, TILE), BF16),
            pltpu.VMEM((most, TILE), BF16),
        ],
        limit=56,
        flops=10 * heads * TILE * pairs,
        exps=heads * pairs,
        after=after,
        carry=carry,
    )


def normalize(values):
    average = jnp.mean(values, axis=1, keepdims=True)
    centred = values - average
    variance = jnp.mean(centred * centred, axis=1, keepdims=True)
    rate = lax.rsqrt(variance + 1e-05)
    return centred * rate, rate


def normalize_back(unit, rate, grad):
    shift = jnp.mean(grad, axis=1, keepdims=True)
    along = jnp.mean(grad * unit, axis=1, keepdims=True)
    return rate * (grad - shift - unit * along)


def piece_of(own_ref, pieces_ref, distance):
    tiles = [
        pieces_ref[pair, distance - 1] if distance else own_ref[pair, 0] for pair in range(PAIRS)
    ]
    return jnp.concatenate(tiles, axis=1)


def piece_specs(places, size):
    return [
        pl.BlockSpec((PAIRS, 1, size, TILE), lambda i, p: (0, 0, i, 0)),
        pl.BlockSpec((PAIRS, places - 1, size, TILE), lambda i, p: (0, 0, i, 0)),
        pl.BlockSpec((size, TILE), lambda i, p: (i, 0)),
    ]


def merge_kernel(places, place_ref, x_ref, w_ref, out_bias_ref, gain_ref, bias_ref, *refs):
    own_ref, pieces_ref, last_ref, hidden_ref, low_ref, flip_ref = refs
    own = 2 * PAIRS * HEAD
    width = hidden_ref.shape[1]
    total = x_ref[:, :width].astype(F32) + out_bias_ref[...]
    for distance in range(places):
        start = pl.multiple_of((place_ref[0] ^ distance) * own, own)
        joined = piece_of(own_ref, pieces_ref, distance)
        total = total + dot(joined, w_ref[pl.ds(start, own), :])
    total = total + dot(last_ref[:, :HEAD], w_ref[width - HEAD :, :])
    hidden_ref[...] = total
    unit, _ = normalize(total)
    low = (unit * gain_ref[...] + bias_ref[...]).astype(BF16)
    low_ref[...] = low
    flip_ref[...] = low.T


def merge(place, rows, w_out, out_bias, gain, bias, pieces, after=(), carry=()):
    row_count, width = rows.shape[0], w_out.shape[1]
    size = 128
    by_row = lambda cols: pl.BlockSpec((size, cols), lambda i, p: (i, 0))
    return launch(
        functools.partial(merge_kernel, pieces[0].shape[1]),
        "merge",
        (place,),
        (row_count // size,),
        (rows, w_out, out_bias[None], gain[None], bias[None], *pieces),
        [by_row(rows.shape[1]), blocks(*w_out.shape)]
        + [blocks(1, width)] * 3
        + piece_specs(pieces[0].shape[1], size),
        [
            (by_row(width), shape_of(row_count, width, kind=F32)),
            (by_row(width), shape_of(row_count, width)),
            (
                pl.BlockSpec((width, size), lambda i, p: (0, i)),
                shape_of(width, row_count),
            ),
        ],
        flops=2 * row_count * width * width,
        after=after,
        carry=carry,
    )


def bend_kernel(
    places,
    prompt_steps,
    place_ref,
    mlp_ref,
    gm_ref,
    hidden_ref,
    g_ref,
    w_ref,
    gain_ref,
    proj_bias_ref,
    *refs,
):
    own_ref, pieces_ref, last_ref, refs = *refs[:3], refs[3:]
    prompt_ref, cont_ref, gh_ref = refs[:3]
    ga_refs, (ga_last_ref, *gw_refs, sums_ref, acc) = refs[3 : 3 + places], refs[3 + places :]
    step = pl.program_id(0)
    own = 2 * PAIRS * HEAD
    width = hidden_ref.shape[1]
    hidden = hidden_ref[...]
    layer_out = (hidden + mlp_ref[...] + proj_bias_ref[...]).astype(BF16)

    @pl.when(step < prompt_steps)
    def _():
        prompt_ref[0] = layer_out

    @pl.when(step >= prompt_steps)
    def _():
        cont_ref[0] = layer_out

    unit, rate = normalize(hidden)
    grad_in = gm_ref[...]
    grad_layer = g_ref[...].astype(F32)
    grad_hidden = grad_layer + normalize_back(unit, rate, grad_in * gain_ref[...])
    gh_ref[...] = grad_hidden
    branch = grad_hidden.astype(BF16)
    sums = [grad_hidden, grad_in * unit, grad_in, grad_layer]
    sums = jnp.concatenate([jnp.sum(entry, axis=0, keepdims=True) for entry in sums], axis=0)

    @pl.when(step == 0)
    def _():
        acc[...] = jnp.zeros_like(acc)
        sums_ref[...] = sums

    @pl.when(step > 0)
    def _():
        sums_ref[...] += sums

    for distance in range(places):
        start = pl.multiple_of((place_ref[0] ^ distance) * own, own)
        rows = pl.ds(start, own)
        ga_refs[distance][...] = dot(branch, w_ref[rows, :], NT).astype(BF16)
        joined = piece_of(own_ref, pieces_ref, distance)
        acc[rows, :] += dot(joined.T, branch)
    last = dot(branch, w_ref[width - HEAD :, :], NT).astype(BF16)
    ga_last_ref[...] = jnp.concatenate([last, jnp.zeros_like(last)], axis=1)
    acc[width - HEAD :, :] += dot(last_ref[:, :HEAD].T, branch)

    @pl.when(step == pl.num_programs(0) - 1)
    def _():
        quarter = width // 4
        core, fsdp = place_ref[0] % 2, place_ref[1]
        for beside, ref in enumerate(gw_refs):
            for away in range(2):
                start = ((fsdp ^ away) * 2 + (core ^ beside)) * quarter
                ref[away] = acc[pl.ds(pl.multiple_of(start, 16), quarter), :].astype(BF16)


def bend(
    place, mlp_out, gm, hidden, g, w_out, gain, proj_bias, pieces, prompt_rows, after=(), carry=()
):
    row_count, width = hidden.shape
    size = 128
    places = pieces[0].shape[1]
    prompt_steps = prompt_rows // size
    own = 2 * PAIRS * HEAD
    by_row = lambda cols: pl.BlockSpec((size, cols), lambda i, p: (i, 0))
    return launch(
        functools.partial(bend_kernel, places, prompt_steps),
        "bend",
        (place,),
        (row_count // size,),
        (mlp_out, gm, hidden, g, w_out, gain[None], proj_bias[None], *pieces),
        [by_row(width)] * 4
        + [blocks(*w_out.shape)]
        + [blocks(1, width)] * 2
        + piece_specs(places, size),
        [
            (
                pl.BlockSpec((1, size, width), lambda i, p: (0, jnp.minimum(i, prompt_steps - 1), 0)),
                shape_of(1, prompt_rows, width),
            ),
            (
                pl.BlockSpec((1, size, width), lambda i, p: (0, jnp.maximum(i - prompt_steps, 0), 0)),
                shape_of(1, row_count - prompt_rows, width),
            ),
            (by_row(width), shape_of(row_count, width, kind=F32)),
        ]
        + [(by_row(own), shape_of(row_count, own))] * places
        + [
            (by_row(TILE), shape_of(row_count, TILE)),
            whole_out(2, width // 4, width),
            whole_out(2, width // 4, width),
            whole_out(4, width, kind=F32),
        ],
        scratch=[pltpu.VMEM((width, width), F32)],
        flops=4 * row_count * width * width,
        traffic=30,
        after=after,
        carry=carry,
    )


GELU_RATE = 0.7978845608028654


def gelu_both(values):
    square = values * values
    bent = jnp.tanh(GELU_RATE * (values + 0.044715 * square * values))
    half = 0.5 * (1.0 + bent)
    slope = half + 0.5 * values * (1.0 - bent * bent) * (GELU_RATE * (1.0 + 0.134145 * square))
    return values * half, slope


def mlp_kernel(
    parts,
    first,
    spot_ref,
    x_ref,
    g_ref,
    xt_ref,
    gt_ref,
    *refs,
):
    own, far, own_2, far_2 = (refs[i * parts : (i + 1) * parts] for i in range(4))
    before_refs = refs[4 * parts : 4 * parts + 2]
    refs = refs[4 * parts + (0 if first else 2) :]
    out_ref, gm_ref, keep_f, send_f, keep_p, send_p, gb_ref = refs[:7]
    wf_s, wp_s, bias_s, biases, act_s, gp_s, wide, sems = refs[7:]
    step = pl.program_id(0)
    core, fsdp = spot_ref[0], spot_ref[1]
    slot = step % 2
    _, width, hidden = wf_s.shape
    quarter = width // 4

    def spot(away, across):
        start = ((fsdp ^ away) * 2 + (core ^ across)) * quarter
        return pl.ds(pl.multiple_of(start, 16), quarter)

    def loads(at, to):
        moves = [(own[at].at[pl.ds(2 * quarter, 16)], bias_s.at[to])]
        for away, sources in enumerate(((own[at], own_2[at]), (far[at], far_2[at]))):
            for across, source in enumerate(sources):
                for weight, target in enumerate((wf_s, wp_s)):
                    moves.append(
                        (
                            source.at[pl.ds(weight * quarter, quarter)],
                            target.at[to, spot(away, across)],
                        )
                    )
        return [
            pltpu.make_async_copy(source, target, sems.at[to, i])
            for i, (source, target) in enumerate(moves)
        ]

    @pl.when(step == 0)
    def _():
        for part in range(parts):
            for copy in loads(part, part):
                copy.start()

    for part in range(parts):

        @pl.when(step == part)
        def _():
            for copy in loads(part, part):
                copy.wait()

    bias = jnp.sum(bias_s[slot, :3, :].astype(F32), axis=0, keepdims=True)
    biases[...] = bias

    def over(total, body):
        whole = total // 256

        @pl.loop(0, whole)
        def _(i):
            body(pl.multiple_of(i * 256, 256), 256)

        if total % 256:
            body(whole * 256, total % 256)

    def up(start, size):
        cols = pl.ds(start, size)
        pre_act = dot(x_ref[...], wf_s[slot, :, cols]) + biases[:, cols]
        grad_act = dot(g_ref[...], wp_s[slot, :, cols])
        activated, slope = gelu_both(pre_act)
        grad_pre = (grad_act * slope).astype(BF16)
        act_s[:, cols] = activated.astype(BF16)
        gp_s[:, cols] = grad_pre
        gb_ref[0, :, cols] = jnp.sum(grad_pre.astype(F32), axis=0, keepdims=True)

    def weights(start, size):
        cols = pl.ds(start, size)
        for left, right, keep, send, by_part in (
            (xt_ref, gp_s, keep_f, send_f, True),
            (gt_ref, act_s, keep_p, send_p, False),
        ):
            wide[:, :size] = dot(left[...], right[:, cols]).astype(BF16)
            for far in range(2):
                for beside, to in enumerate((keep, send)):
                    piece = wide[spot(far, beside), :size]
                    if by_part:
                        to[0, far, :, cols] = piece
                    else:
                        to[far, 0, :, cols] = piece

    over(hidden, up)
    over(hidden, weights)

    if first:

        @pl.when(step == 0)
        def _():
            out_ref[...] = jnp.zeros_like(out_ref)
            gm_ref[...] = jnp.zeros_like(gm_ref)

    else:

        @pl.when(step == 0)
        def _():
            out_ref[...] = before_refs[0][...]
            gm_ref[...] = before_refs[1][...]

    def down(start, size):
        rows = pl.ds(start, size)
        out_ref[:, rows] += dot(act_s[...], wp_s[slot, rows, :], NT)
        gm_ref[:, rows] += dot(gp_s[...], wf_s[slot, rows, :], NT)

    over(width, down)


def mlp(spot, x, g, xt, gt, own, far, own_2, far_2, before=(), after=(), carry=()):
    rows, width = x.shape
    hidden = own[0].shape[1]
    parts, quarter = len(own), width // 4
    once = pl.Buffered(buffer_count=1)
    whole = lambda *shape: pl.BlockSpec(shape, lambda k, s: (0,) * len(shape), pipeline_mode=once)
    by_part = pl.BlockSpec((1, 2, quarter, hidden), lambda k, s: (k, 0, 0, 0))
    by_far = pl.BlockSpec((2, 1, quarter, hidden), lambda k, s: (0, k, 0, 0))
    total = (whole(rows, width), shape_of(rows, width, kind=F32))
    by_part = (by_part, shape_of(parts, 2, quarter, hidden))
    by_far = (by_far, shape_of(2, parts, quarter, hidden))
    return launch(
        functools.partial(mlp_kernel, parts, not before),
        "mlp",
        (spot,),
        (parts,),
        (x, g, xt, gt, *own, *far, *own_2, *far_2, *before),
        [
            whole(rows, width),
            whole(rows, width),
            whole(width, rows),
            whole(width, rows),
        ]
        + [ANYWHERE] * (4 * parts)
        + [whole(rows, width)] * len(before),
        [
            total,
            total,
            by_part,
            by_part,
            by_far,
            by_far,
            (
                pl.BlockSpec((1, 1, hidden), lambda k, s: (k, 0, 0)),
                shape_of(parts, 1, hidden, kind=F32),
            ),
        ],
        scratch=[
            pltpu.VMEM((2, width, hidden), BF16),
            pltpu.VMEM((2, width, hidden), BF16),
            pltpu.VMEM((2, 16, hidden), BF16),
            pltpu.VMEM((1, hidden), F32),
            pltpu.VMEM((rows, hidden), BF16),
            pltpu.VMEM((rows, hidden), BF16),
            pltpu.VMEM((width, 256), BF16),
            pltpu.SemaphoreType.DMA((2, 9)),
        ],
        limit=62,
        flops=12 * rows * width * hidden * parts,
        traffic=40,
        exps=rows * hidden * parts,
        after=after,
        carry=carry,
    )


def tail_kernel(prompt_rows, *refs):
    grads, refs = refs[:9], refs[9:]
    w_ref, norm_ref, rows_ref, gh_ref, keep_ref, come_ref, gain_ref, given_ref = refs[:8]
    prompt_ref, cont_ref, qkv_ref, wo_ref, vec_ref = refs[8:13]
    (
        norms,
        rows_s,
        gh_s,
        joined,
        hold,
        core_out,
        core_in,
        chip_out,
        chip_in,
        acc,
        keep,
        far_out,
        far_in,
        sums,
        sums_in,
        ring_in,
        ring_all,
        whole,
        near_in,
        left_out,
        left_in,
        vec_out,
        vec_in,
        wo_near,
        wo_sum,
        wo_ring,
        wo_chip,
        wo_all,
        wo_core,
        local_sem,
        send_sem,
        recv_sem,
    ) = refs[13:]
    place = lax.axis_index("ctx")
    fsdp = lax.axis_index("fsdp")
    tensor = lax.axis_index("tensor")
    tensors = lax.axis_size("tensor")
    count, row_count = grads[0].shape[1], grads[0].shape[2]
    width = w_ref.shape[0]
    half = width // 2
    own = acc.shape[1]
    shard = ring_in.shape[2]
    chunk = 128
    beside, across, far = {"ctx": place ^ 1}, {"ctx": place ^ 2}, {"fsdp": 1 - fsdp}
    others = [{"tensor": lax.rem(tensor + k, tensors)} for k in range(1, tensors)]

    barrier = pltpu.get_barrier_semaphore()
    for partner in (beside, across, far, *others):
        pl.semaphore_signal(barrier, inc=1, device_id=partner, device_id_type=pl.DeviceIdType.MESH)

    loads = [pltpu.make_async_copy(norm_ref, norms, local_sem.at[0])]
    loads.append(pltpu.make_async_copy(keep_ref, wo_core.at[0], local_sem.at[1]))
    loads.append(pltpu.make_async_copy(come_ref, wo_near, local_sem.at[2]))
    for load in loads:
        load.start()
    sent, used = [], []

    def push(source, target, partner):
        at = len(used)
        used.append(at)
        copy = pltpu.make_async_remote_copy(
            src_ref=source,
            dst_ref=target,
            send_sem=send_sem.at[at],
            recv_sem=recv_sem.at[at],
            device_id=partner,
            device_id_type=pl.DeviceIdType.MESH,
        )
        copy.start()
        sent.append(copy)
        return copy

    quarter, part_rows = wo_sum.shape[0], wo_ring.shape[1]

    def part_start(owner):
        return pl.multiple_of(jnp.minimum(owner * part_rows, quarter - part_rows), 16)

    def rows_grad(distance, out):
        block = place ^ distance
        for i, ref in enumerate(grads):
            joined[:, i * TILE : (i + 1) * TILE] = ref[0, block]

        @pl.loop(0, width // 256)
        def _(i):
            cols = pl.ds(pl.multiple_of(i * 256, 256), 256)
            out[:, cols] = dot(joined[...], w_ref[cols, :], NT).astype(out.dtype)

        if width % 256:
            cols = pl.ds(width // 256 * 256, width % 256)
            out[:, cols] = dot(joined[...], w_ref[cols, :], NT).astype(out.dtype)

    rows_grad(3, core_out)
    pl.semaphore_wait(barrier, 3 + len(others))
    to_core = push(core_out, core_in.at[0], beside)
    loads[1].wait()
    loads[2].wait()
    wo_sum[...] = (wo_core[0].astype(F32) + wo_near[...].astype(F32)).astype(BF16)
    wo_to_ring = [
        push(wo_sum.at[pl.ds(part_start(other["tensor"]), part_rows)], wo_ring.at[k], other)
        for k, other in enumerate(others)
    ]
    rows_grad(2, hold)
    to_core.wait_recv()

    @pl.loop(0, row_count // chunk)
    def _(i):
        rows = pl.ds(pl.multiple_of(i * chunk, chunk), chunk)
        chip_out[rows, :] = (hold[rows, :] + core_in[0, rows, :].astype(F32)).astype(BF16)

    to_chip = push(chip_out, chip_in, across)

    loads[0].wait()
    to_far = [None] * 4

    def weights(part):
        @pl.loop(0, count)
        def _(block):
            if part < 3:
                pieces = [grads[3 * part + pair][0, block] for pair in range(PAIRS)]
            else:
                pieces = [grads[3 * i + PAIRS][0, block][:, :HEAD] for i in range(3)]
                pieces.append(jnp.zeros((row_count, own - 3 * HEAD), BF16))
            piece = dot(norms[block], jnp.concatenate(pieces, axis=1))

            @pl.when(block == 0)
            def _():
                acc[...] = piece

            @pl.when(block > 0)
            def _():
                acc[...] += piece

        sums[part] = acc[width : width + 8, :]
        keep[part] = acc[pl.ds(pl.multiple_of(fsdp * half, 16), half), :]
        far_out[part] = acc[pl.ds(pl.multiple_of((1 - fsdp) * half, 16), half), :].astype(BF16)
        to_far[part] = push(far_out.at[part], far_in.at[part], far)

    def joined_far(part):
        to_far[part].wait_recv()
        return keep[part] + far_in[part].astype(F32)

    def start_of(owner):
        return pl.multiple_of(jnp.minimum(owner * shard, half - shard), 16)

    to_ring, to_all, to_near = [None] * 4, [None] * 4, [None] * 4

    def ring(part, total):
        sums_in[part] = total.astype(BF16)
        to_ring[part] = [
            push(
                sums_in.at[part, pl.ds(start_of(other["tensor"]), shard)],
                ring_in.at[part, k],
                other,
            )
            for k, other in enumerate(others)
        ]

    def spread(part):
        total = sums_in[part, pl.ds(start_of(tensor), shard), :].astype(F32)
        for k, copy in enumerate(to_ring[part]):
            copy.wait_recv()
            total = total + ring_in[part, k].astype(F32)
        ring_all[part, tensor] = total.astype(BF16)
        to_all[part] = [
            push(ring_all.at[part, tensor], ring_all.at[part, tensor], other) for other in others
        ]

    def gather(part):
        for copy in to_all[part]:
            copy.wait_recv()
        for owner in range(tensors - 1):
            whole[part, owner * shard : (owner + 1) * shard] = ring_all[part, owner]
        rest = (tensors - 1) * shard
        whole[part, rest:] = ring_all[part, tensors - 1, tensors * shard - half :]
        if part < 3:
            to_near[part] = [
                push(whole.at[part], near_in.at[part, 0], beside),
                push(whole.at[part], near_in.at[part, 1], across),
            ]

    weights(3)
    to_core.wait_send()
    sent.remove(to_core)
    rows_grad(1, core_out)
    to_core_2 = push(core_out, core_in.at[1], beside)
    left_out[0] = joined_far(3).astype(BF16)
    to_left = push(left_out.at[0], left_in.at[0], beside)
    weights(0)
    to_left.wait_recv()
    left_out[1] = (left_out[0].astype(F32) + left_in[0].astype(F32)).astype(BF16)
    to_left = push(left_out.at[1], left_in.at[1], across)
    ring(0, joined_far(0))
    weights(1)
    wo_total = wo_sum[pl.ds(part_start(tensor), part_rows), :].astype(F32)
    for k, copy in enumerate(wo_to_ring):
        copy.wait_recv()
        wo_total = wo_total + wo_ring[k].astype(F32)
    wo_chip[0] = wo_total.astype(BF16)
    wo_to_chip = push(wo_chip.at[0], wo_chip.at[1], across)
    ring(1, joined_far(1))
    weights(2)
    spread(0)
    rows_grad(0, hold)
    ring(2, joined_far(2))
    to_left.wait_recv()
    ring(3, left_out[1].astype(F32) + left_in[1].astype(F32))
    to_core_2.wait_recv()
    wo_to_chip.wait_recv()
    wo_all[tensor] = (wo_chip[0].astype(F32) + wo_chip[1].astype(F32)).astype(BF16)
    wo_to_all = [push(wo_all.at[tensor], wo_all.at[tensor], other) for other in others]
    spread(1)
    gather(0)
    to_chip.wait_recv()

    vec_out[0, :8] = jnp.zeros((8, vec_out.shape[2]), F32)
    vec_out[0, 8:] = given_ref[...]
    chunks = row_count // chunk

    def chunk_rows(i):
        return pl.ds(pl.multiple_of(i * chunk, chunk), chunk)

    def row_loads(i):
        slot = i % 2
        return [
            pltpu.make_async_copy(gh_ref.at[chunk_rows(i)], gh_s.at[slot], local_sem.at[3 + slot]),
            pltpu.make_async_copy(rows_ref.at[chunk_rows(i)], rows_s.at[slot], local_sem.at[5 + slot]),
        ]

    for load in row_loads(0):
        load.start()

    @pl.loop(0, chunks)
    def _(i):
        @pl.when(i + 1 < chunks)
        def _():
            for load in row_loads(i + 1):
                load.start()

        for load in row_loads(i):
            load.wait()

        rows = chunk_rows(i)
        unit, rate = normalize(rows_s[i % 2, :, :width].astype(F32))
        grad = hold[rows, :] + core_in[1, rows, :].astype(F32) + chip_in[rows, :].astype(F32)
        back = normalize_back(unit, rate, grad * gain_ref[...])
        out = (gh_s[i % 2] + back).astype(BF16)

        @pl.when(i < prompt_rows // chunk)
        def _():
            prompt_ref[0, rows, :] = out

        @pl.when(i >= prompt_rows // chunk)
        def _():
            cont_ref[0, chunk_rows(i - prompt_rows // chunk), :] = out

        vec_out[0, 0:1, :width] += jnp.sum(grad * unit, axis=0, keepdims=True)
        vec_out[0, 1:2, :width] += jnp.sum(grad, axis=0, keepdims=True)

    spread(2)
    for row, part in ((2, 0), (3, 2)):
        cols = pl.ds(pl.multiple_of(place * own, own), own)
        vec_out[0, row : row + 1, cols] = sums[part, 0:1, :]
        left = slice(part * HEAD, (part + 1) * HEAD)
        vec_out[0, row : row + 1, width - HEAD : width] = sums[3, 0:1, left]
    spread(3)
    gather(1)

    def forward(part):
        to_near[part][1].wait_recv()
        return push(near_in.at[part, 1], near_in.at[part, 2], beside)

    def store(part, passed):
        to_near[part][0].wait_recv()
        passed.wait_recv()
        sources = [whole.at[part]] + [near_in.at[part, i] for i in range(3)]
        for distance, source in enumerate(sources):
            for block in range(count):

                @pl.when(place ^ distance == block)
                def _():
                    start = part * width + block * own
                    qkv_ref[:, start : start + own] = source[...]

    partners = (beside, across, far, {"tensor": tensor ^ 1}, {"tensor": tensor ^ 2})

    def exchange(level):
        return push(vec_out.at[level], vec_in.at[level], partners[level])

    def add(level, copy):
        copy.wait_recv()
        vec_out[level + 1] = vec_out[level] + vec_in[level]

    add(0, exchange(0))
    passed_0 = forward(0)
    step = exchange(1)
    gather(2)
    add(1, step)
    step = exchange(2)
    gather(3)
    store(0, passed_0)
    add(2, step)
    for copy in wo_to_all:
        copy.wait_recv()
    for owner in range(tensors - 1):
        wo_core[0, owner * part_rows : (owner + 1) * part_rows] = wo_all[owner]
    rest = (tensors - 1) * part_rows
    wo_core[0, rest:] = wo_all[tensors - 1, tensors * part_rows - quarter :]
    wo_to_core = push(wo_core.at[0], wo_core.at[1], beside)
    step = exchange(3)
    passed_1 = forward(1)
    for part in range(3):
        cols = slice((part + 1) * width - HEAD, (part + 1) * width)
        qkv_ref[:, cols] = whole[3, :, part * HEAD : (part + 1) * HEAD]
    add(3, step)
    step = exchange(4)
    store(1, passed_1)
    passed_2 = forward(2)
    add(4, step)
    vec_ref[...] = vec_out[5]
    wo_to_core.wait_recv()
    core = place % 2
    for away in range(2):
        wo_ref[pl.ds(pl.multiple_of((core ^ away) * quarter, 16), quarter), :] = wo_core[away]
    store(2, passed_2)
    for copy in sent:
        copy.wait_send()


def tail(
    grads, w_own, normed, rows, grad_hidden, gain, vectors, out_keep, out_come, prompt_rows, after=()
):
    count, depth, row_count = normed.shape
    width, cols = w_own.shape
    half, own = width // 2, 2 * PAIRS * HEAD
    tensors = lax.axis_size("tensor")
    shard = -(-half // tensors // 16) * 16
    padded = vectors.shape[1]
    in_vmem = pl.BlockSpec(memory_space=pltpu.VMEM)
    vmem = lambda *shape, kind=BF16: pltpu.VMEM(shape, kind)
    copies = 4 + 4 * 2 * (tensors - 1) + 3 + 3 * 3 + 2 + 5 + 2 * (tensors - 1) + 2
    given = len(grads) + 8
    quarter = width // 4
    part_rows = -(-quarter // tensors // 16) * 16

    def body(*refs):
        tail_kernel(prompt_rows, *refs[:given], *refs[given + len(after) :])

    return pl.pallas_call(
        body,
        in_specs=[in_vmem] * (len(grads) + 1) + [ANYWHERE] * 5 + [in_vmem] * 2 + [ANYWHERE] * len(after),
        out_specs=[in_vmem] * 5,
        out_shape=[
            shape_of(1, prompt_rows, width),
            shape_of(1, row_count - prompt_rows, width),
            shape_of(half, 3 * width),
            shape_of(half, width),
            shape_of(16, padded, kind=F32),
        ],
        scratch_shapes=[
            vmem(*normed.shape),
            vmem(2, TILE, width),
            vmem(2, TILE, width, kind=F32),
            vmem(row_count, cols),
            vmem(row_count, width, kind=F32),
            vmem(row_count, width),
            vmem(2, row_count, width),
            vmem(row_count, width),
            vmem(row_count, width),
            vmem(depth, own, kind=F32),
            vmem(4, half, own, kind=F32),
            vmem(4, half, own),
            vmem(4, half, own),
            vmem(4, 8, own, kind=F32),
            vmem(4, half, own),
            vmem(4, tensors - 1, shard, own),
            vmem(4, tensors, shard, own),
            vmem(4, half, own),
            vmem(3, 3, half, own),
            vmem(2, half, own),
            vmem(2, half, own),
            vmem(6, 16, padded, kind=F32),
            vmem(5, 16, padded, kind=F32),
            vmem(quarter, width),
            vmem(quarter, width),
            vmem(tensors - 1, part_rows, width),
            vmem(2, part_rows, width),
            vmem(tensors, part_rows, width),
            vmem(2, quarter, width),
            pltpu.SemaphoreType.DMA((7,)),
            pltpu.SemaphoreType.DMA((copies,)),
            pltpu.SemaphoreType.DMA((copies,)),
        ],
        compiler_params=pltpu.CompilerParams(
            vmem_limit_bytes=62 << 20, collective_id=1, has_side_effects=True
        ),
        cost_estimate=pl.CostEstimate(
            flops=4 * count * row_count * width * cols, bytes_accessed=30 << 20, transcendentals=0
        ),
        name="tail",
    )(*grads, w_own, normed, rows, grad_hidden, out_keep, out_come, gain[None], vectors, *after)


def join_kernel(spot_ref, *refs):
    firsts, lasts, (keep_o, come_o) = refs[:4], refs[4:8], refs[8:10]
    out_f, sum_f, out_p, sum_p, out_o, sum_o, total = refs[10:]
    step = pl.program_id(0)
    eighth = out_f.shape[2]
    chip = spot_ref[4] // 2
    sums_o = (keep_o[...].astype(F32) + come_o[...].astype(F32)).astype(BF16)
    sum_o[...] = sums_o[0]
    out_o[...] = sums_o[1]
    for entries, here in ((firsts, step < 2), (lasts, step >= 2)):
        keep_f, come_f, keep_p, come_p = entries

        @pl.when(here)
        def _():
            for at in range(2):
                total[...] = keep_f[0, at].astype(F32) + come_f[0, at].astype(F32)
                for target, away in ((sum_f, 0), (out_f, 1)):
                    rows = pl.ds(pl.multiple_of((chip ^ away) * eighth, 8), eighth)
                    target[0, at] = total[rows, :].astype(BF16)
            for target, at in ((sum_p, 0), (out_p, 1)):
                target[0] = (keep_p[at, 0].astype(F32) + come_p[at, 0].astype(F32)).astype(BF16)


def join(spot, firsts, lasts, outs, after=()):
    _, _, quarter, hidden = firsts[0].shape
    specs = []
    for part in (lambda k: jnp.minimum(k, 1), lambda k: jnp.maximum(k - 2, 0)):
        by_part = pl.BlockSpec((1, 2, quarter, hidden), lambda k, s, part=part: (part(k), 0, 0, 0))
        by_far = pl.BlockSpec((2, 1, quarter, hidden), lambda k, s, part=part: (0, part(k), 0, 0))
        specs += [by_part, by_part, by_far, by_far]
    eighth = quarter // 2
    fc = pl.BlockSpec((1, 2, eighth, hidden), lambda k, s: (k, 0, 0, 0))
    proj = pl.BlockSpec((1, quarter, hidden), lambda k, s: (k, 0, 0))
    return launch(
        join_kernel,
        "join",
        (spot,),
        (4,),
        (*firsts, *lasts, *outs),
        specs + [blocks(*entry.shape) for entry in outs],
        [
            (fc, shape_of(4, 2, eighth, hidden)),
            (fc, shape_of(4, 2, eighth, hidden)),
            (proj, shape_of(4, quarter, hidden)),
            (proj, shape_of(4, quarter, hidden)),
            whole_out(*outs[0].shape[1:]),
            whole_out(*outs[0].shape[1:]),
        ],
        scratch=[pltpu.VMEM((quarter, hidden), F32)],
        traffic=30,
        after=after,
    )


def own_columns(matrix, place):
    width = matrix.shape[1] // 3
    own = 2 * PAIRS * HEAD
    blank = jnp.zeros((matrix.shape[0], TILE - HEAD), matrix.dtype)
    pieces = []
    for part in range(3):
        whole = matrix[:, part * width : (part + 1) * width]
        pieces += [
            lax.dynamic_slice_in_dim(whole, place * own, own, 1),
            whole[:, width - HEAD :],
            blank,
        ]
    return jnp.concatenate(pieces, axis=1)


def local_heads(
    prompt_in,
    cont_in,
    cont_seg,
    ln1_gain,
    ln1_bias,
    w_qkv,
    qv_bias,
    w_out,
    out_bias,
    ln2_gain,
    ln2_bias,
    w_fc,
    fc_bias,
    w_proj,
    proj_bias,
    prompt_cot,
    cont_cot,
):
    width = prompt_in.shape[2]
    prompt_rows, cont_rows = prompt_in.shape[1], cont_in.shape[1]
    row_count = prompt_rows + cont_rows
    count = lax.axis_size("ctx")
    place = lax.axis_index("ctx")
    core, chip = place % 2, place // 2
    fsdp = lax.axis_index("fsdp")
    tensor = lax.axis_index("tensor")
    tensors = lax.axis_size("tensor")
    own_width = 2 * PAIRS * HEAD
    half, hidden_units = w_fc.shape
    quarter = half // 2
    eighth = quarter // 2
    padded = (width + TILE - 1) // TILE * TILE
    at = place.reshape(1)
    spot = jnp.stack([core, fsdp, tensor, jnp.int32(tensors), place])

    zero_bias = jnp.zeros_like(qv_bias[0])
    col_bias = own_columns(jnp.concatenate([qv_bias[0], zero_bias, qv_bias[1]])[None], place)[0]
    normed, q, k, v, kt, vt, w_own, rows_own, grad_layer, grad_flip, *mines, out_full = open_up(
        prompt_in,
        cont_in,
        w_qkv,
        w_fc,
        w_proj,
        w_out,
        fc_bias,
        prompt_cot,
        cont_cot,
        ln1_gain,
        ln1_bias,
        col_bias,
        count,
    )

    mine, one_away, three_away, near_far = mines

    labels = cont_seg[0].reshape(count, cont_rows)
    seg_col, seg_row = labels[:, :, None], labels[:, None, :]
    lse, outs, came, last_out, two_away, one_far, three_far, *others = attend(
        q, k, vt, seg_col, seg_row, prompt_rows, (mine, near_far, one_away, three_away)
    )
    mine_2, near_2, one_2, one_far_2, three_2, three_far_2 = others
    two_far = swap(two_away, "fsdp", 1)
    pieces = (outs, came, last_out)
    hidden, mlp_low, mlp_flip = merge(
        at, rows_own, out_full, out_bias, ln2_gain, ln2_bias, pieces
    )

    given = (spot, mlp_low, grad_layer, mlp_flip, grad_flip)
    mlp_out, grad_mlp_in, *grads_first, bias_first = mlp(
        *given, (mine, one_away), (near_far, one_far), (mine_2, one_2), (near_2, one_far_2)
    )
    (two_far,) = behind((two_far,), bias_first)
    two_2, two_far_2 = swap(two_away, "ctx", 1), swap(two_far, "ctx", 1)
    come_first = [swap(grads_first[1], "ctx", 1), swap(grads_first[3], "ctx", 1)]
    mlp_out, grad_mlp_in, *grads_last, bias_last = mlp(
        *given,
        (three_away, two_away),
        (three_far, two_far),
        (three_2, two_2),
        (three_far_2, two_far_2),
        before=(mlp_out, grad_mlp_in),
    )
    come_last = [swap(grads_last[1], "ctx", 1), swap(grads_last[3], "ctx", 1)]
    grad_fc_bias = jnp.concatenate([bias_first, bias_last], axis=0)
    prompt_out, cont_out, grad_hidden, *rest = bend(
        jnp.stack([place, fsdp]),
        mlp_out,
        grad_mlp_in,
        hidden,
        grad_layer,
        out_full,
        ln2_gain,
        proj_bias,
        pieces,
        prompt_rows,
    )
    grads_own, (grad_last, out_keep, out_send, sums2) = rest[:count], rest[count:]
    grads_all = [grads_own[0]] + [swap(grads_own[k], "ctx", k) for k in range(1, count)]

    def added(left, right):
        return left.astype(F32) + right.astype(F32)

    steps_away = (0, 1, 3, 2)

    def over_tensor(parts, token):
        come = [turn(parts[k], "tensor", -steps_away[k]) for k in range(1, tensors)]
        total = parts[0].astype(F32)
        for part in behind(come, token):
            total = total + part.astype(F32)
        return total

    def back(pair, tile, heads, grads, outs, after=()):
        return attend_back(
            pair, tile, heads, at, q, k, v, kt, lse, seg_col, seg_row, grads, outs, prompt_rows, after
        )

    grads_left = back(PAIRS, 0, 1, [grad_last], last_out[None, None])
    out_f, sum_f, out_p, sum_p, out_o, sum_o = join(
        spot,
        (grads_first[0], come_first[0], grads_first[2], come_first[1]),
        (grads_last[0], come_last[0], grads_last[2], come_last[1]),
        (out_keep, swap(out_send, "ctx", 1)),
        (grads_left[0], *grads_all[1:]),
    )
    grads_pair = [back(0, 0, 2, grads_all, outs, (out_f, out_p))]
    come_o = swap(out_o, "fsdp", 1)
    come_f, come_p = swap(out_f, "ctx", 2), swap(out_p, "fsdp", 1)
    come_f, come_p = behind((come_f, come_p), grads_pair[0][0])
    sum_f = added(sum_f, come_f).astype(BF16)
    sum_p = added(sum_p, come_p).astype(BF16)
    out_f, sum_f = sum_f[:, 1], sum_f[:, 0]
    grads_pair.append(back(1, 1, 2, grads_all, outs, (out_f, sum_p, grads_pair[0][0])))
    (come_f,) = behind((swap(out_f, "fsdp", 1),), grads_pair[1][0])
    sum_f = added(sum_f, come_f).astype(BF16)
    sum_p = over_tensor(sum_p, grads_pair[1][0]).astype(BF16)
    ordered = [entry[part] for part in range(3) for entry in (*grads_pair, grads_left)]
    vectors = jnp.concatenate([sums2, jnp.zeros((tensors, hidden_units), F32)], axis=0)
    for k, distance in enumerate(steps_away):
        vectors = lax.dynamic_update_slice(
            vectors, grad_fc_bias[k], (4 + (tensor - distance) % tensors, 0)
        )
    vectors = jnp.pad(vectors, ((0, 0), (0, padded - width)))
    prompt_grad, cont_grad, sum_qkv, sum_out, late = tail(
        ordered,
        w_own,
        normed,
        rows_own,
        grad_hidden,
        ln1_gain,
        vectors,
        sum_o,
        come_o,
        prompt_rows,
        (sum_f, sum_p),
    )
    sum_f = over_tensor(sum_f, late).astype(BF16)
    (come_p,) = behind((swap(sum_p, "ctx", 2),), late)
    sum_p = added(sum_p, come_p).astype(BF16)
    far_f = swap(sum_f, "ctx", 2)
    sum_f = jnp.concatenate(in_order(sum_f, far_f, chip), axis=0)
    both = jnp.stack([sum_f, sum_p])
    both = jnp.concatenate(in_order(both, swap(both, "ctx", 1), core), axis=1).astype(F32)
    own_fc, own_proj = both[0], both[1].T


    fc_bias_sum = lax.dynamic_index_in_dim(late, 12 + tensor, 0, False)[:hidden_units]
    return (
        prompt_out,
        cont_out,
        prompt_grad,
        cont_grad,
        late[0, :width],
        late[1, :width],
        sum_qkv.astype(F32),
        late[2:4, :width],
        sum_out.astype(F32),
        late[8, :width],
        late[9, :width],
        late[10, :width],
        own_fc,
        fc_bias_sum,
        own_proj,
        late[11, :width],
    )


def solution(mesh):
    placed = (
        P(("fsdp", "tensor"), "ctx", None),
        P(("fsdp", "tensor"), "ctx", None),
        P(("fsdp", "tensor"), None),
        P(),
        P(),
        P("fsdp", None),
        P(),
        P("fsdp", None),
        P(),
        P(),
        P(),
        P("fsdp", "tensor"),
        P("tensor"),
        P("tensor", "fsdp"),
        P(),
        P(("fsdp", "tensor"), "ctx", None),
        P(("fsdp", "tensor"), "ctx", None),
    )
    by_heads = HEADS // mesh.shape["ctx"] == PAIRS * 2 and HEADS % mesh.shape["ctx"] == 1
    return jax.shard_map(
        local_heads if by_heads else local_rows,
        mesh=mesh,
        in_specs=placed,
        out_specs=(
            P(("fsdp", "tensor"), "ctx", None),
            P(("fsdp", "tensor"), "ctx", None),
            P(("fsdp", "tensor"), "ctx", None),
            P(("fsdp", "tensor"), "ctx", None),
            P(),
            P(),
            P("fsdp", None),
            P(),
            P("fsdp", None),
            P(),
            P(),
            P(),
            P("fsdp", "tensor"),
            P("tensor"),
            P("tensor", "fsdp"),
            P(),
        ),
        check_vma=False,
    )
```

```python
import functools

import jax
import jax.numpy as jnp
from jax import lax
from jax.experimental import pallas as pl
from jax.experimental.pallas import tpu as pltpu
from jax.sharding import PartitionSpec as P

HEADS = 17
HEAD = 64


def passed_along(value, axis, steps):
    count = lax.axis_size(axis)
    leading, last = (max(0, -steps), min(count, count - steps))
    return lax.ppermute(value, axis, [(source, source + steps) for source in range(leading, last)])


def layer_norm(values, norm_gain, norm_bias):
    average = jnp.mean(values, axis=-1, keepdims=True)
    centred = values - average
    variance = jnp.mean(centred * centred, axis=-1, keepdims=True)
    return centred * lax.rsqrt(variance + 1e-05) * norm_gain + norm_bias


def gelu_tanh(values):
    return jax.nn.gelu(values, approximate=True)


def inner_first(left_op, right_op):
    return lax.dot_general(
        left_op, right_op, (((0,), (0,)), ((), ())), preferred_element_type=jnp.float32
    )


def inner_last(left_op, right_op):
    return lax.dot_general(
        left_op, right_op, (((1,), (1,)), ((), ())), preferred_element_type=jnp.float32
    )


def to_heads(values):
    return jnp.swapaxes(values.reshape(values.shape[0], HEADS, HEAD), 0, 1)


def from_heads(values):
    return jnp.swapaxes(values, 0, 1).reshape(values.shape[1], values.shape[0] * values.shape[2])


def fetch_prompt(rows_kv):
    return lax.all_gather(rows_kv, "ctx", axis=0, tiled=True)


def local_rows(
    prompt_in,
    cont_in,
    cont_seg,
    ln1_gain,
    ln1_bias,
    w_qkv,
    qv_bias,
    w_out,
    out_bias,
    ln2_gain,
    ln2_bias,
    w_fc,
    fc_bias,
    w_proj,
    proj_bias,
    prompt_cot,
    cont_cot,
):
    model_width = prompt_in.shape[2]
    prompt_rows = prompt_in.shape[1]
    cont_rows = cont_in.shape[1]
    row_count = prompt_rows + cont_rows
    ctx_count = lax.axis_size("ctx")
    ctx_place = lax.axis_index("ctx")
    prompt_total = prompt_rows * ctx_count
    qkv_full, out_full = (
        lax.all_gather(w_qkv.astype(jnp.bfloat16), "fsdp", axis=0, tiled=True),
        lax.all_gather(w_out.astype(jnp.bfloat16), "fsdp", axis=0, tiled=True),
    )
    fc_full, proj_full = (
        lax.all_gather(w_fc.astype(jnp.bfloat16), "fsdp", axis=0, tiled=True),
        lax.all_gather(w_proj.astype(jnp.bfloat16), "fsdp", axis=1, tiled=True),
    )
    row_ids = jnp.arange(row_count, dtype=jnp.int32)
    labels_all = cont_seg[0]
    own_labels = lax.dynamic_slice_in_dim(labels_all, ctx_place * cont_rows, cont_rows)
    earlier_labels = lax.dynamic_slice_in_dim(
        labels_all, jnp.maximum(ctx_place - 1, 0) * cont_rows, cont_rows
    )
    query_labels = jnp.concatenate([jnp.full((prompt_rows,), -1, jnp.int32), own_labels])
    query_prompt = ctx_place * prompt_rows + row_ids
    query_cont = ctx_place * cont_rows + row_ids - prompt_rows
    is_cont = row_ids >= prompt_rows
    prompt_ids = jnp.arange(prompt_total, dtype=jnp.int32)
    near_ids = (ctx_place - 1) * cont_rows + jnp.arange(2 * cont_rows, dtype=jnp.int32)
    near_labels = jnp.concatenate([earlier_labels, own_labels])
    allowed_far = is_cont[:, None] | (prompt_ids[None, :] <= query_prompt[:, None])
    allowed_near = (
        (query_labels[:, None] == near_labels[None, :])
        & (near_ids[None, :] <= query_cont[:, None])
        & (near_ids[None, :] >= 0)
    )
    allowed = jnp.concatenate([allowed_far, allowed_near], 1)
    inputs = jnp.concatenate([prompt_in[0], cont_in[0]], 0).astype(jnp.float32)
    normed, norm1_back = jax.vjp(layer_norm, inputs, ln1_gain, ln1_bias)
    normed_low = normed.astype(jnp.bfloat16)
    projected = jnp.dot(normed_low, qkv_full, preferred_element_type=jnp.float32)
    queries = (projected[:, :model_width] + qv_bias[0]).astype(jnp.bfloat16)
    key_value = jnp.concatenate(
        [projected[:, model_width : 2 * model_width], projected[:, 2 * model_width :] + qv_bias[1]],
        1,
    ).astype(jnp.bfloat16)
    own_cont_kv = key_value[prompt_rows:]
    earlier_kv = passed_along(own_cont_kv, "ctx", 1)
    prompt_kv = fetch_prompt(key_value[:prompt_rows])
    keys_all = jnp.concatenate([prompt_kv, earlier_kv, own_cont_kv], 0)
    query_heads = to_heads(queries)
    key_heads = to_heads(keys_all[:, :model_width])
    value_heads = to_heads(keys_all[:, model_width:])

    def head_forward(operands):
        query_head, key_head, value_head = operands
        scores = inner_last(query_head, key_head) * 0.125
        scores = jnp.where(allowed, scores, -1e30)
        row_max = jnp.max(scores, axis=1, keepdims=True)
        exponent = jnp.exp(scores - row_max)
        row_total = jnp.sum(exponent, axis=1, keepdims=True)
        probability = (exponent / row_total).astype(jnp.bfloat16)
        head_out = jnp.dot(probability, value_head, preferred_element_type=jnp.float32)
        return (head_out.astype(jnp.bfloat16), (row_max + jnp.log(row_total))[:, 0])

    heads_out, logsum = lax.map(head_forward, (query_heads, key_heads, value_heads))
    attended = from_heads(heads_out)
    hidden = inputs + jnp.dot(attended, out_full, preferred_element_type=jnp.float32) + out_bias
    mlp_in, norm2_back = jax.vjp(layer_norm, hidden, ln2_gain, ln2_bias)
    mlp_low = mlp_in.astype(jnp.bfloat16)
    mlp_rows = lax.all_gather(mlp_low, "tensor", axis=0, tiled=True)
    pre_act = jnp.dot(mlp_rows, fc_full, preferred_element_type=jnp.float32) + fc_bias
    activated, gelu_back = jax.vjp(gelu_tanh, pre_act)
    act_low = activated.astype(jnp.bfloat16)
    partial_out = jnp.dot(act_low, proj_full, preferred_element_type=jnp.float32)
    mlp_out = lax.psum_scatter(
        partial_out.astype(jnp.bfloat16), "tensor", scatter_dimension=0, tiled=True
    ).astype(jnp.float32)
    layer_out = (hidden + mlp_out + proj_bias).astype(jnp.bfloat16)
    grad_layer = jnp.concatenate([prompt_cot[0], cont_cot[0]], 0)
    grad_float = grad_layer.astype(jnp.float32)
    grad_proj_bias = jnp.sum(grad_float, axis=0)
    grad_rows = lax.all_gather(grad_layer, "tensor", axis=0, tiled=True)
    grad_w_proj = inner_first(act_low, grad_rows)
    grad_act = inner_last(grad_rows, proj_full)
    grad_pre = gelu_back(grad_act)[0].astype(jnp.bfloat16)
    grad_fc_bias = jnp.sum(grad_pre.astype(jnp.float32), axis=0)
    grad_w_fc = inner_first(mlp_rows, grad_pre)
    grad_mlp_part = inner_last(grad_pre, fc_full)
    grad_mlp_in = lax.psum_scatter(grad_mlp_part, "tensor", scatter_dimension=0, tiled=True)
    grad_hidden_norm, grad_ln2_gain, grad_ln2_bias = norm2_back(grad_mlp_in)
    grad_hidden = grad_float + grad_hidden_norm
    grad_out_bias = jnp.sum(grad_hidden, axis=0)
    grad_branch = grad_hidden.astype(jnp.bfloat16)
    grad_w_out = inner_first(attended, grad_branch)
    grad_attended = inner_last(grad_branch, out_full).astype(jnp.bfloat16)
    prompt_again = fetch_prompt(key_value[:prompt_rows])
    keys_back = jnp.concatenate([prompt_again, earlier_kv, own_cont_kv], 0)
    key_back_heads = to_heads(keys_back[:, :model_width])
    value_back_heads = to_heads(keys_back[:, model_width:])

    def head_backward(operands):
        query_head, key_head, value_head, grad_head, logsum_head = operands
        scores = inner_last(query_head, key_head) * 0.125
        scores = jnp.where(allowed, scores, -1e30)
        probability = jnp.exp(scores - logsum_head[:, None])
        prob_low = probability.astype(jnp.bfloat16)
        grad_prob = inner_last(grad_head, value_head)
        centre = jnp.sum(probability * grad_prob, axis=1, keepdims=True)
        grad_scores = (probability * (grad_prob - centre)).astype(jnp.bfloat16)
        grad_query = jnp.dot(grad_scores, key_head, preferred_element_type=jnp.float32) * 0.125
        grad_key = inner_first(grad_scores, query_head) * 0.125
        grad_value = inner_first(prob_low, grad_head)
        return (grad_query, grad_key, grad_value)

    head_operands = (query_heads, key_back_heads, value_back_heads, to_heads(grad_attended), logsum)
    grad_q_heads, grad_k_heads, grad_v_heads = lax.map(head_backward, head_operands)
    grad_queries = from_heads(grad_q_heads).astype(jnp.bfloat16)
    grad_kv = jnp.concatenate([from_heads(grad_k_heads), from_heads(grad_v_heads)], 1)
    prompt_grad_kv = lax.psum_scatter(
        grad_kv[:prompt_total], "ctx", scatter_dimension=0, tiled=True
    )
    from_later = passed_along(
        grad_kv[prompt_total : prompt_total + cont_rows].astype(jnp.bfloat16), "ctx", -1
    ).astype(jnp.float32)
    cont_grad_kv = grad_kv[prompt_total + cont_rows :] + from_later
    grad_kv_rows = jnp.concatenate([prompt_grad_kv, cont_grad_kv], 0).astype(jnp.bfloat16)
    grad_projected = jnp.concatenate([grad_queries, grad_kv_rows], 1)
    grad_qv_bias = jnp.stack(
        [
            jnp.sum(grad_queries.astype(jnp.float32), axis=0),
            jnp.sum(grad_kv_rows[:, model_width:].astype(jnp.float32), axis=0),
        ]
    )
    grad_w_qkv = inner_first(normed_low, grad_projected)
    grad_normed = inner_last(grad_projected, qkv_full)
    grad_inputs_norm, grad_ln1_gain, grad_ln1_bias = norm1_back(grad_normed)
    grad_inputs = (grad_hidden + grad_inputs_norm).astype(jnp.bfloat16)
    shard_qkv, shard_out = (
        lax.psum_scatter(
            grad_w_qkv.astype(jnp.bfloat16), "fsdp", scatter_dimension=0, tiled=True
        ).astype(jnp.float32),
        lax.psum_scatter(
            grad_w_out.astype(jnp.bfloat16), "fsdp", scatter_dimension=0, tiled=True
        ).astype(jnp.float32),
    )
    sum_qkv, sum_out = lax.psum((shard_qkv, shard_out), ("ctx", "tensor"))
    sum_fc, sum_proj, sum_fc_bias = lax.psum(
        (grad_w_fc, grad_w_proj, grad_fc_bias), ("fsdp", "ctx")
    )
    fsdp_place = lax.axis_index("fsdp")
    fsdp_rows = w_fc.shape[0]
    own_fc = lax.dynamic_slice_in_dim(sum_fc, fsdp_place * fsdp_rows, fsdp_rows, 0)
    own_proj = lax.dynamic_slice_in_dim(sum_proj, fsdp_place * fsdp_rows, fsdp_rows, 1)
    small_sums = lax.psum(
        (
            grad_ln1_gain,
            grad_ln1_bias,
            grad_qv_bias,
            grad_out_bias,
            grad_ln2_gain,
            grad_ln2_bias,
            grad_proj_bias,
        ),
        ("fsdp", "ctx", "tensor"),
    )
    return (
        layer_out[:prompt_rows][None],
        layer_out[prompt_rows:][None],
        grad_inputs[:prompt_rows][None],
        grad_inputs[prompt_rows:][None],
        small_sums[0],
        small_sums[1],
        sum_qkv,
        small_sums[2],
        sum_out,
        small_sums[3],
        small_sums[4],
        small_sums[5],
        own_fc,
        sum_fc_bias,
        own_proj,
        small_sums[6],
    )


PAIRS = 2
TILE = 2 * HEAD
BF16 = jnp.bfloat16
F32 = jnp.float32
LOG2E = 1.4426950408889634
SCALE2 = 0.125 * LOG2E
HINT = 0.2
NN = (((1,), (0,)), ((), ()))
NT = (((1,), (1,)), ((), ()))
TN = (((0,), (0,)), ((), ()))


def dot(left_op, right_op, dims=NN):
    return lax.dot_general(left_op, right_op, dims, preferred_element_type=F32)


def swap(value, axis, bit):
    count = lax.axis_size(axis)
    return lax.ppermute(value, axis, [(place, place ^ bit) for place in range(count)])


def turn(value, axis, steps):
    count = lax.axis_size(axis)
    return lax.ppermute(value, axis, [(place, (place + steps) % count) for place in range(count)])


def halves(values, heads=2):
    lane = lax.broadcasted_iota(jnp.int32, values.shape, 1)
    zero = jnp.zeros_like(values)
    return [jnp.where((lane < HEAD) == (head == 0), values, zero) for head in range(heads)]


ANYWHERE = pl.BlockSpec(memory_space=pl.ANY)


def blocks(*shape):
    return pl.BlockSpec(shape, lambda i, *_: (0,) * len(shape))


def shape_of(*shape, kind=BF16):
    return jax.ShapeDtypeStruct(shape, kind)


def launch(
    kernel, name, scalars, grid, operands, in_specs, outs, scratch=(), limit=48, flops=0, traffic=16, exps=0, after=(), carry=(), aliases=None, meet=None
):
    out_specs, out_shapes = [out[0] for out in outs], [out[1] for out in outs]
    given = len(scalars) + len(operands)
    tied = given + len(after) + len(carry)

    def body(*refs):
        made = refs[tied : tied + len(outs)]
        kernel(*refs[:given], *made, *refs[tied + len(outs) + len(carry) :])

    links = {len(scalars) + here: there for here, there in (aliases or {}).items()}
    links.update({given + len(after) + i: len(outs) + i for i in range(len(carry))})
    out = pl.pallas_call(
        body,
        grid_spec=pltpu.PrefetchScalarGridSpec(
            num_scalar_prefetch=len(scalars),
            grid=grid,
            in_specs=list(in_specs) + [ANYWHERE] * (len(after) + len(carry)),
            out_specs=out_specs + [ANYWHERE] * len(carry),
            scratch_shapes=list(scratch),
        ),
        out_shape=out_shapes + [shape_of(*entry.shape, kind=entry.dtype) for entry in carry],
        input_output_aliases=links,
        compiler_params=pltpu.CompilerParams(
            vmem_limit_bytes=limit << 20, collective_id=meet, has_side_effects=meet is not None
        ),
        cost_estimate=pl.CostEstimate(
            flops=int(flops * HINT),
            bytes_accessed=int(traffic * HINT * (1 << 20)),
            transcendentals=int(exps * HINT),
        ),
        name=name,
    )(*scalars, *operands, *after, *carry)
    return (out[: len(outs)], *out[len(outs) :]) if carry else out


def behind(arrays, token):
    out = launch(
        lambda *refs: None, "behind", (), (1,), (), (), (), after=(token,), carry=tuple(arrays)
    )
    return out[1:]


def whole_out(*shape, kind=BF16):
    return blocks(*shape), shape_of(*shape, kind=kind)


def in_order(own, other, place):
    first = place == 0
    return jnp.where(first, own, other), jnp.where(first, other, own)


def open_kernel(*refs):
    prompt_ref, cont_ref, w_ref, fc_ref, proj_ref, wo_ref, gp_ref, gc_ref = refs[:8]
    fc_bias_ref, gain_ref, bias_ref, col_bias_ref = refs[8:12]
    norm_ref, q_ref, k_ref, v_ref, kt_ref, vt_ref = refs[12:18]
    w_own_ref, rows_ref, g_ref, gt_ref, mine_ref, one_ref, three_ref, far_ref, out_ref = refs[18:27]
    (
        rows_t,
        w_s,
        w_own,
        w_out,
        fc_s,
        proj_s,
        mine_s,
        g_t,
        normed,
        norms,
        tall_s,
        flat_s,
        turned,
        wo_f,
        wo_s,
        local_sem,
        send_sem,
        recv_sem,
        out_sem,
    ) = refs[27:]
    place = lax.axis_index("ctx")
    fsdp = lax.axis_index("fsdp")
    tensor = lax.axis_index("tensor")
    tensors = lax.axis_size("tensor")
    core = place % 2
    width, row_count = rows_t.shape[1], rows_t.shape[2]
    prompt_rows = prompt_ref.shape[1]
    half, quarter = width // 2, width // 4
    own = 2 * PAIRS * HEAD
    beside, across, far = {"ctx": place ^ 1}, {"ctx": place ^ 2}, {"fsdp": 1 - fsdp}
    others = [{"tensor": lax.rem(tensor + k, tensors)} for k in range(1, tensors)]

    barrier = pltpu.get_barrier_semaphore()
    for partner in (beside, across, far, *others):
        pl.semaphore_signal(barrier, inc=1, device_id=partner, device_id_type=pl.DeviceIdType.MESH)

    def load(source, target, at):
        copy = pltpu.make_async_copy(source, target, local_sem.at[at])
        copy.start()
        return copy

    def spans(ref):
        return ref.at[:, :prompt_rows], ref.at[:, prompt_rows:]

    own_prompt, own_cont = spans(rows_t.at[0])
    load_rows = [load(prompt_ref, own_prompt, 0), load(cont_ref, own_cont, 1)]
    load_w = load(w_ref, w_s, 2)
    mine_rows = pl.ds(pl.multiple_of(core * quarter, 16), quarter)
    load_mine = [load(fc_ref.at[mine_rows], fc_s, 3), load(proj_ref.at[mine_rows], proj_s, 4)]
    g_prompt, g_cont = spans(g_t)
    load_g = [load(gp_ref, g_prompt, 5), load(gc_ref, g_cont, 6)]
    load_wo = load(wo_ref, wo_f, 7)
    sent, used = [], []

    def push(source, target, partner):
        at = len(used)
        used.append(at)
        copy = pltpu.make_async_remote_copy(
            src_ref=source,
            dst_ref=target,
            send_sem=send_sem.at[at],
            recv_sem=recv_sem.at[at],
            device_id=partner,
            device_id_type=pl.DeviceIdType.MESH,
        )
        copy.start()
        sent.append(copy)
        return copy

    for copy in load_rows:
        copy.wait()
    pl.semaphore_wait(barrier, 3 + len(others))
    to_chip = [
        push(source, target, across) for source, target in zip(spans(rows_t.at[0]), spans(rows_t.at[2]))
    ]
    to_core = push(rows_t.at[0], rows_t.at[1], beside)

    load_w.wait()
    step = w_own.shape[1] // 3
    for part in range(3):
        for at in range((width - HEAD) // own):

            @pl.when(place == at)
            def _():
                start = part * width + at * own
                w_out[:, part * step : part * step + own] = w_s[:, start : start + own].astype(BF16)

        last = w_s[:, (part + 1) * width - HEAD : (part + 1) * width].astype(BF16)
        w_out[:, part * step + own : (part + 1) * step] = jnp.concatenate(
            [last, jnp.zeros((half, step - own - HEAD), BF16)], axis=1
        )
    mine_half = pl.ds(pl.multiple_of(fsdp * half, 16), half)
    to_far = push(w_out, w_own.at[mine_half], far)
    w_own[mine_half, :] = w_out[...]

    for copy in load_mine:
        copy.wait()
    mine_s[:quarter] = fc_s[...].astype(BF16)
    mine_s[quarter : 2 * quarter] = proj_s[...].astype(BF16)
    bias = fc_bias_ref[...]
    pieces = []
    for _ in range(3):
        piece = bias.astype(BF16)
        pieces.append(piece)
        bias = bias - piece.astype(F32)
    pieces.append(jnp.zeros((mine_s.shape[0] - 2 * quarter - 3, width), BF16))
    mine_s[2 * quarter :] = jnp.concatenate(pieces, axis=0)
    to_one = push(mine_s, one_ref, others[0])
    to_near = push(mine_s, far_ref, far)
    to_three = push(mine_s, three_ref, others[2])
    outs, put_at = [], []

    def put(source, target):
        copy = pltpu.make_async_copy(source, target, out_sem.at[len(put_at)])
        put_at.append(len(put_at))
        copy.start()
        outs.append(copy)
        return copy

    def take(copies):
        for copy in copies:
            copy.wait()
        outs[:] = [copy for copy in outs if all(copy is not done for done in copies)]

    put(mine_s, mine_ref)

    load_wo.wait()
    wo_s[...] = wo_f[...].astype(BF16)
    put(wo_s, out_ref.at[mine_half])
    chunk = 128

    def over_rows(body):
        @pl.loop(0, row_count // chunk)
        def _(i):
            body(pl.ds(pl.multiple_of(i * chunk, chunk), chunk))

    for copy in load_g:
        copy.wait()
    put(g_t, gt_ref)

    def turn_rows(source, target):
        def body(rows):
            target[rows, :] = source[:, rows].T

        over_rows(body)

    turn_rows(g_t, turned.at[0])
    put(turned.at[0], g_ref)
    turn_rows(rows_t.at[0], turned.at[1])
    put(turned.at[1], rows_ref)

    extra = norms.shape[1] - width
    at_row = lax.broadcasted_iota(jnp.int32, (extra, row_count), 0)
    ones = jnp.where(at_row == 0, 1.0, 0.0).astype(BF16)
    norms[0, width:] = ones
    norms[1, width:] = ones

    def normalise(distance, slot):
        def body(rows):
            values = rows_t[distance, :, rows].astype(F32)
            average = jnp.mean(values, axis=0, keepdims=True)
            centred = values - average
            variance = jnp.mean(centred * centred, axis=0, keepdims=True)
            low = centred * lax.rsqrt(variance + 1e-05) * gain_ref[...] + bias_ref[...]
            low = low.astype(BF16)
            norms[slot, :width, rows] = low
            normed[rows, :] = low.T

        over_rows(body)

    def project(distance, slot):
        block = place ^ distance
        made = [put(norms.at[slot], norm_ref.at[block])]
        tiles = step // TILE
        for part, (out, flip) in enumerate(((q_ref, None), (k_ref, kt_ref), (v_ref, vt_ref))):
            cols = slice(part * step, (part + 1) * step)
            value = (dot(normed[...], w_own[:, cols]) + col_bias_ref[:, cols]).astype(BF16)
            for tile in range(tiles):
                piece = value[:, tile * TILE : (tile + 1) * TILE]
                tall_s[slot, :, (part * tiles + tile) * TILE : (part * tiles + tile + 1) * TILE] = piece
                if flip is not None:
                    flat_s[slot, part - 1, tile] = piece.T
            for tile in range(tiles):
                lanes = slice((part * tiles + tile) * TILE, (part * tiles + tile + 1) * TILE)
                made.append(put(tall_s.at[slot, :, lanes], out.at[tile, block]))
                if flip is not None:
                    made.append(put(flat_s.at[slot, part - 1, tile], flip.at[tile, block]))
        return made

    normalise(0, 0)
    to_far.wait_recv()
    put(w_own, w_own_ref)
    first = project(0, 0)
    to_core.wait_recv()
    normalise(1, 1)
    second = project(1, 1)
    to_corner = []
    for copy, source, target in zip(to_chip, spans(rows_t.at[2]), spans(rows_t.at[3])):
        copy.wait_recv()
        to_corner.append(push(source, target, beside))
    take(first)
    normalise(2, 0)
    project(2, 0)
    for copy in to_corner:
        copy.wait_recv()
    take(second)
    normalise(3, 1)
    project(3, 1)
    for copy in outs:
        copy.wait()
    for copy in (to_one, to_near, to_three):
        copy.wait_recv()
    for copy in sent:
        copy.wait_send()


def open_up(
    prompt_in, cont_in, w_qkv, w_fc, w_proj, w_out, fc_bias, prompt_cot, cont_cot, gain, bias, col_bias, count
):
    prompt_rows, width = prompt_in.shape[1:]
    row_count = prompt_rows + cont_in.shape[1]
    half, quarter = width // 2, width // 4
    tiles = PAIRS + 1
    cols = 3 * tiles * TILE
    in_vmem = pl.BlockSpec(memory_space=pltpu.VMEM)
    vmem = lambda *shape, kind=BF16: pltpu.VMEM(shape, kind)
    tall, flat = (tiles, count, row_count, TILE), (tiles, count, TILE, row_count)
    mine = (2 * quarter + 16, w_fc.shape[1])
    outs = [
        (count, width + 16, row_count),
        tall,
        tall,
        tall,
        flat,
        flat,
        (width, cols),
        (row_count, width),
        (row_count, width),
        (width, row_count),
        mine,
        mine,
        mine,
        mine,
        (width, width),
    ]
    copies = 2 + 1 + 1 + 3 + 2
    return pl.pallas_call(
        open_kernel,
        in_specs=[ANYWHERE] * 8 + [in_vmem] * 4,
        out_specs=[ANYWHERE] * len(outs),
        out_shape=[shape_of(*out) for out in outs],
        scratch_shapes=[
            vmem(4, width, row_count),
            vmem(*w_qkv.shape, kind=F32),
            vmem(width, cols),
            vmem(half, cols),
            vmem(quarter, w_fc.shape[1], kind=F32),
            vmem(quarter, w_fc.shape[1], kind=F32),
            vmem(*mine),
            vmem(width, row_count),
            vmem(row_count, width),
            vmem(2, width + 16, row_count),
            vmem(2, row_count, cols),
            vmem(2, 2, tiles, TILE, row_count),
            vmem(2, row_count, width),
            vmem(half, width, kind=F32),
            vmem(half, width),
            pltpu.SemaphoreType.DMA((8,)),
            pltpu.SemaphoreType.DMA((copies,)),
            pltpu.SemaphoreType.DMA((copies,)),
            pltpu.SemaphoreType.DMA((80,)),
        ],
        compiler_params=pltpu.CompilerParams(
            vmem_limit_bytes=60 << 20, collective_id=2, has_side_effects=True
        ),
        cost_estimate=pl.CostEstimate(
            flops=2 * count * row_count * width * cols, bytes_accessed=40 << 20, transcendentals=0
        ),
        name="open",
    )(
        prompt_in[0].T,
        cont_in[0].T,
        w_qkv,
        w_fc,
        w_proj.T,
        w_out,
        prompt_cot[0].T,
        cont_cot[0].T,
        fc_bias[None],
        gain[:, None],
        bias[:, None],
        col_bias[None],
    )


def own_mask(rows):
    key_at = lax.broadcasted_iota(jnp.int32, (rows, rows), 0)
    query_at = lax.broadcasted_iota(jnp.int32, (rows, rows), 1)
    return key_at <= query_at


def attend_kernel(prompt_rows, q_ref, k_ref, vt_ref, seg_col_ref, seg_row_ref, *refs):
    mine_ref, near_ref, one_ref, three_ref = refs[:4]
    lse_ref, outs_ref, pieces_ref, last_ref, two_ref, one_far_ref, three_far_ref = refs[5:12]
    beside_refs, out_ref, (acc, o_s, send_sem, recv_sem, out_sem) = refs[12:18], refs[18], refs[19:]
    step = pl.program_id(0)
    place = lax.axis_index("ctx")
    fsdp = lax.axis_index("fsdp")
    tensor = lax.axis_index("tensor")
    tensors = lax.axis_size("tensor")
    count, row_count = k_ref.shape[1], k_ref.shape[2]
    cont_rows = row_count - prompt_rows
    per_pair = 2 * count
    steps = PAIRS * per_pair
    beside, far = {"ctx": place ^ 1}, {"fsdp": 1 - fsdp}
    after, before = lax.rem(tensor + 1, tensors), lax.rem(tensor + tensors - 1, tensors)
    distance = jnp.where(step < steps, count - 1 - step % per_pair // 2, 0)
    block = place ^ distance

    def copy_to(at, source, target, partner):
        return pltpu.make_async_remote_copy(
            src_ref=source,
            dst_ref=target,
            send_sem=send_sem.at[at],
            recv_sem=recv_sem.at[at],
            device_id=partner,
            device_id_type=pl.DeviceIdType.MESH,
        )

    b_mine, b_near, b_one, b_one_far, b_three, b_three_far = beside_refs
    returns = {}
    for pair in range(PAIRS):
        for away in range(1, count):
            returns[pair, away] = copy_to(
                pair * (count - 1) + away - 1,
                o_s.at[pair, away],
                pieces_ref.at[pair, away - 1],
                {"ctx": place ^ away},
            )
    base = PAIRS * (count - 1)
    quarter = out_ref.shape[0] // 4

    def out_rows(away):
        return out_ref.at[pl.ds(pl.multiple_of(((fsdp ^ away) * 2 + place % 2) * quarter, 16), quarter)]

    early = [
        copy_to(base, one_ref, one_far_ref, far),
        copy_to(base + 1, one_ref, two_ref, {"tensor": after}),
        copy_to(base + 2, mine_ref, b_mine, beside),
        copy_to(base + 3, near_ref, b_near, beside),
        copy_to(base + 4, one_ref, b_one, beside),
        copy_to(base + 5, three_ref, b_three, beside),
        copy_to(base + 6, three_ref, three_far_ref, far),
        copy_to(base + 9, out_rows(0), out_rows(0), far),
    ]
    late = [
        copy_to(base + 7, one_far_ref, b_one_far, beside),
        copy_to(base + 8, three_far_ref, b_three_far, beside),
        copy_to(base + 10, out_rows(1), out_rows(1), beside),
    ]

    @pl.when(step == 0)
    def _():
        barrier = pltpu.get_barrier_semaphore()
        partners = [{"ctx": place ^ away} for away in range(1, count)]
        partners += [far, {"tensor": after}, {"tensor": before}]
        for partner in partners:
            pl.semaphore_signal(
                barrier, inc=1, device_id=partner, device_id_type=pl.DeviceIdType.MESH
            )
        pl.semaphore_wait(barrier, len(partners))
        for copy in early[:1] + early[7:] + early[1:7]:
            copy.start()

    @pl.when(step == per_pair + 2)
    def _():
        early[0].wait_recv()
        late[0].start()

    @pl.when(step == per_pair + 5)
    def _():
        early[7].wait_recv()
        late[2].start()

    @pl.when(step == steps + 1)
    def _():
        early[6].wait_recv()
        late[1].start()

    def part(queries, at, start, size, mask, states):
        keys = k_ref[0, at, pl.ds(start, size), :]
        scores = [dot(keys, query, NT) for query in queries]
        if mask is not None:
            scores = [jnp.where(mask, score, -1e30) for score in scores]
        tops = [jnp.max(score, axis=0, keepdims=True) for score in scores]
        if states is not None:
            tops = [jnp.maximum(top, state[0]) for top, state in zip(tops, states)]
        exps = [jnp.exp2(score * SCALE2 - top * SCALE2) for score, top in zip(scores, tops)]
        totals = [jnp.sum(exp, axis=0, keepdims=True) for exp in exps]
        made = []
        for head in range(len(queries)):
            rows = slice(head * HEAD, (head + 1) * HEAD)
            cols = slice(0, queries[head].shape[0])
            out = dot(vt_ref[0, at, rows, pl.ds(start, size)], exps[head].astype(BF16))
            total = totals[head]
            if states is None:
                acc[rows, cols] = out
            else:
                shrink = jnp.exp2((states[head][0] - tops[head]) * SCALE2)
                total = total + states[head][1] * shrink
                acc[rows, cols] = acc[rows, cols] * shrink + out
            made.append((tops[head], total))
        return made

    def finish(start, size, states):
        for head, (top, total) in enumerate(states):
            rows = slice(head * HEAD, (head + 1) * HEAD)
            acc[rows, :size] = acc[rows, :size] / total
            lse_ref[0, block, head : head + 1, pl.ds(start, size)] = top * SCALE2 + jnp.log2(total)
        if len(states) == 1:
            acc[HEAD:, :size] = jnp.zeros((TILE - HEAD, size), F32)
        pair = step // per_pair
        o_s[pair, distance, pl.ds(start, size), :] = acc[:, :size].T.astype(BF16)

    def over_prompt(queries, total, states):
        return lax.fori_loop(
            0, total, lambda c, states: part(queries, c, 0, prompt_rows, None, states), states
        )

    for heads, here in ((2, step < steps), (1, step >= steps)):

        @pl.when(here & (step % 2 == 1))
        def _():
            queries = halves(q_ref[0, block, :prompt_rows, :], heads)
            states = part(queries, block, 0, prompt_rows, own_mask(prompt_rows), None)
            finish(0, prompt_rows, over_prompt(queries, block, states))

        @pl.when(here & (step % 2 == 0))
        def _():
            previous = jnp.maximum(block - 1, 0)
            labels = seg_row_ref[block]
            queries = halves(q_ref[0, block, prompt_rows:, :], heads)
            own = own_mask(cont_rows) & (seg_col_ref[block] == labels)
            near = (seg_col_ref[previous] == labels) & (block > 0)
            states = part(queries, block, prompt_rows, cont_rows, own, None)
            states = part(queries, previous, prompt_rows, cont_rows, near, states)
            finish(prompt_rows, cont_rows, over_prompt(queries, count, states))

    for pair in range(PAIRS):
        for away in range(1, count):

            @pl.when(step == pair * per_pair + 2 * (count - 1 - away) + 1)
            def _():
                returns[pair, away].start()

    @pl.when(step == steps + 1)
    def _():
        stores = [
            pltpu.make_async_copy(o_s.at[pl.ds(0, PAIRS)], outs_ref, out_sem.at[0]),
            pltpu.make_async_copy(o_s.at[PAIRS, 0], last_ref, out_sem.at[1]),
        ]
        for store in stores:
            store.start()
        for copy in early[1:6] + late + list(returns.values()):
            copy.wait_recv()
        for copy in early + late + list(returns.values()):
            copy.wait_send()
        for store in stores:
            store.wait()


def attend(q, k, vt, seg_col, seg_row, prompt_rows, weights, w_out):
    groups, count, row_count, _ = q.shape
    cont_rows = row_count - prompt_rows
    pair = lambda i: (jnp.minimum(i // (2 * count), PAIRS), 0, 0, 0)
    pairs = groups * count * (prompt_rows + 2 * cont_rows) * prompt_rows * count // 2
    mine = weights[0].shape
    copies = PAIRS * (count - 1) + 11
    outs = [
        (pl.BlockSpec((1, count, 2, row_count), pair), shape_of(groups, count, 2, row_count, kind=F32)),
        (ANYWHERE, shape_of(PAIRS, count, row_count, TILE)),
        (ANYWHERE, shape_of(PAIRS, count - 1, row_count, TILE)),
        (ANYWHERE, shape_of(row_count, TILE)),
    ] + [(ANYWHERE, shape_of(*mine))] * 9
    outs.append((ANYWHERE, shape_of(*w_out.shape)))
    return pl.pallas_call(
        functools.partial(attend_kernel, prompt_rows),
        grid=(PAIRS * 2 * count + 2,),
        in_specs=[
            pl.BlockSpec((1, count, row_count, TILE), pair),
            pl.BlockSpec((1, count, row_count, TILE), pair),
            pl.BlockSpec((1, count, TILE, row_count), pair),
            pl.BlockSpec((count, cont_rows, 1), lambda i: (0, 0, 0)),
            pl.BlockSpec((count, 1, cont_rows), lambda i: (0, 0, 0)),
        ]
        + [ANYWHERE] * (len(weights) + 1),
        input_output_aliases={5 + len(weights): len(outs) - 1},
        out_specs=[out[0] for out in outs],
        out_shape=[out[1] for out in outs],
        scratch_shapes=[
            pltpu.VMEM((TILE, max(prompt_rows, cont_rows)), F32),
            pltpu.VMEM((groups, count, row_count, TILE), BF16),
            pltpu.SemaphoreType.DMA((copies,)),
            pltpu.SemaphoreType.DMA((copies,)),
            pltpu.SemaphoreType.DMA((2,)),
        ],
        compiler_params=pltpu.CompilerParams(
            vmem_limit_bytes=56 << 20, collective_id=3, has_side_effects=True
        ),
        cost_estimate=pl.CostEstimate(
            flops=8 * TILE * pairs, bytes_accessed=20 << 20, transcendentals=2 * pairs
        ),
        name="attend",
    )(q, k, vt, seg_col, seg_row, *weights, w_out)


def attend_back_kernel(
    heads,
    spans,
    prompt_rows,
    place_ref,
    q_ref,
    k_ref,
    v_ref,
    kt_ref,
    lse_ref,
    seg_col_ref,
    seg_row_ref,
    *refs,
):
    do_refs, o_refs, refs = refs[:spans], refs[spans : 2 * spans], refs[2 * spans :]
    dq_ref, dk_ref, dv_ref, dk_acc, dv_acc, dq_acc, do_s, o_s = refs
    step = pl.program_id(0)
    distance = step % spans
    block = place_ref[0] ^ distance
    count, row_count = k_ref.shape[1], k_ref.shape[2]
    cont_rows = row_count - prompt_rows

    @pl.when(step == 0)
    def _():
        dk_acc[...] = jnp.zeros_like(dk_acc)
        dv_acc[...] = jnp.zeros_like(dv_acc)
        if spans < count:
            dq_ref[...] = jnp.zeros_like(dq_ref)

    def part(given, at, start, size, mask, first):
        rows = pl.ds(start, size)
        for head in range(heads):
            query, grad, lse, centre = (entry[head] for entry in given)
            cols = slice(0, query.shape[0])
            own = slice(head * HEAD, (head + 1) * HEAD)
            scores = dot(k_ref[0, at, rows, :], query, NT)
            if mask is not None:
                scores = jnp.where(mask, scores, -1e30)
            probability = jnp.exp2(scores * SCALE2 - lse)
            grad_probability = dot(v_ref[0, at, rows, :], grad, NT)
            grad_scores = (probability * (grad_probability - centre)).astype(BF16)
            dv_acc[at, rows, :] += dot(probability.astype(BF16), grad)
            dk_acc[at, rows, :] += dot(grad_scores, query)
            out = dot(kt_ref[0, at, own, rows], grad_scores)
            if first:
                dq_acc[own, cols] = out
            else:
                dq_acc[own, cols] += out

    def setup(start, size):
        rows = pl.ds(start, size)
        for at in range(spans):

            @pl.when(distance == at)
            def _():
                do_s[:size] = do_refs[at][rows, :]
                o_s[:size] = o_refs[at][0, 0, rows, :]

        grad = do_s[:size]
        product = (grad.astype(F32) * o_s[:size].astype(F32)).T
        centres = [
            jnp.sum(product[head * HEAD : (head + 1) * HEAD], axis=0, keepdims=True)
            for head in range(heads)
        ]
        lses = [lse_ref[0, block, head : head + 1, rows] for head in range(heads)]
        return halves(q_ref[0, block, rows, :], heads), halves(grad, heads), lses, centres

    def finish(start, size):
        if heads == 1:
            dq_acc[HEAD:, :size] = jnp.zeros((TILE - HEAD, size), F32)
        dq_ref[0, block, pl.ds(start, size), :] = (dq_acc[:, :size].T * 0.125).astype(BF16)

    @pl.when(step >= spans)
    def _():
        given = setup(0, prompt_rows)
        part(given, block, 0, prompt_rows, own_mask(prompt_rows), True)

        @pl.loop(0, block)
        def _(c):
            part(given, c, 0, prompt_rows, None, False)

        finish(0, prompt_rows)

    @pl.when(step < spans)
    def _():
        before = jnp.maximum(block - 1, 0)
        labels = seg_row_ref[block]
        own = own_mask(cont_rows) & (seg_col_ref[block] == labels)
        near = (seg_col_ref[before] == labels) & (block > 0)
        given = setup(prompt_rows, cont_rows)
        part(given, block, prompt_rows, cont_rows, own, True)
        part(given, before, prompt_rows, cont_rows, near, False)

        @pl.loop(0, count)
        def _(c):
            part(given, c, 0, prompt_rows, None, False)

        finish(prompt_rows, cont_rows)

    @pl.when(step == pl.num_programs(0) - 1)
    def _():
        dk_ref[0] = (dk_acc[...] * 0.125).astype(BF16)
        dv_ref[0] = dv_acc[...].astype(BF16)


def attend_back(
    pair, tile, heads, place, q, k, v, kt, lse, seg_col, seg_row, grads, outs, prompt_rows, after=(), carry=()
):
    _, count, row_count, _ = q.shape
    spans = len(grads)
    cont_rows = row_count - prompt_rows
    pick = lambda i, s: (pair, 0, 0, 0)
    tall = pl.BlockSpec((1, count, row_count, TILE), pick)
    most = max(prompt_rows, cont_rows)
    pairs = spans * (prompt_rows + 2 * cont_rows) * prompt_rows * count // 2
    return launch(
        functools.partial(attend_back_kernel, heads, spans, prompt_rows),
        "attend_back",
        (place,),
        (2 * spans,),
        (q, k, v, kt, lse, seg_col, seg_row, *grads, *[outs] * spans),
        [
            tall,
            tall,
            tall,
            pl.BlockSpec((1, count, TILE, row_count), pick),
            pl.BlockSpec((1, count, 2, row_count), pick),
            blocks(count, cont_rows, 1),
            blocks(count, 1, cont_rows),
        ]
        + [pl.BlockSpec((row_count, TILE), lambda i, s: (0, tile))] * spans
        + [
            pl.BlockSpec((1, 1, row_count, TILE), lambda i, s, away=away: (tile, away, 0, 0))
            for away in range(spans)
        ],
        [whole_out(1, count, row_count, TILE)] * 3,
        scratch=[
            pltpu.VMEM((count, row_count, TILE), F32),
            pltpu.VMEM((count, row_count, TILE), F32),
            pltpu.VMEM((TILE, most), F32),
            pltpu.VMEM((most, TILE), BF16),
            pltpu.VMEM((most, TILE), BF16),
        ],
        limit=56,
        flops=10 * heads * TILE * pairs,
        exps=heads * pairs,
        after=after,
        carry=carry,
    )


def normalize(values):
    average = jnp.mean(values, axis=1, keepdims=True)
    centred = values - average
    variance = jnp.mean(centred * centred, axis=1, keepdims=True)
    rate = lax.rsqrt(variance + 1e-05)
    return centred * rate, rate


def normalize_back(unit, rate, grad):
    shift = jnp.mean(grad, axis=1, keepdims=True)
    along = jnp.mean(grad * unit, axis=1, keepdims=True)
    return rate * (grad - shift - unit * along)


def piece_of(own_ref, pieces_ref, distance):
    tiles = [
        pieces_ref[pair, distance - 1] if distance else own_ref[pair, 0] for pair in range(PAIRS)
    ]
    return jnp.concatenate(tiles, axis=1)


def piece_specs(places, size):
    return [
        pl.BlockSpec((PAIRS, 1, size, TILE), lambda i, *_: (0, 0, i, 0)),
        pl.BlockSpec((PAIRS, places - 1, size, TILE), lambda i, *_: (0, 0, i, 0)),
        pl.BlockSpec((size, TILE), lambda i, *_: (i, 0)),
    ]


def merge_kernel(places, place_ref, x_ref, w_ref, out_bias_ref, gain_ref, bias_ref, *refs):
    own_ref, pieces_ref, last_ref, hidden_ref, low_ref, flip_ref = refs
    own = 2 * PAIRS * HEAD
    width = hidden_ref.shape[1]
    total = x_ref[:, :width].astype(F32) + out_bias_ref[...]
    for distance in range(places):
        start = pl.multiple_of((place_ref[0] ^ distance) * own, own)
        joined = piece_of(own_ref, pieces_ref, distance)
        total = total + dot(joined, w_ref[pl.ds(start, own), :])
    total = total + dot(last_ref[:, :HEAD], w_ref[width - HEAD :, :])
    hidden_ref[...] = total
    unit, _ = normalize(total)
    low = (unit * gain_ref[...] + bias_ref[...]).astype(BF16)
    low_ref[...] = low
    flip_ref[...] = low.T


def merge(place, rows, w_out, out_bias, gain, bias, pieces, after=(), carry=()):
    row_count, width = rows.shape[0], w_out.shape[1]
    size = 128
    by_row = lambda cols: pl.BlockSpec((size, cols), lambda i, p: (i, 0))
    return launch(
        functools.partial(merge_kernel, pieces[0].shape[1]),
        "merge",
        (place,),
        (row_count // size,),
        (rows, w_out, out_bias[None], gain[None], bias[None], *pieces),
        [by_row(rows.shape[1]), blocks(*w_out.shape)]
        + [blocks(1, width)] * 3
        + piece_specs(pieces[0].shape[1], size),
        [
            (by_row(width), shape_of(row_count, width, kind=F32)),
            (by_row(width), shape_of(row_count, width)),
            (
                pl.BlockSpec((width, size), lambda i, p: (0, i)),
                shape_of(width, row_count),
            ),
        ],
        flops=2 * row_count * width * width,
        after=after,
        carry=carry,
    )


def bend_kernel(
    places, mlp_ref, gm_ref, hidden_ref, g_ref, w_ref, gain_ref, proj_bias_ref, own_ref, pieces_ref, last_ref, *refs
):
    out_ref, gh_ref, ga_ref, ga_last_ref, *refs = refs
    come_refs, gw_refs, refs = refs[: places - 1], refs[places - 1 : places + 1], refs[places + 1 :]
    sums_ref, acc, ga_s, send_sem, recv_sem = refs
    step = pl.program_id(0)
    steps = pl.num_programs(0)
    place, fsdp = lax.axis_index("ctx"), lax.axis_index("fsdp")
    own = 2 * PAIRS * HEAD
    size, width = hidden_ref.shape
    mesh_id = pl.DeviceIdType.MESH

    def copies(at):
        rows = pl.ds(pl.multiple_of(at * size, 16), size)
        return [
            pltpu.make_async_remote_copy(
                src_ref=ga_s.at[away - 1, rows],
                dst_ref=come_refs[away - 1].at[rows],
                send_sem=send_sem.at[at, away - 1],
                recv_sem=recv_sem.at[at, away - 1],
                device_id={"ctx": place ^ away},
                device_id_type=mesh_id,
            )
            for away in range(1, places)
        ]

    @pl.when(step == 0)
    def _():
        barrier = pltpu.get_barrier_semaphore()
        for away in range(1, places):
            pl.semaphore_signal(
                barrier, inc=1, device_id={"ctx": place ^ away}, device_id_type=mesh_id
            )

    hidden = hidden_ref[...]
    out_ref[...] = (hidden + mlp_ref[...] + proj_bias_ref[...]).astype(BF16)
    unit, rate = normalize(hidden)
    grad_in = gm_ref[...]
    grad_layer = g_ref[...].astype(F32)
    grad_hidden = grad_layer + normalize_back(unit, rate, grad_in * gain_ref[...])
    gh_ref[...] = grad_hidden
    branch = grad_hidden.astype(BF16)
    rows = pl.ds(pl.multiple_of(step * size, 16), size)
    for distance in range(places - 1, -1, -1):
        heads = pl.ds(pl.multiple_of((place ^ distance) * own, own), own)
        piece = dot(branch, w_ref[heads, :], NT).astype(BF16)
        if distance:
            ga_s[distance - 1, rows, :] = piece
        else:
            ga_ref[...] = piece

    @pl.when(step == 0)
    def _():
        pl.semaphore_wait(pltpu.get_barrier_semaphore(), places - 1)

    for copy in copies(step):
        copy.start()
    last = dot(branch, w_ref[width - HEAD :, :], NT).astype(BF16)
    ga_last_ref[...] = jnp.concatenate([last, jnp.zeros_like(last)], axis=1)
    sums = [grad_hidden, grad_in * unit, grad_in, grad_layer]
    sums = jnp.concatenate([jnp.sum(entry, axis=0, keepdims=True) for entry in sums], axis=0)

    @pl.when(step == 0)
    def _():
        acc[...] = jnp.zeros_like(acc)
        sums_ref[...] = sums

    @pl.when(step > 0)
    def _():
        sums_ref[...] += sums

    for distance in range(places):
        heads = pl.ds(pl.multiple_of((place ^ distance) * own, own), own)
        joined = piece_of(own_ref, pieces_ref, distance)
        acc[heads, :] += dot(joined.T, branch)
    acc[width - HEAD :, :] += dot(last_ref[:, :HEAD].T, branch)

    @pl.when(step == steps - 1)
    def _():
        quarter = width // 4
        for beside, ref in enumerate(gw_refs):
            for away in range(2):
                start = ((fsdp ^ away) * 2 + (place % 2 ^ beside)) * quarter
                ref[away] = acc[pl.ds(pl.multiple_of(start, 16), quarter), :].astype(BF16)

        @pl.loop(0, steps)
        def _(i):
            for copy in copies(i):
                copy.wait_recv()
                copy.wait_send()


def bend(mlp_out, gm, hidden, g, w_out, gain, proj_bias, pieces):
    row_count, width = hidden.shape
    size = row_count // 4
    places = pieces[0].shape[1]
    own = 2 * PAIRS * HEAD
    by_row = lambda cols: pl.BlockSpec((size, cols), lambda i: (i, 0))
    return launch(
        functools.partial(bend_kernel, places),
        "bend",
        (),
        (row_count // size,),
        (mlp_out, gm, hidden, g, w_out, gain[None], proj_bias[None], *pieces),
        [by_row(width)] * 4
        + [blocks(*w_out.shape)]
        + [blocks(1, width)] * 2
        + piece_specs(places, size),
        [
            (by_row(width), shape_of(row_count, width)),
            (by_row(width), shape_of(row_count, width, kind=F32)),
            (by_row(own), shape_of(row_count, own)),
            (by_row(TILE), shape_of(row_count, TILE)),
        ]
        + [(ANYWHERE, shape_of(row_count, own))] * (places - 1)
        + [
            whole_out(2, width // 4, width),
            whole_out(2, width // 4, width),
            whole_out(4, width, kind=F32),
        ],
        scratch=[
            pltpu.VMEM((width, width), F32),
            pltpu.VMEM((places - 1, row_count, own), BF16),
            pltpu.SemaphoreType.DMA((row_count // size, places - 1)),
            pltpu.SemaphoreType.DMA((row_count // size, places - 1)),
        ],
        limit=56,
        flops=4 * row_count * width * width,
        traffic=30,
        meet=6,
    )


GELU_RATE = 0.7978845608028654


def gelu_both(values):
    square = values * values
    bent = jnp.tanh(GELU_RATE * (values + 0.044715 * square * values))
    half = 0.5 * (1.0 + bent)
    slope = half + 0.5 * values * (1.0 - bent * bent) * (GELU_RATE * (1.0 + 0.134145 * square))
    return values * half, slope


def mlp_kernel(
    parts,
    first,
    x_ref,
    g_ref,
    xt_ref,
    gt_ref,
    *refs,
):
    own, far, own_2, far_2 = (refs[i * parts : (i + 1) * parts] for i in range(4))
    before_refs = refs[4 * parts : 4 * parts + 2]
    refs = refs[4 * parts + (0 if first else 2) :]
    out_ref, gm_ref, keep_f, send_f, keep_p, send_p, gb_ref = refs[:7]
    wf_s, wp_s, bias_s, biases, act_s, gp_s, wide, keep_s, send_s, come_s, total = refs[7:18]
    sems, send_sem, recv_sem = refs[18:]
    step = pl.program_id(0)
    place, fsdp = lax.axis_index("ctx"), lax.axis_index("fsdp")
    core, chip = place % 2, place // 2
    beside = {"ctx": place ^ 1}
    mesh_id = pl.DeviceIdType.MESH
    slot = step % 2
    _, width, hidden = wf_s.shape
    quarter = width // 4

    def spot(away, across):
        start = ((fsdp ^ away) * 2 + (core ^ across)) * quarter
        return pl.ds(pl.multiple_of(start, 16), quarter)

    def loads(at, to):
        moves = [(own[at].at[pl.ds(2 * quarter, 16)], bias_s.at[to])]
        for away, sources in enumerate(((own[at], own_2[at]), (far[at], far_2[at]))):
            for across, source in enumerate(sources):
                for weight, target in enumerate((wf_s, wp_s)):
                    moves.append(
                        (
                            source.at[pl.ds(weight * quarter, quarter)],
                            target.at[to, spot(away, across)],
                        )
                    )
        return [
            pltpu.make_async_copy(source, target, sems.at[to, i])
            for i, (source, target) in enumerate(moves)
        ]

    def exchange(at):
        return pltpu.make_async_remote_copy(
            src_ref=send_s,
            dst_ref=come_s.at[at],
            send_sem=send_sem.at[at],
            recv_sem=recv_sem.at[at],
            device_id=beside,
            device_id_type=mesh_id,
        )

    @pl.when(step == 0)
    def _():
        for part in range(parts):
            for copy in loads(part, part):
                copy.start()
        barrier = pltpu.get_barrier_semaphore()
        pl.semaphore_signal(barrier, inc=1, device_id=beside, device_id_type=mesh_id)
        pl.semaphore_wait(barrier, 1)

    for part in range(parts):

        @pl.when(step == part)
        def _():
            for copy in loads(part, part):
                copy.wait()

    bias = jnp.sum(bias_s[slot, :3, :].astype(F32), axis=0, keepdims=True)
    biases[...] = bias

    def over(total, body):
        whole = total // 256

        @pl.loop(0, whole)
        def _(i):
            body(pl.multiple_of(i * 256, 256), 256)

        if total % 256:
            body(whole * 256, total % 256)

    def up(start, size):
        cols = pl.ds(start, size)
        pre_act = dot(x_ref[...], wf_s[slot, :, cols]) + biases[:, cols]
        grad_act = dot(g_ref[...], wp_s[slot, :, cols])
        activated, slope = gelu_both(pre_act)
        grad_pre = (grad_act * slope).astype(BF16)
        act_s[:, cols] = activated.astype(BF16)
        gp_s[:, cols] = grad_pre
        gb_ref[0, :, cols] = jnp.sum(grad_pre.astype(F32), axis=0, keepdims=True)

    def weights(start, size):
        cols = pl.ds(start, size)
        for weight, (left, right) in enumerate(((xt_ref, gp_s), (gt_ref, act_s))):
            wide[:, :size] = dot(left[...], right[:, cols]).astype(BF16)
            for far in range(2):
                for across, to in enumerate((keep_s, send_s)):
                    to[weight, far, :, cols] = wide[spot(far, across), :size]

    over(hidden, up)
    for part in range(1, parts):

        @pl.when(step == part)
        def _():
            exchange(part - 1).wait_send()

    over(hidden, weights)
    for part in range(parts):

        @pl.when(step == part)
        def _():
            exchange(part).start()

    if first:

        @pl.when(step == 0)
        def _():
            out_ref[...] = jnp.zeros_like(out_ref)
            gm_ref[...] = jnp.zeros_like(gm_ref)

    else:

        @pl.when(step == 0)
        def _():
            out_ref[...] = before_refs[0][...]
            gm_ref[...] = before_refs[1][...]

    def down(start, size):
        rows = pl.ds(start, size)
        out_ref[:, rows] += dot(act_s[...], wp_s[slot, rows, :], NT)
        gm_ref[:, rows] += dot(gp_s[...], wf_s[slot, rows, :], NT)

    over(width, down)
    for part in range(parts):

        @pl.when(step == part)
        def _():
            exchange(part).wait_recv()
            for far in range(2):
                total[...] = keep_s[0, far].astype(F32) + come_s[part, 0, far].astype(F32)
                for to, away in ((keep_f, 0), (send_f, 1)):
                    eighth = quarter // 2
                    rows = pl.ds(pl.multiple_of((chip ^ away) * eighth, 8), eighth)
                    to[far, 0] = total[rows, :].astype(BF16)
            for far, to in enumerate((keep_p, send_p)):
                to[0] = (keep_s[1, far].astype(F32) + come_s[part, 1, far].astype(F32)).astype(BF16)
            if part == parts - 1:
                exchange(part).wait_send()


def mlp(meet, x, g, xt, gt, own, far, own_2, far_2, before=(), after=(), carry=()):
    rows, width = x.shape
    hidden = own[0].shape[1]
    parts, quarter = len(own), width // 4
    once = pl.Buffered(buffer_count=1)
    whole = lambda *shape: pl.BlockSpec(shape, lambda k: (0,) * len(shape), pipeline_mode=once)
    by_far = pl.BlockSpec((2, 1, quarter // 2, hidden), lambda k: (0, k, 0, 0))
    by_part = pl.BlockSpec((1, quarter, hidden), lambda k: (k, 0, 0))
    total = (whole(rows, width), shape_of(rows, width, kind=F32))
    by_far = (by_far, shape_of(2, parts, quarter // 2, hidden))
    by_part = (by_part, shape_of(parts, quarter, hidden))
    return launch(
        functools.partial(mlp_kernel, parts, not before),
        "mlp",
        (),
        (parts,),
        (x, g, xt, gt, *own, *far, *own_2, *far_2, *before),
        [
            whole(rows, width),
            whole(rows, width),
            whole(width, rows),
            whole(width, rows),
        ]
        + [ANYWHERE] * (4 * parts)
        + [whole(rows, width)] * len(before),
        [
            total,
            total,
            by_far,
            by_far,
            by_part,
            by_part,
            (
                pl.BlockSpec((1, 1, hidden), lambda k: (k, 0, 0)),
                shape_of(parts, 1, hidden, kind=F32),
            ),
        ],
        scratch=[
            pltpu.VMEM((2, width, hidden), BF16),
            pltpu.VMEM((2, width, hidden), BF16),
            pltpu.VMEM((2, 16, hidden), BF16),
            pltpu.VMEM((1, hidden), F32),
            pltpu.VMEM((rows, hidden), BF16),
            pltpu.VMEM((rows, hidden), BF16),
            pltpu.VMEM((width, 256), BF16),
            pltpu.VMEM((2, 2, quarter, hidden), BF16),
            pltpu.VMEM((2, 2, quarter, hidden), BF16),
            pltpu.VMEM((parts, 2, 2, quarter, hidden), BF16),
            pltpu.VMEM((quarter, hidden), F32),
            pltpu.SemaphoreType.DMA((2, 9)),
            pltpu.SemaphoreType.DMA((parts,)),
            pltpu.SemaphoreType.DMA((parts,)),
        ],
        meet=meet,
        limit=62,
        flops=12 * rows * width * hidden * parts,
        traffic=40,
        exps=rows * hidden * parts,
        after=after,
        carry=carry,
    )


def tail_kernel(prompt_rows, *refs):
    grads, refs = refs[:9], refs[9:]
    w_ref, norm_ref, rows_ref, gh_ref, keep_ref, come_ref, gain_ref, given_ref = refs[:8]
    prompt_ref, cont_ref, qkv_ref, wo_ref, vec_ref = refs[8:13]
    (
        norms,
        rows_s,
        gh_s,
        joined,
        hold,
        core_out,
        core_in,
        chip_out,
        chip_in,
        acc,
        keep,
        far_out,
        far_in,
        sums,
        sums_in,
        ring_in,
        ring_all,
        whole,
        near_in,
        left_out,
        left_in,
        vec_out,
        vec_in,
        wo_sum,
        wo_ring,
        wo_half,
        wo_all,
        wo_core,
        local_sem,
        send_sem,
        recv_sem,
    ) = refs[13:]
    place = lax.axis_index("ctx")
    fsdp = lax.axis_index("fsdp")
    tensor = lax.axis_index("tensor")
    tensors = lax.axis_size("tensor")
    count, row_count = grads[0].shape[1], grads[0].shape[2]
    width = w_ref.shape[0]
    half = width // 2
    own = acc.shape[1]
    shard = ring_in.shape[2]
    chunk = 128
    beside, across, far = {"ctx": place ^ 1}, {"ctx": place ^ 2}, {"fsdp": 1 - fsdp}
    others = [{"tensor": lax.rem(tensor + k, tensors)} for k in range(1, tensors)]

    barrier = pltpu.get_barrier_semaphore()
    for partner in (beside, across, far, *others):
        pl.semaphore_signal(barrier, inc=1, device_id=partner, device_id_type=pl.DeviceIdType.MESH)

    loads = [pltpu.make_async_copy(norm_ref, norms, local_sem.at[0])]
    loads.append(pltpu.make_async_copy(keep_ref, wo_core.at[0], local_sem.at[1]))
    loads.append(pltpu.make_async_copy(come_ref, core_out.at[pl.ds(0, come_ref.shape[0])], local_sem.at[2]))
    for load in loads:
        load.start()
    sent, used = [], []

    def push(source, target, partner):
        at = len(used)
        used.append(at)
        copy = pltpu.make_async_remote_copy(
            src_ref=source,
            dst_ref=target,
            send_sem=send_sem.at[at],
            recv_sem=recv_sem.at[at],
            device_id=partner,
            device_id_type=pl.DeviceIdType.MESH,
        )
        copy.start()
        sent.append(copy)
        return copy

    quarter, part_rows, most_rows = wo_sum.shape[0], wo_ring.shape[1], wo_half.shape[1]
    chip = place // 2

    def part_start(owner):
        return pl.multiple_of(jnp.minimum(owner * part_rows, most_rows - part_rows), 16)

    def chip_start(owner):
        return pl.ds(pl.multiple_of(owner * (quarter - most_rows), 16), most_rows)

    def rows_grad(distance, out):
        block = place ^ distance
        for i, ref in enumerate(grads):
            joined[:, i * TILE : (i + 1) * TILE] = ref[0, block]

        @pl.loop(0, width // 256)
        def _(i):
            cols = pl.ds(pl.multiple_of(i * 256, 256), 256)
            out[:, cols] = dot(joined[...], w_ref[cols, :], NT).astype(out.dtype)

        if width % 256:
            cols = pl.ds(width // 256 * 256, width % 256)
            out[:, cols] = dot(joined[...], w_ref[cols, :], NT).astype(out.dtype)

    to_far = [None] * 4

    def weights(part):
        @pl.loop(0, count)
        def _(block):
            if part < 3:
                pieces = [grads[3 * part + pair][0, block] for pair in range(PAIRS)]
            else:
                pieces = [grads[3 * i + PAIRS][0, block][:, :HEAD] for i in range(3)]
                pieces.append(jnp.zeros((row_count, own - 3 * HEAD), BF16))
            piece = dot(norms[block], jnp.concatenate(pieces, axis=1))

            @pl.when(block == 0)
            def _():
                acc[...] = piece

            @pl.when(block > 0)
            def _():
                acc[...] += piece

        sums[part] = acc[width : width + 8, :]
        keep[part] = acc[pl.ds(pl.multiple_of(fsdp * half, 16), half), :]
        far_out[part] = acc[pl.ds(pl.multiple_of((1 - fsdp) * half, 16), half), :].astype(BF16)
        to_far[part] = push(far_out.at[part], far_in.at[part], far)

    def joined_far(part):
        to_far[part].wait_recv()
        return keep[part] + far_in[part].astype(F32)

    def start_of(owner):
        return pl.multiple_of(jnp.minimum(owner * shard, half - shard), 16)

    to_ring, to_all, to_near = [None] * 4, [None] * 4, [None] * 4

    def ring(part, total):
        sums_in[part] = total.astype(BF16)
        to_ring[part] = [
            push(
                sums_in.at[part, pl.ds(start_of(other["tensor"]), shard)],
                ring_in.at[part, k],
                other,
            )
            for k, other in enumerate(others)
        ]

    def spread(part):
        total = sums_in[part, pl.ds(start_of(tensor), shard), :].astype(F32)
        for k, copy in enumerate(to_ring[part]):
            copy.wait_recv()
            total = total + ring_in[part, k].astype(F32)
        ring_all[part, tensor] = total.astype(BF16)
        to_all[part] = [
            push(ring_all.at[part, tensor], ring_all.at[part, tensor], other) for other in others
        ]

    def gather(part):
        for copy in to_all[part]:
            copy.wait_recv()
        for owner in range(tensors - 1):
            whole[part, owner * shard : (owner + 1) * shard] = ring_all[part, owner]
        rest = (tensors - 1) * shard
        whole[part, rest:] = ring_all[part, tensors - 1, tensors * shard - half :]
        if part < 3:
            to_near[part] = [
                push(whole.at[part], near_in.at[part, 0], beside),
                push(whole.at[part], near_in.at[part, 1], across),
            ]

    loads[1].wait()
    loads[2].wait()
    wo_sum[...] = (wo_core[0].astype(F32) + core_out[:quarter].astype(F32)).astype(BF16)
    pl.semaphore_wait(barrier, 3 + len(others))
    wo_to_chip = push(wo_sum.at[chip_start(1 - chip)], wo_half.at[1], across)
    loads[0].wait()
    weights(3)
    weights(0)

    rows_grad(3, core_out)
    to_core = push(core_out, core_in.at[0], beside)
    left_out[0] = joined_far(3).astype(BF16)
    to_left = push(left_out.at[0], left_in.at[0], beside)
    wo_to_chip.wait_recv()
    wo_half[0] = (wo_sum[chip_start(chip), :].astype(F32) + wo_half[1].astype(F32)).astype(BF16)
    wo_to_ring = [
        push(wo_half.at[0, pl.ds(part_start(other["tensor"]), part_rows)], wo_ring.at[k], other)
        for k, other in enumerate(others)
    ]
    ring(0, joined_far(0))
    rows_grad(2, hold)
    to_core.wait_recv()

    @pl.loop(0, row_count // chunk)
    def _(i):
        rows = pl.ds(pl.multiple_of(i * chunk, chunk), chunk)
        chip_out[rows, :] = (hold[rows, :] + core_in[0, rows, :].astype(F32)).astype(BF16)

    to_left.wait_recv()
    left_out[1] = (left_out[0].astype(F32) + left_in[0].astype(F32)).astype(BF16)
    to_left = push(left_out.at[1], left_in.at[1], across)
    to_chip = push(chip_out, chip_in, across)
    weights(1)
    wo_total = wo_half[0, pl.ds(part_start(tensor), part_rows), :].astype(F32)
    for k, copy in enumerate(wo_to_ring):
        copy.wait_recv()
        wo_total = wo_total + wo_ring[k].astype(F32)
    wo_all[tensor] = wo_total.astype(BF16)
    wo_to_all = [push(wo_all.at[tensor], wo_all.at[tensor], other) for other in others]
    to_left.wait_recv()
    ring(3, left_out[1].astype(F32) + left_in[1].astype(F32))
    ring(1, joined_far(1))
    weights(2)
    spread(0)
    to_core.wait_send()
    sent[:] = [copy for copy in sent if copy is not to_core]
    rows_grad(1, core_out)
    to_core_2 = push(core_out, core_in.at[1], beside)
    ring(2, joined_far(2))
    spread(3)
    rows_grad(0, hold)
    spread(1)
    for copy in wo_to_all:
        copy.wait_recv()
    for owner in range(tensors):
        start = min(owner * part_rows, most_rows - part_rows)
        wo_half[2, start : start + part_rows] = wo_all[owner]
    wo_to_other = push(wo_half.at[2], wo_half.at[3], across)
    gather(0)
    to_core_2.wait_recv()
    to_chip.wait_recv()

    vec_out[0, :8] = jnp.zeros((8, vec_out.shape[2]), F32)
    vec_out[0, 8:] = given_ref[...]
    chunks = row_count // chunk

    def chunk_rows(i):
        return pl.ds(pl.multiple_of(i * chunk, chunk), chunk)

    def row_loads(i):
        slot = i % 2
        return [
            pltpu.make_async_copy(gh_ref.at[chunk_rows(i)], gh_s.at[slot], local_sem.at[3 + slot]),
            pltpu.make_async_copy(rows_ref.at[chunk_rows(i)], rows_s.at[slot], local_sem.at[5 + slot]),
        ]

    for load in row_loads(0):
        load.start()

    @pl.loop(0, chunks)
    def _(i):
        @pl.when(i + 1 < chunks)
        def _():
            for load in row_loads(i + 1):
                load.start()

        for load in row_loads(i):
            load.wait()

        rows = chunk_rows(i)
        unit, rate = normalize(rows_s[i % 2, :, :width].astype(F32))
        grad = hold[rows, :] + core_in[1, rows, :].astype(F32) + chip_in[rows, :].astype(F32)
        back = normalize_back(unit, rate, grad * gain_ref[...])
        out = (gh_s[i % 2] + back).astype(BF16)

        @pl.when(i < prompt_rows // chunk)
        def _():
            prompt_ref[0, rows, :] = out

        @pl.when(i >= prompt_rows // chunk)
        def _():
            cont_ref[0, chunk_rows(i - prompt_rows // chunk), :] = out

        vec_out[0, 0:1, :width] += jnp.sum(grad * unit, axis=0, keepdims=True)
        vec_out[0, 1:2, :width] += jnp.sum(grad, axis=0, keepdims=True)

    spread(2)
    for row, part in ((2, 0), (3, 2)):
        cols = pl.ds(pl.multiple_of(place * own, own), own)
        vec_out[0, row : row + 1, cols] = sums[part, 0:1, :]
        left = slice(part * HEAD, (part + 1) * HEAD)
        vec_out[0, row : row + 1, width - HEAD : width] = sums[3, 0:1, left]
    gather(1)

    def forward(part):
        to_near[part][1].wait_recv()
        return push(near_in.at[part, 1], near_in.at[part, 2], beside)

    def store(part, passed):
        to_near[part][0].wait_recv()
        passed.wait_recv()
        sources = [whole.at[part]] + [near_in.at[part, i] for i in range(3)]
        for distance, source in enumerate(sources):
            for block in range(count):

                @pl.when(place ^ distance == block)
                def _():
                    start = part * width + block * own
                    qkv_ref[:, start : start + own] = source[...]

    partners = (beside, across, far, {"tensor": tensor ^ 1}, {"tensor": tensor ^ 2})

    def exchange(level):
        return push(vec_out.at[level], vec_in.at[level], partners[level])

    def add(level, copy):
        copy.wait_recv()
        vec_out[level + 1] = vec_out[level] + vec_in[level]

    add(0, exchange(0))
    passed_0 = forward(0)
    step = exchange(1)
    gather(2)
    add(1, step)
    step = exchange(2)
    gather(3)
    store(0, passed_0)
    add(2, step)
    wo_to_other.wait_recv()
    for at in range(2):

        @pl.when(chip == at)
        def _():
            wo_core[0, :most_rows] = wo_half[2 + at]
            wo_core[0, most_rows:] = wo_half[3 - at, 2 * most_rows - quarter :]

    wo_to_core = push(wo_core.at[0], wo_core.at[1], beside)
    step = exchange(3)
    passed_1 = forward(1)
    for part in range(3):
        cols = slice((part + 1) * width - HEAD, (part + 1) * width)
        qkv_ref[:, cols] = whole[3, :, part * HEAD : (part + 1) * HEAD]
    add(3, step)
    step = exchange(4)
    store(1, passed_1)
    passed_2 = forward(2)
    add(4, step)
    vec_ref[...] = vec_out[5]
    wo_to_core.wait_recv()
    core = place % 2
    for away in range(2):
        wo_ref[pl.ds(pl.multiple_of((core ^ away) * quarter, 16), quarter), :] = wo_core[away]
    store(2, passed_2)
    for copy in sent:
        copy.wait_send()


def tail(
    grads, w_own, normed, rows, grad_hidden, gain, vectors, out_keep, out_come, prompt_rows, after=()
):
    count, depth, row_count = normed.shape
    width, cols = w_own.shape
    half, own = width // 2, 2 * PAIRS * HEAD
    tensors = lax.axis_size("tensor")
    shard = -(-half // tensors // 16) * 16
    padded = vectors.shape[1]
    in_vmem = pl.BlockSpec(memory_space=pltpu.VMEM)
    vmem = lambda *shape, kind=BF16: pltpu.VMEM(shape, kind)
    copies = 4 + 4 * 2 * (tensors - 1) + 3 + 3 * 3 + 2 + 5 + 2 * (tensors - 1) + 3
    given = len(grads) + 8
    quarter = width // 4
    most_rows = -(-quarter // 2 // 16) * 16
    part_rows = -(-most_rows // tensors // 16) * 16

    def body(*refs):
        tail_kernel(prompt_rows, *refs[:given], *refs[given + len(after) :])

    return pl.pallas_call(
        body,
        in_specs=[in_vmem] * (len(grads) + 1) + [ANYWHERE] * 5 + [in_vmem] * 2 + [ANYWHERE] * len(after),
        out_specs=[in_vmem] * 5,
        out_shape=[
            shape_of(1, prompt_rows, width),
            shape_of(1, row_count - prompt_rows, width),
            shape_of(half, 3 * width),
            shape_of(half, width),
            shape_of(16, padded, kind=F32),
        ],
        scratch_shapes=[
            vmem(*normed.shape),
            vmem(2, TILE, width),
            vmem(2, TILE, width, kind=F32),
            vmem(row_count, cols),
            vmem(row_count, width, kind=F32),
            vmem(row_count, width),
            vmem(2, row_count, width),
            vmem(row_count, width),
            vmem(row_count, width),
            vmem(depth, own, kind=F32),
            vmem(4, half, own, kind=F32),
            vmem(4, half, own),
            vmem(4, half, own),
            vmem(4, 8, own, kind=F32),
            vmem(4, half, own),
            vmem(4, tensors - 1, shard, own),
            vmem(4, tensors, shard, own),
            vmem(4, half, own),
            vmem(3, 3, half, own),
            vmem(2, half, own),
            vmem(2, half, own),
            vmem(6, 16, padded, kind=F32),
            vmem(5, 16, padded, kind=F32),
            vmem(quarter, width),
            vmem(tensors - 1, part_rows, width),
            vmem(4, most_rows, width),
            vmem(tensors, part_rows, width),
            vmem(2, quarter, width),
            pltpu.SemaphoreType.DMA((7,)),
            pltpu.SemaphoreType.DMA((copies,)),
            pltpu.SemaphoreType.DMA((copies,)),
        ],
        compiler_params=pltpu.CompilerParams(
            vmem_limit_bytes=62 << 20, collective_id=1, has_side_effects=True
        ),
        cost_estimate=pl.CostEstimate(
            flops=4 * count * row_count * width * cols, bytes_accessed=30 << 20, transcendentals=0
        ),
        name="tail",
    )(*grads, w_own, normed, rows, grad_hidden, out_keep, out_come, gain[None], vectors, *after)


def own_columns(matrix, place):
    width = matrix.shape[1] // 3
    own = 2 * PAIRS * HEAD
    blank = jnp.zeros((matrix.shape[0], TILE - HEAD), matrix.dtype)
    pieces = []
    for part in range(3):
        whole = matrix[:, part * width : (part + 1) * width]
        pieces += [
            lax.dynamic_slice_in_dim(whole, place * own, own, 1),
            whole[:, width - HEAD :],
            blank,
        ]
    return jnp.concatenate(pieces, axis=1)


def local_heads(
    prompt_in,
    cont_in,
    cont_seg,
    ln1_gain,
    ln1_bias,
    w_qkv,
    qv_bias,
    w_out,
    out_bias,
    ln2_gain,
    ln2_bias,
    w_fc,
    fc_bias,
    w_proj,
    proj_bias,
    prompt_cot,
    cont_cot,
):
    width = prompt_in.shape[2]
    prompt_rows, cont_rows = prompt_in.shape[1], cont_in.shape[1]
    row_count = prompt_rows + cont_rows
    count = lax.axis_size("ctx")
    place = lax.axis_index("ctx")
    core, chip = place % 2, place // 2
    fsdp = lax.axis_index("fsdp")
    tensor = lax.axis_index("tensor")
    tensors = lax.axis_size("tensor")
    own_width = 2 * PAIRS * HEAD
    half, hidden_units = w_fc.shape
    quarter = half // 2
    eighth = quarter // 2
    padded = (width + TILE - 1) // TILE * TILE
    at = place.reshape(1)
    spot = jnp.stack([core, fsdp, tensor, jnp.int32(tensors), place])

    zero_bias = jnp.zeros_like(qv_bias[0])
    col_bias = own_columns(jnp.concatenate([qv_bias[0], zero_bias, qv_bias[1]])[None], place)[0]
    normed, q, k, v, kt, vt, w_own, rows_own, grad_layer, grad_flip, *mines, out_own = open_up(
        prompt_in,
        cont_in,
        w_qkv,
        w_fc,
        w_proj,
        w_out,
        fc_bias,
        prompt_cot,
        cont_cot,
        ln1_gain,
        ln1_bias,
        col_bias,
        count,
    )

    mine, one_away, three_away, near_far = mines

    labels = cont_seg[0].reshape(count, cont_rows)
    seg_col, seg_row = labels[:, :, None], labels[:, None, :]
    lse, outs, came, last_out, two_away, one_far, three_far, *others, out_full = attend(
        q, k, vt, seg_col, seg_row, prompt_rows, (mine, near_far, one_away, three_away), out_own
    )
    mine_2, near_2, one_2, one_far_2, three_2, three_far_2 = others
    two_far = swap(two_away, "fsdp", 1)
    pieces = (outs, came, last_out)
    hidden, mlp_low, mlp_flip = merge(
        at, rows_own, out_full, out_bias, ln2_gain, ln2_bias, pieces
    )

    given = (mlp_low, grad_layer, mlp_flip, grad_flip)
    mlp_out, grad_mlp_in, *grads_first, bias_first = mlp(
        4,
        *given, (mine, one_away), (near_far, one_far), (mine_2, one_2), (near_2, one_far_2)
    )
    (two_far,) = behind((two_far,), bias_first)
    two_2, two_far_2 = swap(two_away, "ctx", 1), swap(two_far, "ctx", 1)
    mlp_out, grad_mlp_in, *grads_last, bias_last = mlp(
        5,
        *given,
        (three_away, two_away),
        (three_far, two_far),
        (three_2, two_2),
        (three_far_2, two_far_2),
        before=(mlp_out, grad_mlp_in),
    )
    grad_fc_bias = jnp.concatenate([bias_first, bias_last], axis=0)
    layer_out, grad_hidden, grads_own, grad_last, *rest = bend(
        mlp_out, grad_mlp_in, hidden, grad_layer, out_full, ln2_gain, proj_bias, pieces
    )
    grads_all, (out_keep, out_send, sums2) = [grads_own, *rest[:-3]], rest[-3:]

    def added(left, right):
        return left.astype(F32) + right.astype(F32)

    steps_away = (0, 1, 3, 2)

    def over_tensor(parts, token):
        come = [turn(parts[k], "tensor", -steps_away[k]) for k in range(1, tensors)]
        total = parts[0].astype(F32)
        for part in behind(come, token):
            total = total + part.astype(F32)
        return total

    def back(pair, tile, heads, grads, outs, after=()):
        return attend_back(
            pair, tile, heads, at, q, k, v, kt, lse, seg_col, seg_row, grads, outs, prompt_rows, after
        )

    come_o = swap(out_send, "ctx", 1)
    fc_parts, pj_parts = (grads_first[:2], grads_last[:2]), (grads_first[2:], grads_last[2:])
    fc_come = [swap(send, "ctx", 2) for _, send in fc_parts]
    pj_come = [swap(send, "fsdp", 1) for _, send in pj_parts]
    grads_pair = [back(0, 0, 2, grads_all, outs)]
    grads_left = back(PAIRS, 0, 1, [grad_last], last_out[None, None], (grads_pair[0][0],))
    come_o, *come = behind((come_o, *fc_come, *pj_come), grads_left[0])
    near_f = [added(keep[0], part[0]).astype(BF16) for (keep, _), part in zip(fc_parts, come[:2])]
    far_f = [added(keep[1], part[1]).astype(BF16) for (keep, _), part in zip(fc_parts, come[:2])]
    sum_p = [added(keep, part) for (keep, _), part in zip(pj_parts, come[2:])]
    near_f, far_f = jnp.concatenate(near_f), jnp.concatenate(far_f)
    sum_p = jnp.concatenate(sum_p).astype(BF16)
    sum_o = added(out_keep, come_o).astype(BF16)
    sum_o, out_o = sum_o[0], sum_o[1]
    come_f, come_o = swap(far_f, "fsdp", 1), swap(out_o, "fsdp", 1)
    grads_pair.append(back(1, 1, 2, grads_all, outs, (far_f, sum_p, out_o, grads_left[0])))
    (come_f,) = behind((come_f,), grads_pair[1][0])
    sum_f = added(near_f, come_f).astype(BF16)
    sum_p = over_tensor(sum_p, grads_pair[1][0]).astype(BF16)
    ordered = [entry[part] for part in range(3) for entry in (*grads_pair, grads_left)]
    vectors = jnp.concatenate([sums2, jnp.zeros((tensors, hidden_units), F32)], axis=0)
    for k, distance in enumerate(steps_away):
        vectors = lax.dynamic_update_slice(
            vectors, grad_fc_bias[k], (4 + (tensor - distance) % tensors, 0)
        )
    vectors = jnp.pad(vectors, ((0, 0), (0, padded - width)))
    prompt_grad, cont_grad, sum_qkv, sum_out, late = tail(
        ordered,
        w_own,
        normed,
        rows_own,
        grad_hidden,
        ln1_gain,
        vectors,
        sum_o,
        come_o,
        prompt_rows,
        (sum_f, sum_p),
    )
    sum_f = over_tensor(sum_f, late).astype(BF16)
    (come_p,) = behind((swap(sum_p, "ctx", 2),), late)
    sum_p = added(sum_p, come_p).astype(BF16)
    far_f = swap(sum_f, "ctx", 2)
    sum_f = jnp.concatenate(in_order(sum_f, far_f, chip), axis=0)
    both = jnp.stack([sum_f, sum_p])
    both = jnp.concatenate(in_order(both, swap(both, "ctx", 1), core), axis=1).astype(F32)
    own_fc, own_proj = both[0], both[1].T


    fc_bias_sum = lax.dynamic_index_in_dim(late, 12 + tensor, 0, False)[:hidden_units]
    return (
        layer_out[:prompt_rows][None],
        layer_out[prompt_rows:][None],
        prompt_grad,
        cont_grad,
        late[0, :width],
        late[1, :width],
        sum_qkv.astype(F32),
        late[2:4, :width],
        sum_out.astype(F32),
        late[8, :width],
        late[9, :width],
        late[10, :width],
        own_fc,
        fc_bias_sum,
        own_proj,
        late[11, :width],
    )


def solution(mesh):
    placed = (
        P(("fsdp", "tensor"), "ctx", None),
        P(("fsdp", "tensor"), "ctx", None),
        P(("fsdp", "tensor"), None),
        P(),
        P(),
        P("fsdp", None),
        P(),
        P("fsdp", None),
        P(),
        P(),
        P(),
        P("fsdp", "tensor"),
        P("tensor"),
        P("tensor", "fsdp"),
        P(),
        P(("fsdp", "tensor"), "ctx", None),
        P(("fsdp", "tensor"), "ctx", None),
    )
    by_heads = HEADS // mesh.shape["ctx"] == PAIRS * 2 and HEADS % mesh.shape["ctx"] == 1
    return jax.shard_map(
        local_heads if by_heads else local_rows,
        mesh=mesh,
        in_specs=placed,
        out_specs=(
            P(("fsdp", "tensor"), "ctx", None),
            P(("fsdp", "tensor"), "ctx", None),
            P(("fsdp", "tensor"), "ctx", None),
            P(("fsdp", "tensor"), "ctx", None),
            P(),
            P(),
            P("fsdp", None),
            P(),
            P("fsdp", None),
            P(),
            P(),
            P(),
            P("fsdp", "tensor"),
            P("tensor"),
            P("tensor", "fsdp"),
            P(),
        ),
        check_vma=False,
    )
```

```python
import functools

import jax
import jax.numpy as jnp
from jax import lax
from jax.experimental import pallas as pl
from jax.experimental.pallas import tpu as pltpu
from jax.sharding import PartitionSpec as P

HEADS = 17
HEAD = 64


def passed_along(value, axis, steps):
    count = lax.axis_size(axis)
    leading, last = (max(0, -steps), min(count, count - steps))
    return lax.ppermute(value, axis, [(source, source + steps) for source in range(leading, last)])


def layer_norm(values, norm_gain, norm_bias):
    average = jnp.mean(values, axis=-1, keepdims=True)
    centred = values - average
    variance = jnp.mean(centred * centred, axis=-1, keepdims=True)
    return centred * lax.rsqrt(variance + 1e-05) * norm_gain + norm_bias


def gelu_tanh(values):
    return jax.nn.gelu(values, approximate=True)


def inner_first(left_op, right_op):
    return lax.dot_general(
        left_op, right_op, (((0,), (0,)), ((), ())), preferred_element_type=jnp.float32
    )


def inner_last(left_op, right_op):
    return lax.dot_general(
        left_op, right_op, (((1,), (1,)), ((), ())), preferred_element_type=jnp.float32
    )


def to_heads(values):
    return jnp.swapaxes(values.reshape(values.shape[0], HEADS, HEAD), 0, 1)


def from_heads(values):
    return jnp.swapaxes(values, 0, 1).reshape(values.shape[1], values.shape[0] * values.shape[2])


def fetch_prompt(rows_kv):
    return lax.all_gather(rows_kv, "ctx", axis=0, tiled=True)


def local_rows(
    prompt_in,
    cont_in,
    cont_seg,
    ln1_gain,
    ln1_bias,
    w_qkv,
    qv_bias,
    w_out,
    out_bias,
    ln2_gain,
    ln2_bias,
    w_fc,
    fc_bias,
    w_proj,
    proj_bias,
    prompt_cot,
    cont_cot,
):
    model_width = prompt_in.shape[2]
    prompt_rows = prompt_in.shape[1]
    cont_rows = cont_in.shape[1]
    row_count = prompt_rows + cont_rows
    ctx_count = lax.axis_size("ctx")
    ctx_place = lax.axis_index("ctx")
    prompt_total = prompt_rows * ctx_count
    qkv_full, out_full = (
        lax.all_gather(w_qkv.astype(jnp.bfloat16), "fsdp", axis=0, tiled=True),
        lax.all_gather(w_out.astype(jnp.bfloat16), "fsdp", axis=0, tiled=True),
    )
    fc_full, proj_full = (
        lax.all_gather(w_fc.astype(jnp.bfloat16), "fsdp", axis=0, tiled=True),
        lax.all_gather(w_proj.astype(jnp.bfloat16), "fsdp", axis=1, tiled=True),
    )
    row_ids = jnp.arange(row_count, dtype=jnp.int32)
    labels_all = cont_seg[0]
    own_labels = lax.dynamic_slice_in_dim(labels_all, ctx_place * cont_rows, cont_rows)
    earlier_labels = lax.dynamic_slice_in_dim(
        labels_all, jnp.maximum(ctx_place - 1, 0) * cont_rows, cont_rows
    )
    query_labels = jnp.concatenate([jnp.full((prompt_rows,), -1, jnp.int32), own_labels])
    query_prompt = ctx_place * prompt_rows + row_ids
    query_cont = ctx_place * cont_rows + row_ids - prompt_rows
    is_cont = row_ids >= prompt_rows
    prompt_ids = jnp.arange(prompt_total, dtype=jnp.int32)
    near_ids = (ctx_place - 1) * cont_rows + jnp.arange(2 * cont_rows, dtype=jnp.int32)
    near_labels = jnp.concatenate([earlier_labels, own_labels])
    allowed_far = is_cont[:, None] | (prompt_ids[None, :] <= query_prompt[:, None])
    allowed_near = (
        (query_labels[:, None] == near_labels[None, :])
        & (near_ids[None, :] <= query_cont[:, None])
        & (near_ids[None, :] >= 0)
    )
    allowed = jnp.concatenate([allowed_far, allowed_near], 1)
    inputs = jnp.concatenate([prompt_in[0], cont_in[0]], 0).astype(jnp.float32)
    normed, norm1_back = jax.vjp(layer_norm, inputs, ln1_gain, ln1_bias)
    normed_low = normed.astype(jnp.bfloat16)
    projected = jnp.dot(normed_low, qkv_full, preferred_element_type=jnp.float32)
    queries = (projected[:, :model_width] + qv_bias[0]).astype(jnp.bfloat16)
    key_value = jnp.concatenate(
        [projected[:, model_width : 2 * model_width], projected[:, 2 * model_width :] + qv_bias[1]],
        1,
    ).astype(jnp.bfloat16)
    own_cont_kv = key_value[prompt_rows:]
    earlier_kv = passed_along(own_cont_kv, "ctx", 1)
    prompt_kv = fetch_prompt(key_value[:prompt_rows])
    keys_all = jnp.concatenate([prompt_kv, earlier_kv, own_cont_kv], 0)
    query_heads = to_heads(queries)
    key_heads = to_heads(keys_all[:, :model_width])
    value_heads = to_heads(keys_all[:, model_width:])

    def head_forward(operands):
        query_head, key_head, value_head = operands
        scores = inner_last(query_head, key_head) * 0.125
        scores = jnp.where(allowed, scores, -1e30)
        row_max = jnp.max(scores, axis=1, keepdims=True)
        exponent = jnp.exp(scores - row_max)
        row_total = jnp.sum(exponent, axis=1, keepdims=True)
        probability = (exponent / row_total).astype(jnp.bfloat16)
        head_out = jnp.dot(probability, value_head, preferred_element_type=jnp.float32)
        return (head_out.astype(jnp.bfloat16), (row_max + jnp.log(row_total))[:, 0])

    heads_out, logsum = lax.map(head_forward, (query_heads, key_heads, value_heads))
    attended = from_heads(heads_out)
    hidden = inputs + jnp.dot(attended, out_full, preferred_element_type=jnp.float32) + out_bias
    mlp_in, norm2_back = jax.vjp(layer_norm, hidden, ln2_gain, ln2_bias)
    mlp_low = mlp_in.astype(jnp.bfloat16)
    mlp_rows = lax.all_gather(mlp_low, "tensor", axis=0, tiled=True)
    pre_act = jnp.dot(mlp_rows, fc_full, preferred_element_type=jnp.float32) + fc_bias
    activated, gelu_back = jax.vjp(gelu_tanh, pre_act)
    act_low = activated.astype(jnp.bfloat16)
    partial_out = jnp.dot(act_low, proj_full, preferred_element_type=jnp.float32)
    mlp_out = lax.psum_scatter(
        partial_out.astype(jnp.bfloat16), "tensor", scatter_dimension=0, tiled=True
    ).astype(jnp.float32)
    layer_out = (hidden + mlp_out + proj_bias).astype(jnp.bfloat16)
    grad_layer = jnp.concatenate([prompt_cot[0], cont_cot[0]], 0)
    grad_float = grad_layer.astype(jnp.float32)
    grad_proj_bias = jnp.sum(grad_float, axis=0)
    grad_rows = lax.all_gather(grad_layer, "tensor", axis=0, tiled=True)
    grad_w_proj = inner_first(act_low, grad_rows)
    grad_act = inner_last(grad_rows, proj_full)
    grad_pre = gelu_back(grad_act)[0].astype(jnp.bfloat16)
    grad_fc_bias = jnp.sum(grad_pre.astype(jnp.float32), axis=0)
    grad_w_fc = inner_first(mlp_rows, grad_pre)
    grad_mlp_part = inner_last(grad_pre, fc_full)
    grad_mlp_in = lax.psum_scatter(grad_mlp_part, "tensor", scatter_dimension=0, tiled=True)
    grad_hidden_norm, grad_ln2_gain, grad_ln2_bias = norm2_back(grad_mlp_in)
    grad_hidden = grad_float + grad_hidden_norm
    grad_out_bias = jnp.sum(grad_hidden, axis=0)
    grad_branch = grad_hidden.astype(jnp.bfloat16)
    grad_w_out = inner_first(attended, grad_branch)
    grad_attended = inner_last(grad_branch, out_full).astype(jnp.bfloat16)
    prompt_again = fetch_prompt(key_value[:prompt_rows])
    keys_back = jnp.concatenate([prompt_again, earlier_kv, own_cont_kv], 0)
    key_back_heads = to_heads(keys_back[:, :model_width])
    value_back_heads = to_heads(keys_back[:, model_width:])

    def head_backward(operands):
        query_head, key_head, value_head, grad_head, logsum_head = operands
        scores = inner_last(query_head, key_head) * 0.125
        scores = jnp.where(allowed, scores, -1e30)
        probability = jnp.exp(scores - logsum_head[:, None])
        prob_low = probability.astype(jnp.bfloat16)
        grad_prob = inner_last(grad_head, value_head)
        centre = jnp.sum(probability * grad_prob, axis=1, keepdims=True)
        grad_scores = (probability * (grad_prob - centre)).astype(jnp.bfloat16)
        grad_query = jnp.dot(grad_scores, key_head, preferred_element_type=jnp.float32) * 0.125
        grad_key = inner_first(grad_scores, query_head) * 0.125
        grad_value = inner_first(prob_low, grad_head)
        return (grad_query, grad_key, grad_value)

    head_operands = (query_heads, key_back_heads, value_back_heads, to_heads(grad_attended), logsum)
    grad_q_heads, grad_k_heads, grad_v_heads = lax.map(head_backward, head_operands)
    grad_queries = from_heads(grad_q_heads).astype(jnp.bfloat16)
    grad_kv = jnp.concatenate([from_heads(grad_k_heads), from_heads(grad_v_heads)], 1)
    prompt_grad_kv = lax.psum_scatter(
        grad_kv[:prompt_total], "ctx", scatter_dimension=0, tiled=True
    )
    from_later = passed_along(
        grad_kv[prompt_total : prompt_total + cont_rows].astype(jnp.bfloat16), "ctx", -1
    ).astype(jnp.float32)
    cont_grad_kv = grad_kv[prompt_total + cont_rows :] + from_later
    grad_kv_rows = jnp.concatenate([prompt_grad_kv, cont_grad_kv], 0).astype(jnp.bfloat16)
    grad_projected = jnp.concatenate([grad_queries, grad_kv_rows], 1)
    grad_qv_bias = jnp.stack(
        [
            jnp.sum(grad_queries.astype(jnp.float32), axis=0),
            jnp.sum(grad_kv_rows[:, model_width:].astype(jnp.float32), axis=0),
        ]
    )
    grad_w_qkv = inner_first(normed_low, grad_projected)
    grad_normed = inner_last(grad_projected, qkv_full)
    grad_inputs_norm, grad_ln1_gain, grad_ln1_bias = norm1_back(grad_normed)
    grad_inputs = (grad_hidden + grad_inputs_norm).astype(jnp.bfloat16)
    shard_qkv, shard_out = (
        lax.psum_scatter(
            grad_w_qkv.astype(jnp.bfloat16), "fsdp", scatter_dimension=0, tiled=True
        ).astype(jnp.float32),
        lax.psum_scatter(
            grad_w_out.astype(jnp.bfloat16), "fsdp", scatter_dimension=0, tiled=True
        ).astype(jnp.float32),
    )
    sum_qkv, sum_out = lax.psum((shard_qkv, shard_out), ("ctx", "tensor"))
    sum_fc, sum_proj, sum_fc_bias = lax.psum(
        (grad_w_fc, grad_w_proj, grad_fc_bias), ("fsdp", "ctx")
    )
    fsdp_place = lax.axis_index("fsdp")
    fsdp_rows = w_fc.shape[0]
    own_fc = lax.dynamic_slice_in_dim(sum_fc, fsdp_place * fsdp_rows, fsdp_rows, 0)
    own_proj = lax.dynamic_slice_in_dim(sum_proj, fsdp_place * fsdp_rows, fsdp_rows, 1)
    small_sums = lax.psum(
        (
            grad_ln1_gain,
            grad_ln1_bias,
            grad_qv_bias,
            grad_out_bias,
            grad_ln2_gain,
            grad_ln2_bias,
            grad_proj_bias,
        ),
        ("fsdp", "ctx", "tensor"),
    )
    return (
        layer_out[:prompt_rows][None],
        layer_out[prompt_rows:][None],
        grad_inputs[:prompt_rows][None],
        grad_inputs[prompt_rows:][None],
        small_sums[0],
        small_sums[1],
        sum_qkv,
        small_sums[2],
        sum_out,
        small_sums[3],
        small_sums[4],
        small_sums[5],
        own_fc,
        sum_fc_bias,
        own_proj,
        small_sums[6],
    )


PAIRS = 2
TILE = 2 * HEAD
BF16 = jnp.bfloat16
F32 = jnp.float32
LOG2E = 1.4426950408889634
SCALE2 = 0.125 * LOG2E
HINT = 0.2
NN = (((1,), (0,)), ((), ()))
NT = (((1,), (1,)), ((), ()))
TN = (((0,), (0,)), ((), ()))


def dot(left_op, right_op, dims=NN):
    return lax.dot_general(left_op, right_op, dims, preferred_element_type=F32)


def swap(value, axis, bit):
    count = lax.axis_size(axis)
    return lax.ppermute(value, axis, [(place, place ^ bit) for place in range(count)])


def turn(value, axis, steps):
    count = lax.axis_size(axis)
    return lax.ppermute(value, axis, [(place, (place + steps) % count) for place in range(count)])


def halves(values, heads=2):
    lane = lax.broadcasted_iota(jnp.int32, values.shape, 1)
    zero = jnp.zeros_like(values)
    return [jnp.where((lane < HEAD) == (head == 0), values, zero) for head in range(heads)]


ANYWHERE = pl.BlockSpec(memory_space=pl.ANY)


def blocks(*shape):
    return pl.BlockSpec(shape, lambda i, *_: (0,) * len(shape))


def shape_of(*shape, kind=BF16):
    return jax.ShapeDtypeStruct(shape, kind)


def launch(
    kernel, name, scalars, grid, operands, in_specs, outs, scratch=(), limit=48, flops=0, traffic=16, exps=0, after=(), carry=(), aliases=None, meet=None
):
    out_specs, out_shapes = [out[0] for out in outs], [out[1] for out in outs]
    given = len(scalars) + len(operands)
    tied = given + len(after) + len(carry)

    def body(*refs):
        made = refs[tied : tied + len(outs)]
        kernel(*refs[:given], *made, *refs[tied + len(outs) + len(carry) :])

    links = {len(scalars) + here: there for here, there in (aliases or {}).items()}
    links.update({given + len(after) + i: len(outs) + i for i in range(len(carry))})
    out = pl.pallas_call(
        body,
        grid_spec=pltpu.PrefetchScalarGridSpec(
            num_scalar_prefetch=len(scalars),
            grid=grid,
            in_specs=list(in_specs) + [ANYWHERE] * (len(after) + len(carry)),
            out_specs=out_specs + [ANYWHERE] * len(carry),
            scratch_shapes=list(scratch),
        ),
        out_shape=out_shapes + [shape_of(*entry.shape, kind=entry.dtype) for entry in carry],
        input_output_aliases=links,
        compiler_params=pltpu.CompilerParams(
            vmem_limit_bytes=limit << 20, collective_id=meet, has_side_effects=meet is not None
        ),
        cost_estimate=pl.CostEstimate(
            flops=int(flops * HINT),
            bytes_accessed=int(traffic * HINT * (1 << 20)),
            transcendentals=int(exps * HINT),
        ),
        name=name,
    )(*scalars, *operands, *after, *carry)
    return (out[: len(outs)], *out[len(outs) :]) if carry else out


def behind(arrays, *tokens):
    out = launch(
        lambda *refs: None, "behind", (), (1,), (), (), (), after=tokens, carry=tuple(arrays)
    )
    return out[1:]


def whole_out(*shape, kind=BF16):
    return blocks(*shape), shape_of(*shape, kind=kind)


def in_order(own, other, place):
    first = place == 0
    return jnp.where(first, own, other), jnp.where(first, other, own)


def open_kernel(*refs):
    prompt_ref, cont_ref, w_ref, fc_ref, proj_ref, wo_ref, gp_ref, gc_ref = refs[:8]
    fc_bias_ref, gain_ref, bias_ref, col_bias_ref = refs[8:12]
    norm_ref, q_ref, k_ref, v_ref, kt_ref, vt_ref = refs[12:18]
    w_own_ref, rows_ref, g_ref, gt_ref, mine_ref, one_ref, three_ref, far_ref, out_ref = refs[18:27]
    (
        rows_t,
        w_s,
        w_own,
        w_out,
        fc_s,
        proj_s,
        mine_s,
        g_t,
        normed,
        norms,
        tall_s,
        flat_s,
        turned,
        wo_f,
        wo_s,
        local_sem,
        send_sem,
        recv_sem,
        out_sem,
    ) = refs[27:]
    place = lax.axis_index("ctx")
    fsdp = lax.axis_index("fsdp")
    tensor = lax.axis_index("tensor")
    tensors = lax.axis_size("tensor")
    core = place % 2
    width, row_count = rows_t.shape[1], rows_t.shape[2]
    prompt_rows = prompt_ref.shape[1]
    half, quarter = width // 2, width // 4
    own = 2 * PAIRS * HEAD
    beside, across, far = {"ctx": place ^ 1}, {"ctx": place ^ 2}, {"fsdp": 1 - fsdp}
    others = [{"tensor": lax.rem(tensor + k, tensors)} for k in range(1, tensors)]

    barrier = pltpu.get_barrier_semaphore()
    for partner in (beside, across, far, *others):
        pl.semaphore_signal(barrier, inc=1, device_id=partner, device_id_type=pl.DeviceIdType.MESH)

    def load(source, target, at):
        copy = pltpu.make_async_copy(source, target, local_sem.at[at])
        copy.start()
        return copy

    def spans(ref):
        return ref.at[:, :prompt_rows], ref.at[:, prompt_rows:]

    own_prompt, own_cont = spans(rows_t.at[0])
    load_rows = [load(prompt_ref, own_prompt, 0), load(cont_ref, own_cont, 1)]
    load_w = load(w_ref, w_s, 2)
    mine_rows = pl.ds(pl.multiple_of(core * quarter, 16), quarter)
    load_mine = [load(fc_ref.at[mine_rows], fc_s, 3), load(proj_ref.at[mine_rows], proj_s, 4)]
    g_prompt, g_cont = spans(g_t)
    load_g = [load(gp_ref, g_prompt, 5), load(gc_ref, g_cont, 6)]
    load_wo = load(wo_ref, wo_f, 7)
    sent, used = [], []

    def push(source, target, partner):
        at = len(used)
        used.append(at)
        copy = pltpu.make_async_remote_copy(
            src_ref=source,
            dst_ref=target,
            send_sem=send_sem.at[at],
            recv_sem=recv_sem.at[at],
            device_id=partner,
            device_id_type=pl.DeviceIdType.MESH,
        )
        copy.start()
        sent.append(copy)
        return copy

    for copy in load_rows:
        copy.wait()
    pl.semaphore_wait(barrier, 3 + len(others))
    to_chip = [
        push(source, target, across) for source, target in zip(spans(rows_t.at[0]), spans(rows_t.at[2]))
    ]
    to_core = push(rows_t.at[0], rows_t.at[1], beside)

    load_w.wait()
    step = w_own.shape[1] // 3
    for part in range(3):
        for at in range((width - HEAD) // own):

            @pl.when(place == at)
            def _():
                start = part * width + at * own
                w_out[:, part * step : part * step + own] = w_s[:, start : start + own].astype(BF16)

        last = w_s[:, (part + 1) * width - HEAD : (part + 1) * width].astype(BF16)
        w_out[:, part * step + own : (part + 1) * step] = jnp.concatenate(
            [last, jnp.zeros((half, step - own - HEAD), BF16)], axis=1
        )
    mine_half = pl.ds(pl.multiple_of(fsdp * half, 16), half)
    to_far = push(w_out, w_own.at[mine_half], far)
    w_own[mine_half, :] = w_out[...]

    for copy in load_mine:
        copy.wait()
    mine_s[:quarter] = fc_s[...].astype(BF16)
    mine_s[quarter : 2 * quarter] = proj_s[...].astype(BF16)
    bias = fc_bias_ref[...]
    pieces = []
    for _ in range(3):
        piece = bias.astype(BF16)
        pieces.append(piece)
        bias = bias - piece.astype(F32)
    pieces.append(jnp.zeros((mine_s.shape[0] - 2 * quarter - 3, width), BF16))
    mine_s[2 * quarter :] = jnp.concatenate(pieces, axis=0)
    to_one = push(mine_s, one_ref, others[0])
    to_near = push(mine_s, far_ref, far)
    to_three = push(mine_s, three_ref, others[2])
    outs, put_at = [], []

    def put(source, target):
        copy = pltpu.make_async_copy(source, target, out_sem.at[len(put_at)])
        put_at.append(len(put_at))
        copy.start()
        outs.append(copy)
        return copy

    def take(copies):
        for copy in copies:
            copy.wait()
        outs[:] = [copy for copy in outs if all(copy is not done for done in copies)]

    put(mine_s, mine_ref)

    load_wo.wait()
    wo_s[...] = wo_f[...].astype(BF16)
    put(wo_s, out_ref.at[mine_half])
    chunk = 128

    def over_rows(body):
        @pl.loop(0, row_count // chunk)
        def _(i):
            body(pl.ds(pl.multiple_of(i * chunk, chunk), chunk))

    for copy in load_g:
        copy.wait()
    put(g_t, gt_ref)

    def turn_rows(source, target):
        def body(rows):
            target[rows, :] = source[:, rows].T

        over_rows(body)

    turn_rows(g_t, turned.at[0])
    put(turned.at[0], g_ref)
    turn_rows(rows_t.at[0], turned.at[1])
    put(turned.at[1], rows_ref)

    gain_col = jnp.broadcast_to(gain_ref[...], (8, width)).T[:, :1]
    bias_col = jnp.broadcast_to(bias_ref[...], (8, width)).T[:, :1]
    extra = norms.shape[1] - width
    at_row = lax.broadcasted_iota(jnp.int32, (extra, row_count), 0)
    ones = jnp.where(at_row == 0, 1.0, 0.0).astype(BF16)
    norms[0, width:] = ones
    norms[1, width:] = ones

    def normalise(distance, slot):
        def body(rows):
            values = rows_t[distance, :, rows].astype(F32)
            average = jnp.mean(values, axis=0, keepdims=True)
            centred = values - average
            variance = jnp.mean(centred * centred, axis=0, keepdims=True)
            low = centred * lax.rsqrt(variance + 1e-05) * gain_col + bias_col
            low = low.astype(BF16)
            norms[slot, :width, rows] = low
            normed[rows, :] = low.T

        over_rows(body)

    def project(distance, slot):
        block = place ^ distance
        made = [put(norms.at[slot], norm_ref.at[block])]
        tiles = step // TILE
        for part, (out, flip) in enumerate(((q_ref, None), (k_ref, kt_ref), (v_ref, vt_ref))):
            cols = slice(part * step, (part + 1) * step)
            value = (dot(normed[...], w_own[:, cols]) + col_bias_ref[:, cols]).astype(BF16)
            for tile in range(tiles):
                piece = value[:, tile * TILE : (tile + 1) * TILE]
                tall_s[slot, :, (part * tiles + tile) * TILE : (part * tiles + tile + 1) * TILE] = piece
                if flip is not None:
                    flat_s[slot, part - 1, tile] = piece.T
            for tile in range(tiles):
                lanes = slice((part * tiles + tile) * TILE, (part * tiles + tile + 1) * TILE)
                made.append(put(tall_s.at[slot, :, lanes], out.at[tile, block]))
                if flip is not None:
                    made.append(put(flat_s.at[slot, part - 1, tile], flip.at[tile, block]))
        return made

    normalise(0, 0)
    to_far.wait_recv()
    put(w_own, w_own_ref)
    first = project(0, 0)
    to_core.wait_recv()
    normalise(1, 1)
    second = project(1, 1)
    to_corner = []
    for copy, source, target in zip(to_chip, spans(rows_t.at[2]), spans(rows_t.at[3])):
        copy.wait_recv()
        to_corner.append(push(source, target, beside))
    take(first)
    normalise(2, 0)
    project(2, 0)
    for copy in to_corner:
        copy.wait_recv()
    take(second)
    normalise(3, 1)
    project(3, 1)
    for copy in outs:
        copy.wait()
    for copy in (to_one, to_near, to_three):
        copy.wait_recv()
    for copy in sent:
        copy.wait_send()


def open_up(
    prompt_in, cont_in, w_qkv, w_fc, w_proj, w_out, fc_bias, prompt_cot, cont_cot, gain, bias, col_bias, count
):
    prompt_rows, width = prompt_in.shape[1:]
    row_count = prompt_rows + cont_in.shape[1]
    half, quarter = width // 2, width // 4
    tiles = PAIRS + 1
    cols = 3 * tiles * TILE
    in_vmem = pl.BlockSpec(memory_space=pltpu.VMEM)
    vmem = lambda *shape, kind=BF16: pltpu.VMEM(shape, kind)
    tall, flat = (tiles, count, row_count, TILE), (tiles, count, TILE, row_count)
    mine = (2 * quarter + 16, w_fc.shape[1])
    outs = [
        (count, width + 16, row_count),
        tall,
        tall,
        tall,
        flat,
        flat,
        (width, cols),
        (row_count, width),
        (row_count, width),
        (width, row_count),
        mine,
        mine,
        mine,
        mine,
        (width, width),
    ]
    copies = 2 + 1 + 1 + 3 + 2
    return pl.pallas_call(
        open_kernel,
        in_specs=[ANYWHERE] * 8 + [in_vmem] * 4,
        out_specs=[ANYWHERE] * len(outs),
        out_shape=[shape_of(*out) for out in outs],
        scratch_shapes=[
            vmem(4, width, row_count),
            vmem(*w_qkv.shape, kind=F32),
            vmem(width, cols),
            vmem(half, cols),
            vmem(quarter, w_fc.shape[1], kind=F32),
            vmem(quarter, w_fc.shape[1], kind=F32),
            vmem(*mine),
            vmem(width, row_count),
            vmem(row_count, width),
            vmem(2, width + 16, row_count),
            vmem(2, row_count, cols),
            vmem(2, 2, tiles, TILE, row_count),
            vmem(2, row_count, width),
            vmem(half, width, kind=F32),
            vmem(half, width),
            pltpu.SemaphoreType.DMA((8,)),
            pltpu.SemaphoreType.DMA((copies,)),
            pltpu.SemaphoreType.DMA((copies,)),
            pltpu.SemaphoreType.DMA((80,)),
        ],
        compiler_params=pltpu.CompilerParams(
            vmem_limit_bytes=60 << 20, collective_id=2, has_side_effects=True
        ),
        cost_estimate=pl.CostEstimate(
            flops=2 * count * row_count * width * cols, bytes_accessed=40 << 20, transcendentals=0
        ),
        name="open",
    )(
        prompt_in[0].T,
        cont_in[0].T,
        w_qkv,
        w_fc,
        w_proj.T,
        w_out,
        prompt_cot[0].T,
        cont_cot[0].T,
        fc_bias[None],
        gain[None],
        bias[None],
        col_bias[None],
    )


def own_mask(rows):
    key_at = lax.broadcasted_iota(jnp.int32, (rows, rows), 0)
    query_at = lax.broadcasted_iota(jnp.int32, (rows, rows), 1)
    return key_at <= query_at


def attend_kernel(prompt_rows, q_ref, k_ref, vt_ref, seg_col_ref, seg_row_ref, *refs):
    mine_ref, near_ref, one_ref, three_ref = refs[:4]
    lse_ref, outs_ref, pieces_ref, last_ref, two_ref, one_far_ref = refs[5:11]
    beside_refs, out_ref, (acc, o_s, send_sem, recv_sem, out_sem) = refs[11:17], refs[17], refs[18:]
    step = pl.program_id(0)
    place = lax.axis_index("ctx")
    fsdp = lax.axis_index("fsdp")
    tensor = lax.axis_index("tensor")
    tensors = lax.axis_size("tensor")
    count, row_count = k_ref.shape[1], k_ref.shape[2]
    cont_rows = row_count - prompt_rows
    per_pair = 2 * count
    steps = PAIRS * per_pair
    beside, far = {"ctx": place ^ 1}, {"fsdp": 1 - fsdp}
    after, before = lax.rem(tensor + 1, tensors), lax.rem(tensor + tensors - 1, tensors)
    distance = jnp.where(step < steps, count - 1 - step % per_pair // 2, 0)
    block = place ^ distance

    def copy_to(at, source, target, partner):
        return pltpu.make_async_remote_copy(
            src_ref=source,
            dst_ref=target,
            send_sem=send_sem.at[at],
            recv_sem=recv_sem.at[at],
            device_id=partner,
            device_id_type=pl.DeviceIdType.MESH,
        )

    b_mine, b_near, b_one, b_one_far, b_three, b_two = beside_refs
    returns = {}
    for pair in range(PAIRS):
        for away in range(1, count):
            returns[pair, away] = copy_to(
                pair * (count - 1) + away - 1,
                o_s.at[pair, away],
                pieces_ref.at[pair, away - 1],
                {"ctx": place ^ away},
            )
    base = PAIRS * (count - 1)
    quarter = out_ref.shape[0] // 4

    def out_rows(away):
        return out_ref.at[pl.ds(pl.multiple_of(((fsdp ^ away) * 2 + place % 2) * quarter, 16), quarter)]

    early = [
        copy_to(base, one_ref, one_far_ref, far),
        copy_to(base + 1, one_ref, two_ref, {"tensor": after}),
        copy_to(base + 2, mine_ref, b_mine, beside),
        copy_to(base + 3, near_ref, b_near, beside),
        copy_to(base + 4, one_ref, b_one, beside),
        copy_to(base + 5, three_ref, b_three, beside),
        copy_to(base + 6, out_rows(0), out_rows(0), far),
    ]
    late = [
        copy_to(base + 7, one_far_ref, b_one_far, beside),
        copy_to(base + 8, out_rows(1), out_rows(1), beside),
        copy_to(base + 9, two_ref, b_two, beside),
    ]

    @pl.when(step == 0)
    def _():
        barrier = pltpu.get_barrier_semaphore()
        partners = [{"ctx": place ^ away} for away in range(1, count)]
        partners += [far, {"tensor": after}, {"tensor": before}]
        for partner in partners:
            pl.semaphore_signal(
                barrier, inc=1, device_id=partner, device_id_type=pl.DeviceIdType.MESH
            )
        pl.semaphore_wait(barrier, len(partners))
        for copy in early:
            copy.start()

    @pl.when(step == per_pair + 2)
    def _():
        early[0].wait_recv()
        late[0].start()

    @pl.when(step == per_pair + 5)
    def _():
        early[6].wait_recv()
        late[1].start()

    @pl.when(step == per_pair + 7)
    def _():
        early[1].wait_recv()
        late[2].start()

    def part(queries, at, start, size, mask, states):
        keys = k_ref[0, at, pl.ds(start, size), :]
        scores = [dot(keys, query, NT) for query in queries]
        if mask is not None:
            scores = [jnp.where(mask, score, -1e30) for score in scores]
        tops = [jnp.max(score, axis=0, keepdims=True) for score in scores]
        if states is not None:
            tops = [jnp.maximum(top, state[0]) for top, state in zip(tops, states)]
        exps = [jnp.exp2(score * SCALE2 - top * SCALE2) for score, top in zip(scores, tops)]
        totals = [jnp.sum(exp, axis=0, keepdims=True) for exp in exps]
        made = []
        for head in range(len(queries)):
            rows = slice(head * HEAD, (head + 1) * HEAD)
            cols = slice(0, queries[head].shape[0])
            out = dot(vt_ref[0, at, rows, pl.ds(start, size)], exps[head].astype(BF16))
            total = totals[head]
            if states is None:
                acc[rows, cols] = out
            else:
                shrink = jnp.exp2((states[head][0] - tops[head]) * SCALE2)
                total = total + states[head][1] * shrink
                acc[rows, cols] = acc[rows, cols] * shrink + out
            made.append((tops[head], total))
        return made

    def finish(start, size, states):
        for head, (top, total) in enumerate(states):
            rows = slice(head * HEAD, (head + 1) * HEAD)
            acc[rows, :size] = acc[rows, :size] / total
            lse_ref[0, block, head : head + 1, pl.ds(start, size)] = top * SCALE2 + jnp.log2(total)
        if len(states) == 1:
            acc[HEAD:, :size] = jnp.zeros((TILE - HEAD, size), F32)
        pair = step // per_pair
        o_s[pair, distance, pl.ds(start, size), :] = acc[:, :size].T.astype(BF16)

    def over_prompt(queries, total, states):
        return lax.fori_loop(
            0, total, lambda c, states: part(queries, c, 0, prompt_rows, None, states), states
        )

    for heads, here in ((2, step < steps), (1, step >= steps)):

        @pl.when(here & (step % 2 == 1))
        def _():
            queries = halves(q_ref[0, block, :prompt_rows, :], heads)
            states = part(queries, block, 0, prompt_rows, own_mask(prompt_rows), None)
            finish(0, prompt_rows, over_prompt(queries, block, states))

        @pl.when(here & (step % 2 == 0))
        def _():
            previous = jnp.maximum(block - 1, 0)
            labels = seg_row_ref[block]
            queries = halves(q_ref[0, block, prompt_rows:, :], heads)
            own = own_mask(cont_rows) & (seg_col_ref[block] == labels)
            near = (seg_col_ref[previous] == labels) & (block > 0)
            states = part(queries, block, prompt_rows, cont_rows, own, None)
            states = part(queries, previous, prompt_rows, cont_rows, near, states)
            finish(prompt_rows, cont_rows, over_prompt(queries, count, states))

    for pair in range(PAIRS):
        for away in range(1, count):

            @pl.when(step == pair * per_pair + 2 * (count - 1 - away) + 1)
            def _():
                returns[pair, away].start()

    @pl.when(step == steps + 1)
    def _():
        stores = [
            pltpu.make_async_copy(o_s.at[pl.ds(0, PAIRS)], outs_ref, out_sem.at[0]),
            pltpu.make_async_copy(o_s.at[PAIRS, 0], last_ref, out_sem.at[1]),
        ]
        for store in stores:
            store.start()
        for copy in early[2:6] + late + list(returns.values()):
            copy.wait_recv()
        for copy in early + late + list(returns.values()):
            copy.wait_send()
        for store in stores:
            store.wait()


def attend(q, k, vt, seg_col, seg_row, prompt_rows, weights, w_out):
    groups, count, row_count, _ = q.shape
    cont_rows = row_count - prompt_rows
    pair = lambda i: (jnp.minimum(i // (2 * count), PAIRS), 0, 0, 0)
    pairs = groups * count * (prompt_rows + 2 * cont_rows) * prompt_rows * count // 2
    mine = weights[0].shape
    copies = PAIRS * (count - 1) + 10
    outs = [
        (pl.BlockSpec((1, count, 2, row_count), pair), shape_of(groups, count, 2, row_count, kind=F32)),
        (ANYWHERE, shape_of(PAIRS, count, row_count, TILE)),
        (ANYWHERE, shape_of(PAIRS, count - 1, row_count, TILE)),
        (ANYWHERE, shape_of(row_count, TILE)),
    ] + [(ANYWHERE, shape_of(*mine))] * 8
    outs.append((ANYWHERE, shape_of(*w_out.shape)))
    return pl.pallas_call(
        functools.partial(attend_kernel, prompt_rows),
        grid=(PAIRS * 2 * count + 2,),
        in_specs=[
            pl.BlockSpec((1, count, row_count, TILE), pair),
            pl.BlockSpec((1, count, row_count, TILE), pair),
            pl.BlockSpec((1, count, TILE, row_count), pair),
            pl.BlockSpec((count, cont_rows, 1), lambda i: (0, 0, 0)),
            pl.BlockSpec((count, 1, cont_rows), lambda i: (0, 0, 0)),
        ]
        + [ANYWHERE] * (len(weights) + 1),
        input_output_aliases={5 + len(weights): len(outs) - 1},
        out_specs=[out[0] for out in outs],
        out_shape=[out[1] for out in outs],
        scratch_shapes=[
            pltpu.VMEM((TILE, max(prompt_rows, cont_rows)), F32),
            pltpu.VMEM((groups, count, row_count, TILE), BF16),
            pltpu.SemaphoreType.DMA((copies,)),
            pltpu.SemaphoreType.DMA((copies,)),
            pltpu.SemaphoreType.DMA((2,)),
        ],
        compiler_params=pltpu.CompilerParams(
            vmem_limit_bytes=56 << 20, collective_id=3, has_side_effects=True
        ),
        cost_estimate=pl.CostEstimate(
            flops=8 * TILE * pairs, bytes_accessed=20 << 20, transcendentals=2 * pairs
        ),
        name="attend",
    )(q, k, vt, seg_col, seg_row, *weights, w_out)


def attend_back_kernel(
    heads,
    spans,
    prompt_rows,
    place_ref,
    q_ref,
    k_ref,
    v_ref,
    kt_ref,
    lse_ref,
    seg_col_ref,
    seg_row_ref,
    *refs,
):
    do_refs, o_refs, refs = refs[:spans], refs[spans : 2 * spans], refs[2 * spans :]
    dq_ref, dk_ref, dv_ref, dk_acc, dv_acc, dq_acc, do_s, o_s = refs
    step = pl.program_id(0)
    distance = step % spans
    block = place_ref[0] ^ distance
    count, row_count = k_ref.shape[1], k_ref.shape[2]
    cont_rows = row_count - prompt_rows

    @pl.when(step == 0)
    def _():
        dk_acc[...] = jnp.zeros_like(dk_acc)
        dv_acc[...] = jnp.zeros_like(dv_acc)
        if spans < count:
            dq_ref[...] = jnp.zeros_like(dq_ref)

    def part(given, at, start, size, mask, first):
        rows = pl.ds(start, size)
        for head in range(heads):
            query, grad, lse, centre = (entry[head] for entry in given)
            cols = slice(0, query.shape[0])
            own = slice(head * HEAD, (head + 1) * HEAD)
            scores = dot(k_ref[0, at, rows, :], query, NT)
            if mask is not None:
                scores = jnp.where(mask, scores, -1e30)
            probability = jnp.exp2(scores * SCALE2 - lse)
            grad_probability = dot(v_ref[0, at, rows, :], grad, NT)
            grad_scores = (probability * (grad_probability - centre)).astype(BF16)
            dv_acc[at, rows, :] += dot(probability.astype(BF16), grad)
            dk_acc[at, rows, :] += dot(grad_scores, query)
            out = dot(kt_ref[0, at, own, rows], grad_scores)
            if first:
                dq_acc[own, cols] = out
            else:
                dq_acc[own, cols] += out

    def setup(start, size):
        rows = pl.ds(start, size)
        for at in range(spans):

            @pl.when(distance == at)
            def _():
                do_s[:size] = do_refs[at][rows, :]
                o_s[:size] = o_refs[at][0, 0, rows, :]

        grad = do_s[:size]
        product = (grad.astype(F32) * o_s[:size].astype(F32)).T
        centres = [
            jnp.sum(product[head * HEAD : (head + 1) * HEAD], axis=0, keepdims=True)
            for head in range(heads)
        ]
        lses = [lse_ref[0, block, head : head + 1, rows] for head in range(heads)]
        return halves(q_ref[0, block, rows, :], heads), halves(grad, heads), lses, centres

    def finish(start, size):
        if heads == 1:
            dq_acc[HEAD:, :size] = jnp.zeros((TILE - HEAD, size), F32)
        dq_ref[0, block, pl.ds(start, size), :] = (dq_acc[:, :size].T * 0.125).astype(BF16)

    @pl.when(step >= spans)
    def _():
        given = setup(0, prompt_rows)
        part(given, block, 0, prompt_rows, own_mask(prompt_rows), True)

        @pl.loop(0, block)
        def _(c):
            part(given, c, 0, prompt_rows, None, False)

        finish(0, prompt_rows)

    @pl.when(step < spans)
    def _():
        before = jnp.maximum(block - 1, 0)
        labels = seg_row_ref[block]
        own = own_mask(cont_rows) & (seg_col_ref[block] == labels)
        near = (seg_col_ref[before] == labels) & (block > 0)
        given = setup(prompt_rows, cont_rows)
        part(given, block, prompt_rows, cont_rows, own, True)
        part(given, before, prompt_rows, cont_rows, near, False)

        @pl.loop(0, count)
        def _(c):
            part(given, c, 0, prompt_rows, None, False)

        finish(prompt_rows, cont_rows)

    @pl.when(step == pl.num_programs(0) - 1)
    def _():
        dk_ref[0] = (dk_acc[...] * 0.125).astype(BF16)
        dv_ref[0] = dv_acc[...].astype(BF16)


def attend_back(
    pair, tile, heads, place, q, k, v, kt, lse, seg_col, seg_row, grads, outs, prompt_rows, after=(), carry=()
):
    _, count, row_count, _ = q.shape
    spans = len(grads)
    cont_rows = row_count - prompt_rows
    pick = lambda i, s: (pair, 0, 0, 0)
    tall = pl.BlockSpec((1, count, row_count, TILE), pick)
    most = max(prompt_rows, cont_rows)
    pairs = spans * (prompt_rows + 2 * cont_rows) * prompt_rows * count // 2
    return launch(
        functools.partial(attend_back_kernel, heads, spans, prompt_rows),
        "attend_back",
        (place,),
        (2 * spans,),
        (q, k, v, kt, lse, seg_col, seg_row, *grads, *[outs] * spans),
        [
            tall,
            tall,
            tall,
            pl.BlockSpec((1, count, TILE, row_count), pick),
            pl.BlockSpec((1, count, 2, row_count), pick),
            blocks(count, cont_rows, 1),
            blocks(count, 1, cont_rows),
        ]
        + [pl.BlockSpec((row_count, TILE), lambda i, s: (0, tile))] * spans
        + [
            pl.BlockSpec((1, 1, row_count, TILE), lambda i, s, away=away: (tile, away, 0, 0))
            for away in range(spans)
        ],
        [whole_out(1, count, row_count, TILE)] * 3,
        scratch=[
            pltpu.VMEM((count, row_count, TILE), F32),
            pltpu.VMEM((count, row_count, TILE), F32),
            pltpu.VMEM((TILE, most), F32),
            pltpu.VMEM((most, TILE), BF16),
            pltpu.VMEM((most, TILE), BF16),
        ],
        limit=56,
        flops=10 * heads * TILE * pairs,
        exps=heads * pairs,
        after=after,
        carry=carry,
    )


def normalize(values):
    average = jnp.mean(values, axis=1, keepdims=True)
    centred = values - average
    variance = jnp.mean(centred * centred, axis=1, keepdims=True)
    rate = lax.rsqrt(variance + 1e-05)
    return centred * rate, rate


def normalize_back(unit, rate, grad):
    shift = jnp.mean(grad, axis=1, keepdims=True)
    along = jnp.mean(grad * unit, axis=1, keepdims=True)
    return rate * (grad - shift - unit * along)


def piece_of(own_ref, pieces_ref, distance):
    tiles = [
        pieces_ref[pair, distance - 1] if distance else own_ref[pair, 0] for pair in range(PAIRS)
    ]
    return jnp.concatenate(tiles, axis=1)


def piece_specs(places, size):
    return [
        pl.BlockSpec((PAIRS, 1, size, TILE), lambda i, *_: (0, 0, i, 0)),
        pl.BlockSpec((PAIRS, places - 1, size, TILE), lambda i, *_: (0, 0, i, 0)),
        pl.BlockSpec((size, TILE), lambda i, *_: (i, 0)),
    ]


def merge_kernel(places, place_ref, x_ref, w_ref, out_bias_ref, gain_ref, bias_ref, *refs):
    own_ref, pieces_ref, last_ref, hidden_ref, low_ref, flip_ref = refs
    own = 2 * PAIRS * HEAD
    width = hidden_ref.shape[1]
    total = x_ref[:, :width].astype(F32) + out_bias_ref[...]
    for distance in range(places):
        start = pl.multiple_of((place_ref[0] ^ distance) * own, own)
        joined = piece_of(own_ref, pieces_ref, distance)
        total = total + dot(joined, w_ref[pl.ds(start, own), :])
    total = total + dot(last_ref[:, :HEAD], w_ref[width - HEAD :, :])
    hidden_ref[...] = total
    unit, _ = normalize(total)
    low = (unit * gain_ref[...] + bias_ref[...]).astype(BF16)
    low_ref[...] = low
    flip_ref[...] = low.T


def merge(place, rows, w_out, out_bias, gain, bias, pieces, after=(), carry=()):
    row_count, width = rows.shape[0], w_out.shape[1]
    size = 128
    by_row = lambda cols: pl.BlockSpec((size, cols), lambda i, p: (i, 0))
    return launch(
        functools.partial(merge_kernel, pieces[0].shape[1]),
        "merge",
        (place,),
        (row_count // size,),
        (rows, w_out, out_bias[None], gain[None], bias[None], *pieces),
        [by_row(rows.shape[1]), blocks(*w_out.shape)]
        + [blocks(1, width)] * 3
        + piece_specs(pieces[0].shape[1], size),
        [
            (by_row(width), shape_of(row_count, width, kind=F32)),
            (by_row(width), shape_of(row_count, width)),
            (
                pl.BlockSpec((width, size), lambda i, p: (0, i)),
                shape_of(width, row_count),
            ),
        ],
        flops=2 * row_count * width * width,
        after=after,
        carry=carry,
    )


def bend_kernel(
    places, mlp_ref, gm_ref, hidden_ref, g_ref, w_ref, gain_ref, proj_bias_ref, own_ref, pieces_ref, last_ref, *refs
):
    out_ref, gh_ref, ga_ref, ga_last_ref, *refs = refs
    come_refs, gw_refs, refs = refs[: places - 1], refs[places - 1 : places + 1], refs[places + 1 :]
    sums_ref, acc, ga_s, send_sem, recv_sem = refs
    step = pl.program_id(0)
    steps = pl.num_programs(0)
    place, fsdp = lax.axis_index("ctx"), lax.axis_index("fsdp")
    own = 2 * PAIRS * HEAD
    size, width = hidden_ref.shape
    mesh_id = pl.DeviceIdType.MESH

    def copies(at):
        rows = pl.ds(pl.multiple_of(at * size, 16), size)
        return [
            pltpu.make_async_remote_copy(
                src_ref=ga_s.at[away - 1, rows],
                dst_ref=come_refs[away - 1].at[rows],
                send_sem=send_sem.at[at, away - 1],
                recv_sem=recv_sem.at[at, away - 1],
                device_id={"ctx": place ^ away},
                device_id_type=mesh_id,
            )
            for away in range(1, places)
        ]

    @pl.when(step == 0)
    def _():
        barrier = pltpu.get_barrier_semaphore()
        for away in range(1, places):
            pl.semaphore_signal(
                barrier, inc=1, device_id={"ctx": place ^ away}, device_id_type=mesh_id
            )

    hidden = hidden_ref[...]
    out_ref[...] = (hidden + mlp_ref[...] + proj_bias_ref[...]).astype(BF16)
    unit, rate = normalize(hidden)
    grad_in = gm_ref[...]
    grad_layer = g_ref[...].astype(F32)
    grad_hidden = grad_layer + normalize_back(unit, rate, grad_in * gain_ref[...])
    gh_ref[...] = grad_hidden
    branch = grad_hidden.astype(BF16)
    rows = pl.ds(pl.multiple_of(step * size, 16), size)
    for distance in range(places - 1, -1, -1):
        heads = pl.ds(pl.multiple_of((place ^ distance) * own, own), own)
        piece = dot(branch, w_ref[heads, :], NT).astype(BF16)
        if distance:
            ga_s[distance - 1, rows, :] = piece
        else:
            ga_ref[...] = piece

    @pl.when(step == 0)
    def _():
        pl.semaphore_wait(pltpu.get_barrier_semaphore(), places - 1)

    for copy in copies(step):
        copy.start()
    last = dot(branch, w_ref[width - HEAD :, :], NT).astype(BF16)
    ga_last_ref[...] = jnp.concatenate([last, jnp.zeros_like(last)], axis=1)
    sums = [grad_hidden, grad_in * unit, grad_in, grad_layer]
    sums = jnp.concatenate([jnp.sum(entry, axis=0, keepdims=True) for entry in sums], axis=0)

    @pl.when(step == 0)
    def _():
        acc[...] = jnp.zeros_like(acc)
        sums_ref[...] = sums

    @pl.when(step > 0)
    def _():
        sums_ref[...] += sums

    for distance in range(places):
        heads = pl.ds(pl.multiple_of((place ^ distance) * own, own), own)
        joined = piece_of(own_ref, pieces_ref, distance)
        acc[heads, :] += dot(joined.T, branch)
    acc[width - HEAD :, :] += dot(last_ref[:, :HEAD].T, branch)

    @pl.when(step == steps - 1)
    def _():
        quarter = width // 4
        for beside, ref in enumerate(gw_refs):
            for away in range(2):
                start = ((fsdp ^ away) * 2 + (place % 2 ^ beside)) * quarter
                ref[away] = acc[pl.ds(pl.multiple_of(start, 16), quarter), :].astype(BF16)

        @pl.loop(0, steps)
        def _(i):
            for copy in copies(i):
                copy.wait_recv()
                copy.wait_send()


def bend(mlp_out, gm, hidden, g, w_out, gain, proj_bias, pieces, after):
    row_count, width = hidden.shape
    size = row_count // 4
    places = pieces[0].shape[1]
    own = 2 * PAIRS * HEAD
    by_row = lambda cols: pl.BlockSpec((size, cols), lambda i: (i, 0))
    return launch(
        functools.partial(bend_kernel, places),
        "bend",
        (),
        (row_count // size,),
        (mlp_out, gm, hidden, g, w_out, gain[None], proj_bias[None], *pieces),
        [by_row(width)] * 4
        + [blocks(*w_out.shape)]
        + [blocks(1, width)] * 2
        + piece_specs(places, size),
        [
            (by_row(width), shape_of(row_count, width)),
            (by_row(width), shape_of(row_count, width, kind=F32)),
            (by_row(own), shape_of(row_count, own)),
            (by_row(TILE), shape_of(row_count, TILE)),
        ]
        + [(ANYWHERE, shape_of(row_count, own))] * (places - 1)
        + [
            whole_out(2, width // 4, width),
            whole_out(2, width // 4, width),
            whole_out(4, width, kind=F32),
        ],
        scratch=[
            pltpu.VMEM((width, width), F32),
            pltpu.VMEM((places - 1, row_count, own), BF16),
            pltpu.SemaphoreType.DMA((row_count // size, places - 1)),
            pltpu.SemaphoreType.DMA((row_count // size, places - 1)),
        ],
        limit=56,
        flops=4 * row_count * width * width,
        traffic=30,
        after=after,
        meet=6,
    )


GELU_RATE = 0.7978845608028654


def gelu_both(values):
    square = values * values
    bent = jnp.tanh(GELU_RATE * (values + 0.044715 * square * values))
    half = 0.5 * (1.0 + bent)
    slope = half + 0.5 * values * (1.0 - bent * bent) * (GELU_RATE * (1.0 + 0.134145 * square))
    return values * half, slope


def mlp_kernel(
    parts,
    first,
    x_ref,
    g_ref,
    xt_ref,
    gt_ref,
    *refs,
):
    own, far, own_2, far_2 = (refs[i * parts : (i + 1) * parts] for i in range(4))
    before_refs = refs[4 * parts : 4 * parts + 2]
    refs = refs[4 * parts + (0 if first else 2) :]
    out_ref, gm_ref, keep_f, send_f, gb_ref = refs[:5]
    sums_p, refs = refs[5 : 5 + parts], refs[5 + parts :]
    wf_s, wp_s, bias_s, biases, act_s, gp_s, wide, keep_s, send_s, come_s, total = refs[:11]
    sems, send_sem, recv_sem = refs[11:]
    step = pl.program_id(0)
    place, fsdp = lax.axis_index("ctx"), lax.axis_index("fsdp")
    core, chip = place % 2, place // 2
    beside = {"ctx": place ^ 1}
    mesh_id = pl.DeviceIdType.MESH
    slot = step % 2
    _, width, hidden = wf_s.shape
    quarter = width // 4

    def spot(away, across):
        start = ((fsdp ^ away) * 2 + (core ^ across)) * quarter
        return pl.ds(pl.multiple_of(start, 16), quarter)

    def loads(at, to):
        moves = [(own[at].at[pl.ds(2 * quarter, 16)], bias_s.at[to])]
        for away, sources in enumerate(((own[at], own_2[at]), (far[at], far_2[at]))):
            for across, source in enumerate(sources):
                for weight, target in enumerate((wf_s, wp_s)):
                    moves.append(
                        (
                            source.at[pl.ds(weight * quarter, quarter)],
                            target.at[to, spot(away, across)],
                        )
                    )
        return [
            pltpu.make_async_copy(source, target, sems.at[to, i])
            for i, (source, target) in enumerate(moves)
        ]

    def exchange(at):
        return pltpu.make_async_remote_copy(
            src_ref=send_s,
            dst_ref=come_s.at[at],
            send_sem=send_sem.at[at],
            recv_sem=recv_sem.at[at],
            device_id=beside,
            device_id_type=mesh_id,
        )

    @pl.when(step == 0)
    def _():
        for part in range(parts):
            for copy in loads(part, part):
                copy.start()
        barrier = pltpu.get_barrier_semaphore()
        pl.semaphore_signal(barrier, inc=1, device_id=beside, device_id_type=mesh_id)
        pl.semaphore_wait(barrier, 1)

    for part in range(parts):

        @pl.when(step == part)
        def _():
            for copy in loads(part, part):
                copy.wait()

    bias = jnp.sum(bias_s[slot, :3, :].astype(F32), axis=0, keepdims=True)
    biases[...] = bias

    def over(total, body):
        whole = total // 256

        @pl.loop(0, whole)
        def _(i):
            body(pl.multiple_of(i * 256, 256), 256)

        if total % 256:
            body(whole * 256, total % 256)

    def up(start, size):
        cols = pl.ds(start, size)
        pre_act = dot(x_ref[...], wf_s[slot, :, cols]) + biases[:, cols]
        grad_act = dot(g_ref[...], wp_s[slot, :, cols])
        activated, slope = gelu_both(pre_act)
        grad_pre = (grad_act * slope).astype(BF16)
        act_s[:, cols] = activated.astype(BF16)
        gp_s[:, cols] = grad_pre
        gb_ref[0, :, cols] = jnp.sum(grad_pre.astype(F32), axis=0, keepdims=True)

    def weights(start, size):
        cols = pl.ds(start, size)
        for weight, (left, right) in enumerate(((xt_ref, gp_s), (gt_ref, act_s))):
            wide[:, :size] = dot(left[...], right[:, cols]).astype(BF16)
            for far in range(2):
                for across, to in enumerate((keep_s, send_s)):
                    to[weight, far, :, cols] = wide[spot(far, across), :size]

    over(hidden, up)
    for part in range(1, parts):

        @pl.when(step == part)
        def _():
            exchange(part - 1).wait_send()

    over(hidden, weights)
    for part in range(parts):

        @pl.when(step == part)
        def _():
            exchange(part).start()

    if first:

        @pl.when(step == 0)
        def _():
            out_ref[...] = jnp.zeros_like(out_ref)
            gm_ref[...] = jnp.zeros_like(gm_ref)

    else:

        @pl.when(step == 0)
        def _():
            out_ref[...] = before_refs[0][...]
            gm_ref[...] = before_refs[1][...]

    def down(start, size):
        rows = pl.ds(start, size)
        out_ref[:, rows] += dot(act_s[...], wp_s[slot, rows, :], NT)
        gm_ref[:, rows] += dot(gp_s[...], wf_s[slot, rows, :], NT)

    over(width, down)
    for part in range(parts):

        @pl.when(step == part)
        def _():
            exchange(part).wait_recv()
            for far in range(2):
                total[...] = keep_s[0, far].astype(F32) + come_s[part, 0, far].astype(F32)
                for to, away in ((keep_f, 0), (send_f, 1)):
                    eighth = quarter // 2
                    rows = pl.ds(pl.multiple_of((chip ^ away) * eighth, 8), eighth)
                    to[0, far] = total[rows, :].astype(BF16)
                sums_p[part][far] = (
                    keep_s[1, far].astype(F32) + come_s[part, 1, far].astype(F32)
                ).astype(BF16)
            if part == parts - 1:
                exchange(part).wait_send()


def mlp(meet, x, g, xt, gt, own, far, own_2, far_2, before=(), after=(), carry=()):
    rows, width = x.shape
    hidden = own[0].shape[1]
    parts, quarter = len(own), width // 4
    once = pl.Buffered(buffer_count=1)
    whole = lambda *shape: pl.BlockSpec(shape, lambda k: (0,) * len(shape), pipeline_mode=once)
    by_half = pl.BlockSpec((1, 2, quarter // 2, hidden), lambda k: (k, 0, 0, 0))
    total = (whole(rows, width), shape_of(rows, width, kind=F32))
    by_half = (by_half, shape_of(parts, 2, quarter // 2, hidden))
    by_part = (whole(2, quarter, hidden), shape_of(2, quarter, hidden))
    return launch(
        functools.partial(mlp_kernel, parts, not before),
        "mlp",
        (),
        (parts,),
        (x, g, xt, gt, *own, *far, *own_2, *far_2, *before),
        [
            whole(rows, width),
            whole(rows, width),
            whole(width, rows),
            whole(width, rows),
        ]
        + [ANYWHERE] * (4 * parts)
        + [whole(rows, width)] * len(before),
        [
            total,
            total,
            by_half,
            by_half,
            (
                pl.BlockSpec((1, 1, hidden), lambda k: (k, 0, 0)),
                shape_of(parts, 1, hidden, kind=F32),
            ),
        ]
        + [by_part] * parts,
        scratch=[
            pltpu.VMEM((2, width, hidden), BF16),
            pltpu.VMEM((2, width, hidden), BF16),
            pltpu.VMEM((2, 16, hidden), BF16),
            pltpu.VMEM((1, hidden), F32),
            pltpu.VMEM((rows, hidden), BF16),
            pltpu.VMEM((rows, hidden), BF16),
            pltpu.VMEM((width, 256), BF16),
            pltpu.VMEM((2, 2, quarter, hidden), BF16),
            pltpu.VMEM((2, 2, quarter, hidden), BF16),
            pltpu.VMEM((parts, 2, 2, quarter, hidden), BF16),
            pltpu.VMEM((quarter, hidden), F32),
            pltpu.SemaphoreType.DMA((2, 9)),
            pltpu.SemaphoreType.DMA((parts,)),
            pltpu.SemaphoreType.DMA((parts,)),
        ],
        meet=meet,
        limit=62,
        flops=12 * rows * width * hidden * parts,
        traffic=40,
        exps=rows * hidden * parts,
        after=after,
        carry=carry,
    )


def tail_kernel(prompt_rows, *refs):
    grads, refs = refs[:9], refs[9:]
    w_ref, norm_ref, rows_ref, gh_ref, keep_ref, come_ref, gain_ref, given_ref = refs[:8]
    prompt_ref, cont_ref, qkv_ref, wo_ref, vec_ref = refs[8:13]
    (
        norms,
        rows_s,
        gh_s,
        joined,
        hold,
        core_out,
        core_in,
        chip_out,
        chip_in,
        acc,
        keep,
        far_out,
        far_in,
        sums,
        sums_in,
        ring_in,
        ring_all,
        whole,
        near_in,
        left_out,
        left_in,
        vec_out,
        vec_in,
        wo_sum,
        wo_ring,
        wo_half,
        wo_all,
        wo_core,
        local_sem,
        send_sem,
        recv_sem,
    ) = refs[13:]
    place = lax.axis_index("ctx")
    fsdp = lax.axis_index("fsdp")
    tensor = lax.axis_index("tensor")
    tensors = lax.axis_size("tensor")
    count, row_count = grads[0].shape[1], grads[0].shape[2]
    width = w_ref.shape[0]
    half = width // 2
    own = acc.shape[1]
    shard = ring_in.shape[2]
    chunk = 128
    beside, across, far = {"ctx": place ^ 1}, {"ctx": place ^ 2}, {"fsdp": 1 - fsdp}
    others = [{"tensor": lax.rem(tensor + k, tensors)} for k in range(1, tensors)]

    barrier = pltpu.get_barrier_semaphore()
    for partner in (beside, across, far, *others):
        pl.semaphore_signal(barrier, inc=1, device_id=partner, device_id_type=pl.DeviceIdType.MESH)

    loads = [pltpu.make_async_copy(norm_ref, norms, local_sem.at[0])]
    loads.append(pltpu.make_async_copy(keep_ref, wo_core.at[0], local_sem.at[1]))
    loads.append(pltpu.make_async_copy(come_ref, core_out.at[pl.ds(0, come_ref.shape[0])], local_sem.at[2]))
    for load in loads:
        load.start()
    sent, used = [], []

    def push(source, target, partner):
        at = len(used)
        used.append(at)
        copy = pltpu.make_async_remote_copy(
            src_ref=source,
            dst_ref=target,
            send_sem=send_sem.at[at],
            recv_sem=recv_sem.at[at],
            device_id=partner,
            device_id_type=pl.DeviceIdType.MESH,
        )
        copy.start()
        sent.append(copy)
        return copy

    quarter, part_rows, most_rows = wo_sum.shape[0], wo_ring.shape[1], wo_half.shape[1]
    chip = place // 2

    def part_start(owner):
        return pl.multiple_of(jnp.minimum(owner * part_rows, most_rows - part_rows), 16)

    def chip_start(owner):
        return pl.ds(pl.multiple_of(owner * (quarter - most_rows), 16), most_rows)

    def rows_grad(distance, out):
        block = place ^ distance
        for i, ref in enumerate(grads):
            joined[:, i * TILE : (i + 1) * TILE] = ref[0, block]

        @pl.loop(0, width // 256)
        def _(i):
            cols = pl.ds(pl.multiple_of(i * 256, 256), 256)
            out[:, cols] = dot(joined[...], w_ref[cols, :], NT).astype(out.dtype)

        if width % 256:
            cols = pl.ds(width // 256 * 256, width % 256)
            out[:, cols] = dot(joined[...], w_ref[cols, :], NT).astype(out.dtype)

    to_far = [None] * 4

    def weights(part):
        @pl.loop(0, count)
        def _(block):
            if part < 3:
                pieces = [grads[3 * part + pair][0, block] for pair in range(PAIRS)]
            else:
                pieces = [grads[3 * i + PAIRS][0, block][:, :HEAD] for i in range(3)]
                pieces.append(jnp.zeros((row_count, own - 3 * HEAD), BF16))
            piece = dot(norms[block], jnp.concatenate(pieces, axis=1))

            @pl.when(block == 0)
            def _():
                acc[...] = piece

            @pl.when(block > 0)
            def _():
                acc[...] += piece

        sums[part] = acc[width : width + 8, :]
        keep[part] = acc[pl.ds(pl.multiple_of(fsdp * half, 16), half), :]
        far_out[part] = acc[pl.ds(pl.multiple_of((1 - fsdp) * half, 16), half), :].astype(BF16)
        to_far[part] = push(far_out.at[part], far_in.at[part], far)

    def joined_far(part):
        to_far[part].wait_recv()
        return keep[part] + far_in[part].astype(F32)

    def start_of(owner):
        return pl.multiple_of(jnp.minimum(owner * shard, half - shard), 16)

    to_ring, to_all, to_near = [None] * 4, [None] * 4, [None] * 4

    def ring(part, total):
        sums_in[part] = total.astype(BF16)
        to_ring[part] = [
            push(
                sums_in.at[part, pl.ds(start_of(other["tensor"]), shard)],
                ring_in.at[part, k],
                other,
            )
            for k, other in enumerate(others)
        ]

    def spread(part):
        total = sums_in[part, pl.ds(start_of(tensor), shard), :].astype(F32)
        for k, copy in enumerate(to_ring[part]):
            copy.wait_recv()
            total = total + ring_in[part, k].astype(F32)
        ring_all[part, tensor] = total.astype(BF16)
        to_all[part] = [
            push(ring_all.at[part, tensor], ring_all.at[part, tensor], other) for other in others
        ]

    def gather(part):
        for copy in to_all[part]:
            copy.wait_recv()
        for owner in range(tensors - 1):
            whole[part, owner * shard : (owner + 1) * shard] = ring_all[part, owner]
        rest = (tensors - 1) * shard
        whole[part, rest:] = ring_all[part, tensors - 1, tensors * shard - half :]
        if part < 3:
            to_near[part] = [
                push(whole.at[part], near_in.at[part, 0], beside),
                push(whole.at[part], near_in.at[part, 1], across),
            ]

    loads[1].wait()
    loads[2].wait()
    wo_sum[...] = (wo_core[0].astype(F32) + core_out[:quarter].astype(F32)).astype(BF16)
    pl.semaphore_wait(barrier, 3 + len(others))
    wo_to_chip = push(wo_sum.at[chip_start(1 - chip)], wo_half.at[1], across)
    loads[0].wait()
    weights(3)
    weights(0)

    rows_grad(3, core_out)
    to_core = push(core_out, core_in.at[0], beside)
    left_out[0] = joined_far(3).astype(BF16)
    to_left = push(left_out.at[0], left_in.at[0], beside)
    wo_to_chip.wait_recv()
    wo_half[0] = (wo_sum[chip_start(chip), :].astype(F32) + wo_half[1].astype(F32)).astype(BF16)
    wo_to_ring = [
        push(wo_half.at[0, pl.ds(part_start(other["tensor"]), part_rows)], wo_ring.at[k], other)
        for k, other in enumerate(others)
    ]
    ring(0, joined_far(0))
    rows_grad(2, hold)
    to_core.wait_recv()

    @pl.loop(0, row_count // chunk)
    def _(i):
        rows = pl.ds(pl.multiple_of(i * chunk, chunk), chunk)
        chip_out[rows, :] = (hold[rows, :] + core_in[0, rows, :].astype(F32)).astype(BF16)

    to_left.wait_recv()
    left_out[1] = (left_out[0].astype(F32) + left_in[0].astype(F32)).astype(BF16)
    to_left = push(left_out.at[1], left_in.at[1], across)
    to_chip = push(chip_out, chip_in, across)
    weights(1)
    wo_total = wo_half[0, pl.ds(part_start(tensor), part_rows), :].astype(F32)
    for k, copy in enumerate(wo_to_ring):
        copy.wait_recv()
        wo_total = wo_total + wo_ring[k].astype(F32)
    wo_all[tensor] = wo_total.astype(BF16)
    wo_to_all = [push(wo_all.at[tensor], wo_all.at[tensor], other) for other in others]
    to_left.wait_recv()
    ring(3, left_out[1].astype(F32) + left_in[1].astype(F32))
    ring(1, joined_far(1))
    weights(2)
    spread(0)
    to_core.wait_send()
    sent[:] = [copy for copy in sent if copy is not to_core]
    rows_grad(1, core_out)
    to_core_2 = push(core_out, core_in.at[1], beside)
    ring(2, joined_far(2))
    spread(3)
    rows_grad(0, hold)
    spread(1)
    for copy in wo_to_all:
        copy.wait_recv()
    for owner in range(tensors):
        start = min(owner * part_rows, most_rows - part_rows)
        wo_half[2, start : start + part_rows] = wo_all[owner]
    wo_to_other = push(wo_half.at[2], wo_half.at[3], across)
    gather(0)
    to_core_2.wait_recv()
    to_chip.wait_recv()

    vec_out[0, :8] = jnp.zeros((8, vec_out.shape[2]), F32)
    vec_out[0, 8:] = given_ref[...]
    chunks = row_count // chunk

    def chunk_rows(i):
        return pl.ds(pl.multiple_of(i * chunk, chunk), chunk)

    def row_loads(i):
        slot = i % 2
        return [
            pltpu.make_async_copy(gh_ref.at[chunk_rows(i)], gh_s.at[slot], local_sem.at[3 + slot]),
            pltpu.make_async_copy(rows_ref.at[chunk_rows(i)], rows_s.at[slot], local_sem.at[5 + slot]),
        ]

    for load in row_loads(0):
        load.start()

    @pl.loop(0, chunks)
    def _(i):
        @pl.when(i + 1 < chunks)
        def _():
            for load in row_loads(i + 1):
                load.start()

        for load in row_loads(i):
            load.wait()

        rows = chunk_rows(i)
        unit, rate = normalize(rows_s[i % 2, :, :width].astype(F32))
        grad = hold[rows, :] + core_in[1, rows, :].astype(F32) + chip_in[rows, :].astype(F32)
        back = normalize_back(unit, rate, grad * gain_ref[...])
        out = (gh_s[i % 2] + back).astype(BF16)

        @pl.when(i < prompt_rows // chunk)
        def _():
            prompt_ref[0, rows, :] = out

        @pl.when(i >= prompt_rows // chunk)
        def _():
            cont_ref[0, chunk_rows(i - prompt_rows // chunk), :] = out

        vec_out[0, 0:1, :width] += jnp.sum(grad * unit, axis=0, keepdims=True)
        vec_out[0, 1:2, :width] += jnp.sum(grad, axis=0, keepdims=True)

    spread(2)
    for row, part in ((2, 0), (3, 2)):
        cols = pl.ds(pl.multiple_of(place * own, own), own)
        vec_out[0, row : row + 1, cols] = sums[part, 0:1, :]
        left = slice(part * HEAD, (part + 1) * HEAD)
        vec_out[0, row : row + 1, width - HEAD : width] = sums[3, 0:1, left]
    gather(1)

    def forward(part):
        to_near[part][1].wait_recv()
        return push(near_in.at[part, 1], near_in.at[part, 2], beside)

    def store(part, passed):
        to_near[part][0].wait_recv()
        passed.wait_recv()
        sources = [whole.at[part]] + [near_in.at[part, i] for i in range(3)]
        for distance, source in enumerate(sources):
            for block in range(count):

                @pl.when(place ^ distance == block)
                def _():
                    start = part * width + block * own
                    qkv_ref[:, start : start + own] = source[...]

    levels = (
        (place, [(place ^ away, {"ctx": place ^ away}) for away in range(1, count)]),
        (tensor, [(other["tensor"], other) for other in others]),
        (fsdp, [(1 - fsdp, far)]),
    )

    def exchange(level):
        own_at, partners = levels[level]
        vec_in[level, own_at] = vec_out[level]
        return [push(vec_out.at[level], vec_in.at[level, own_at], other) for _, other in partners]

    def add(level, copies):
        for copy in copies:
            copy.wait_recv()
        total = vec_in[level, 0]
        for at in range(1, len(copies) + 1):
            total = total + vec_in[level, at]
        vec_out[level + 1] = total

    step = exchange(0)
    passed_0 = forward(0)
    gather(2)
    add(0, step)
    step = exchange(1)
    passed_1 = forward(1)
    gather(3)
    store(0, passed_0)
    add(1, step)
    step = exchange(2)
    wo_to_other.wait_recv()
    for at in range(2):

        @pl.when(chip == at)
        def _():
            wo_core[0, :most_rows] = wo_half[2 + at]
            wo_core[0, most_rows:] = wo_half[3 - at, 2 * most_rows - quarter :]

    wo_to_core = push(wo_core.at[0], wo_core.at[1], beside)
    for part in range(3):
        cols = slice((part + 1) * width - HEAD, (part + 1) * width)
        qkv_ref[:, cols] = whole[3, :, part * HEAD : (part + 1) * HEAD]
    add(2, step)
    vec_ref[...] = vec_out[3]
    passed_2 = forward(2)
    store(1, passed_1)
    wo_to_core.wait_recv()
    core = place % 2
    for away in range(2):
        wo_ref[pl.ds(pl.multiple_of((core ^ away) * quarter, 16), quarter), :] = wo_core[away]
    store(2, passed_2)
    for copy in sent:
        copy.wait_send()


def tail(
    grads, w_own, normed, rows, grad_hidden, gain, vectors, out_keep, out_come, prompt_rows, after=()
):
    count, depth, row_count = normed.shape
    width, cols = w_own.shape
    half, own = width // 2, 2 * PAIRS * HEAD
    tensors = lax.axis_size("tensor")
    shard = -(-half // tensors // 16) * 16
    padded = vectors.shape[1]
    in_vmem = pl.BlockSpec(memory_space=pltpu.VMEM)
    vmem = lambda *shape, kind=BF16: pltpu.VMEM(shape, kind)
    copies = 4 + 4 * 2 * (tensors - 1) + 4 + 3 * 3 + 2 + count + tensors - 1 + 2 * (tensors - 1) + 3
    given = len(grads) + 8
    quarter = width // 4
    most_rows = -(-quarter // 2 // 16) * 16
    part_rows = -(-most_rows // tensors // 16) * 16

    def body(*refs):
        tail_kernel(prompt_rows, *refs[:given], *refs[given + len(after) :])

    return pl.pallas_call(
        body,
        in_specs=[in_vmem] * (len(grads) + 1) + [ANYWHERE] * 5 + [in_vmem] * 2 + [ANYWHERE] * len(after),
        out_specs=[in_vmem] * 5,
        out_shape=[
            shape_of(1, prompt_rows, width),
            shape_of(1, row_count - prompt_rows, width),
            shape_of(half, 3 * width),
            shape_of(half, width),
            shape_of(16, padded, kind=F32),
        ],
        scratch_shapes=[
            vmem(*normed.shape),
            vmem(2, TILE, width),
            vmem(2, TILE, width, kind=F32),
            vmem(row_count, cols),
            vmem(row_count, width, kind=F32),
            vmem(row_count, width),
            vmem(2, row_count, width),
            vmem(row_count, width),
            vmem(row_count, width),
            vmem(depth, own, kind=F32),
            vmem(4, half, own, kind=F32),
            vmem(4, half, own),
            vmem(4, half, own),
            vmem(4, 8, own, kind=F32),
            vmem(4, half, own),
            vmem(4, tensors - 1, shard, own),
            vmem(4, tensors, shard, own),
            vmem(4, half, own),
            vmem(3, 3, half, own),
            vmem(2, half, own),
            vmem(2, half, own),
            vmem(4, 16, padded, kind=F32),
            vmem(3, max(count, tensors), 16, padded, kind=F32),
            vmem(quarter, width),
            vmem(tensors - 1, part_rows, width),
            vmem(4, most_rows, width),
            vmem(tensors, part_rows, width),
            vmem(2, quarter, width),
            pltpu.SemaphoreType.DMA((7,)),
            pltpu.SemaphoreType.DMA((copies,)),
            pltpu.SemaphoreType.DMA((copies,)),
        ],
        compiler_params=pltpu.CompilerParams(
            vmem_limit_bytes=62 << 20, collective_id=1, has_side_effects=True
        ),
        cost_estimate=pl.CostEstimate(
            flops=4 * count * row_count * width * cols, bytes_accessed=30 << 20, transcendentals=0
        ),
        name="tail",
    )(*grads, w_own, normed, rows, grad_hidden, out_keep, out_come, gain[None], vectors, *after)


def own_columns(matrix, place):
    width = matrix.shape[1] // 3
    own = 2 * PAIRS * HEAD
    blank = jnp.zeros((matrix.shape[0], TILE - HEAD), matrix.dtype)
    pieces = []
    for part in range(3):
        whole = matrix[:, part * width : (part + 1) * width]
        pieces += [
            lax.dynamic_slice_in_dim(whole, place * own, own, 1),
            whole[:, width - HEAD :],
            blank,
        ]
    return jnp.concatenate(pieces, axis=1)


def local_heads(
    prompt_in,
    cont_in,
    cont_seg,
    ln1_gain,
    ln1_bias,
    w_qkv,
    qv_bias,
    w_out,
    out_bias,
    ln2_gain,
    ln2_bias,
    w_fc,
    fc_bias,
    w_proj,
    proj_bias,
    prompt_cot,
    cont_cot,
):
    width = prompt_in.shape[2]
    prompt_rows, cont_rows = prompt_in.shape[1], cont_in.shape[1]
    row_count = prompt_rows + cont_rows
    count = lax.axis_size("ctx")
    place = lax.axis_index("ctx")
    core, chip = place % 2, place // 2
    fsdp = lax.axis_index("fsdp")
    tensor = lax.axis_index("tensor")
    tensors = lax.axis_size("tensor")
    own_width = 2 * PAIRS * HEAD
    half, hidden_units = w_fc.shape
    quarter = half // 2
    eighth = quarter // 2
    padded = (width + TILE - 1) // TILE * TILE
    at = place.reshape(1)
    spot = jnp.stack([core, fsdp, tensor, jnp.int32(tensors), place])

    zero_bias = jnp.zeros_like(qv_bias[0])
    col_bias = own_columns(jnp.concatenate([qv_bias[0], zero_bias, qv_bias[1]])[None], place)[0]
    normed, q, k, v, kt, vt, w_own, rows_own, grad_layer, grad_flip, *mines, out_own = open_up(
        prompt_in,
        cont_in,
        w_qkv,
        w_fc,
        w_proj,
        w_out,
        fc_bias,
        prompt_cot,
        cont_cot,
        ln1_gain,
        ln1_bias,
        col_bias,
        count,
    )

    mine, one_away, three_away, near_far = mines

    labels = cont_seg[0].reshape(count, cont_rows)
    seg_col, seg_row = labels[:, :, None], labels[:, None, :]
    lse, outs, came, last_out, two_away, one_far, *others, out_full = attend(
        q, k, vt, seg_col, seg_row, prompt_rows, (mine, near_far, one_away, three_away), out_own
    )
    mine_2, near_2, one_2, one_far_2, three_2, two_2 = others
    three_far, two_far = swap(three_away, "fsdp", 1), swap(two_away, "fsdp", 1)
    pieces = (outs, came, last_out)
    hidden, mlp_low, mlp_flip = merge(
        at, rows_own, out_full, out_bias, ln2_gain, ln2_bias, pieces
    )

    steps_away = (0, 1, 3, 2)
    given = (mlp_low, grad_layer, mlp_flip, grad_flip)
    mlp_out, grad_mlp_in, keep_1, send_1, bias_first, proj_0, proj_1 = mlp(
        4,
        *given, (mine, one_away), (near_far, one_far), (mine_2, one_2), (near_2, one_far_2)
    )
    three_far, two_far = behind((three_far, two_far), bias_first)
    three_far_2, two_far_2 = swap(three_far, "ctx", 1), swap(two_far, "ctx", 1)
    mlp_out, grad_mlp_in, keep_2, send_2, bias_last, proj_2, proj_3 = mlp(
        5,
        *given,
        (three_away, two_away),
        (three_far, two_far),
        (three_2, two_2),
        (three_far_2, two_far_2),
        before=(mlp_out, grad_mlp_in),
    )
    grad_fc_bias = jnp.concatenate([bias_first, bias_last], axis=0)
    proj_2, proj_3 = behind((proj_2, proj_3), mlp_out)
    come_p = [
        turn(part, "tensor", -steps_away[k + 1]) for k, part in enumerate((proj_1, proj_2, proj_3))
    ]
    layer_out, grad_hidden, grads_own, grad_last, *rest = bend(
        mlp_out,
        grad_mlp_in,
        hidden,
        grad_layer,
        out_full,
        ln2_gain,
        proj_bias,
        pieces,
        (proj_2, proj_3),
    )
    grads_all, (out_keep, out_send, sums2) = [grads_own, *rest[:-3]], rest[-3:]

    def added(left, right):
        return left.astype(F32) + right.astype(F32)

    def back(pair, tile, heads, grads, outs, after=()):
        return attend_back(
            pair, tile, heads, at, q, k, v, kt, lse, seg_col, seg_row, grads, outs, prompt_rows, after
        )

    (send_2,) = behind((send_2,), grads_own)
    come_o = swap(out_send, "ctx", 1)
    come_1, come_2 = swap(send_1, "ctx", 2), swap(send_2, "ctx", 2)
    grads_pair = [back(0, 0, 2, grads_all, outs)]
    grads_left = back(PAIRS, 0, 1, [grad_last], last_out[None, None], (grads_pair[0][0],))
    come_o, come_1, come_2, *come_p = behind((come_o, come_1, come_2, *come_p), grads_left[0])
    sums_f = [
        added(keep[k], come[k]).astype(BF16)
        for keep, come in ((keep_1, come_1), (keep_2, come_2))
        for k in range(2)
    ]
    near_p, far_p = (
        sum((come[away].astype(F32) for come in come_p), proj_0[away].astype(F32)).astype(BF16)
        for away in range(2)
    )
    near_o, far_o = (added(out_keep[away], come_o[away]).astype(BF16) for away in range(2))
    come_f = [turn(sums_f[k], "tensor", -steps_away[k]) for k in range(1, tensors)]
    come_p, come_o = swap(far_p, "fsdp", 1), swap(far_o, "fsdp", 1)
    grads_pair.append(back(1, 1, 2, grads_all, outs, (*sums_f[1:], far_p, far_o, grads_left[0])))
    come_p, *come_f = behind((come_p, *come_f), grads_pair[1][0])
    near_f, far_f = (
        sum((come[away].astype(F32) for come in come_f), sums_f[0][away].astype(F32)).astype(BF16)
        for away in range(2)
    )
    sum_p = added(near_p, come_p).astype(BF16)
    ordered = [entry[part] for part in range(3) for entry in (*grads_pair, grads_left)]
    vectors = jnp.concatenate([sums2, jnp.zeros((tensors, hidden_units), F32)], axis=0)
    for k, distance in enumerate(steps_away):
        vectors = lax.dynamic_update_slice(
            vectors, grad_fc_bias[k], (4 + (tensor - distance) % tensors, 0)
        )
    vectors = jnp.pad(vectors, ((0, 0), (0, padded - width)))
    prompt_grad, cont_grad, sum_qkv, sum_out, late = tail(
        ordered,
        w_own,
        normed,
        rows_own,
        grad_hidden,
        ln1_gain,
        vectors,
        near_o,
        come_o,
        prompt_rows,
        (far_f, sum_p),
    )
    come_f, come_p = behind((swap(far_f, "fsdp", 1), swap(sum_p, "ctx", 2)), late)
    sum_f, sum_p = added(near_f, come_f).astype(BF16), added(sum_p, come_p).astype(BF16)
    prompt_grad, cont_grad, sum_qkv, sum_out = behind(
        (prompt_grad, cont_grad, sum_qkv, sum_out), sum_f, sum_p
    )
    by_away = [sum_f] + [swap(sum_f, "ctx", away) for away in range(1, count)]
    halves_f = [
        jnp.concatenate(in_order(by_away[i], by_away[i ^ 2], chip), axis=0) for i in range(2)
    ]
    own_fc = jnp.concatenate(in_order(*halves_f, core), axis=0).astype(F32)
    own_proj = jnp.concatenate(in_order(sum_p, swap(sum_p, "ctx", 1), core), axis=0).astype(F32).T

    fc_bias_sum = lax.dynamic_index_in_dim(late, 12 + tensor, 0, False)[:hidden_units]
    return (
        layer_out[:prompt_rows][None],
        layer_out[prompt_rows:][None],
        prompt_grad,
        cont_grad,
        late[0, :width],
        late[1, :width],
        sum_qkv.astype(F32),
        late[2:4, :width],
        sum_out.astype(F32),
        late[8, :width],
        late[9, :width],
        late[10, :width],
        own_fc,
        fc_bias_sum,
        own_proj,
        late[11, :width],
    )


def solution(mesh):
    placed = (
        P(("fsdp", "tensor"), "ctx", None),
        P(("fsdp", "tensor"), "ctx", None),
        P(("fsdp", "tensor"), None),
        P(),
        P(),
        P("fsdp", None),
        P(),
        P("fsdp", None),
        P(),
        P(),
        P(),
        P("fsdp", "tensor"),
        P("tensor"),
        P("tensor", "fsdp"),
        P(),
        P(("fsdp", "tensor"), "ctx", None),
        P(("fsdp", "tensor"), "ctx", None),
    )
    by_heads = HEADS // mesh.shape["ctx"] == PAIRS * 2 and HEADS % mesh.shape["ctx"] == 1
    return jax.shard_map(
        local_heads if by_heads else local_rows,
        mesh=mesh,
        in_specs=placed,
        out_specs=(
            P(("fsdp", "tensor"), "ctx", None),
            P(("fsdp", "tensor"), "ctx", None),
            P(("fsdp", "tensor"), "ctx", None),
            P(("fsdp", "tensor"), "ctx", None),
            P(),
            P(),
            P("fsdp", None),
            P(),
            P("fsdp", None),
            P(),
            P(),
            P(),
            P("fsdp", "tensor"),
            P("tensor"),
            P("tensor", "fsdp"),
            P(),
        ),
        check_vma=False,
    )
```

```python
import functools

import jax
import jax.numpy as jnp
from jax import lax
from jax.experimental import pallas as pl
from jax.experimental.pallas import tpu as pltpu
from jax.sharding import PartitionSpec as P

HEADS = 17
HEAD = 64


def passed_along(value, axis, steps):
    count = lax.axis_size(axis)
    leading, last = (max(0, -steps), min(count, count - steps))
    return lax.ppermute(value, axis, [(source, source + steps) for source in range(leading, last)])


def layer_norm(values, norm_gain, norm_bias):
    average = jnp.mean(values, axis=-1, keepdims=True)
    centred = values - average
    variance = jnp.mean(centred * centred, axis=-1, keepdims=True)
    return centred * lax.rsqrt(variance + 1e-05) * norm_gain + norm_bias


def gelu_tanh(values):
    return jax.nn.gelu(values, approximate=True)


def inner_first(left_op, right_op):
    return lax.dot_general(
        left_op, right_op, (((0,), (0,)), ((), ())), preferred_element_type=jnp.float32
    )


def inner_last(left_op, right_op):
    return lax.dot_general(
        left_op, right_op, (((1,), (1,)), ((), ())), preferred_element_type=jnp.float32
    )


def to_heads(values):
    return jnp.swapaxes(values.reshape(values.shape[0], HEADS, HEAD), 0, 1)


def from_heads(values):
    return jnp.swapaxes(values, 0, 1).reshape(values.shape[1], values.shape[0] * values.shape[2])


def fetch_prompt(rows_kv):
    return lax.all_gather(rows_kv, "ctx", axis=0, tiled=True)


def local_rows(
    prompt_in,
    cont_in,
    cont_seg,
    ln1_gain,
    ln1_bias,
    w_qkv,
    qv_bias,
    w_out,
    out_bias,
    ln2_gain,
    ln2_bias,
    w_fc,
    fc_bias,
    w_proj,
    proj_bias,
    prompt_cot,
    cont_cot,
):
    model_width = prompt_in.shape[2]
    prompt_rows = prompt_in.shape[1]
    cont_rows = cont_in.shape[1]
    row_count = prompt_rows + cont_rows
    ctx_count = lax.axis_size("ctx")
    ctx_place = lax.axis_index("ctx")
    prompt_total = prompt_rows * ctx_count
    qkv_full, out_full = (
        lax.all_gather(w_qkv.astype(jnp.bfloat16), "fsdp", axis=0, tiled=True),
        lax.all_gather(w_out.astype(jnp.bfloat16), "fsdp", axis=0, tiled=True),
    )
    fc_full, proj_full = (
        lax.all_gather(w_fc.astype(jnp.bfloat16), "fsdp", axis=0, tiled=True),
        lax.all_gather(w_proj.astype(jnp.bfloat16), "fsdp", axis=1, tiled=True),
    )
    row_ids = jnp.arange(row_count, dtype=jnp.int32)
    labels_all = cont_seg[0]
    own_labels = lax.dynamic_slice_in_dim(labels_all, ctx_place * cont_rows, cont_rows)
    earlier_labels = lax.dynamic_slice_in_dim(
        labels_all, jnp.maximum(ctx_place - 1, 0) * cont_rows, cont_rows
    )
    query_labels = jnp.concatenate([jnp.full((prompt_rows,), -1, jnp.int32), own_labels])
    query_prompt = ctx_place * prompt_rows + row_ids
    query_cont = ctx_place * cont_rows + row_ids - prompt_rows
    is_cont = row_ids >= prompt_rows
    prompt_ids = jnp.arange(prompt_total, dtype=jnp.int32)
    near_ids = (ctx_place - 1) * cont_rows + jnp.arange(2 * cont_rows, dtype=jnp.int32)
    near_labels = jnp.concatenate([earlier_labels, own_labels])
    allowed_far = is_cont[:, None] | (prompt_ids[None, :] <= query_prompt[:, None])
    allowed_near = (
        (query_labels[:, None] == near_labels[None, :])
        & (near_ids[None, :] <= query_cont[:, None])
        & (near_ids[None, :] >= 0)
    )
    allowed = jnp.concatenate([allowed_far, allowed_near], 1)
    inputs = jnp.concatenate([prompt_in[0], cont_in[0]], 0).astype(jnp.float32)
    normed, norm1_back = jax.vjp(layer_norm, inputs, ln1_gain, ln1_bias)
    normed_low = normed.astype(jnp.bfloat16)
    projected = jnp.dot(normed_low, qkv_full, preferred_element_type=jnp.float32)
    queries = (projected[:, :model_width] + qv_bias[0]).astype(jnp.bfloat16)
    key_value = jnp.concatenate(
        [projected[:, model_width : 2 * model_width], projected[:, 2 * model_width :] + qv_bias[1]],
        1,
    ).astype(jnp.bfloat16)
    own_cont_kv = key_value[prompt_rows:]
    earlier_kv = passed_along(own_cont_kv, "ctx", 1)
    prompt_kv = fetch_prompt(key_value[:prompt_rows])
    keys_all = jnp.concatenate([prompt_kv, earlier_kv, own_cont_kv], 0)
    query_heads = to_heads(queries)
    key_heads = to_heads(keys_all[:, :model_width])
    value_heads = to_heads(keys_all[:, model_width:])

    def head_forward(operands):
        query_head, key_head, value_head = operands
        scores = inner_last(query_head, key_head) * 0.125
        scores = jnp.where(allowed, scores, -1e30)
        row_max = jnp.max(scores, axis=1, keepdims=True)
        exponent = jnp.exp(scores - row_max)
        row_total = jnp.sum(exponent, axis=1, keepdims=True)
        probability = (exponent / row_total).astype(jnp.bfloat16)
        head_out = jnp.dot(probability, value_head, preferred_element_type=jnp.float32)
        return (head_out.astype(jnp.bfloat16), (row_max + jnp.log(row_total))[:, 0])

    heads_out, logsum = lax.map(head_forward, (query_heads, key_heads, value_heads))
    attended = from_heads(heads_out)
    hidden = inputs + jnp.dot(attended, out_full, preferred_element_type=jnp.float32) + out_bias
    mlp_in, norm2_back = jax.vjp(layer_norm, hidden, ln2_gain, ln2_bias)
    mlp_low = mlp_in.astype(jnp.bfloat16)
    mlp_rows = lax.all_gather(mlp_low, "tensor", axis=0, tiled=True)
    pre_act = jnp.dot(mlp_rows, fc_full, preferred_element_type=jnp.float32) + fc_bias
    activated, gelu_back = jax.vjp(gelu_tanh, pre_act)
    act_low = activated.astype(jnp.bfloat16)
    partial_out = jnp.dot(act_low, proj_full, preferred_element_type=jnp.float32)
    mlp_out = lax.psum_scatter(
        partial_out.astype(jnp.bfloat16), "tensor", scatter_dimension=0, tiled=True
    ).astype(jnp.float32)
    layer_out = (hidden + mlp_out + proj_bias).astype(jnp.bfloat16)
    grad_layer = jnp.concatenate([prompt_cot[0], cont_cot[0]], 0)
    grad_float = grad_layer.astype(jnp.float32)
    grad_proj_bias = jnp.sum(grad_float, axis=0)
    grad_rows = lax.all_gather(grad_layer, "tensor", axis=0, tiled=True)
    grad_w_proj = inner_first(act_low, grad_rows)
    grad_act = inner_last(grad_rows, proj_full)
    grad_pre = gelu_back(grad_act)[0].astype(jnp.bfloat16)
    grad_fc_bias = jnp.sum(grad_pre.astype(jnp.float32), axis=0)
    grad_w_fc = inner_first(mlp_rows, grad_pre)
    grad_mlp_part = inner_last(grad_pre, fc_full)
    grad_mlp_in = lax.psum_scatter(grad_mlp_part, "tensor", scatter_dimension=0, tiled=True)
    grad_hidden_norm, grad_ln2_gain, grad_ln2_bias = norm2_back(grad_mlp_in)
    grad_hidden = grad_float + grad_hidden_norm
    grad_out_bias = jnp.sum(grad_hidden, axis=0)
    grad_branch = grad_hidden.astype(jnp.bfloat16)
    grad_w_out = inner_first(attended, grad_branch)
    grad_attended = inner_last(grad_branch, out_full).astype(jnp.bfloat16)
    prompt_again = fetch_prompt(key_value[:prompt_rows])
    keys_back = jnp.concatenate([prompt_again, earlier_kv, own_cont_kv], 0)
    key_back_heads = to_heads(keys_back[:, :model_width])
    value_back_heads = to_heads(keys_back[:, model_width:])

    def head_backward(operands):
        query_head, key_head, value_head, grad_head, logsum_head = operands
        scores = inner_last(query_head, key_head) * 0.125
        scores = jnp.where(allowed, scores, -1e30)
        probability = jnp.exp(scores - logsum_head[:, None])
        prob_low = probability.astype(jnp.bfloat16)
        grad_prob = inner_last(grad_head, value_head)
        centre = jnp.sum(probability * grad_prob, axis=1, keepdims=True)
        grad_scores = (probability * (grad_prob - centre)).astype(jnp.bfloat16)
        grad_query = jnp.dot(grad_scores, key_head, preferred_element_type=jnp.float32) * 0.125
        grad_key = inner_first(grad_scores, query_head) * 0.125
        grad_value = inner_first(prob_low, grad_head)
        return (grad_query, grad_key, grad_value)

    head_operands = (query_heads, key_back_heads, value_back_heads, to_heads(grad_attended), logsum)
    grad_q_heads, grad_k_heads, grad_v_heads = lax.map(head_backward, head_operands)
    grad_queries = from_heads(grad_q_heads).astype(jnp.bfloat16)
    grad_kv = jnp.concatenate([from_heads(grad_k_heads), from_heads(grad_v_heads)], 1)
    prompt_grad_kv = lax.psum_scatter(
        grad_kv[:prompt_total], "ctx", scatter_dimension=0, tiled=True
    )
    from_later = passed_along(
        grad_kv[prompt_total : prompt_total + cont_rows].astype(jnp.bfloat16), "ctx", -1
    ).astype(jnp.float32)
    cont_grad_kv = grad_kv[prompt_total + cont_rows :] + from_later
    grad_kv_rows = jnp.concatenate([prompt_grad_kv, cont_grad_kv], 0).astype(jnp.bfloat16)
    grad_projected = jnp.concatenate([grad_queries, grad_kv_rows], 1)
    grad_qv_bias = jnp.stack(
        [
            jnp.sum(grad_queries.astype(jnp.float32), axis=0),
            jnp.sum(grad_kv_rows[:, model_width:].astype(jnp.float32), axis=0),
        ]
    )
    grad_w_qkv = inner_first(normed_low, grad_projected)
    grad_normed = inner_last(grad_projected, qkv_full)
    grad_inputs_norm, grad_ln1_gain, grad_ln1_bias = norm1_back(grad_normed)
    grad_inputs = (grad_hidden + grad_inputs_norm).astype(jnp.bfloat16)
    shard_qkv, shard_out = (
        lax.psum_scatter(
            grad_w_qkv.astype(jnp.bfloat16), "fsdp", scatter_dimension=0, tiled=True
        ).astype(jnp.float32),
        lax.psum_scatter(
            grad_w_out.astype(jnp.bfloat16), "fsdp", scatter_dimension=0, tiled=True
        ).astype(jnp.float32),
    )
    sum_qkv, sum_out = lax.psum((shard_qkv, shard_out), ("ctx", "tensor"))
    sum_fc, sum_proj, sum_fc_bias = lax.psum(
        (grad_w_fc, grad_w_proj, grad_fc_bias), ("fsdp", "ctx")
    )
    fsdp_place = lax.axis_index("fsdp")
    fsdp_rows = w_fc.shape[0]
    own_fc = lax.dynamic_slice_in_dim(sum_fc, fsdp_place * fsdp_rows, fsdp_rows, 0)
    own_proj = lax.dynamic_slice_in_dim(sum_proj, fsdp_place * fsdp_rows, fsdp_rows, 1)
    small_sums = lax.psum(
        (
            grad_ln1_gain,
            grad_ln1_bias,
            grad_qv_bias,
            grad_out_bias,
            grad_ln2_gain,
            grad_ln2_bias,
            grad_proj_bias,
        ),
        ("fsdp", "ctx", "tensor"),
    )
    return (
        layer_out[:prompt_rows][None],
        layer_out[prompt_rows:][None],
        grad_inputs[:prompt_rows][None],
        grad_inputs[prompt_rows:][None],
        small_sums[0],
        small_sums[1],
        sum_qkv,
        small_sums[2],
        sum_out,
        small_sums[3],
        small_sums[4],
        small_sums[5],
        own_fc,
        sum_fc_bias,
        own_proj,
        small_sums[6],
    )


PAIRS = 2
TILE = 2 * HEAD
BF16 = jnp.bfloat16
F32 = jnp.float32
LOG2E = 1.4426950408889634
SCALE2 = 0.125 * LOG2E
HINT = 0.2
NN = (((1,), (0,)), ((), ()))
NT = (((1,), (1,)), ((), ()))
TN = (((0,), (0,)), ((), ()))


def dot(left_op, right_op, dims=NN):
    return lax.dot_general(left_op, right_op, dims, preferred_element_type=F32)


def swap(value, axis, bit):
    count = lax.axis_size(axis)
    return lax.ppermute(value, axis, [(place, place ^ bit) for place in range(count)])


def turn(value, axis, steps):
    count = lax.axis_size(axis)
    return lax.ppermute(value, axis, [(place, (place + steps) % count) for place in range(count)])


def halves(values, heads=2):
    lane = lax.broadcasted_iota(jnp.int32, values.shape, 1)
    zero = jnp.zeros_like(values)
    return [jnp.where((lane < HEAD) == (head == 0), values, zero) for head in range(heads)]


ANYWHERE = pl.BlockSpec(memory_space=pl.ANY)


def blocks(*shape):
    return pl.BlockSpec(shape, lambda i, *_: (0,) * len(shape))


def shape_of(*shape, kind=BF16):
    return jax.ShapeDtypeStruct(shape, kind)


def launch(
    kernel, name, scalars, grid, operands, in_specs, outs, scratch=(), limit=48, flops=0, traffic=16, exps=0, after=(), carry=(), aliases=None, meet=None
):
    out_specs, out_shapes = [out[0] for out in outs], [out[1] for out in outs]
    given = len(scalars) + len(operands)
    tied = given + len(after) + len(carry)

    def body(*refs):
        made = refs[tied : tied + len(outs)]
        kernel(*refs[:given], *made, *refs[tied + len(outs) + len(carry) :])

    links = {len(scalars) + here: there for here, there in (aliases or {}).items()}
    links.update({given + len(after) + i: len(outs) + i for i in range(len(carry))})
    out = pl.pallas_call(
        body,
        grid_spec=pltpu.PrefetchScalarGridSpec(
            num_scalar_prefetch=len(scalars),
            grid=grid,
            in_specs=list(in_specs) + [ANYWHERE] * (len(after) + len(carry)),
            out_specs=out_specs + [ANYWHERE] * len(carry),
            scratch_shapes=list(scratch),
        ),
        out_shape=out_shapes + [shape_of(*entry.shape, kind=entry.dtype) for entry in carry],
        input_output_aliases=links,
        compiler_params=pltpu.CompilerParams(
            vmem_limit_bytes=limit << 20, collective_id=meet, has_side_effects=meet is not None
        ),
        cost_estimate=pl.CostEstimate(
            flops=int(flops * HINT),
            bytes_accessed=int(traffic * HINT * (1 << 20)),
            transcendentals=int(exps * HINT),
        ),
        name=name,
    )(*scalars, *operands, *after, *carry)
    return (out[: len(outs)], *out[len(outs) :]) if carry else out


def behind(arrays, *tokens):
    out = launch(
        lambda *refs: None, "behind", (), (1,), (), (), (), after=tokens, carry=tuple(arrays)
    )
    return out[1:]


def whole_out(*shape, kind=BF16):
    return blocks(*shape), shape_of(*shape, kind=kind)


def in_order(own, other, place):
    first = place == 0
    return jnp.where(first, own, other), jnp.where(first, other, own)


def open_kernel(*refs):
    prompt_ref, cont_ref, w_ref, fc_ref, proj_ref, wo_ref, gp_ref, gc_ref = refs[:8]
    fc_bias_ref, gain_ref, bias_ref, col_bias_ref = refs[8:12]
    norm_ref, q_ref, k_ref, v_ref, kt_ref, vt_ref = refs[12:18]
    w_own_ref, rows_ref, g_ref, gt_ref, mine_ref, one_ref, three_ref, far_ref, out_ref = refs[18:27]
    (
        rows_t,
        w_s,
        w_own,
        w_out,
        fc_s,
        proj_s,
        mine_s,
        g_t,
        normed,
        norms,
        tall_s,
        flat_s,
        turned,
        wo_f,
        wo_s,
        local_sem,
        send_sem,
        recv_sem,
        out_sem,
    ) = refs[27:]
    place = lax.axis_index("ctx")
    fsdp = lax.axis_index("fsdp")
    tensor = lax.axis_index("tensor")
    tensors = lax.axis_size("tensor")
    core = place % 2
    width, row_count = rows_t.shape[1], rows_t.shape[2]
    prompt_rows = prompt_ref.shape[1]
    half, quarter = width // 2, width // 4
    own = 2 * PAIRS * HEAD
    beside, across, far = {"ctx": place ^ 1}, {"ctx": place ^ 2}, {"fsdp": 1 - fsdp}
    others = [{"tensor": lax.rem(tensor + k, tensors)} for k in range(1, tensors)]

    barrier = pltpu.get_barrier_semaphore()
    for partner in (beside, across, far, *others):
        pl.semaphore_signal(barrier, inc=1, device_id=partner, device_id_type=pl.DeviceIdType.MESH)

    def load(source, target, at):
        copy = pltpu.make_async_copy(source, target, local_sem.at[at])
        copy.start()
        return copy

    def spans(ref):
        return ref.at[:, :prompt_rows], ref.at[:, prompt_rows:]

    own_prompt, own_cont = spans(rows_t.at[0])
    load_rows = [load(prompt_ref, own_prompt, 0), load(cont_ref, own_cont, 1)]
    load_w = load(w_ref, w_s, 2)
    mine_rows = pl.ds(pl.multiple_of(core * quarter, 16), quarter)
    load_mine = [load(fc_ref.at[mine_rows], fc_s, 3), load(proj_ref.at[mine_rows], proj_s, 4)]
    g_prompt, g_cont = spans(g_t)
    load_g = [load(gp_ref, g_prompt, 5), load(gc_ref, g_cont, 6)]
    load_wo = load(wo_ref, wo_f, 7)
    sent, used = [], []

    def push(source, target, partner):
        at = len(used)
        used.append(at)
        copy = pltpu.make_async_remote_copy(
            src_ref=source,
            dst_ref=target,
            send_sem=send_sem.at[at],
            recv_sem=recv_sem.at[at],
            device_id=partner,
            device_id_type=pl.DeviceIdType.MESH,
        )
        copy.start()
        sent.append(copy)
        return copy

    for copy in load_rows:
        copy.wait()
    pl.semaphore_wait(barrier, 3 + len(others))
    to_chip = [
        push(source, target, across) for source, target in zip(spans(rows_t.at[0]), spans(rows_t.at[2]))
    ]
    to_core = push(rows_t.at[0], rows_t.at[1], beside)

    load_w.wait()
    step = w_own.shape[1] // 3
    for part in range(3):
        for at in range((width - HEAD) // own):

            @pl.when(place == at)
            def _():
                start = part * width + at * own
                w_out[:, part * step : part * step + own] = w_s[:, start : start + own].astype(BF16)

        last = w_s[:, (part + 1) * width - HEAD : (part + 1) * width].astype(BF16)
        w_out[:, part * step + own : (part + 1) * step] = jnp.concatenate(
            [last, jnp.zeros((half, step - own - HEAD), BF16)], axis=1
        )
    mine_half = pl.ds(pl.multiple_of(fsdp * half, 16), half)
    to_far = push(w_out, w_own.at[mine_half], far)
    w_own[mine_half, :] = w_out[...]

    for copy in load_mine:
        copy.wait()
    mine_s[:quarter] = fc_s[...].astype(BF16)
    mine_s[quarter : 2 * quarter] = proj_s[...].astype(BF16)
    bias = fc_bias_ref[...]
    pieces = []
    for _ in range(3):
        piece = bias.astype(BF16)
        pieces.append(piece)
        bias = bias - piece.astype(F32)
    pieces.append(jnp.zeros((mine_s.shape[0] - 2 * quarter - 3, width), BF16))
    mine_s[2 * quarter :] = jnp.concatenate(pieces, axis=0)
    to_one = push(mine_s, one_ref, others[0])
    to_near = push(mine_s, far_ref, far)
    to_three = push(mine_s, three_ref, others[2])
    outs, put_at = [], []

    def put(source, target):
        copy = pltpu.make_async_copy(source, target, out_sem.at[len(put_at)])
        put_at.append(len(put_at))
        copy.start()
        outs.append(copy)
        return copy

    def take(copies):
        for copy in copies:
            copy.wait()
        outs[:] = [copy for copy in outs if all(copy is not done for done in copies)]

    put(mine_s, mine_ref)

    load_wo.wait()
    wo_s[...] = wo_f[...].astype(BF16)
    put(wo_s, out_ref.at[mine_half])
    chunk = 128

    def over_rows(body):
        @pl.loop(0, row_count // chunk)
        def _(i):
            body(pl.ds(pl.multiple_of(i * chunk, chunk), chunk))

    for copy in load_g:
        copy.wait()
    put(g_t, gt_ref)

    def turn_rows(source, target):
        def body(rows):
            target[rows, :] = source[:, rows].T

        over_rows(body)

    turn_rows(g_t, turned.at[0])
    put(turned.at[0], g_ref)
    turn_rows(rows_t.at[0], turned.at[1])
    put(turned.at[1], rows_ref)

    gain_col = jnp.broadcast_to(gain_ref[...], (8, width)).T[:, :1]
    bias_col = jnp.broadcast_to(bias_ref[...], (8, width)).T[:, :1]
    extra = norms.shape[1] - width
    at_row = lax.broadcasted_iota(jnp.int32, (extra, row_count), 0)
    ones = jnp.where(at_row == 0, 1.0, 0.0).astype(BF16)
    norms[0, width:] = ones
    norms[1, width:] = ones

    def normalise(distance, slot):
        def body(rows):
            values = rows_t[distance, :, rows].astype(F32)
            average = jnp.mean(values, axis=0, keepdims=True)
            centred = values - average
            variance = jnp.mean(centred * centred, axis=0, keepdims=True)
            low = centred * lax.rsqrt(variance + 1e-05) * gain_col + bias_col
            low = low.astype(BF16)
            norms[slot, :width, rows] = low
            normed[rows, :] = low.T

        over_rows(body)

    def project(distance, slot):
        block = place ^ distance
        made = [put(norms.at[slot], norm_ref.at[block])]
        tiles = step // TILE
        for part, (out, flip) in enumerate(((q_ref, None), (k_ref, kt_ref), (v_ref, vt_ref))):
            cols = slice(part * step, (part + 1) * step)
            value = (dot(normed[...], w_own[:, cols]) + col_bias_ref[:, cols]).astype(BF16)
            for tile in range(tiles):
                piece = value[:, tile * TILE : (tile + 1) * TILE]
                tall_s[slot, :, (part * tiles + tile) * TILE : (part * tiles + tile + 1) * TILE] = piece
                if flip is not None:
                    flat_s[slot, part - 1, tile] = piece.T
            for tile in range(tiles):
                lanes = slice((part * tiles + tile) * TILE, (part * tiles + tile + 1) * TILE)
                made.append(put(tall_s.at[slot, :, lanes], out.at[tile, block]))
                if flip is not None:
                    made.append(put(flat_s.at[slot, part - 1, tile], flip.at[tile, block]))
        return made

    normalise(0, 0)
    to_far.wait_recv()
    put(w_own, w_own_ref)
    first = project(0, 0)
    to_core.wait_recv()
    normalise(1, 1)
    second = project(1, 1)
    to_corner = []
    for copy, source, target in zip(to_chip, spans(rows_t.at[2]), spans(rows_t.at[3])):
        copy.wait_recv()
        to_corner.append(push(source, target, beside))
    take(first)
    normalise(2, 0)
    project(2, 0)
    for copy in to_corner:
        copy.wait_recv()
    take(second)
    normalise(3, 1)
    project(3, 1)
    for copy in outs:
        copy.wait()
    for copy in (to_one, to_near, to_three):
        copy.wait_recv()
    for copy in sent:
        copy.wait_send()


def open_up(
    prompt_in, cont_in, w_qkv, w_fc, w_proj, w_out, fc_bias, prompt_cot, cont_cot, gain, bias, col_bias, count
):
    prompt_rows, width = prompt_in.shape[1:]
    row_count = prompt_rows + cont_in.shape[1]
    half, quarter = width // 2, width // 4
    tiles = PAIRS + 1
    cols = 3 * tiles * TILE
    in_vmem = pl.BlockSpec(memory_space=pltpu.VMEM)
    vmem = lambda *shape, kind=BF16: pltpu.VMEM(shape, kind)
    tall, flat = (tiles, count, row_count, TILE), (tiles, count, TILE, row_count)
    mine = (2 * quarter + 16, w_fc.shape[1])
    outs = [
        (count, width + 16, row_count),
        tall,
        tall,
        tall,
        flat,
        flat,
        (width, cols),
        (row_count, width),
        (row_count, width),
        (width, row_count),
        mine,
        mine,
        mine,
        mine,
        (width, width),
    ]
    copies = 2 + 1 + 1 + 3 + 2
    return pl.pallas_call(
        open_kernel,
        in_specs=[ANYWHERE] * 8 + [in_vmem] * 4,
        out_specs=[ANYWHERE] * len(outs),
        out_shape=[shape_of(*out) for out in outs],
        scratch_shapes=[
            vmem(4, width, row_count),
            vmem(*w_qkv.shape, kind=F32),
            vmem(width, cols),
            vmem(half, cols),
            vmem(quarter, w_fc.shape[1], kind=F32),
            vmem(quarter, w_fc.shape[1], kind=F32),
            vmem(*mine),
            vmem(width, row_count),
            vmem(row_count, width),
            vmem(2, width + 16, row_count),
            vmem(2, row_count, cols),
            vmem(2, 2, tiles, TILE, row_count),
            vmem(2, row_count, width),
            vmem(half, width, kind=F32),
            vmem(half, width),
            pltpu.SemaphoreType.DMA((8,)),
            pltpu.SemaphoreType.DMA((copies,)),
            pltpu.SemaphoreType.DMA((copies,)),
            pltpu.SemaphoreType.DMA((80,)),
        ],
        compiler_params=pltpu.CompilerParams(
            vmem_limit_bytes=60 << 20, collective_id=2, has_side_effects=True
        ),
        cost_estimate=pl.CostEstimate(
            flops=2 * count * row_count * width * cols, bytes_accessed=40 << 20, transcendentals=0
        ),
        name="open",
    )(
        prompt_in[0].T,
        cont_in[0].T,
        w_qkv,
        w_fc,
        w_proj.T,
        w_out,
        prompt_cot[0].T,
        cont_cot[0].T,
        fc_bias[None],
        gain[None],
        bias[None],
        col_bias[None],
    )


def own_mask(rows):
    key_at = lax.broadcasted_iota(jnp.int32, (rows, rows), 0)
    query_at = lax.broadcasted_iota(jnp.int32, (rows, rows), 1)
    return key_at <= query_at


def attend_kernel(prompt_rows, q_ref, k_ref, vt_ref, seg_col_ref, seg_row_ref, *refs):
    mine_ref, near_ref, one_ref, three_ref = refs[:4]
    lse_ref, outs_ref, pieces_ref, last_ref, two_ref, one_far_ref = refs[5:11]
    beside_refs, out_ref, (acc, o_s, send_sem, recv_sem, out_sem) = refs[11:17], refs[17], refs[18:]
    step = pl.program_id(0)
    place = lax.axis_index("ctx")
    fsdp = lax.axis_index("fsdp")
    tensor = lax.axis_index("tensor")
    tensors = lax.axis_size("tensor")
    count, row_count = k_ref.shape[1], k_ref.shape[2]
    cont_rows = row_count - prompt_rows
    per_pair = 2 * count
    steps = PAIRS * per_pair
    beside, far = {"ctx": place ^ 1}, {"fsdp": 1 - fsdp}
    after, before = lax.rem(tensor + 1, tensors), lax.rem(tensor + tensors - 1, tensors)
    distance = jnp.where(step < steps, count - 1 - step % per_pair // 2, 0)
    block = place ^ distance

    def copy_to(at, source, target, partner):
        return pltpu.make_async_remote_copy(
            src_ref=source,
            dst_ref=target,
            send_sem=send_sem.at[at],
            recv_sem=recv_sem.at[at],
            device_id=partner,
            device_id_type=pl.DeviceIdType.MESH,
        )

    b_mine, b_near, b_one, b_one_far, b_three, b_two = beside_refs
    returns = {}
    for pair in range(PAIRS):
        for away in range(1, count):
            returns[pair, away] = copy_to(
                pair * (count - 1) + away - 1,
                o_s.at[pair, away],
                pieces_ref.at[pair, away - 1],
                {"ctx": place ^ away},
            )
    base = PAIRS * (count - 1)
    quarter = out_ref.shape[0] // 4

    def out_rows(away):
        return out_ref.at[pl.ds(pl.multiple_of(((fsdp ^ away) * 2 + place % 2) * quarter, 16), quarter)]

    early = [
        copy_to(base, one_ref, one_far_ref, far),
        copy_to(base + 1, one_ref, two_ref, {"tensor": after}),
        copy_to(base + 2, mine_ref, b_mine, beside),
        copy_to(base + 3, near_ref, b_near, beside),
        copy_to(base + 4, one_ref, b_one, beside),
        copy_to(base + 5, three_ref, b_three, beside),
        copy_to(base + 6, out_rows(0), out_rows(0), far),
    ]
    late = [
        copy_to(base + 7, one_far_ref, b_one_far, beside),
        copy_to(base + 8, out_rows(1), out_rows(1), beside),
        copy_to(base + 9, two_ref, b_two, beside),
    ]

    @pl.when(step == 0)
    def _():
        barrier = pltpu.get_barrier_semaphore()
        partners = [{"ctx": place ^ away} for away in range(1, count)]
        partners += [far, {"tensor": after}, {"tensor": before}]
        for partner in partners:
            pl.semaphore_signal(
                barrier, inc=1, device_id=partner, device_id_type=pl.DeviceIdType.MESH
            )
        pl.semaphore_wait(barrier, len(partners))
        for copy in early:
            copy.start()

    @pl.when(step == per_pair + 2)
    def _():
        early[0].wait_recv()
        late[0].start()

    @pl.when(step == per_pair + 5)
    def _():
        early[6].wait_recv()
        late[1].start()

    @pl.when(step == per_pair + 7)
    def _():
        early[1].wait_recv()
        late[2].start()

    def part(queries, at, start, size, mask, states):
        keys = k_ref[0, at, pl.ds(start, size), :]
        scores = [dot(keys, query, NT) for query in queries]
        if mask is not None:
            scores = [jnp.where(mask, score, -1e30) for score in scores]
        tops = [jnp.max(score, axis=0, keepdims=True) for score in scores]
        if states is not None:
            tops = [jnp.maximum(top, state[0]) for top, state in zip(tops, states)]
        exps = [jnp.exp2(score * SCALE2 - top * SCALE2) for score, top in zip(scores, tops)]
        totals = [jnp.sum(exp, axis=0, keepdims=True) for exp in exps]
        made = []
        for head in range(len(queries)):
            rows = slice(head * HEAD, (head + 1) * HEAD)
            cols = slice(0, queries[head].shape[0])
            out = dot(vt_ref[0, at, rows, pl.ds(start, size)], exps[head].astype(BF16))
            total = totals[head]
            if states is None:
                acc[rows, cols] = out
            else:
                shrink = jnp.exp2((states[head][0] - tops[head]) * SCALE2)
                total = total + states[head][1] * shrink
                acc[rows, cols] = acc[rows, cols] * shrink + out
            made.append((tops[head], total))
        return made

    def finish(start, size, states):
        for head, (top, total) in enumerate(states):
            rows = slice(head * HEAD, (head + 1) * HEAD)
            acc[rows, :size] = acc[rows, :size] / total
            lse_ref[0, block, head : head + 1, pl.ds(start, size)] = top * SCALE2 + jnp.log2(total)
        if len(states) == 1:
            acc[HEAD:, :size] = jnp.zeros((TILE - HEAD, size), F32)
        pair = step // per_pair
        o_s[pair, distance, pl.ds(start, size), :] = acc[:, :size].T.astype(BF16)

    def over_prompt(queries, total, states):
        return lax.fori_loop(
            0, total, lambda c, states: part(queries, c, 0, prompt_rows, None, states), states
        )

    for heads, here in ((2, step < steps), (1, step >= steps)):

        @pl.when(here & (step % 2 == 1))
        def _():
            queries = halves(q_ref[0, block, :prompt_rows, :], heads)
            states = part(queries, block, 0, prompt_rows, own_mask(prompt_rows), None)
            finish(0, prompt_rows, over_prompt(queries, block, states))

        @pl.when(here & (step % 2 == 0))
        def _():
            previous = jnp.maximum(block - 1, 0)
            labels = seg_row_ref[block]
            queries = halves(q_ref[0, block, prompt_rows:, :], heads)
            own = own_mask(cont_rows) & (seg_col_ref[block] == labels)
            near = (seg_col_ref[previous] == labels) & (block > 0)
            states = part(queries, block, prompt_rows, cont_rows, own, None)
            states = part(queries, previous, prompt_rows, cont_rows, near, states)
            finish(prompt_rows, cont_rows, over_prompt(queries, count, states))

    for pair in range(PAIRS):
        for away in range(1, count):

            @pl.when(step == pair * per_pair + 2 * (count - 1 - away) + 1)
            def _():
                returns[pair, away].start()

    @pl.when(step == steps + 1)
    def _():
        stores = [
            pltpu.make_async_copy(o_s.at[pl.ds(0, PAIRS)], outs_ref, out_sem.at[0]),
            pltpu.make_async_copy(o_s.at[PAIRS, 0], last_ref, out_sem.at[1]),
        ]
        for store in stores:
            store.start()
        for copy in early[2:6] + late + list(returns.values()):
            copy.wait_recv()
        for copy in early + late + list(returns.values()):
            copy.wait_send()
        for store in stores:
            store.wait()


def attend(q, k, vt, seg_col, seg_row, prompt_rows, weights, w_out):
    groups, count, row_count, _ = q.shape
    cont_rows = row_count - prompt_rows
    pair = lambda i: (jnp.minimum(i // (2 * count), PAIRS), 0, 0, 0)
    pairs = groups * count * (prompt_rows + 2 * cont_rows) * prompt_rows * count // 2
    mine = weights[0].shape
    copies = PAIRS * (count - 1) + 10
    outs = [
        (pl.BlockSpec((1, count, 2, row_count), pair), shape_of(groups, count, 2, row_count, kind=F32)),
        (ANYWHERE, shape_of(PAIRS, count, row_count, TILE)),
        (ANYWHERE, shape_of(PAIRS, count - 1, row_count, TILE)),
        (ANYWHERE, shape_of(row_count, TILE)),
    ] + [(ANYWHERE, shape_of(*mine))] * 8
    outs.append((ANYWHERE, shape_of(*w_out.shape)))
    return pl.pallas_call(
        functools.partial(attend_kernel, prompt_rows),
        grid=(PAIRS * 2 * count + 2,),
        in_specs=[
            pl.BlockSpec((1, count, row_count, TILE), pair),
            pl.BlockSpec((1, count, row_count, TILE), pair),
            pl.BlockSpec((1, count, TILE, row_count), pair),
            pl.BlockSpec((count, cont_rows, 1), lambda i: (0, 0, 0)),
            pl.BlockSpec((count, 1, cont_rows), lambda i: (0, 0, 0)),
        ]
        + [ANYWHERE] * (len(weights) + 1),
        input_output_aliases={5 + len(weights): len(outs) - 1},
        out_specs=[out[0] for out in outs],
        out_shape=[out[1] for out in outs],
        scratch_shapes=[
            pltpu.VMEM((TILE, max(prompt_rows, cont_rows)), F32),
            pltpu.VMEM((groups, count, row_count, TILE), BF16),
            pltpu.SemaphoreType.DMA((copies,)),
            pltpu.SemaphoreType.DMA((copies,)),
            pltpu.SemaphoreType.DMA((2,)),
        ],
        compiler_params=pltpu.CompilerParams(
            vmem_limit_bytes=56 << 20, collective_id=3, has_side_effects=True
        ),
        cost_estimate=pl.CostEstimate(
            flops=8 * TILE * pairs, bytes_accessed=20 << 20, transcendentals=2 * pairs
        ),
        name="attend",
    )(q, k, vt, seg_col, seg_row, *weights, w_out)


def attend_back_kernel(
    heads,
    spans,
    prompt_rows,
    place_ref,
    q_ref,
    k_ref,
    v_ref,
    kt_ref,
    lse_ref,
    seg_col_ref,
    seg_row_ref,
    *refs,
):
    do_refs, o_refs, refs = refs[:spans], refs[spans : 2 * spans], refs[2 * spans :]
    dq_ref, dk_ref, dv_ref, dk_acc, dv_acc, dq_acc, do_s, o_s = refs
    step = pl.program_id(0)
    distance = step % spans
    block = place_ref[0] ^ distance
    count, row_count = k_ref.shape[1], k_ref.shape[2]
    cont_rows = row_count - prompt_rows

    @pl.when(step == 0)
    def _():
        dk_acc[...] = jnp.zeros_like(dk_acc)
        dv_acc[...] = jnp.zeros_like(dv_acc)
        if spans < count:
            dq_ref[...] = jnp.zeros_like(dq_ref)

    def part(given, at, start, size, mask, first):
        rows = pl.ds(start, size)
        for head in range(heads):
            query, grad, lse, centre = (entry[head] for entry in given)
            cols = slice(0, query.shape[0])
            own = slice(head * HEAD, (head + 1) * HEAD)
            scores = dot(k_ref[0, at, rows, :], query, NT)
            if mask is not None:
                scores = jnp.where(mask, scores, -1e30)
            probability = jnp.exp2(scores * SCALE2 - lse)
            grad_probability = dot(v_ref[0, at, rows, :], grad, NT)
            grad_scores = (probability * (grad_probability - centre)).astype(BF16)
            dv_acc[at, rows, :] += dot(probability.astype(BF16), grad)
            dk_acc[at, rows, :] += dot(grad_scores, query)
            out = dot(kt_ref[0, at, own, rows], grad_scores)
            if first:
                dq_acc[own, cols] = out
            else:
                dq_acc[own, cols] += out

    def setup(start, size):
        rows = pl.ds(start, size)
        for at in range(spans):

            @pl.when(distance == at)
            def _():
                do_s[:size] = do_refs[at][rows, :]
                o_s[:size] = o_refs[at][0, 0, rows, :]

        grad = do_s[:size]
        product = (grad.astype(F32) * o_s[:size].astype(F32)).T
        centres = [
            jnp.sum(product[head * HEAD : (head + 1) * HEAD], axis=0, keepdims=True)
            for head in range(heads)
        ]
        lses = [lse_ref[0, block, head : head + 1, rows] for head in range(heads)]
        return halves(q_ref[0, block, rows, :], heads), halves(grad, heads), lses, centres

    def finish(start, size):
        if heads == 1:
            dq_acc[HEAD:, :size] = jnp.zeros((TILE - HEAD, size), F32)
        dq_ref[0, block, pl.ds(start, size), :] = (dq_acc[:, :size].T * 0.125).astype(BF16)

    @pl.when(step >= spans)
    def _():
        given = setup(0, prompt_rows)
        part(given, block, 0, prompt_rows, own_mask(prompt_rows), True)

        @pl.loop(0, block)
        def _(c):
            part(given, c, 0, prompt_rows, None, False)

        finish(0, prompt_rows)

    @pl.when(step < spans)
    def _():
        before = jnp.maximum(block - 1, 0)
        labels = seg_row_ref[block]
        own = own_mask(cont_rows) & (seg_col_ref[block] == labels)
        near = (seg_col_ref[before] == labels) & (block > 0)
        given = setup(prompt_rows, cont_rows)
        part(given, block, prompt_rows, cont_rows, own, True)
        part(given, before, prompt_rows, cont_rows, near, False)

        @pl.loop(0, count)
        def _(c):
            part(given, c, 0, prompt_rows, None, False)

        finish(prompt_rows, cont_rows)

    @pl.when(step == pl.num_programs(0) - 1)
    def _():
        dk_ref[0] = (dk_acc[...] * 0.125).astype(BF16)
        dv_ref[0] = dv_acc[...].astype(BF16)


def attend_back(
    pair, tile, heads, place, q, k, v, kt, lse, seg_col, seg_row, grads, outs, prompt_rows, after=(), carry=()
):
    _, count, row_count, _ = q.shape
    spans = len(grads)
    cont_rows = row_count - prompt_rows
    pick = lambda i, s: (pair, 0, 0, 0)
    tall = pl.BlockSpec((1, count, row_count, TILE), pick)
    most = max(prompt_rows, cont_rows)
    pairs = spans * (prompt_rows + 2 * cont_rows) * prompt_rows * count // 2
    return launch(
        functools.partial(attend_back_kernel, heads, spans, prompt_rows),
        "attend_back",
        (place,),
        (2 * spans,),
        (q, k, v, kt, lse, seg_col, seg_row, *grads, *[outs] * spans),
        [
            tall,
            tall,
            tall,
            pl.BlockSpec((1, count, TILE, row_count), pick),
            pl.BlockSpec((1, count, 2, row_count), pick),
            blocks(count, cont_rows, 1),
            blocks(count, 1, cont_rows),
        ]
        + [pl.BlockSpec((row_count, TILE), lambda i, s: (0, tile))] * spans
        + [
            pl.BlockSpec((1, 1, row_count, TILE), lambda i, s, away=away: (tile, away, 0, 0))
            for away in range(spans)
        ],
        [whole_out(1, count, row_count, TILE)] * 3,
        scratch=[
            pltpu.VMEM((count, row_count, TILE), F32),
            pltpu.VMEM((count, row_count, TILE), F32),
            pltpu.VMEM((TILE, most), F32),
            pltpu.VMEM((most, TILE), BF16),
            pltpu.VMEM((most, TILE), BF16),
        ],
        limit=56,
        flops=10 * heads * TILE * pairs,
        exps=heads * pairs,
        after=after,
        carry=carry,
    )


def normalize(values):
    average = jnp.mean(values, axis=1, keepdims=True)
    centred = values - average
    variance = jnp.mean(centred * centred, axis=1, keepdims=True)
    rate = lax.rsqrt(variance + 1e-05)
    return centred * rate, rate


def normalize_back(unit, rate, grad):
    shift = jnp.mean(grad, axis=1, keepdims=True)
    along = jnp.mean(grad * unit, axis=1, keepdims=True)
    return rate * (grad - shift - unit * along)


def piece_of(own_ref, pieces_ref, distance):
    tiles = [
        pieces_ref[pair, distance - 1] if distance else own_ref[pair, 0] for pair in range(PAIRS)
    ]
    return jnp.concatenate(tiles, axis=1)


def piece_specs(places, size):
    return [
        pl.BlockSpec((PAIRS, 1, size, TILE), lambda i, *_: (0, 0, i, 0)),
        pl.BlockSpec((PAIRS, places - 1, size, TILE), lambda i, *_: (0, 0, i, 0)),
        pl.BlockSpec((size, TILE), lambda i, *_: (i, 0)),
    ]


def merge_kernel(places, place_ref, x_ref, w_ref, out_bias_ref, gain_ref, bias_ref, *refs):
    own_ref, pieces_ref, last_ref, hidden_ref, low_ref, flip_ref = refs
    own = 2 * PAIRS * HEAD
    width = hidden_ref.shape[1]
    total = x_ref[:, :width].astype(F32) + out_bias_ref[...]
    for distance in range(places):
        start = pl.multiple_of((place_ref[0] ^ distance) * own, own)
        joined = piece_of(own_ref, pieces_ref, distance)
        total = total + dot(joined, w_ref[pl.ds(start, own), :])
    total = total + dot(last_ref[:, :HEAD], w_ref[width - HEAD :, :])
    hidden_ref[...] = total
    unit, _ = normalize(total)
    low = (unit * gain_ref[...] + bias_ref[...]).astype(BF16)
    low_ref[...] = low
    flip_ref[...] = low.T


def merge(place, rows, w_out, out_bias, gain, bias, pieces, after=(), carry=()):
    row_count, width = rows.shape[0], w_out.shape[1]
    size = 128
    by_row = lambda cols: pl.BlockSpec((size, cols), lambda i, p: (i, 0))
    return launch(
        functools.partial(merge_kernel, pieces[0].shape[1]),
        "merge",
        (place,),
        (row_count // size,),
        (rows, w_out, out_bias[None], gain[None], bias[None], *pieces),
        [by_row(rows.shape[1]), blocks(*w_out.shape)]
        + [blocks(1, width)] * 3
        + piece_specs(pieces[0].shape[1], size),
        [
            (by_row(width), shape_of(row_count, width, kind=F32)),
            (by_row(width), shape_of(row_count, width)),
            (
                pl.BlockSpec((width, size), lambda i, p: (0, i)),
                shape_of(width, row_count),
            ),
        ],
        flops=2 * row_count * width * width,
        after=after,
        carry=carry,
    )


def bend_kernel(
    places, mlp_ref, gm_ref, hidden_ref, g_ref, w_ref, gain_ref, proj_bias_ref, own_ref, pieces_ref, last_ref, *refs
):
    out_ref, gh_ref, ga_ref, ga_last_ref, *refs = refs
    come_refs, gw_refs, refs = refs[: places - 1], refs[places - 1 : places + 1], refs[places + 1 :]
    sums_ref, acc, ga_s, send_sem, recv_sem = refs
    step = pl.program_id(0)
    steps = pl.num_programs(0)
    place, fsdp = lax.axis_index("ctx"), lax.axis_index("fsdp")
    own = 2 * PAIRS * HEAD
    size, width = hidden_ref.shape
    mesh_id = pl.DeviceIdType.MESH

    def copies(at):
        rows = pl.ds(pl.multiple_of(at * size, 16), size)
        return [
            pltpu.make_async_remote_copy(
                src_ref=ga_s.at[away - 1, rows],
                dst_ref=come_refs[away - 1].at[rows],
                send_sem=send_sem.at[at, away - 1],
                recv_sem=recv_sem.at[at, away - 1],
                device_id={"ctx": place ^ away},
                device_id_type=mesh_id,
            )
            for away in range(1, places)
        ]

    @pl.when(step == 0)
    def _():
        barrier = pltpu.get_barrier_semaphore()
        for away in range(1, places):
            pl.semaphore_signal(
                barrier, inc=1, device_id={"ctx": place ^ away}, device_id_type=mesh_id
            )

    hidden = hidden_ref[...]
    out_ref[...] = (hidden + mlp_ref[...] + proj_bias_ref[...]).astype(BF16)
    unit, rate = normalize(hidden)
    grad_in = gm_ref[...]
    grad_layer = g_ref[...].astype(F32)
    grad_hidden = grad_layer + normalize_back(unit, rate, grad_in * gain_ref[...])
    gh_ref[...] = grad_hidden
    branch = grad_hidden.astype(BF16)
    rows = pl.ds(pl.multiple_of(step * size, 16), size)
    for distance in range(places - 1, -1, -1):
        heads = pl.ds(pl.multiple_of((place ^ distance) * own, own), own)
        piece = dot(branch, w_ref[heads, :], NT).astype(BF16)
        if distance:
            ga_s[distance - 1, rows, :] = piece
        else:
            ga_ref[...] = piece

    @pl.when(step == 0)
    def _():
        pl.semaphore_wait(pltpu.get_barrier_semaphore(), places - 1)

    for copy in copies(step):
        copy.start()
    last = dot(branch, w_ref[width - HEAD :, :], NT).astype(BF16)
    ga_last_ref[...] = jnp.concatenate([last, jnp.zeros_like(last)], axis=1)
    sums = [grad_hidden, grad_in * unit, grad_in, grad_layer]
    sums = jnp.concatenate([jnp.sum(entry, axis=0, keepdims=True) for entry in sums], axis=0)

    @pl.when(step == 0)
    def _():
        acc[...] = jnp.zeros_like(acc)
        sums_ref[...] = sums

    @pl.when(step > 0)
    def _():
        sums_ref[...] += sums

    for distance in range(places):
        heads = pl.ds(pl.multiple_of((place ^ distance) * own, own), own)
        joined = piece_of(own_ref, pieces_ref, distance)
        acc[heads, :] += dot(joined.T, branch)
    acc[width - HEAD :, :] += dot(last_ref[:, :HEAD].T, branch)

    @pl.when(step == steps - 1)
    def _():
        quarter = width // 4
        for beside, ref in enumerate(gw_refs):
            for away in range(2):
                start = ((fsdp ^ away) * 2 + (place % 2 ^ beside)) * quarter
                ref[away] = acc[pl.ds(pl.multiple_of(start, 16), quarter), :].astype(BF16)

        @pl.loop(0, steps)
        def _(i):
            for copy in copies(i):
                copy.wait_recv()
                copy.wait_send()


def bend(mlp_out, gm, hidden, g, w_out, gain, proj_bias, pieces, after):
    row_count, width = hidden.shape
    size = row_count // 4
    places = pieces[0].shape[1]
    own = 2 * PAIRS * HEAD
    by_row = lambda cols: pl.BlockSpec((size, cols), lambda i: (i, 0))
    return launch(
        functools.partial(bend_kernel, places),
        "bend",
        (),
        (row_count // size,),
        (mlp_out, gm, hidden, g, w_out, gain[None], proj_bias[None], *pieces),
        [by_row(width)] * 4
        + [blocks(*w_out.shape)]
        + [blocks(1, width)] * 2
        + piece_specs(places, size),
        [
            (by_row(width), shape_of(row_count, width)),
            (by_row(width), shape_of(row_count, width, kind=F32)),
            (by_row(own), shape_of(row_count, own)),
            (by_row(TILE), shape_of(row_count, TILE)),
        ]
        + [(ANYWHERE, shape_of(row_count, own))] * (places - 1)
        + [
            whole_out(2, width // 4, width),
            whole_out(2, width // 4, width),
            whole_out(4, width, kind=F32),
        ],
        scratch=[
            pltpu.VMEM((width, width), F32),
            pltpu.VMEM((places - 1, row_count, own), BF16),
            pltpu.SemaphoreType.DMA((row_count // size, places - 1)),
            pltpu.SemaphoreType.DMA((row_count // size, places - 1)),
        ],
        limit=56,
        flops=4 * row_count * width * width,
        traffic=30,
        after=after,
        meet=6,
    )


GELU_RATE = 0.7978845608028654


def gelu_both(values):
    square = values * values
    bent = jnp.tanh(GELU_RATE * (values + 0.044715 * square * values))
    half = 0.5 * (1.0 + bent)
    slope = half + 0.5 * values * (1.0 - bent * bent) * (GELU_RATE * (1.0 + 0.134145 * square))
    return values * half, slope


def mlp_kernel(
    parts,
    first,
    x_ref,
    g_ref,
    xt_ref,
    gt_ref,
    *refs,
):
    own, far, own_2, far_2 = (refs[i * parts : (i + 1) * parts] for i in range(4))
    before_refs = refs[4 * parts : 4 * parts + 2]
    refs = refs[4 * parts + (0 if first else 2) :]
    out_ref, gm_ref, keep_f, send_f, gb_ref = refs[:5]
    sums_p, refs = refs[5 : 5 + parts], refs[5 + parts :]
    wf_s, wp_s, bias_s, biases, act_s, gp_s, wide, keep_s, send_s, come_s, total = refs[:11]
    sems, send_sem, recv_sem = refs[11:]
    step = pl.program_id(0)
    place, fsdp = lax.axis_index("ctx"), lax.axis_index("fsdp")
    core, chip = place % 2, place // 2
    beside = {"ctx": place ^ 1}
    mesh_id = pl.DeviceIdType.MESH
    slot = step % 2
    _, width, hidden = wf_s.shape
    quarter = width // 4

    def spot(away, across):
        start = ((fsdp ^ away) * 2 + (core ^ across)) * quarter
        return pl.ds(pl.multiple_of(start, 16), quarter)

    def loads(at, to):
        moves = [(own[at].at[pl.ds(2 * quarter, 16)], bias_s.at[to])]
        for away, sources in enumerate(((own[at], own_2[at]), (far[at], far_2[at]))):
            for across, source in enumerate(sources):
                for weight, target in enumerate((wf_s, wp_s)):
                    moves.append(
                        (
                            source.at[pl.ds(weight * quarter, quarter)],
                            target.at[to, spot(away, across)],
                        )
                    )
        return [
            pltpu.make_async_copy(source, target, sems.at[to, i])
            for i, (source, target) in enumerate(moves)
        ]

    def exchange(at):
        return pltpu.make_async_remote_copy(
            src_ref=send_s,
            dst_ref=come_s.at[at],
            send_sem=send_sem.at[at],
            recv_sem=recv_sem.at[at],
            device_id=beside,
            device_id_type=mesh_id,
        )

    @pl.when(step == 0)
    def _():
        for part in range(parts):
            for copy in loads(part, part):
                copy.start()
        barrier = pltpu.get_barrier_semaphore()
        pl.semaphore_signal(barrier, inc=1, device_id=beside, device_id_type=mesh_id)
        pl.semaphore_wait(barrier, 1)

    for part in range(parts):

        @pl.when(step == part)
        def _():
            for copy in loads(part, part):
                copy.wait()

    bias = jnp.sum(bias_s[slot, :3, :].astype(F32), axis=0, keepdims=True)
    biases[...] = bias

    def over(total, body):
        whole = total // 256

        @pl.loop(0, whole)
        def _(i):
            body(pl.multiple_of(i * 256, 256), 256)

        if total % 256:
            body(whole * 256, total % 256)

    def up(*blocks_of):
        made = []
        for start, size in blocks_of:
            cols = pl.ds(start, size)
            pre_act = dot(x_ref[...], wf_s[slot, :, cols]) + biases[:, cols]
            made.append((cols, pre_act, dot(g_ref[...], wp_s[slot, :, cols])))
        for cols, pre_act, grad_act in made:
            activated, slope = gelu_both(pre_act)
            grad_pre = (grad_act * slope).astype(BF16)
            act_s[:, cols] = activated.astype(BF16)
            gp_s[:, cols] = grad_pre
            gb_ref[0, :, cols] = jnp.sum(grad_pre.astype(F32), axis=0, keepdims=True)

    def weights(start, size):
        cols = pl.ds(start, size)
        for weight, (left, right) in enumerate(((xt_ref, gp_s), (gt_ref, act_s))):
            wide[:, :size] = dot(left[...], right[:, cols]).astype(BF16)
            for far in range(2):
                for across, to in enumerate((keep_s, send_s)):
                    to[weight, far, :, cols] = wide[spot(far, across), :size]

    pairs = hidden // 512

    @pl.loop(0, pairs)
    def _(i):
        start = pl.multiple_of(i * 512, 512)
        up((start, 256), (start + 256, 256))

    for start in range(pairs * 512, hidden, 256):
        up((start, min(256, hidden - start)))

    for part in range(1, parts):

        @pl.when(step == part)
        def _():
            exchange(part - 1).wait_send()

    over(hidden, weights)
    for part in range(parts):

        @pl.when(step == part)
        def _():
            exchange(part).start()

    if first:

        @pl.when(step == 0)
        def _():
            out_ref[...] = jnp.zeros_like(out_ref)
            gm_ref[...] = jnp.zeros_like(gm_ref)

    else:

        @pl.when(step == 0)
        def _():
            out_ref[...] = before_refs[0][...]
            gm_ref[...] = before_refs[1][...]

    def down(start, size):
        rows = pl.ds(start, size)
        out_ref[:, rows] += dot(act_s[...], wp_s[slot, rows, :], NT)
        gm_ref[:, rows] += dot(gp_s[...], wf_s[slot, rows, :], NT)

    over(width, down)
    for part in range(parts):

        @pl.when(step == part)
        def _():
            exchange(part).wait_recv()
            for far in range(2):
                total[...] = keep_s[0, far].astype(F32) + come_s[part, 0, far].astype(F32)
                for to, away in ((keep_f, 0), (send_f, 1)):
                    eighth = quarter // 2
                    rows = pl.ds(pl.multiple_of((chip ^ away) * eighth, 8), eighth)
                    to[0, far] = total[rows, :].astype(BF16)
                sums_p[part][far] = (
                    keep_s[1, far].astype(F32) + come_s[part, 1, far].astype(F32)
                ).astype(BF16)
            if part == parts - 1:
                exchange(part).wait_send()


def mlp(meet, x, g, xt, gt, own, far, own_2, far_2, before=(), after=(), carry=()):
    rows, width = x.shape
    hidden = own[0].shape[1]
    parts, quarter = len(own), width // 4
    once = pl.Buffered(buffer_count=1)
    whole = lambda *shape: pl.BlockSpec(shape, lambda k: (0,) * len(shape), pipeline_mode=once)
    by_half = pl.BlockSpec((1, 2, quarter // 2, hidden), lambda k: (k, 0, 0, 0))
    total = (whole(rows, width), shape_of(rows, width, kind=F32))
    by_half = (by_half, shape_of(parts, 2, quarter // 2, hidden))
    by_part = (whole(2, quarter, hidden), shape_of(2, quarter, hidden))
    return launch(
        functools.partial(mlp_kernel, parts, not before),
        "mlp",
        (),
        (parts,),
        (x, g, xt, gt, *own, *far, *own_2, *far_2, *before),
        [
            whole(rows, width),
            whole(rows, width),
            whole(width, rows),
            whole(width, rows),
        ]
        + [ANYWHERE] * (4 * parts)
        + [whole(rows, width)] * len(before),
        [
            total,
            total,
            by_half,
            by_half,
            (
                pl.BlockSpec((1, 1, hidden), lambda k: (k, 0, 0)),
                shape_of(parts, 1, hidden, kind=F32),
            ),
        ]
        + [by_part] * parts,
        scratch=[
            pltpu.VMEM((2, width, hidden), BF16),
            pltpu.VMEM((2, width, hidden), BF16),
            pltpu.VMEM((2, 16, hidden), BF16),
            pltpu.VMEM((1, hidden), F32),
            pltpu.VMEM((rows, hidden), BF16),
            pltpu.VMEM((rows, hidden), BF16),
            pltpu.VMEM((width, 256), BF16),
            pltpu.VMEM((2, 2, quarter, hidden), BF16),
            pltpu.VMEM((2, 2, quarter, hidden), BF16),
            pltpu.VMEM((parts, 2, 2, quarter, hidden), BF16),
            pltpu.VMEM((quarter, hidden), F32),
            pltpu.SemaphoreType.DMA((2, 9)),
            pltpu.SemaphoreType.DMA((parts,)),
            pltpu.SemaphoreType.DMA((parts,)),
        ],
        meet=meet,
        limit=62,
        flops=12 * rows * width * hidden * parts,
        traffic=40,
        exps=rows * hidden * parts,
        after=after,
        carry=carry,
    )


def tail_kernel(prompt_rows, *refs):
    grads, refs = refs[:9], refs[9:]
    w_ref, norm_ref, rows_ref, gh_ref, keep_ref, come_ref, gain_ref, given_ref = refs[:8]
    prompt_ref, cont_ref, qkv_ref, wo_ref, vec_ref = refs[8:13]
    (
        norms,
        rows_s,
        gh_s,
        joined,
        hold,
        core_out,
        core_in,
        chip_out,
        chip_in,
        acc,
        keep,
        far_out,
        far_in,
        sums,
        sums_in,
        ring_in,
        ring_all,
        whole,
        near_in,
        left_out,
        left_in,
        vec_out,
        vec_in,
        wo_sum,
        wo_ring,
        wo_half,
        wo_all,
        wo_core,
        local_sem,
        send_sem,
        recv_sem,
    ) = refs[13:]
    place = lax.axis_index("ctx")
    fsdp = lax.axis_index("fsdp")
    tensor = lax.axis_index("tensor")
    tensors = lax.axis_size("tensor")
    count, row_count = grads[0].shape[1], grads[0].shape[2]
    width = w_ref.shape[0]
    half = width // 2
    own = acc.shape[1]
    shard = ring_in.shape[2]
    chunk = 128
    beside, across, far = {"ctx": place ^ 1}, {"ctx": place ^ 2}, {"fsdp": 1 - fsdp}
    others = [{"tensor": lax.rem(tensor + k, tensors)} for k in range(1, tensors)]

    barrier = pltpu.get_barrier_semaphore()
    for partner in (beside, across, far, *others):
        pl.semaphore_signal(barrier, inc=1, device_id=partner, device_id_type=pl.DeviceIdType.MESH)

    loads = [pltpu.make_async_copy(norm_ref, norms, local_sem.at[0])]
    loads.append(pltpu.make_async_copy(keep_ref, wo_core.at[0], local_sem.at[1]))
    loads.append(pltpu.make_async_copy(come_ref, core_out.at[pl.ds(0, come_ref.shape[0])], local_sem.at[2]))
    for load in loads:
        load.start()
    sent, used = [], []

    def push(source, target, partner):
        at = len(used)
        used.append(at)
        copy = pltpu.make_async_remote_copy(
            src_ref=source,
            dst_ref=target,
            send_sem=send_sem.at[at],
            recv_sem=recv_sem.at[at],
            device_id=partner,
            device_id_type=pl.DeviceIdType.MESH,
        )
        copy.start()
        sent.append(copy)
        return copy

    quarter, part_rows, most_rows = wo_sum.shape[0], wo_ring.shape[1], wo_half.shape[1]
    chip = place // 2

    def part_start(owner):
        return pl.multiple_of(jnp.minimum(owner * part_rows, most_rows - part_rows), 16)

    def chip_start(owner):
        return pl.ds(pl.multiple_of(owner * (quarter - most_rows), 16), most_rows)

    def rows_grad(distance, out):
        block = place ^ distance
        for i, ref in enumerate(grads):
            joined[:, i * TILE : (i + 1) * TILE] = ref[0, block]

        @pl.loop(0, width // 256)
        def _(i):
            cols = pl.ds(pl.multiple_of(i * 256, 256), 256)
            out[:, cols] = dot(joined[...], w_ref[cols, :], NT).astype(out.dtype)

        if width % 256:
            cols = pl.ds(width // 256 * 256, width % 256)
            out[:, cols] = dot(joined[...], w_ref[cols, :], NT).astype(out.dtype)

    to_far = [None] * 4

    def weights(part):
        @pl.loop(0, count)
        def _(block):
            if part < 3:
                pieces = [grads[3 * part + pair][0, block] for pair in range(PAIRS)]
            else:
                pieces = [grads[3 * i + PAIRS][0, block][:, :HEAD] for i in range(3)]
                pieces.append(jnp.zeros((row_count, own - 3 * HEAD), BF16))
            piece = dot(norms[block], jnp.concatenate(pieces, axis=1))

            @pl.when(block == 0)
            def _():
                acc[...] = piece

            @pl.when(block > 0)
            def _():
                acc[...] += piece

        sums[part] = acc[width : width + 8, :]
        keep[part] = acc[pl.ds(pl.multiple_of(fsdp * half, 16), half), :]
        far_out[part] = acc[pl.ds(pl.multiple_of((1 - fsdp) * half, 16), half), :].astype(BF16)
        to_far[part] = push(far_out.at[part], far_in.at[part], far)

    def joined_far(part):
        to_far[part].wait_recv()
        return keep[part] + far_in[part].astype(F32)

    def start_of(owner):
        return pl.multiple_of(jnp.minimum(owner * shard, half - shard), 16)

    to_ring, to_all, to_near = [None] * 4, [None] * 4, [None] * 4

    def ring(part, total):
        sums_in[part] = total.astype(BF16)
        to_ring[part] = [
            push(
                sums_in.at[part, pl.ds(start_of(other["tensor"]), shard)],
                ring_in.at[part, k],
                other,
            )
            for k, other in enumerate(others)
        ]

    def spread(part):
        total = sums_in[part, pl.ds(start_of(tensor), shard), :].astype(F32)
        for k, copy in enumerate(to_ring[part]):
            copy.wait_recv()
            total = total + ring_in[part, k].astype(F32)
        ring_all[part, tensor] = total.astype(BF16)
        to_all[part] = [
            push(ring_all.at[part, tensor], ring_all.at[part, tensor], other) for other in others
        ]

    def gather(part):
        for copy in to_all[part]:
            copy.wait_recv()
        for owner in range(tensors - 1):
            whole[part, owner * shard : (owner + 1) * shard] = ring_all[part, owner]
        rest = (tensors - 1) * shard
        whole[part, rest:] = ring_all[part, tensors - 1, tensors * shard - half :]
        if part < 3:
            to_near[part] = [
                push(whole.at[part], near_in.at[part, 0], beside),
                push(whole.at[part], near_in.at[part, 1], across),
            ]

    loads[1].wait()
    loads[2].wait()
    wo_sum[...] = (wo_core[0].astype(F32) + core_out[:quarter].astype(F32)).astype(BF16)
    pl.semaphore_wait(barrier, 3 + len(others))
    wo_to_chip = push(wo_sum.at[chip_start(1 - chip)], wo_half.at[1], across)
    loads[0].wait()
    weights(3)
    weights(0)

    rows_grad(3, core_out)
    to_core = push(core_out, core_in.at[0], beside)
    left_out[0] = joined_far(3).astype(BF16)
    to_left = push(left_out.at[0], left_in.at[0], beside)
    wo_to_chip.wait_recv()
    wo_half[0] = (wo_sum[chip_start(chip), :].astype(F32) + wo_half[1].astype(F32)).astype(BF16)
    wo_to_ring = [
        push(wo_half.at[0, pl.ds(part_start(other["tensor"]), part_rows)], wo_ring.at[k], other)
        for k, other in enumerate(others)
    ]
    ring(0, joined_far(0))
    rows_grad(2, hold)
    to_core.wait_recv()

    @pl.loop(0, row_count // chunk)
    def _(i):
        rows = pl.ds(pl.multiple_of(i * chunk, chunk), chunk)
        chip_out[rows, :] = (hold[rows, :] + core_in[0, rows, :].astype(F32)).astype(BF16)

    to_left.wait_recv()
    left_out[1] = (left_out[0].astype(F32) + left_in[0].astype(F32)).astype(BF16)
    to_left = push(left_out.at[1], left_in.at[1], across)
    to_chip = push(chip_out, chip_in, across)
    weights(1)
    wo_total = wo_half[0, pl.ds(part_start(tensor), part_rows), :].astype(F32)
    for k, copy in enumerate(wo_to_ring):
        copy.wait_recv()
        wo_total = wo_total + wo_ring[k].astype(F32)
    wo_all[tensor] = wo_total.astype(BF16)
    wo_to_all = [push(wo_all.at[tensor], wo_all.at[tensor], other) for other in others]
    to_left.wait_recv()
    ring(3, left_out[1].astype(F32) + left_in[1].astype(F32))
    ring(1, joined_far(1))
    weights(2)
    spread(0)
    to_core.wait_send()
    sent[:] = [copy for copy in sent if copy is not to_core]
    rows_grad(1, core_out)
    to_core_2 = push(core_out, core_in.at[1], beside)
    ring(2, joined_far(2))
    spread(3)
    rows_grad(0, hold)
    spread(1)
    for copy in wo_to_all:
        copy.wait_recv()
    for owner in range(tensors):
        start = min(owner * part_rows, most_rows - part_rows)
        wo_half[2, start : start + part_rows] = wo_all[owner]
    wo_to_other = push(wo_half.at[2], wo_half.at[3], across)
    gather(0)
    to_core_2.wait_recv()
    to_chip.wait_recv()

    vec_out[0, :8] = jnp.zeros((8, vec_out.shape[2]), F32)
    vec_out[0, 8:] = given_ref[...]
    chunks = row_count // chunk

    def chunk_rows(i):
        return pl.ds(pl.multiple_of(i * chunk, chunk), chunk)

    def row_loads(i):
        slot = i % 2
        return [
            pltpu.make_async_copy(gh_ref.at[chunk_rows(i)], gh_s.at[slot], local_sem.at[3 + slot]),
            pltpu.make_async_copy(rows_ref.at[chunk_rows(i)], rows_s.at[slot], local_sem.at[5 + slot]),
        ]

    for load in row_loads(0):
        load.start()

    @pl.loop(0, chunks)
    def _(i):
        @pl.when(i + 1 < chunks)
        def _():
            for load in row_loads(i + 1):
                load.start()

        for load in row_loads(i):
            load.wait()

        rows = chunk_rows(i)
        unit, rate = normalize(rows_s[i % 2, :, :width].astype(F32))
        grad = hold[rows, :] + core_in[1, rows, :].astype(F32) + chip_in[rows, :].astype(F32)
        back = normalize_back(unit, rate, grad * gain_ref[...])
        out = (gh_s[i % 2] + back).astype(BF16)

        @pl.when(i < prompt_rows // chunk)
        def _():
            prompt_ref[0, rows, :] = out

        @pl.when(i >= prompt_rows // chunk)
        def _():
            cont_ref[0, chunk_rows(i - prompt_rows // chunk), :] = out

        vec_out[0, 0:1, :width] += jnp.sum(grad * unit, axis=0, keepdims=True)
        vec_out[0, 1:2, :width] += jnp.sum(grad, axis=0, keepdims=True)

    spread(2)
    for row, part in ((2, 0), (3, 2)):
        cols = pl.ds(pl.multiple_of(place * own, own), own)
        vec_out[0, row : row + 1, cols] = sums[part, 0:1, :]
        left = slice(part * HEAD, (part + 1) * HEAD)
        vec_out[0, row : row + 1, width - HEAD : width] = sums[3, 0:1, left]
    gather(1)

    def forward(part):
        to_near[part][1].wait_recv()
        return push(near_in.at[part, 1], near_in.at[part, 2], beside)

    def store(part, passed):
        to_near[part][0].wait_recv()
        passed.wait_recv()
        sources = [whole.at[part]] + [near_in.at[part, i] for i in range(3)]
        for distance, source in enumerate(sources):
            for block in range(count):

                @pl.when(place ^ distance == block)
                def _():
                    start = part * width + block * own
                    qkv_ref[:, start : start + own] = source[...]

    levels = (
        (place, [(place ^ away, {"ctx": place ^ away}) for away in range(1, count)]),
        (tensor, [(other["tensor"], other) for other in others]),
        (fsdp, [(1 - fsdp, far)]),
    )

    def exchange(level):
        own_at, partners = levels[level]
        vec_in[level, own_at] = vec_out[level]
        return [push(vec_out.at[level], vec_in.at[level, own_at], other) for _, other in partners]

    def add(level, copies):
        for copy in copies:
            copy.wait_recv()
        total = vec_in[level, 0]
        for at in range(1, len(copies) + 1):
            total = total + vec_in[level, at]
        vec_out[level + 1] = total

    step = exchange(0)
    passed_0 = forward(0)
    gather(2)
    add(0, step)
    step = exchange(1)
    passed_1 = forward(1)
    gather(3)
    store(0, passed_0)
    add(1, step)
    step = exchange(2)
    wo_to_other.wait_recv()
    for at in range(2):

        @pl.when(chip == at)
        def _():
            wo_core[0, :most_rows] = wo_half[2 + at]
            wo_core[0, most_rows:] = wo_half[3 - at, 2 * most_rows - quarter :]

    wo_to_core = push(wo_core.at[0], wo_core.at[1], beside)
    for part in range(3):
        cols = slice((part + 1) * width - HEAD, (part + 1) * width)
        qkv_ref[:, cols] = whole[3, :, part * HEAD : (part + 1) * HEAD]
    add(2, step)
    vec_ref[...] = vec_out[3]
    passed_2 = forward(2)
    store(1, passed_1)
    wo_to_core.wait_recv()
    core = place % 2
    for away in range(2):
        wo_ref[pl.ds(pl.multiple_of((core ^ away) * quarter, 16), quarter), :] = wo_core[away]
    store(2, passed_2)
    for copy in sent:
        copy.wait_send()


def tail(
    grads, w_own, normed, rows, grad_hidden, gain, vectors, out_keep, out_come, prompt_rows, after=()
):
    count, depth, row_count = normed.shape
    width, cols = w_own.shape
    half, own = width // 2, 2 * PAIRS * HEAD
    tensors = lax.axis_size("tensor")
    shard = -(-half // tensors // 16) * 16
    padded = vectors.shape[1]
    in_vmem = pl.BlockSpec(memory_space=pltpu.VMEM)
    vmem = lambda *shape, kind=BF16: pltpu.VMEM(shape, kind)
    copies = 4 + 4 * 2 * (tensors - 1) + 4 + 3 * 3 + 2 + count + tensors - 1 + 2 * (tensors - 1) + 3
    given = len(grads) + 8
    quarter = width // 4
    most_rows = -(-quarter // 2 // 16) * 16
    part_rows = -(-most_rows // tensors // 16) * 16

    def body(*refs):
        tail_kernel(prompt_rows, *refs[:given], *refs[given + len(after) :])

    return pl.pallas_call(
        body,
        in_specs=[in_vmem] * (len(grads) + 1) + [ANYWHERE] * 5 + [in_vmem] * 2 + [ANYWHERE] * len(after),
        out_specs=[in_vmem] * 5,
        out_shape=[
            shape_of(1, prompt_rows, width),
            shape_of(1, row_count - prompt_rows, width),
            shape_of(half, 3 * width),
            shape_of(half, width),
            shape_of(16, padded, kind=F32),
        ],
        scratch_shapes=[
            vmem(*normed.shape),
            vmem(2, TILE, width),
            vmem(2, TILE, width, kind=F32),
            vmem(row_count, cols),
            vmem(row_count, width, kind=F32),
            vmem(row_count, width),
            vmem(2, row_count, width),
            vmem(row_count, width),
            vmem(row_count, width),
            vmem(depth, own, kind=F32),
            vmem(4, half, own, kind=F32),
            vmem(4, half, own),
            vmem(4, half, own),
            vmem(4, 8, own, kind=F32),
            vmem(4, half, own),
            vmem(4, tensors - 1, shard, own),
            vmem(4, tensors, shard, own),
            vmem(4, half, own),
            vmem(3, 3, half, own),
            vmem(2, half, own),
            vmem(2, half, own),
            vmem(4, 16, padded, kind=F32),
            vmem(3, max(count, tensors), 16, padded, kind=F32),
            vmem(quarter, width),
            vmem(tensors - 1, part_rows, width),
            vmem(4, most_rows, width),
            vmem(tensors, part_rows, width),
            vmem(2, quarter, width),
            pltpu.SemaphoreType.DMA((7,)),
            pltpu.SemaphoreType.DMA((copies,)),
            pltpu.SemaphoreType.DMA((copies,)),
        ],
        compiler_params=pltpu.CompilerParams(
            vmem_limit_bytes=62 << 20, collective_id=1, has_side_effects=True
        ),
        cost_estimate=pl.CostEstimate(
            flops=4 * count * row_count * width * cols, bytes_accessed=30 << 20, transcendentals=0
        ),
        name="tail",
    )(*grads, w_own, normed, rows, grad_hidden, out_keep, out_come, gain[None], vectors, *after)


def own_columns(matrix, place):
    width = matrix.shape[1] // 3
    own = 2 * PAIRS * HEAD
    blank = jnp.zeros((matrix.shape[0], TILE - HEAD), matrix.dtype)
    pieces = []
    for part in range(3):
        whole = matrix[:, part * width : (part + 1) * width]
        pieces += [
            lax.dynamic_slice_in_dim(whole, place * own, own, 1),
            whole[:, width - HEAD :],
            blank,
        ]
    return jnp.concatenate(pieces, axis=1)


def local_heads(
    prompt_in,
    cont_in,
    cont_seg,
    ln1_gain,
    ln1_bias,
    w_qkv,
    qv_bias,
    w_out,
    out_bias,
    ln2_gain,
    ln2_bias,
    w_fc,
    fc_bias,
    w_proj,
    proj_bias,
    prompt_cot,
    cont_cot,
):
    width = prompt_in.shape[2]
    prompt_rows, cont_rows = prompt_in.shape[1], cont_in.shape[1]
    row_count = prompt_rows + cont_rows
    count = lax.axis_size("ctx")
    place = lax.axis_index("ctx")
    core, chip = place % 2, place // 2
    fsdp = lax.axis_index("fsdp")
    tensor = lax.axis_index("tensor")
    tensors = lax.axis_size("tensor")
    own_width = 2 * PAIRS * HEAD
    half, hidden_units = w_fc.shape
    quarter = half // 2
    eighth = quarter // 2
    padded = (width + TILE - 1) // TILE * TILE
    at = place.reshape(1)
    spot = jnp.stack([core, fsdp, tensor, jnp.int32(tensors), place])

    zero_bias = jnp.zeros_like(qv_bias[0])
    col_bias = own_columns(jnp.concatenate([qv_bias[0], zero_bias, qv_bias[1]])[None], place)[0]
    normed, q, k, v, kt, vt, w_own, rows_own, grad_layer, grad_flip, *mines, out_own = open_up(
        prompt_in,
        cont_in,
        w_qkv,
        w_fc,
        w_proj,
        w_out,
        fc_bias,
        prompt_cot,
        cont_cot,
        ln1_gain,
        ln1_bias,
        col_bias,
        count,
    )

    mine, one_away, three_away, near_far = mines

    labels = cont_seg[0].reshape(count, cont_rows)
    seg_col, seg_row = labels[:, :, None], labels[:, None, :]
    lse, outs, came, last_out, two_away, one_far, *others, out_full = attend(
        q, k, vt, seg_col, seg_row, prompt_rows, (mine, near_far, one_away, three_away), out_own
    )
    mine_2, near_2, one_2, one_far_2, three_2, two_2 = others
    three_far, two_far = swap(three_away, "fsdp", 1), swap(two_away, "fsdp", 1)
    pieces = (outs, came, last_out)
    hidden, mlp_low, mlp_flip = merge(
        at, rows_own, out_full, out_bias, ln2_gain, ln2_bias, pieces
    )

    steps_away = (0, 1, 3, 2)
    given = (mlp_low, grad_layer, mlp_flip, grad_flip)
    mlp_out, grad_mlp_in, keep_1, send_1, bias_first, proj_0, proj_1 = mlp(
        4,
        *given, (mine, one_away), (near_far, one_far), (mine_2, one_2), (near_2, one_far_2)
    )
    three_far, two_far = behind((three_far, two_far), bias_first)
    three_far_2, two_far_2 = swap(three_far, "ctx", 1), swap(two_far, "ctx", 1)
    mlp_out, grad_mlp_in, keep_2, send_2, bias_last, proj_2, proj_3 = mlp(
        5,
        *given,
        (three_away, two_away),
        (three_far, two_far),
        (three_2, two_2),
        (three_far_2, two_far_2),
        before=(mlp_out, grad_mlp_in),
    )
    grad_fc_bias = jnp.concatenate([bias_first, bias_last], axis=0)
    proj_2, proj_3 = behind((proj_2, proj_3), mlp_out)
    come_p = [
        turn(part, "tensor", -steps_away[k + 1]) for k, part in enumerate((proj_1, proj_2, proj_3))
    ]
    layer_out, grad_hidden, grads_own, grad_last, *rest = bend(
        mlp_out,
        grad_mlp_in,
        hidden,
        grad_layer,
        out_full,
        ln2_gain,
        proj_bias,
        pieces,
        (proj_2, proj_3),
    )
    grads_all, (out_keep, out_send, sums2) = [grads_own, *rest[:-3]], rest[-3:]

    def added(left, right):
        return left.astype(F32) + right.astype(F32)

    def back(pair, tile, heads, grads, outs, after=()):
        return attend_back(
            pair, tile, heads, at, q, k, v, kt, lse, seg_col, seg_row, grads, outs, prompt_rows, after
        )

    (send_2,) = behind((send_2,), grads_own)
    come_o = swap(out_send, "ctx", 1)
    come_1, come_2 = swap(send_1, "ctx", 2), swap(send_2, "ctx", 2)
    grads_pair = [back(0, 0, 2, grads_all, outs)]
    grads_left = back(PAIRS, 0, 1, [grad_last], last_out[None, None], (grads_pair[0][0],))
    come_o, come_1, come_2, *come_p = behind((come_o, come_1, come_2, *come_p), grads_left[0])
    sums_f = [
        added(keep[k], come[k]).astype(BF16)
        for keep, come in ((keep_1, come_1), (keep_2, come_2))
        for k in range(2)
    ]
    near_p, far_p = (
        sum((come[away].astype(F32) for come in come_p), proj_0[away].astype(F32)).astype(BF16)
        for away in range(2)
    )
    near_o, far_o = (added(out_keep[away], come_o[away]).astype(BF16) for away in range(2))
    come_f = [turn(sums_f[k], "tensor", -steps_away[k]) for k in range(1, tensors)]
    come_p, come_o = swap(far_p, "fsdp", 1), swap(far_o, "fsdp", 1)
    grads_pair.append(back(1, 1, 2, grads_all, outs, (*sums_f[1:], far_p, far_o, grads_left[0])))
    come_p, *come_f = behind((come_p, *come_f), grads_pair[1][0])
    near_f, far_f = (
        sum((come[away].astype(F32) for come in come_f), sums_f[0][away].astype(F32)).astype(BF16)
        for away in range(2)
    )
    sum_p = added(near_p, come_p).astype(BF16)
    ordered = [entry[part] for part in range(3) for entry in (*grads_pair, grads_left)]
    vectors = jnp.concatenate([sums2, jnp.zeros((tensors, hidden_units), F32)], axis=0)
    for k, distance in enumerate(steps_away):
        vectors = lax.dynamic_update_slice(
            vectors, grad_fc_bias[k], (4 + (tensor - distance) % tensors, 0)
        )
    vectors = jnp.pad(vectors, ((0, 0), (0, padded - width)))
    prompt_grad, cont_grad, sum_qkv, sum_out, late = tail(
        ordered,
        w_own,
        normed,
        rows_own,
        grad_hidden,
        ln1_gain,
        vectors,
        near_o,
        come_o,
        prompt_rows,
        (far_f, sum_p),
    )
    come_f, come_p = behind((swap(far_f, "fsdp", 1), swap(sum_p, "ctx", 2)), late)
    sum_f, sum_p = added(near_f, come_f).astype(BF16), added(sum_p, come_p).astype(BF16)
    prompt_grad, cont_grad, sum_qkv, sum_out = behind(
        (prompt_grad, cont_grad, sum_qkv, sum_out), sum_f, sum_p
    )
    by_away = [sum_f] + [swap(sum_f, "ctx", away) for away in range(1, count)]
    halves_f = [
        jnp.concatenate(in_order(by_away[i], by_away[i ^ 2], chip), axis=0) for i in range(2)
    ]
    own_fc = jnp.concatenate(in_order(*halves_f, core), axis=0).astype(F32)
    own_proj = jnp.concatenate(in_order(sum_p, swap(sum_p, "ctx", 1), core), axis=0).astype(F32).T

    fc_bias_sum = lax.dynamic_index_in_dim(late, 12 + tensor, 0, False)[:hidden_units]
    return (
        layer_out[:prompt_rows][None],
        layer_out[prompt_rows:][None],
        prompt_grad,
        cont_grad,
        late[0, :width],
        late[1, :width],
        sum_qkv.astype(F32),
        late[2:4, :width],
        sum_out.astype(F32),
        late[8, :width],
        late[9, :width],
        late[10, :width],
        own_fc,
        fc_bias_sum,
        own_proj,
        late[11, :width],
    )


def solution(mesh):
    placed = (
        P(("fsdp", "tensor"), "ctx", None),
        P(("fsdp", "tensor"), "ctx", None),
        P(("fsdp", "tensor"), None),
        P(),
        P(),
        P("fsdp", None),
        P(),
        P("fsdp", None),
        P(),
        P(),
        P(),
        P("fsdp", "tensor"),
        P("tensor"),
        P("tensor", "fsdp"),
        P(),
        P(("fsdp", "tensor"), "ctx", None),
        P(("fsdp", "tensor"), "ctx", None),
    )
    by_heads = HEADS // mesh.shape["ctx"] == PAIRS * 2 and HEADS % mesh.shape["ctx"] == 1
    return jax.shard_map(
        local_heads if by_heads else local_rows,
        mesh=mesh,
        in_specs=placed,
        out_specs=(
            P(("fsdp", "tensor"), "ctx", None),
            P(("fsdp", "tensor"), "ctx", None),
            P(("fsdp", "tensor"), "ctx", None),
            P(("fsdp", "tensor"), "ctx", None),
            P(),
            P(),
            P("fsdp", None),
            P(),
            P("fsdp", None),
            P(),
            P(),
            P(),
            P("fsdp", "tensor"),
            P("tensor"),
            P("tensor", "fsdp"),
            P(),
        ),
        check_vma=False,
    )
```

```python
import functools

import jax
import jax.numpy as jnp
from jax import lax
from jax.experimental import pallas as pl
from jax.experimental.pallas import tpu as pltpu
from jax.sharding import PartitionSpec as P

HEADS = 17
HEAD = 64


def passed_along(value, axis, steps):
    count = lax.axis_size(axis)
    leading, last = (max(0, -steps), min(count, count - steps))
    return lax.ppermute(value, axis, [(source, source + steps) for source in range(leading, last)])


def layer_norm(values, norm_gain, norm_bias):
    average = jnp.mean(values, axis=-1, keepdims=True)
    centred = values - average
    variance = jnp.mean(centred * centred, axis=-1, keepdims=True)
    return centred * lax.rsqrt(variance + 1e-05) * norm_gain + norm_bias


def gelu_tanh(values):
    return jax.nn.gelu(values, approximate=True)


def inner_first(left_op, right_op):
    return lax.dot_general(
        left_op, right_op, (((0,), (0,)), ((), ())), preferred_element_type=jnp.float32
    )


def inner_last(left_op, right_op):
    return lax.dot_general(
        left_op, right_op, (((1,), (1,)), ((), ())), preferred_element_type=jnp.float32
    )


def to_heads(values):
    return jnp.swapaxes(values.reshape(values.shape[0], HEADS, HEAD), 0, 1)


def from_heads(values):
    return jnp.swapaxes(values, 0, 1).reshape(values.shape[1], values.shape[0] * values.shape[2])


def fetch_prompt(rows_kv):
    return lax.all_gather(rows_kv, "ctx", axis=0, tiled=True)


def local_rows(
    prompt_in,
    cont_in,
    cont_seg,
    ln1_gain,
    ln1_bias,
    w_qkv,
    qv_bias,
    w_out,
    out_bias,
    ln2_gain,
    ln2_bias,
    w_fc,
    fc_bias,
    w_proj,
    proj_bias,
    prompt_cot,
    cont_cot,
):
    model_width = prompt_in.shape[2]
    prompt_rows = prompt_in.shape[1]
    cont_rows = cont_in.shape[1]
    row_count = prompt_rows + cont_rows
    ctx_count = lax.axis_size("ctx")
    ctx_place = lax.axis_index("ctx")
    prompt_total = prompt_rows * ctx_count
    qkv_full, out_full = (
        lax.all_gather(w_qkv.astype(jnp.bfloat16), "fsdp", axis=0, tiled=True),
        lax.all_gather(w_out.astype(jnp.bfloat16), "fsdp", axis=0, tiled=True),
    )
    fc_full, proj_full = (
        lax.all_gather(w_fc.astype(jnp.bfloat16), "fsdp", axis=0, tiled=True),
        lax.all_gather(w_proj.astype(jnp.bfloat16), "fsdp", axis=1, tiled=True),
    )
    row_ids = jnp.arange(row_count, dtype=jnp.int32)
    labels_all = cont_seg[0]
    own_labels = lax.dynamic_slice_in_dim(labels_all, ctx_place * cont_rows, cont_rows)
    earlier_labels = lax.dynamic_slice_in_dim(
        labels_all, jnp.maximum(ctx_place - 1, 0) * cont_rows, cont_rows
    )
    query_labels = jnp.concatenate([jnp.full((prompt_rows,), -1, jnp.int32), own_labels])
    query_prompt = ctx_place * prompt_rows + row_ids
    query_cont = ctx_place * cont_rows + row_ids - prompt_rows
    is_cont = row_ids >= prompt_rows
    prompt_ids = jnp.arange(prompt_total, dtype=jnp.int32)
    near_ids = (ctx_place - 1) * cont_rows + jnp.arange(2 * cont_rows, dtype=jnp.int32)
    near_labels = jnp.concatenate([earlier_labels, own_labels])
    allowed_far = is_cont[:, None] | (prompt_ids[None, :] <= query_prompt[:, None])
    allowed_near = (
        (query_labels[:, None] == near_labels[None, :])
        & (near_ids[None, :] <= query_cont[:, None])
        & (near_ids[None, :] >= 0)
    )
    allowed = jnp.concatenate([allowed_far, allowed_near], 1)
    inputs = jnp.concatenate([prompt_in[0], cont_in[0]], 0).astype(jnp.float32)
    normed, norm1_back = jax.vjp(layer_norm, inputs, ln1_gain, ln1_bias)
    normed_low = normed.astype(jnp.bfloat16)
    projected = jnp.dot(normed_low, qkv_full, preferred_element_type=jnp.float32)
    queries = (projected[:, :model_width] + qv_bias[0]).astype(jnp.bfloat16)
    key_value = jnp.concatenate(
        [projected[:, model_width : 2 * model_width], projected[:, 2 * model_width :] + qv_bias[1]],
        1,
    ).astype(jnp.bfloat16)
    own_cont_kv = key_value[prompt_rows:]
    earlier_kv = passed_along(own_cont_kv, "ctx", 1)
    prompt_kv = fetch_prompt(key_value[:prompt_rows])
    keys_all = jnp.concatenate([prompt_kv, earlier_kv, own_cont_kv], 0)
    query_heads = to_heads(queries)
    key_heads = to_heads(keys_all[:, :model_width])
    value_heads = to_heads(keys_all[:, model_width:])

    def head_forward(operands):
        query_head, key_head, value_head = operands
        scores = inner_last(query_head, key_head) * 0.125
        scores = jnp.where(allowed, scores, -1e30)
        row_max = jnp.max(scores, axis=1, keepdims=True)
        exponent = jnp.exp(scores - row_max)
        row_total = jnp.sum(exponent, axis=1, keepdims=True)
        probability = (exponent / row_total).astype(jnp.bfloat16)
        head_out = jnp.dot(probability, value_head, preferred_element_type=jnp.float32)
        return (head_out.astype(jnp.bfloat16), (row_max + jnp.log(row_total))[:, 0])

    heads_out, logsum = lax.map(head_forward, (query_heads, key_heads, value_heads))
    attended = from_heads(heads_out)
    hidden = inputs + jnp.dot(attended, out_full, preferred_element_type=jnp.float32) + out_bias
    mlp_in, norm2_back = jax.vjp(layer_norm, hidden, ln2_gain, ln2_bias)
    mlp_low = mlp_in.astype(jnp.bfloat16)
    mlp_rows = lax.all_gather(mlp_low, "tensor", axis=0, tiled=True)
    pre_act = jnp.dot(mlp_rows, fc_full, preferred_element_type=jnp.float32) + fc_bias
    activated, gelu_back = jax.vjp(gelu_tanh, pre_act)
    act_low = activated.astype(jnp.bfloat16)
    partial_out = jnp.dot(act_low, proj_full, preferred_element_type=jnp.float32)
    mlp_out = lax.psum_scatter(
        partial_out.astype(jnp.bfloat16), "tensor", scatter_dimension=0, tiled=True
    ).astype(jnp.float32)
    layer_out = (hidden + mlp_out + proj_bias).astype(jnp.bfloat16)
    grad_layer = jnp.concatenate([prompt_cot[0], cont_cot[0]], 0)
    grad_float = grad_layer.astype(jnp.float32)
    grad_proj_bias = jnp.sum(grad_float, axis=0)
    grad_rows = lax.all_gather(grad_layer, "tensor", axis=0, tiled=True)
    grad_w_proj = inner_first(act_low, grad_rows)
    grad_act = inner_last(grad_rows, proj_full)
    grad_pre = gelu_back(grad_act)[0].astype(jnp.bfloat16)
    grad_fc_bias = jnp.sum(grad_pre.astype(jnp.float32), axis=0)
    grad_w_fc = inner_first(mlp_rows, grad_pre)
    grad_mlp_part = inner_last(grad_pre, fc_full)
    grad_mlp_in = lax.psum_scatter(grad_mlp_part, "tensor", scatter_dimension=0, tiled=True)
    grad_hidden_norm, grad_ln2_gain, grad_ln2_bias = norm2_back(grad_mlp_in)
    grad_hidden = grad_float + grad_hidden_norm
    grad_out_bias = jnp.sum(grad_hidden, axis=0)
    grad_branch = grad_hidden.astype(jnp.bfloat16)
    grad_w_out = inner_first(attended, grad_branch)
    grad_attended = inner_last(grad_branch, out_full).astype(jnp.bfloat16)
    prompt_again = fetch_prompt(key_value[:prompt_rows])
    keys_back = jnp.concatenate([prompt_again, earlier_kv, own_cont_kv], 0)
    key_back_heads = to_heads(keys_back[:, :model_width])
    value_back_heads = to_heads(keys_back[:, model_width:])

    def head_backward(operands):
        query_head, key_head, value_head, grad_head, logsum_head = operands
        scores = inner_last(query_head, key_head) * 0.125
        scores = jnp.where(allowed, scores, -1e30)
        probability = jnp.exp(scores - logsum_head[:, None])
        prob_low = probability.astype(jnp.bfloat16)
        grad_prob = inner_last(grad_head, value_head)
        centre = jnp.sum(probability * grad_prob, axis=1, keepdims=True)
        grad_scores = (probability * (grad_prob - centre)).astype(jnp.bfloat16)
        grad_query = jnp.dot(grad_scores, key_head, preferred_element_type=jnp.float32) * 0.125
        grad_key = inner_first(grad_scores, query_head) * 0.125
        grad_value = inner_first(prob_low, grad_head)
        return (grad_query, grad_key, grad_value)

    head_operands = (query_heads, key_back_heads, value_back_heads, to_heads(grad_attended), logsum)
    grad_q_heads, grad_k_heads, grad_v_heads = lax.map(head_backward, head_operands)
    grad_queries = from_heads(grad_q_heads).astype(jnp.bfloat16)
    grad_kv = jnp.concatenate([from_heads(grad_k_heads), from_heads(grad_v_heads)], 1)
    prompt_grad_kv = lax.psum_scatter(
        grad_kv[:prompt_total], "ctx", scatter_dimension=0, tiled=True
    )
    from_later = passed_along(
        grad_kv[prompt_total : prompt_total + cont_rows].astype(jnp.bfloat16), "ctx", -1
    ).astype(jnp.float32)
    cont_grad_kv = grad_kv[prompt_total + cont_rows :] + from_later
    grad_kv_rows = jnp.concatenate([prompt_grad_kv, cont_grad_kv], 0).astype(jnp.bfloat16)
    grad_projected = jnp.concatenate([grad_queries, grad_kv_rows], 1)
    grad_qv_bias = jnp.stack(
        [
            jnp.sum(grad_queries.astype(jnp.float32), axis=0),
            jnp.sum(grad_kv_rows[:, model_width:].astype(jnp.float32), axis=0),
        ]
    )
    grad_w_qkv = inner_first(normed_low, grad_projected)
    grad_normed = inner_last(grad_projected, qkv_full)
    grad_inputs_norm, grad_ln1_gain, grad_ln1_bias = norm1_back(grad_normed)
    grad_inputs = (grad_hidden + grad_inputs_norm).astype(jnp.bfloat16)
    shard_qkv, shard_out = (
        lax.psum_scatter(
            grad_w_qkv.astype(jnp.bfloat16), "fsdp", scatter_dimension=0, tiled=True
        ).astype(jnp.float32),
        lax.psum_scatter(
            grad_w_out.astype(jnp.bfloat16), "fsdp", scatter_dimension=0, tiled=True
        ).astype(jnp.float32),
    )
    sum_qkv, sum_out = lax.psum((shard_qkv, shard_out), ("ctx", "tensor"))
    sum_fc, sum_proj, sum_fc_bias = lax.psum(
        (grad_w_fc, grad_w_proj, grad_fc_bias), ("fsdp", "ctx")
    )
    fsdp_place = lax.axis_index("fsdp")
    fsdp_rows = w_fc.shape[0]
    own_fc = lax.dynamic_slice_in_dim(sum_fc, fsdp_place * fsdp_rows, fsdp_rows, 0)
    own_proj = lax.dynamic_slice_in_dim(sum_proj, fsdp_place * fsdp_rows, fsdp_rows, 1)
    small_sums = lax.psum(
        (
            grad_ln1_gain,
            grad_ln1_bias,
            grad_qv_bias,
            grad_out_bias,
            grad_ln2_gain,
            grad_ln2_bias,
            grad_proj_bias,
        ),
        ("fsdp", "ctx", "tensor"),
    )
    return (
        layer_out[:prompt_rows][None],
        layer_out[prompt_rows:][None],
        grad_inputs[:prompt_rows][None],
        grad_inputs[prompt_rows:][None],
        small_sums[0],
        small_sums[1],
        sum_qkv,
        small_sums[2],
        sum_out,
        small_sums[3],
        small_sums[4],
        small_sums[5],
        own_fc,
        sum_fc_bias,
        own_proj,
        small_sums[6],
    )


PAIRS = 2
TILE = 2 * HEAD
BF16 = jnp.bfloat16
F32 = jnp.float32
LOG2E = 1.4426950408889634
SCALE2 = 0.125 * LOG2E
HINT = 0.2
NN = (((1,), (0,)), ((), ()))
NT = (((1,), (1,)), ((), ()))
TN = (((0,), (0,)), ((), ()))


def dot(left_op, right_op, dims=NN):
    return lax.dot_general(left_op, right_op, dims, preferred_element_type=F32)


def swap(value, axis, bit):
    count = lax.axis_size(axis)
    return lax.ppermute(value, axis, [(place, place ^ bit) for place in range(count)])


def turn(value, axis, steps):
    count = lax.axis_size(axis)
    return lax.ppermute(value, axis, [(place, (place + steps) % count) for place in range(count)])


def halves(values, heads=2):
    lane = lax.broadcasted_iota(jnp.int32, values.shape, 1)
    zero = jnp.zeros_like(values)
    return [jnp.where((lane < HEAD) == (head == 0), values, zero) for head in range(heads)]


ANYWHERE = pl.BlockSpec(memory_space=pl.ANY)


def blocks(*shape):
    return pl.BlockSpec(shape, lambda i, *_: (0,) * len(shape))


def shape_of(*shape, kind=BF16):
    return jax.ShapeDtypeStruct(shape, kind)


def launch(
    kernel, name, scalars, grid, operands, in_specs, outs, scratch=(), limit=48, flops=0, traffic=16, exps=0, after=(), carry=(), aliases=None, meet=None
):
    out_specs, out_shapes = [out[0] for out in outs], [out[1] for out in outs]
    given = len(scalars) + len(operands)
    tied = given + len(after) + len(carry)

    def body(*refs):
        made = refs[tied : tied + len(outs)]
        kernel(*refs[:given], *made, *refs[tied + len(outs) + len(carry) :])

    links = {len(scalars) + here: there for here, there in (aliases or {}).items()}
    links.update({given + len(after) + i: len(outs) + i for i in range(len(carry))})
    out = pl.pallas_call(
        body,
        grid_spec=pltpu.PrefetchScalarGridSpec(
            num_scalar_prefetch=len(scalars),
            grid=grid,
            in_specs=list(in_specs) + [ANYWHERE] * (len(after) + len(carry)),
            out_specs=out_specs + [ANYWHERE] * len(carry),
            scratch_shapes=list(scratch),
        ),
        out_shape=out_shapes + [shape_of(*entry.shape, kind=entry.dtype) for entry in carry],
        input_output_aliases=links,
        compiler_params=pltpu.CompilerParams(
            vmem_limit_bytes=limit << 20, collective_id=meet, has_side_effects=meet is not None
        ),
        cost_estimate=pl.CostEstimate(
            flops=int(flops * HINT),
            bytes_accessed=int(traffic * HINT * (1 << 20)),
            transcendentals=int(exps * HINT),
        ),
        name=name,
    )(*scalars, *operands, *after, *carry)
    return (out[: len(outs)], *out[len(outs) :]) if carry else out


def behind(arrays, *tokens):
    out = launch(
        lambda *refs: None, "behind", (), (1,), (), (), (), after=tokens, carry=tuple(arrays)
    )
    return out[1:]


def whole_out(*shape, kind=BF16):
    return blocks(*shape), shape_of(*shape, kind=kind)


def in_order(own, other, place):
    first = place == 0
    return jnp.where(first, own, other), jnp.where(first, other, own)


def open_kernel(*refs):
    prompt_ref, cont_ref, w_ref, fc_ref, proj_ref, wo_ref, gp_ref, gc_ref = refs[:8]
    vector_ref, col_bias_ref = refs[8:10]
    norm_ref, q_ref, k_ref, v_ref, kt_ref, vt_ref = refs[10:16]
    w_own_ref, rows_ref, g_ref, gt_ref, mine_ref, one_ref, three_ref, far_ref, out_ref = refs[16:25]
    (
        rows_t,
        w_s,
        w_own,
        w_out,
        fc_s,
        proj_s,
        mine_s,
        g_t,
        normed,
        norms,
        tall_s,
        flat_s,
        turned,
        wo_f,
        wo_s,
        local_sem,
        send_sem,
        recv_sem,
        out_sem,
    ) = refs[25:]
    place = lax.axis_index("ctx")
    fsdp = lax.axis_index("fsdp")
    tensor = lax.axis_index("tensor")
    tensors = lax.axis_size("tensor")
    core = place % 2
    width, row_count = rows_t.shape[1], rows_t.shape[2]
    prompt_rows = prompt_ref.shape[1]
    half, quarter = width // 2, width // 4
    own = 2 * PAIRS * HEAD
    beside, across, far = {"ctx": place ^ 1}, {"ctx": place ^ 2}, {"fsdp": 1 - fsdp}
    others = [{"tensor": lax.rem(tensor + k, tensors)} for k in range(1, tensors)]

    barrier = pltpu.get_barrier_semaphore()
    for partner in (beside, across, far, *others):
        pl.semaphore_signal(barrier, inc=1, device_id=partner, device_id_type=pl.DeviceIdType.MESH)

    def load(source, target, at):
        copy = pltpu.make_async_copy(source, target, local_sem.at[at])
        copy.start()
        return copy

    def spans(ref):
        return ref.at[:, :prompt_rows], ref.at[:, prompt_rows:]

    own_prompt, own_cont = spans(rows_t.at[0])
    load_rows = [load(prompt_ref, own_prompt, 0), load(cont_ref, own_cont, 1)]
    load_w = load(w_ref, w_s, 2)
    mine_rows = pl.ds(pl.multiple_of(core * quarter, 16), quarter)
    load_mine = [load(fc_ref.at[mine_rows], fc_s, 3), load(proj_ref.at[mine_rows], proj_s, 4)]
    g_prompt, g_cont = spans(g_t)
    load_g = [load(gp_ref, g_prompt, 5), load(gc_ref, g_cont, 6)]
    load_wo = load(wo_ref, wo_f, 7)
    sent, used = [], []

    def push(source, target, partner):
        at = len(used)
        used.append(at)
        copy = pltpu.make_async_remote_copy(
            src_ref=source,
            dst_ref=target,
            send_sem=send_sem.at[at],
            recv_sem=recv_sem.at[at],
            device_id=partner,
            device_id_type=pl.DeviceIdType.MESH,
        )
        copy.start()
        sent.append(copy)
        return copy

    for copy in load_rows:
        copy.wait()
    pl.semaphore_wait(barrier, 3 + len(others))
    to_chip = [
        push(source, target, across) for source, target in zip(spans(rows_t.at[0]), spans(rows_t.at[2]))
    ]
    to_core = push(rows_t.at[0], rows_t.at[1], beside)

    load_w.wait()
    step = w_own.shape[1] // 3
    for part in range(3):
        for at in range((width - HEAD) // own):

            @pl.when(place == at)
            def _():
                start = part * width + at * own
                w_out[:, part * step : part * step + own] = w_s[:, start : start + own].astype(BF16)

        last = w_s[:, (part + 1) * width - HEAD : (part + 1) * width].astype(BF16)
        w_out[:, part * step + own : (part + 1) * step] = jnp.concatenate(
            [last, jnp.zeros((half, step - own - HEAD), BF16)], axis=1
        )
    mine_half = pl.ds(pl.multiple_of(fsdp * half, 16), half)
    to_far = push(w_out, w_own.at[mine_half], far)
    w_own[mine_half, :] = w_out[...]

    for copy in load_mine:
        copy.wait()
    mine_s[:quarter] = fc_s[...].astype(BF16)
    mine_s[quarter : 2 * quarter] = proj_s[...].astype(BF16)
    bias = vector_ref[2:3]
    pieces = []
    for _ in range(3):
        piece = bias.astype(BF16)
        pieces.append(piece)
        bias = bias - piece.astype(F32)
    pieces.append(jnp.zeros((mine_s.shape[0] - 2 * quarter - 3, width), BF16))
    mine_s[2 * quarter :] = jnp.concatenate(pieces, axis=0)
    to_one = push(mine_s, one_ref, others[0])
    to_near = push(mine_s, far_ref, far)
    to_three = push(mine_s, three_ref, others[2])
    outs, put_at = [], []

    def put(source, target):
        copy = pltpu.make_async_copy(source, target, out_sem.at[len(put_at)])
        put_at.append(len(put_at))
        copy.start()
        outs.append(copy)
        return copy

    def take(copies):
        for copy in copies:
            copy.wait()
        outs[:] = [copy for copy in outs if all(copy is not done for done in copies)]

    put(mine_s, mine_ref)

    load_wo.wait()
    wo_s[...] = wo_f[...].astype(BF16)
    put(wo_s, out_ref.at[mine_half])
    chunk = 128

    def over_rows(body):
        @pl.loop(0, row_count // chunk)
        def _(i):
            body(pl.ds(pl.multiple_of(i * chunk, chunk), chunk))

    for copy in load_g:
        copy.wait()
    put(g_t, gt_ref)

    def turn_rows(source, target):
        def body(rows):
            target[rows, :] = source[:, rows].T

        over_rows(body)

    turn_rows(g_t, turned.at[0])
    put(turned.at[0], g_ref)
    turn_rows(rows_t.at[0], turned.at[1])
    put(turned.at[1], rows_ref)

    gain_col = jnp.broadcast_to(vector_ref[0:1], (8, width)).T[:, :1]
    bias_col = jnp.broadcast_to(vector_ref[1:2], (8, width)).T[:, :1]
    extra = norms.shape[1] - width
    at_row = lax.broadcasted_iota(jnp.int32, (extra, row_count), 0)
    ones = jnp.where(at_row == 0, 1.0, 0.0).astype(BF16)
    norms[0, width:] = ones
    norms[1, width:] = ones

    def normalise(distance, slot):
        def body(rows):
            values = rows_t[distance, :, rows].astype(F32)
            average = jnp.mean(values, axis=0, keepdims=True)
            centred = values - average
            variance = jnp.mean(centred * centred, axis=0, keepdims=True)
            low = centred * lax.rsqrt(variance + 1e-05) * gain_col + bias_col
            low = low.astype(BF16)
            norms[slot, :width, rows] = low
            normed[rows, :] = low.T

        over_rows(body)

    def project(distance, slot):
        block = place ^ distance
        made = [put(norms.at[slot], norm_ref.at[block])]
        tiles = step // TILE
        for part, (out, flip) in enumerate(((q_ref, None), (k_ref, kt_ref), (v_ref, vt_ref))):
            cols = slice(part * step, (part + 1) * step)
            value = (dot(normed[...], w_own[:, cols]) + col_bias_ref[:, cols]).astype(BF16)
            for tile in range(tiles):
                piece = value[:, tile * TILE : (tile + 1) * TILE]
                tall_s[slot, :, (part * tiles + tile) * TILE : (part * tiles + tile + 1) * TILE] = piece
                if flip is not None:
                    flat_s[slot, part - 1, tile] = piece.T
            for tile in range(tiles):
                lanes = slice((part * tiles + tile) * TILE, (part * tiles + tile + 1) * TILE)
                made.append(put(tall_s.at[slot, :, lanes], out.at[tile, block]))
                if flip is not None:
                    made.append(put(flat_s.at[slot, part - 1, tile], flip.at[tile, block]))
        return made

    normalise(0, 0)
    to_far.wait_recv()
    put(w_own, w_own_ref)
    first = project(0, 0)
    to_core.wait_recv()
    normalise(1, 1)
    second = project(1, 1)
    to_corner = []
    for copy, source, target in zip(to_chip, spans(rows_t.at[2]), spans(rows_t.at[3])):
        copy.wait_recv()
        to_corner.append(push(source, target, beside))
    take(first)
    normalise(2, 0)
    project(2, 0)
    for copy in to_corner:
        copy.wait_recv()
    take(second)
    normalise(3, 1)
    project(3, 1)
    for copy in outs:
        copy.wait()
    for copy in (to_one, to_near, to_three):
        copy.wait_recv()
    for copy in sent:
        copy.wait_send()


def open_up(
    prompt_in, cont_in, w_qkv, w_fc, w_proj, w_out, prompt_cot, cont_cot, vectors, col_bias, count
):
    prompt_rows, width = prompt_in.shape[1:]
    row_count = prompt_rows + cont_in.shape[1]
    half, quarter = width // 2, width // 4
    tiles = PAIRS + 1
    cols = 3 * tiles * TILE
    in_vmem = pl.BlockSpec(memory_space=pltpu.VMEM)
    vmem = lambda *shape, kind=BF16: pltpu.VMEM(shape, kind)
    tall, flat = (tiles, count, row_count, TILE), (tiles, count, TILE, row_count)
    mine = (2 * quarter + 16, w_fc.shape[1])
    outs = [
        (count, width + 16, row_count),
        tall,
        tall,
        tall,
        flat,
        flat,
        (width, cols),
        (row_count, width),
        (row_count, width),
        (width, row_count),
        mine,
        mine,
        mine,
        mine,
        (width, width),
    ]
    copies = 2 + 1 + 1 + 3 + 2
    return pl.pallas_call(
        open_kernel,
        in_specs=[ANYWHERE] * 8 + [in_vmem] * 2,
        out_specs=[ANYWHERE] * len(outs),
        out_shape=[shape_of(*out) for out in outs],
        scratch_shapes=[
            vmem(4, width, row_count),
            vmem(*w_qkv.shape, kind=F32),
            vmem(width, cols),
            vmem(half, cols),
            vmem(quarter, w_fc.shape[1], kind=F32),
            vmem(quarter, w_fc.shape[1], kind=F32),
            vmem(*mine),
            vmem(width, row_count),
            vmem(row_count, width),
            vmem(2, width + 16, row_count),
            vmem(2, row_count, cols),
            vmem(2, 2, tiles, TILE, row_count),
            vmem(2, row_count, width),
            vmem(half, width, kind=F32),
            vmem(half, width),
            pltpu.SemaphoreType.DMA((8,)),
            pltpu.SemaphoreType.DMA((copies,)),
            pltpu.SemaphoreType.DMA((copies,)),
            pltpu.SemaphoreType.DMA((80,)),
        ],
        compiler_params=pltpu.CompilerParams(
            vmem_limit_bytes=60 << 20, collective_id=2, has_side_effects=True
        ),
        cost_estimate=pl.CostEstimate(
            flops=2 * count * row_count * width * cols, bytes_accessed=40 << 20, transcendentals=0
        ),
        name="open",
    )(
        prompt_in[0].T,
        cont_in[0].T,
        w_qkv,
        w_fc,
        w_proj.T,
        w_out,
        prompt_cot[0].T,
        cont_cot[0].T,
        vectors,
        col_bias[None],
    )


def own_mask(rows):
    key_at = lax.broadcasted_iota(jnp.int32, (rows, rows), 0)
    query_at = lax.broadcasted_iota(jnp.int32, (rows, rows), 1)
    return key_at <= query_at


def attend_kernel(prompt_rows, q_ref, k_ref, vt_ref, seg_col_ref, seg_row_ref, *refs):
    mine_ref, near_ref, one_ref, three_ref = refs[:4]
    lse_ref, outs_ref, pieces_ref, last_ref, two_ref, one_far_ref = refs[5:11]
    beside_refs, out_ref, (acc, o_s, send_sem, recv_sem, out_sem) = refs[11:17], refs[17], refs[18:]
    step = pl.program_id(0)
    place = lax.axis_index("ctx")
    fsdp = lax.axis_index("fsdp")
    tensor = lax.axis_index("tensor")
    tensors = lax.axis_size("tensor")
    count, row_count = k_ref.shape[1], k_ref.shape[2]
    cont_rows = row_count - prompt_rows
    per_pair = 2 * count
    steps = PAIRS * per_pair
    beside, far = {"ctx": place ^ 1}, {"fsdp": 1 - fsdp}
    after, before = lax.rem(tensor + 1, tensors), lax.rem(tensor + tensors - 1, tensors)
    distance = jnp.where(step < steps, count - 1 - step % per_pair // 2, 0)
    block = place ^ distance

    def copy_to(at, source, target, partner):
        return pltpu.make_async_remote_copy(
            src_ref=source,
            dst_ref=target,
            send_sem=send_sem.at[at],
            recv_sem=recv_sem.at[at],
            device_id=partner,
            device_id_type=pl.DeviceIdType.MESH,
        )

    b_mine, b_near, b_one, b_one_far, b_three, b_two = beside_refs
    returns = {}
    for pair in range(PAIRS):
        for away in range(1, count):
            returns[pair, away] = copy_to(
                pair * (count - 1) + away - 1,
                o_s.at[pair, away],
                pieces_ref.at[pair, away - 1],
                {"ctx": place ^ away},
            )
    base = PAIRS * (count - 1)
    quarter = out_ref.shape[0] // 4

    def out_rows(away):
        return out_ref.at[pl.ds(pl.multiple_of(((fsdp ^ away) * 2 + place % 2) * quarter, 16), quarter)]

    early = [
        copy_to(base, one_ref, one_far_ref, far),
        copy_to(base + 1, one_ref, two_ref, {"tensor": after}),
        copy_to(base + 2, mine_ref, b_mine, beside),
        copy_to(base + 3, near_ref, b_near, beside),
        copy_to(base + 4, one_ref, b_one, beside),
        copy_to(base + 5, three_ref, b_three, beside),
        copy_to(base + 6, out_rows(0), out_rows(0), far),
    ]
    late = [
        copy_to(base + 7, one_far_ref, b_one_far, beside),
        copy_to(base + 8, out_rows(1), out_rows(1), beside),
        copy_to(base + 9, two_ref, b_two, beside),
    ]

    @pl.when(step == 0)
    def _():
        barrier = pltpu.get_barrier_semaphore()
        partners = [{"ctx": place ^ away} for away in range(1, count)]
        partners += [far, {"tensor": after}, {"tensor": before}]
        for partner in partners:
            pl.semaphore_signal(
                barrier, inc=1, device_id=partner, device_id_type=pl.DeviceIdType.MESH
            )
        pl.semaphore_wait(barrier, len(partners))
        for copy in early:
            copy.start()

    @pl.when(step == per_pair + 2)
    def _():
        early[0].wait_recv()
        late[0].start()

    @pl.when(step == per_pair + 5)
    def _():
        early[6].wait_recv()
        late[1].start()

    @pl.when(step == per_pair + 7)
    def _():
        early[1].wait_recv()
        late[2].start()

    def part(queries, at, start, size, mask, states):
        keys = k_ref[0, at, pl.ds(start, size), :]
        scores = [dot(keys, query, NT) for query in queries]
        if mask is not None:
            scores = [jnp.where(mask, score, -1e30) for score in scores]
        tops = [jnp.max(score, axis=0, keepdims=True) for score in scores]
        if states is not None:
            tops = [jnp.maximum(top, state[0]) for top, state in zip(tops, states)]
        exps = [jnp.exp2(score * SCALE2 - top * SCALE2) for score, top in zip(scores, tops)]
        totals = [jnp.sum(exp, axis=0, keepdims=True) for exp in exps]
        made = []
        for head in range(len(queries)):
            rows = slice(head * HEAD, (head + 1) * HEAD)
            cols = slice(0, queries[head].shape[0])
            out = dot(vt_ref[0, at, rows, pl.ds(start, size)], exps[head].astype(BF16))
            total = totals[head]
            if states is None:
                acc[rows, cols] = out
            else:
                shrink = jnp.exp2((states[head][0] - tops[head]) * SCALE2)
                total = total + states[head][1] * shrink
                acc[rows, cols] = acc[rows, cols] * shrink + out
            made.append((tops[head], total))
        return made

    def finish(start, size, states):
        for head, (top, total) in enumerate(states):
            rows = slice(head * HEAD, (head + 1) * HEAD)
            acc[rows, :size] = acc[rows, :size] / total
            lse_ref[0, block, head : head + 1, pl.ds(start, size)] = top * SCALE2 + jnp.log2(total)
        if len(states) == 1:
            acc[HEAD:, :size] = jnp.zeros((TILE - HEAD, size), F32)
        pair = step // per_pair
        o_s[pair, distance, pl.ds(start, size), :] = acc[:, :size].T.astype(BF16)

    def over_prompt(queries, total, states):
        return lax.fori_loop(
            0, total, lambda c, states: part(queries, c, 0, prompt_rows, None, states), states
        )

    for heads, here in ((2, step < steps), (1, step >= steps)):

        @pl.when(here & (step % 2 == 1))
        def _():
            queries = halves(q_ref[0, block, :prompt_rows, :], heads)
            states = part(queries, block, 0, prompt_rows, own_mask(prompt_rows), None)
            finish(0, prompt_rows, over_prompt(queries, block, states))

        @pl.when(here & (step % 2 == 0))
        def _():
            previous = jnp.maximum(block - 1, 0)
            labels = seg_row_ref[block]
            queries = halves(q_ref[0, block, prompt_rows:, :], heads)
            own = own_mask(cont_rows) & (seg_col_ref[block] == labels)
            near = (seg_col_ref[previous] == labels) & (block > 0)
            states = part(queries, block, prompt_rows, cont_rows, own, None)
            states = part(queries, previous, prompt_rows, cont_rows, near, states)
            finish(prompt_rows, cont_rows, over_prompt(queries, count, states))

    for pair in range(PAIRS):
        for away in range(1, count):

            @pl.when(step == pair * per_pair + 2 * (count - 1 - away) + 1)
            def _():
                returns[pair, away].start()

    @pl.when(step == steps + 1)
    def _():
        stores = [
            pltpu.make_async_copy(o_s.at[pl.ds(0, PAIRS)], outs_ref, out_sem.at[0]),
            pltpu.make_async_copy(o_s.at[PAIRS, 0], last_ref, out_sem.at[1]),
        ]
        for store in stores:
            store.start()
        for copy in early[2:6] + late + list(returns.values()):
            copy.wait_recv()
        for copy in early + late + list(returns.values()):
            copy.wait_send()
        for store in stores:
            store.wait()


def attend(q, k, vt, seg_col, seg_row, prompt_rows, weights, w_out):
    groups, count, row_count, _ = q.shape
    cont_rows = row_count - prompt_rows
    pair = lambda i: (jnp.minimum(i // (2 * count), PAIRS), 0, 0, 0)
    pairs = groups * count * (prompt_rows + 2 * cont_rows) * prompt_rows * count // 2
    mine = weights[0].shape
    copies = PAIRS * (count - 1) + 10
    outs = [
        (pl.BlockSpec((1, count, 2, row_count), pair), shape_of(groups, count, 2, row_count, kind=F32)),
        (ANYWHERE, shape_of(PAIRS, count, row_count, TILE)),
        (ANYWHERE, shape_of(PAIRS, count - 1, row_count, TILE)),
        (ANYWHERE, shape_of(row_count, TILE)),
    ] + [(ANYWHERE, shape_of(*mine))] * 8
    outs.append((ANYWHERE, shape_of(*w_out.shape)))
    return pl.pallas_call(
        functools.partial(attend_kernel, prompt_rows),
        grid=(PAIRS * 2 * count + 2,),
        in_specs=[
            pl.BlockSpec((1, count, row_count, TILE), pair),
            pl.BlockSpec((1, count, row_count, TILE), pair),
            pl.BlockSpec((1, count, TILE, row_count), pair),
            pl.BlockSpec((count, cont_rows, 1), lambda i: (0, 0, 0)),
            pl.BlockSpec((count, 1, cont_rows), lambda i: (0, 0, 0)),
        ]
        + [ANYWHERE] * (len(weights) + 1),
        input_output_aliases={5 + len(weights): len(outs) - 1},
        out_specs=[out[0] for out in outs],
        out_shape=[out[1] for out in outs],
        scratch_shapes=[
            pltpu.VMEM((TILE, max(prompt_rows, cont_rows)), F32),
            pltpu.VMEM((groups, count, row_count, TILE), BF16),
            pltpu.SemaphoreType.DMA((copies,)),
            pltpu.SemaphoreType.DMA((copies,)),
            pltpu.SemaphoreType.DMA((2,)),
        ],
        compiler_params=pltpu.CompilerParams(
            vmem_limit_bytes=56 << 20, collective_id=3, has_side_effects=True
        ),
        cost_estimate=pl.CostEstimate(
            flops=8 * TILE * pairs, bytes_accessed=20 << 20, transcendentals=2 * pairs
        ),
        name="attend",
    )(q, k, vt, seg_col, seg_row, *weights, w_out)


def attend_back_kernel(
    heads,
    spans,
    prompt_rows,
    place_ref,
    q_ref,
    k_ref,
    v_ref,
    kt_ref,
    lse_ref,
    seg_col_ref,
    seg_row_ref,
    *refs,
):
    do_refs, o_refs, refs = refs[:spans], refs[spans : 2 * spans], refs[2 * spans :]
    dq_ref, dk_ref, dv_ref, dk_acc, dv_acc, dq_acc, do_s, o_s = refs
    step = pl.program_id(0)
    distance = step % spans
    block = place_ref[0] ^ distance
    count, row_count = k_ref.shape[1], k_ref.shape[2]
    cont_rows = row_count - prompt_rows

    @pl.when(step == 0)
    def _():
        dk_acc[...] = jnp.zeros_like(dk_acc)
        dv_acc[...] = jnp.zeros_like(dv_acc)
        if spans < count:
            dq_ref[...] = jnp.zeros_like(dq_ref)

    def part(given, at, start, size, mask, first):
        rows = pl.ds(start, size)
        for head in range(heads):
            query, grad, lse, centre = (entry[head] for entry in given)
            cols = slice(0, query.shape[0])
            own = slice(head * HEAD, (head + 1) * HEAD)
            scores = dot(k_ref[0, at, rows, :], query, NT)
            if mask is not None:
                scores = jnp.where(mask, scores, -1e30)
            probability = jnp.exp2(scores * SCALE2 - lse)
            grad_probability = dot(v_ref[0, at, rows, :], grad, NT)
            grad_scores = (probability * (grad_probability - centre)).astype(BF16)
            dv_acc[at, rows, :] += dot(probability.astype(BF16), grad)
            dk_acc[at, rows, :] += dot(grad_scores, query)
            out = dot(kt_ref[0, at, own, rows], grad_scores)
            if first:
                dq_acc[own, cols] = out
            else:
                dq_acc[own, cols] += out

    def setup(start, size):
        rows = pl.ds(start, size)
        for at in range(spans):

            @pl.when(distance == at)
            def _():
                do_s[:size] = do_refs[at][rows, :]
                o_s[:size] = o_refs[at][0, 0, rows, :]

        grad = do_s[:size]
        product = (grad.astype(F32) * o_s[:size].astype(F32)).T
        centres = [
            jnp.sum(product[head * HEAD : (head + 1) * HEAD], axis=0, keepdims=True)
            for head in range(heads)
        ]
        lses = [lse_ref[0, block, head : head + 1, rows] for head in range(heads)]
        return halves(q_ref[0, block, rows, :], heads), halves(grad, heads), lses, centres

    def finish(start, size):
        if heads == 1:
            dq_acc[HEAD:, :size] = jnp.zeros((TILE - HEAD, size), F32)
        dq_ref[0, block, pl.ds(start, size), :] = (dq_acc[:, :size].T * 0.125).astype(BF16)

    @pl.when(step >= spans)
    def _():
        given = setup(0, prompt_rows)
        part(given, block, 0, prompt_rows, own_mask(prompt_rows), True)

        @pl.loop(0, block)
        def _(c):
            part(given, c, 0, prompt_rows, None, False)

        finish(0, prompt_rows)

    @pl.when(step < spans)
    def _():
        before = jnp.maximum(block - 1, 0)
        labels = seg_row_ref[block]
        own = own_mask(cont_rows) & (seg_col_ref[block] == labels)
        near = (seg_col_ref[before] == labels) & (block > 0)
        given = setup(prompt_rows, cont_rows)
        part(given, block, prompt_rows, cont_rows, own, True)
        part(given, before, prompt_rows, cont_rows, near, False)

        @pl.loop(0, count)
        def _(c):
            part(given, c, 0, prompt_rows, None, False)

        finish(prompt_rows, cont_rows)

    @pl.when(step == pl.num_programs(0) - 1)
    def _():
        dk_ref[0] = (dk_acc[...] * 0.125).astype(BF16)
        dv_ref[0] = dv_acc[...].astype(BF16)


def attend_back(
    pair, tile, heads, place, q, k, v, kt, lse, seg_col, seg_row, grads, outs, prompt_rows, after=(), carry=()
):
    _, count, row_count, _ = q.shape
    spans = len(grads)
    cont_rows = row_count - prompt_rows
    pick = lambda i, s: (pair, 0, 0, 0)
    tall = pl.BlockSpec((1, count, row_count, TILE), pick)
    most = max(prompt_rows, cont_rows)
    pairs = spans * (prompt_rows + 2 * cont_rows) * prompt_rows * count // 2
    return launch(
        functools.partial(attend_back_kernel, heads, spans, prompt_rows),
        "attend_back",
        (place,),
        (2 * spans,),
        (q, k, v, kt, lse, seg_col, seg_row, *grads, *[outs] * spans),
        [
            tall,
            tall,
            tall,
            pl.BlockSpec((1, count, TILE, row_count), pick),
            pl.BlockSpec((1, count, 2, row_count), pick),
            blocks(count, cont_rows, 1),
            blocks(count, 1, cont_rows),
        ]
        + [pl.BlockSpec((row_count, TILE), lambda i, s: (0, tile))] * spans
        + [
            pl.BlockSpec((1, 1, row_count, TILE), lambda i, s, away=away: (tile, away, 0, 0))
            for away in range(spans)
        ],
        [whole_out(1, count, row_count, TILE)] * 3,
        scratch=[
            pltpu.VMEM((count, row_count, TILE), F32),
            pltpu.VMEM((count, row_count, TILE), F32),
            pltpu.VMEM((TILE, most), F32),
            pltpu.VMEM((most, TILE), BF16),
            pltpu.VMEM((most, TILE), BF16),
        ],
        limit=56,
        flops=10 * heads * TILE * pairs,
        exps=heads * pairs,
        after=after,
        carry=carry,
    )


def normalize(values):
    average = jnp.mean(values, axis=1, keepdims=True)
    centred = values - average
    variance = jnp.mean(centred * centred, axis=1, keepdims=True)
    rate = lax.rsqrt(variance + 1e-05)
    return centred * rate, rate


def normalize_back(unit, rate, grad):
    shift = jnp.mean(grad, axis=1, keepdims=True)
    along = jnp.mean(grad * unit, axis=1, keepdims=True)
    return rate * (grad - shift - unit * along)


def piece_of(own_ref, pieces_ref, distance):
    tiles = [
        pieces_ref[pair, distance - 1] if distance else own_ref[pair, 0] for pair in range(PAIRS)
    ]
    return jnp.concatenate(tiles, axis=1)


def piece_specs(places, size):
    return [
        pl.BlockSpec((PAIRS, 1, size, TILE), lambda i, *_: (0, 0, i, 0)),
        pl.BlockSpec((PAIRS, places - 1, size, TILE), lambda i, *_: (0, 0, i, 0)),
        pl.BlockSpec((size, TILE), lambda i, *_: (i, 0)),
    ]


def merge_kernel(places, place_ref, x_ref, w_ref, out_bias_ref, gain_ref, bias_ref, *refs):
    own_ref, pieces_ref, last_ref, hidden_ref, low_ref, flip_ref = refs
    own = 2 * PAIRS * HEAD
    width = hidden_ref.shape[1]
    total = x_ref[:, :width].astype(F32) + out_bias_ref[...]
    for distance in range(places):
        start = pl.multiple_of((place_ref[0] ^ distance) * own, own)
        joined = piece_of(own_ref, pieces_ref, distance)
        total = total + dot(joined, w_ref[pl.ds(start, own), :])
    total = total + dot(last_ref[:, :HEAD], w_ref[width - HEAD :, :])
    hidden_ref[...] = total
    unit, _ = normalize(total)
    low = (unit * gain_ref[...] + bias_ref[...]).astype(BF16)
    low_ref[...] = low
    flip_ref[...] = low.T


def merge(place, rows, w_out, out_bias, gain, bias, pieces, after=(), carry=()):
    row_count, width = rows.shape[0], w_out.shape[1]
    size = 128
    by_row = lambda cols: pl.BlockSpec((size, cols), lambda i, p: (i, 0))
    return launch(
        functools.partial(merge_kernel, pieces[0].shape[1]),
        "merge",
        (place,),
        (row_count // size,),
        (rows, w_out, out_bias[None], gain[None], bias[None], *pieces),
        [by_row(rows.shape[1]), blocks(*w_out.shape)]
        + [blocks(1, width)] * 3
        + piece_specs(pieces[0].shape[1], size),
        [
            (by_row(width), shape_of(row_count, width, kind=F32)),
            (by_row(width), shape_of(row_count, width)),
            (
                pl.BlockSpec((width, size), lambda i, p: (0, i)),
                shape_of(width, row_count),
            ),
        ],
        flops=2 * row_count * width * width,
        after=after,
        carry=carry,
    )


def bend_kernel(
    places, mlp_ref, gm_ref, hidden_ref, g_ref, w_ref, gain_ref, proj_bias_ref, own_ref, pieces_ref, last_ref, *refs
):
    out_ref, gh_ref, ga_ref, ga_last_ref, *refs = refs
    come_refs, gw_refs, refs = refs[: places - 1], refs[places - 1 : places + 1], refs[places + 1 :]
    sums_ref, acc, ga_s, send_sem, recv_sem = refs
    step = pl.program_id(0)
    steps = pl.num_programs(0)
    place, fsdp = lax.axis_index("ctx"), lax.axis_index("fsdp")
    own = 2 * PAIRS * HEAD
    size, width = hidden_ref.shape
    mesh_id = pl.DeviceIdType.MESH

    def copies(at):
        rows = pl.ds(pl.multiple_of(at * size, 16), size)
        return [
            pltpu.make_async_remote_copy(
                src_ref=ga_s.at[away - 1, rows],
                dst_ref=come_refs[away - 1].at[rows],
                send_sem=send_sem.at[at, away - 1],
                recv_sem=recv_sem.at[at, away - 1],
                device_id={"ctx": place ^ away},
                device_id_type=mesh_id,
            )
            for away in range(1, places)
        ]

    @pl.when(step == 0)
    def _():
        barrier = pltpu.get_barrier_semaphore()
        for away in range(1, places):
            pl.semaphore_signal(
                barrier, inc=1, device_id={"ctx": place ^ away}, device_id_type=mesh_id
            )

    hidden = hidden_ref[...]
    out_ref[...] = (hidden + mlp_ref[...] + proj_bias_ref[...]).astype(BF16)
    unit, rate = normalize(hidden)
    grad_in = gm_ref[...]
    grad_layer = g_ref[...].astype(F32)
    grad_hidden = grad_layer + normalize_back(unit, rate, grad_in * gain_ref[...])
    gh_ref[...] = grad_hidden
    branch = grad_hidden.astype(BF16)
    rows = pl.ds(pl.multiple_of(step * size, 16), size)
    for distance in range(places - 1, -1, -1):
        heads = pl.ds(pl.multiple_of((place ^ distance) * own, own), own)
        piece = dot(branch, w_ref[heads, :], NT).astype(BF16)
        if distance:
            ga_s[distance - 1, rows, :] = piece
        else:
            ga_ref[...] = piece

    @pl.when(step == 0)
    def _():
        pl.semaphore_wait(pltpu.get_barrier_semaphore(), places - 1)

    for copy in copies(step):
        copy.start()
    last = dot(branch, w_ref[width - HEAD :, :], NT).astype(BF16)
    ga_last_ref[...] = jnp.concatenate([last, jnp.zeros_like(last)], axis=1)
    sums = [grad_hidden, grad_in * unit, grad_in, grad_layer]
    sums = jnp.concatenate([jnp.sum(entry, axis=0, keepdims=True) for entry in sums], axis=0)

    @pl.when(step == 0)
    def _():
        acc[...] = jnp.zeros_like(acc)
        sums_ref[...] = sums

    @pl.when(step > 0)
    def _():
        sums_ref[...] += sums

    for distance in range(places):
        heads = pl.ds(pl.multiple_of((place ^ distance) * own, own), own)
        joined = piece_of(own_ref, pieces_ref, distance)
        acc[heads, :] += dot(joined.T, branch)
    acc[width - HEAD :, :] += dot(last_ref[:, :HEAD].T, branch)

    @pl.when(step == steps - 1)
    def _():
        quarter = width // 4
        for beside, ref in enumerate(gw_refs):
            for away in range(2):
                start = ((fsdp ^ away) * 2 + (place % 2 ^ beside)) * quarter
                ref[away] = acc[pl.ds(pl.multiple_of(start, 16), quarter), :].astype(BF16)

        @pl.loop(0, steps)
        def _(i):
            for copy in copies(i):
                copy.wait_recv()
                copy.wait_send()


def bend(mlp_out, gm, hidden, g, w_out, gain, proj_bias, pieces, after):
    row_count, width = hidden.shape
    size = row_count // 4
    places = pieces[0].shape[1]
    own = 2 * PAIRS * HEAD
    by_row = lambda cols: pl.BlockSpec((size, cols), lambda i: (i, 0))
    return launch(
        functools.partial(bend_kernel, places),
        "bend",
        (),
        (row_count // size,),
        (mlp_out, gm, hidden, g, w_out, gain[None], proj_bias[None], *pieces),
        [by_row(width)] * 4
        + [blocks(*w_out.shape)]
        + [blocks(1, width)] * 2
        + piece_specs(places, size),
        [
            (by_row(width), shape_of(row_count, width)),
            (by_row(width), shape_of(row_count, width, kind=F32)),
            (by_row(own), shape_of(row_count, own)),
            (by_row(TILE), shape_of(row_count, TILE)),
        ]
        + [(ANYWHERE, shape_of(row_count, own))] * (places - 1)
        + [
            whole_out(2, width // 4, width),
            whole_out(2, width // 4, width),
            whole_out(4, width, kind=F32),
        ],
        scratch=[
            pltpu.VMEM((width, width), F32),
            pltpu.VMEM((places - 1, row_count, own), BF16),
            pltpu.SemaphoreType.DMA((row_count // size, places - 1)),
            pltpu.SemaphoreType.DMA((row_count // size, places - 1)),
        ],
        limit=56,
        flops=4 * row_count * width * width,
        traffic=30,
        after=after,
        meet=6,
    )


GELU_RATE = 0.7978845608028654


def gelu_both(values):
    square = values * values
    bent = jnp.tanh(GELU_RATE * (values + 0.044715 * square * values))
    half = 0.5 * (1.0 + bent)
    slope = half + 0.5 * values * (1.0 - bent * bent) * (GELU_RATE * (1.0 + 0.134145 * square))
    return values * half, slope


def mlp_kernel(
    parts,
    first,
    x_ref,
    g_ref,
    xt_ref,
    gt_ref,
    *refs,
):
    own, far, own_2, far_2 = (refs[i * parts : (i + 1) * parts] for i in range(4))
    before_refs = refs[4 * parts : 4 * parts + 2]
    refs = refs[4 * parts + (0 if first else 2) :]
    out_ref, gm_ref, keep_f, send_f, gb_ref = refs[:5]
    sums_p, refs = refs[5 : 5 + parts], refs[5 + parts :]
    wf_s, wp_s, bias_s, biases, act_s, gp_s, wide, keep_s, send_s, come_s, total = refs[:11]
    sems, send_sem, recv_sem = refs[11:]
    step = pl.program_id(0)
    place, fsdp = lax.axis_index("ctx"), lax.axis_index("fsdp")
    core, chip = place % 2, place // 2
    beside = {"ctx": place ^ 1}
    mesh_id = pl.DeviceIdType.MESH
    slot = step % 2
    _, width, hidden = wf_s.shape
    quarter = width // 4

    def spot(away, across):
        start = ((fsdp ^ away) * 2 + (core ^ across)) * quarter
        return pl.ds(pl.multiple_of(start, 16), quarter)

    def loads(at, to):
        moves = [(own[at].at[pl.ds(2 * quarter, 16)], bias_s.at[to])]
        for away, sources in enumerate(((own[at], own_2[at]), (far[at], far_2[at]))):
            for across, source in enumerate(sources):
                for weight, target in enumerate((wf_s, wp_s)):
                    moves.append(
                        (
                            source.at[pl.ds(weight * quarter, quarter)],
                            target.at[to, spot(away, across)],
                        )
                    )
        return [
            pltpu.make_async_copy(source, target, sems.at[to, i])
            for i, (source, target) in enumerate(moves)
        ]

    def exchange(at):
        return pltpu.make_async_remote_copy(
            src_ref=send_s,
            dst_ref=come_s.at[at],
            send_sem=send_sem.at[at],
            recv_sem=recv_sem.at[at],
            device_id=beside,
            device_id_type=mesh_id,
        )

    @pl.when(step == 0)
    def _():
        for part in range(parts):
            for copy in loads(part, part):
                copy.start()
        barrier = pltpu.get_barrier_semaphore()
        pl.semaphore_signal(barrier, inc=1, device_id=beside, device_id_type=mesh_id)
        pl.semaphore_wait(barrier, 1)

    for part in range(parts):

        @pl.when(step == part)
        def _():
            for copy in loads(part, part):
                copy.wait()

    bias = jnp.sum(bias_s[slot, :3, :].astype(F32), axis=0, keepdims=True)
    biases[...] = bias

    def over(total, body):
        whole = total // 256

        @pl.loop(0, whole)
        def _(i):
            body(pl.multiple_of(i * 256, 256), 256)

        if total % 256:
            body(whole * 256, total % 256)

    def up(*blocks_of):
        made = []
        for start, size in blocks_of:
            cols = pl.ds(start, size)
            pre_act = dot(x_ref[...], wf_s[slot, :, cols]) + biases[:, cols]
            made.append((cols, pre_act, dot(g_ref[...], wp_s[slot, :, cols])))
        for cols, pre_act, grad_act in made:
            activated, slope = gelu_both(pre_act)
            grad_pre = (grad_act * slope).astype(BF16)
            act_s[:, cols] = activated.astype(BF16)
            gp_s[:, cols] = grad_pre
            gb_ref[0, :, cols] = jnp.sum(grad_pre.astype(F32), axis=0, keepdims=True)

    def weights(start, size):
        cols = pl.ds(start, size)
        for weight, (left, right) in enumerate(((xt_ref, gp_s), (gt_ref, act_s))):
            wide[:, :size] = dot(left[...], right[:, cols]).astype(BF16)
            for far in range(2):
                for across, to in enumerate((keep_s, send_s)):
                    to[weight, far, :, cols] = wide[spot(far, across), :size]

    pairs = hidden // 512

    @pl.loop(0, pairs)
    def _(i):
        start = pl.multiple_of(i * 512, 512)
        up((start, 256), (start + 256, 256))

    for start in range(pairs * 512, hidden, 256):
        up((start, min(256, hidden - start)))

    for part in range(1, parts):

        @pl.when(step == part)
        def _():
            exchange(part - 1).wait_send()

    over(hidden, weights)
    for part in range(parts):

        @pl.when(step == part)
        def _():
            exchange(part).start()

    if first:

        @pl.when(step == 0)
        def _():
            out_ref[...] = jnp.zeros_like(out_ref)
            gm_ref[...] = jnp.zeros_like(gm_ref)

    else:

        @pl.when(step == 0)
        def _():
            out_ref[...] = before_refs[0][...]
            gm_ref[...] = before_refs[1][...]

    def down(start, size):
        rows = pl.ds(start, size)
        out_ref[:, rows] += dot(act_s[...], wp_s[slot, rows, :], NT)
        gm_ref[:, rows] += dot(gp_s[...], wf_s[slot, rows, :], NT)

    over(width, down)
    for part in range(parts):

        @pl.when(step == part)
        def _():
            exchange(part).wait_recv()
            for far in range(2):
                total[...] = keep_s[0, far].astype(F32) + come_s[part, 0, far].astype(F32)
                for to, away in ((keep_f, 0), (send_f, 1)):
                    eighth = quarter // 2
                    rows = pl.ds(pl.multiple_of((chip ^ away) * eighth, 8), eighth)
                    to[0, far] = total[rows, :].astype(BF16)
                sums_p[part][far] = (
                    keep_s[1, far].astype(F32) + come_s[part, 1, far].astype(F32)
                ).astype(BF16)
            if part == parts - 1:
                exchange(part).wait_send()


def mlp(meet, x, g, xt, gt, own, far, own_2, far_2, before=(), after=(), carry=()):
    rows, width = x.shape
    hidden = own[0].shape[1]
    parts, quarter = len(own), width // 4
    once = pl.Buffered(buffer_count=1)
    whole = lambda *shape: pl.BlockSpec(shape, lambda k: (0,) * len(shape), pipeline_mode=once)
    by_half = pl.BlockSpec((1, 2, quarter // 2, hidden), lambda k: (k, 0, 0, 0))
    total = (whole(rows, width), shape_of(rows, width, kind=F32))
    by_half = (by_half, shape_of(parts, 2, quarter // 2, hidden))
    by_part = (whole(2, quarter, hidden), shape_of(2, quarter, hidden))
    return launch(
        functools.partial(mlp_kernel, parts, not before),
        "mlp",
        (),
        (parts,),
        (x, g, xt, gt, *own, *far, *own_2, *far_2, *before),
        [
            whole(rows, width),
            whole(rows, width),
            whole(width, rows),
            whole(width, rows),
        ]
        + [ANYWHERE] * (4 * parts)
        + [whole(rows, width)] * len(before),
        [
            total,
            total,
            by_half,
            by_half,
            (
                pl.BlockSpec((1, 1, hidden), lambda k: (k, 0, 0)),
                shape_of(parts, 1, hidden, kind=F32),
            ),
        ]
        + [by_part] * parts,
        scratch=[
            pltpu.VMEM((2, width, hidden), BF16),
            pltpu.VMEM((2, width, hidden), BF16),
            pltpu.VMEM((2, 16, hidden), BF16),
            pltpu.VMEM((1, hidden), F32),
            pltpu.VMEM((rows, hidden), BF16),
            pltpu.VMEM((rows, hidden), BF16),
            pltpu.VMEM((width, 256), BF16),
            pltpu.VMEM((2, 2, quarter, hidden), BF16),
            pltpu.VMEM((2, 2, quarter, hidden), BF16),
            pltpu.VMEM((parts, 2, 2, quarter, hidden), BF16),
            pltpu.VMEM((quarter, hidden), F32),
            pltpu.SemaphoreType.DMA((2, 9)),
            pltpu.SemaphoreType.DMA((parts,)),
            pltpu.SemaphoreType.DMA((parts,)),
        ],
        meet=meet,
        limit=62,
        flops=12 * rows * width * hidden * parts,
        traffic=40,
        exps=rows * hidden * parts,
        after=after,
        carry=carry,
    )


def tail_kernel(prompt_rows, *refs):
    grads, refs = refs[:9], refs[9:]
    w_ref, norm_ref, rows_ref, gh_ref, keep_ref, come_ref, gain_ref, given_ref = refs[:8]
    prompt_ref, cont_ref, qkv_ref, wo_ref, vec_ref = refs[8:13]
    (
        norms,
        rows_s,
        gh_s,
        joined,
        hold,
        core_out,
        core_in,
        chip_out,
        chip_in,
        acc,
        keep,
        far_out,
        far_in,
        sums,
        sums_in,
        ring_in,
        ring_all,
        whole,
        near_in,
        left_out,
        left_in,
        vec_out,
        vec_in,
        wo_sum,
        wo_ring,
        wo_half,
        wo_all,
        wo_core,
        local_sem,
        send_sem,
        recv_sem,
    ) = refs[13:]
    place = lax.axis_index("ctx")
    fsdp = lax.axis_index("fsdp")
    tensor = lax.axis_index("tensor")
    tensors = lax.axis_size("tensor")
    count, row_count = grads[0].shape[1], grads[0].shape[2]
    width = w_ref.shape[0]
    half = width // 2
    own = acc.shape[1]
    shard = ring_in.shape[2]
    chunk = 128
    beside, across, far = {"ctx": place ^ 1}, {"ctx": place ^ 2}, {"fsdp": 1 - fsdp}
    others = [{"tensor": lax.rem(tensor + k, tensors)} for k in range(1, tensors)]

    barrier = pltpu.get_barrier_semaphore()
    for partner in (beside, across, far, *others):
        pl.semaphore_signal(barrier, inc=1, device_id=partner, device_id_type=pl.DeviceIdType.MESH)

    loads = [pltpu.make_async_copy(norm_ref, norms, local_sem.at[0])]
    loads.append(pltpu.make_async_copy(keep_ref, wo_core.at[0], local_sem.at[1]))
    loads.append(pltpu.make_async_copy(come_ref, core_out.at[pl.ds(0, come_ref.shape[0])], local_sem.at[2]))
    for load in loads:
        load.start()
    sent, used = [], []

    def push(source, target, partner):
        at = len(used)
        used.append(at)
        copy = pltpu.make_async_remote_copy(
            src_ref=source,
            dst_ref=target,
            send_sem=send_sem.at[at],
            recv_sem=recv_sem.at[at],
            device_id=partner,
            device_id_type=pl.DeviceIdType.MESH,
        )
        copy.start()
        sent.append(copy)
        return copy

    quarter, part_rows, most_rows = wo_sum.shape[0], wo_ring.shape[1], wo_half.shape[1]
    chip = place // 2

    def part_start(owner):
        return pl.multiple_of(jnp.minimum(owner * part_rows, most_rows - part_rows), 16)

    def chip_start(owner):
        return pl.ds(pl.multiple_of(owner * (quarter - most_rows), 16), most_rows)

    def rows_grad(distance, out):
        block = place ^ distance
        for i, ref in enumerate(grads):
            joined[:, i * TILE : (i + 1) * TILE] = ref[0, block]

        @pl.loop(0, width // 256)
        def _(i):
            cols = pl.ds(pl.multiple_of(i * 256, 256), 256)
            out[:, cols] = dot(joined[...], w_ref[cols, :], NT).astype(out.dtype)

        if width % 256:
            cols = pl.ds(width // 256 * 256, width % 256)
            out[:, cols] = dot(joined[...], w_ref[cols, :], NT).astype(out.dtype)

    to_far = [None] * 4

    def weights(part):
        @pl.loop(0, count)
        def _(block):
            if part < 3:
                pieces = [grads[3 * part + pair][0, block] for pair in range(PAIRS)]
            else:
                pieces = [grads[3 * i + PAIRS][0, block][:, :HEAD] for i in range(3)]
                pieces.append(jnp.zeros((row_count, own - 3 * HEAD), BF16))
            piece = dot(norms[block], jnp.concatenate(pieces, axis=1))

            @pl.when(block == 0)
            def _():
                acc[...] = piece

            @pl.when(block > 0)
            def _():
                acc[...] += piece

        sums[part] = acc[width : width + 8, :]
        keep[part] = acc[pl.ds(pl.multiple_of(fsdp * half, 16), half), :]
        far_out[part] = acc[pl.ds(pl.multiple_of((1 - fsdp) * half, 16), half), :].astype(BF16)
        to_far[part] = push(far_out.at[part], far_in.at[part], far)

    def joined_far(part):
        to_far[part].wait_recv()
        return keep[part] + far_in[part].astype(F32)

    def start_of(owner):
        return pl.multiple_of(jnp.minimum(owner * shard, half - shard), 16)

    to_ring, to_all, to_near = [None] * 4, [None] * 4, [None] * 4

    def ring(part, total):
        sums_in[part] = total.astype(BF16)
        to_ring[part] = [
            push(
                sums_in.at[part, pl.ds(start_of(other["tensor"]), shard)],
                ring_in.at[part, k],
                other,
            )
            for k, other in enumerate(others)
        ]

    def spread(part):
        total = sums_in[part, pl.ds(start_of(tensor), shard), :].astype(F32)
        for k, copy in enumerate(to_ring[part]):
            copy.wait_recv()
            total = total + ring_in[part, k].astype(F32)
        ring_all[part, tensor] = total.astype(BF16)
        to_all[part] = [
            push(ring_all.at[part, tensor], ring_all.at[part, tensor], other) for other in others
        ]

    def gather(part):
        for copy in to_all[part]:
            copy.wait_recv()
        for owner in range(tensors - 1):
            whole[part, owner * shard : (owner + 1) * shard] = ring_all[part, owner]
        rest = (tensors - 1) * shard
        whole[part, rest:] = ring_all[part, tensors - 1, tensors * shard - half :]
        if part < 3:
            to_near[part] = [
                push(whole.at[part], near_in.at[part, 0], beside),
                push(whole.at[part], near_in.at[part, 1], across),
            ]

    loads[1].wait()
    loads[2].wait()
    wo_sum[...] = (wo_core[0].astype(F32) + core_out[:quarter].astype(F32)).astype(BF16)
    pl.semaphore_wait(barrier, 3 + len(others))
    wo_to_chip = push(wo_sum.at[chip_start(1 - chip)], wo_half.at[1], across)
    loads[0].wait()
    weights(3)
    weights(0)

    rows_grad(3, core_out)
    to_core = push(core_out, core_in.at[0], beside)
    left_out[0] = joined_far(3).astype(BF16)
    to_left = push(left_out.at[0], left_in.at[0], beside)
    wo_to_chip.wait_recv()
    wo_half[0] = (wo_sum[chip_start(chip), :].astype(F32) + wo_half[1].astype(F32)).astype(BF16)
    wo_to_ring = [
        push(wo_half.at[0, pl.ds(part_start(other["tensor"]), part_rows)], wo_ring.at[k], other)
        for k, other in enumerate(others)
    ]
    ring(0, joined_far(0))
    rows_grad(2, hold)
    to_core.wait_recv()

    @pl.loop(0, row_count // chunk)
    def _(i):
        rows = pl.ds(pl.multiple_of(i * chunk, chunk), chunk)
        chip_out[rows, :] = (hold[rows, :] + core_in[0, rows, :].astype(F32)).astype(BF16)

    to_left.wait_recv()
    left_out[1] = (left_out[0].astype(F32) + left_in[0].astype(F32)).astype(BF16)
    to_left = push(left_out.at[1], left_in.at[1], across)
    to_chip = push(chip_out, chip_in, across)
    weights(1)
    wo_total = wo_half[0, pl.ds(part_start(tensor), part_rows), :].astype(F32)
    for k, copy in enumerate(wo_to_ring):
        copy.wait_recv()
        wo_total = wo_total + wo_ring[k].astype(F32)
    wo_all[tensor] = wo_total.astype(BF16)
    wo_to_all = [push(wo_all.at[tensor], wo_all.at[tensor], other) for other in others]
    to_left.wait_recv()
    ring(3, left_out[1].astype(F32) + left_in[1].astype(F32))
    ring(1, joined_far(1))
    weights(2)
    spread(0)
    to_core.wait_send()
    sent[:] = [copy for copy in sent if copy is not to_core]
    rows_grad(1, core_out)
    to_core_2 = push(core_out, core_in.at[1], beside)
    ring(2, joined_far(2))
    spread(3)
    rows_grad(0, hold)
    spread(1)
    for copy in wo_to_all:
        copy.wait_recv()
    for owner in range(tensors):
        start = min(owner * part_rows, most_rows - part_rows)
        wo_half[2, start : start + part_rows] = wo_all[owner]
    wo_to_other = push(wo_half.at[2], wo_half.at[3], across)
    gather(0)
    to_core_2.wait_recv()
    to_chip.wait_recv()

    vec_out[0, :8] = jnp.zeros((8, vec_out.shape[2]), F32)
    vec_out[0, 8:] = given_ref[...]
    chunks = row_count // chunk

    def chunk_rows(i):
        return pl.ds(pl.multiple_of(i * chunk, chunk), chunk)

    def row_loads(i):
        slot = i % 2
        return [
            pltpu.make_async_copy(gh_ref.at[chunk_rows(i)], gh_s.at[slot], local_sem.at[3 + slot]),
            pltpu.make_async_copy(rows_ref.at[chunk_rows(i)], rows_s.at[slot], local_sem.at[5 + slot]),
        ]

    for load in row_loads(0):
        load.start()

    @pl.loop(0, chunks)
    def _(i):
        @pl.when(i + 1 < chunks)
        def _():
            for load in row_loads(i + 1):
                load.start()

        for load in row_loads(i):
            load.wait()

        rows = chunk_rows(i)
        unit, rate = normalize(rows_s[i % 2, :, :width].astype(F32))
        grad = hold[rows, :] + core_in[1, rows, :].astype(F32) + chip_in[rows, :].astype(F32)
        back = normalize_back(unit, rate, grad * gain_ref[0:1])
        out = (gh_s[i % 2] + back).astype(BF16)

        @pl.when(i < prompt_rows // chunk)
        def _():
            prompt_ref[0, rows, :] = out

        @pl.when(i >= prompt_rows // chunk)
        def _():
            cont_ref[0, chunk_rows(i - prompt_rows // chunk), :] = out

        vec_out[0, 0:1, :width] += jnp.sum(grad * unit, axis=0, keepdims=True)
        vec_out[0, 1:2, :width] += jnp.sum(grad, axis=0, keepdims=True)

    spread(2)
    for row, part in ((2, 0), (3, 2)):
        cols = pl.ds(pl.multiple_of(place * own, own), own)
        vec_out[0, row : row + 1, cols] = sums[part, 0:1, :]
        left = slice(part * HEAD, (part + 1) * HEAD)
        vec_out[0, row : row + 1, width - HEAD : width] = sums[3, 0:1, left]
    gather(1)

    def forward(part):
        to_near[part][1].wait_recv()
        return push(near_in.at[part, 1], near_in.at[part, 2], beside)

    def store(part, passed):
        to_near[part][0].wait_recv()
        passed.wait_recv()
        sources = [whole.at[part]] + [near_in.at[part, i] for i in range(3)]
        for distance, source in enumerate(sources):
            for block in range(count):

                @pl.when(place ^ distance == block)
                def _():
                    start = part * width + block * own
                    qkv_ref[:, start : start + own] = source[...]

    levels = (
        (place, [(place ^ away, {"ctx": place ^ away}) for away in range(1, count)]),
        (tensor, [(other["tensor"], other) for other in others]),
        (fsdp, [(1 - fsdp, far)]),
    )

    def exchange(level):
        own_at, partners = levels[level]
        vec_in[level, own_at] = vec_out[level]
        return [push(vec_out.at[level], vec_in.at[level, own_at], other) for _, other in partners]

    def add(level, copies):
        for copy in copies:
            copy.wait_recv()
        total = vec_in[level, 0]
        for at in range(1, len(copies) + 1):
            total = total + vec_in[level, at]
        vec_out[level + 1] = total

    step = exchange(0)
    passed_0 = forward(0)
    gather(2)
    add(0, step)
    step = exchange(1)
    passed_1 = forward(1)
    gather(3)
    store(0, passed_0)
    add(1, step)
    step = exchange(2)
    wo_to_other.wait_recv()
    for at in range(2):

        @pl.when(chip == at)
        def _():
            wo_core[0, :most_rows] = wo_half[2 + at]
            wo_core[0, most_rows:] = wo_half[3 - at, 2 * most_rows - quarter :]

    wo_to_core = push(wo_core.at[0], wo_core.at[1], beside)
    for part in range(3):
        cols = slice((part + 1) * width - HEAD, (part + 1) * width)
        qkv_ref[:, cols] = whole[3, :, part * HEAD : (part + 1) * HEAD]
    add(2, step)
    vec_ref[...] = vec_out[3]
    passed_2 = forward(2)
    store(1, passed_1)
    wo_to_core.wait_recv()
    core = place % 2
    for away in range(2):
        wo_ref[pl.ds(pl.multiple_of((core ^ away) * quarter, 16), quarter), :] = wo_core[away]
    store(2, passed_2)
    for copy in sent:
        copy.wait_send()


def tail(
    grads, w_own, normed, rows, grad_hidden, gain, vectors, out_keep, out_come, prompt_rows, after=()
):
    count, depth, row_count = normed.shape
    width, cols = w_own.shape
    half, own = width // 2, 2 * PAIRS * HEAD
    tensors = lax.axis_size("tensor")
    shard = -(-half // tensors // 16) * 16
    padded = vectors.shape[1]
    in_vmem = pl.BlockSpec(memory_space=pltpu.VMEM)
    vmem = lambda *shape, kind=BF16: pltpu.VMEM(shape, kind)
    copies = 4 + 4 * 2 * (tensors - 1) + 4 + 3 * 3 + 2 + count + tensors - 1 + 2 * (tensors - 1) + 3
    given = len(grads) + 8
    quarter = width // 4
    most_rows = -(-quarter // 2 // 16) * 16
    part_rows = -(-most_rows // tensors // 16) * 16

    def body(*refs):
        tail_kernel(prompt_rows, *refs[:given], *refs[given + len(after) :])

    return pl.pallas_call(
        body,
        in_specs=[in_vmem] * (len(grads) + 1) + [ANYWHERE] * 5 + [in_vmem] * 2 + [ANYWHERE] * len(after),
        out_specs=[in_vmem] * 5,
        out_shape=[
            shape_of(1, prompt_rows, width),
            shape_of(1, row_count - prompt_rows, width),
            shape_of(half, 3 * width),
            shape_of(half, width),
            shape_of(16, padded, kind=F32),
        ],
        scratch_shapes=[
            vmem(*normed.shape),
            vmem(2, TILE, width),
            vmem(2, TILE, width, kind=F32),
            vmem(row_count, cols),
            vmem(row_count, width, kind=F32),
            vmem(row_count, width),
            vmem(2, row_count, width),
            vmem(row_count, width),
            vmem(row_count, width),
            vmem(depth, own, kind=F32),
            vmem(4, half, own, kind=F32),
            vmem(4, half, own),
            vmem(4, half, own),
            vmem(4, 8, own, kind=F32),
            vmem(4, half, own),
            vmem(4, tensors - 1, shard, own),
            vmem(4, tensors, shard, own),
            vmem(4, half, own),
            vmem(3, 3, half, own),
            vmem(2, half, own),
            vmem(2, half, own),
            vmem(4, 16, padded, kind=F32),
            vmem(3, max(count, tensors), 16, padded, kind=F32),
            vmem(quarter, width),
            vmem(tensors - 1, part_rows, width),
            vmem(4, most_rows, width),
            vmem(tensors, part_rows, width),
            vmem(2, quarter, width),
            pltpu.SemaphoreType.DMA((7,)),
            pltpu.SemaphoreType.DMA((copies,)),
            pltpu.SemaphoreType.DMA((copies,)),
        ],
        compiler_params=pltpu.CompilerParams(
            vmem_limit_bytes=62 << 20, collective_id=1, has_side_effects=True
        ),
        cost_estimate=pl.CostEstimate(
            flops=4 * count * row_count * width * cols, bytes_accessed=30 << 20, transcendentals=0
        ),
        name="tail",
    )(*grads, w_own, normed, rows, grad_hidden, out_keep, out_come, gain, vectors, *after)


def own_columns(matrix, place):
    width = matrix.shape[1] // 3
    own = 2 * PAIRS * HEAD
    blank = jnp.zeros((matrix.shape[0], TILE - HEAD), matrix.dtype)
    pieces = []
    for part in range(3):
        whole = matrix[:, part * width : (part + 1) * width]
        pieces += [
            lax.dynamic_slice_in_dim(whole, place * own, own, 1),
            whole[:, width - HEAD :],
            blank,
        ]
    return jnp.concatenate(pieces, axis=1)


def local_heads(
    prompt_in,
    cont_in,
    cont_seg,
    ln1_gain,
    ln1_bias,
    w_qkv,
    qv_bias,
    w_out,
    out_bias,
    ln2_gain,
    ln2_bias,
    w_fc,
    fc_bias,
    w_proj,
    proj_bias,
    prompt_cot,
    cont_cot,
):
    width = prompt_in.shape[2]
    prompt_rows, cont_rows = prompt_in.shape[1], cont_in.shape[1]
    row_count = prompt_rows + cont_rows
    count = lax.axis_size("ctx")
    place = lax.axis_index("ctx")
    core, chip = place % 2, place // 2
    fsdp = lax.axis_index("fsdp")
    tensor = lax.axis_index("tensor")
    tensors = lax.axis_size("tensor")
    own_width = 2 * PAIRS * HEAD
    half, hidden_units = w_fc.shape
    quarter = half // 2
    eighth = quarter // 2
    padded = (width + TILE - 1) // TILE * TILE
    at = place.reshape(1)
    spot = jnp.stack([core, fsdp, tensor, jnp.int32(tensors), place])

    zero_bias = jnp.zeros_like(qv_bias[0])
    col_bias = own_columns(jnp.concatenate([qv_bias[0], zero_bias, qv_bias[1]])[None], place)[0]
    open_vectors = jnp.stack([ln1_gain, ln1_bias, fc_bias])
    normed, q, k, v, kt, vt, w_own, rows_own, grad_layer, grad_flip, *mines, out_own = open_up(
        prompt_in,
        cont_in,
        w_qkv,
        w_fc,
        w_proj,
        w_out,
        prompt_cot,
        cont_cot,
        open_vectors,
        col_bias,
        count,
    )

    mine, one_away, three_away, near_far = mines

    labels = cont_seg[0].reshape(count, cont_rows)
    seg_col, seg_row = labels[:, :, None], labels[:, None, :]
    lse, outs, came, last_out, two_away, one_far, *others, out_full = attend(
        q, k, vt, seg_col, seg_row, prompt_rows, (mine, near_far, one_away, three_away), out_own
    )
    mine_2, near_2, one_2, one_far_2, three_2, two_2 = others
    three_far, two_far = swap(three_away, "fsdp", 1), swap(two_away, "fsdp", 1)
    pieces = (outs, came, last_out)
    hidden, mlp_low, mlp_flip = merge(
        at, rows_own, out_full, out_bias, ln2_gain, ln2_bias, pieces
    )

    steps_away = (0, 1, 3, 2)
    given = (mlp_low, grad_layer, mlp_flip, grad_flip)
    mlp_out, grad_mlp_in, keep_1, send_1, bias_first, proj_0, proj_1 = mlp(
        4,
        *given, (mine, one_away), (near_far, one_far), (mine_2, one_2), (near_2, one_far_2)
    )
    three_far, two_far = behind((three_far, two_far), bias_first)
    three_far_2, two_far_2 = swap(three_far, "ctx", 1), swap(two_far, "ctx", 1)
    mlp_out, grad_mlp_in, keep_2, send_2, bias_last, proj_2, proj_3 = mlp(
        5,
        *given,
        (three_away, two_away),
        (three_far, two_far),
        (three_2, two_2),
        (three_far_2, two_far_2),
        before=(mlp_out, grad_mlp_in),
    )
    grad_fc_bias = jnp.concatenate([bias_first, bias_last], axis=0)
    proj_2, proj_3 = behind((proj_2, proj_3), mlp_out)
    come_p = [
        turn(part, "tensor", -steps_away[k + 1]) for k, part in enumerate((proj_1, proj_2, proj_3))
    ]
    layer_out, grad_hidden, grads_own, grad_last, *rest = bend(
        mlp_out,
        grad_mlp_in,
        hidden,
        grad_layer,
        out_full,
        ln2_gain,
        proj_bias,
        pieces,
        (proj_2, proj_3),
    )
    grads_all, (out_keep, out_send, sums2) = [grads_own, *rest[:-3]], rest[-3:]

    def added(left, right):
        return left.astype(F32) + right.astype(F32)

    def back(pair, tile, heads, grads, outs, after=()):
        return attend_back(
            pair, tile, heads, at, q, k, v, kt, lse, seg_col, seg_row, grads, outs, prompt_rows, after
        )

    (send_2,) = behind((send_2,), grads_own)
    come_o = swap(out_send, "ctx", 1)
    come_1, come_2 = swap(send_1, "ctx", 2), swap(send_2, "ctx", 2)
    grads_pair = [back(0, 0, 2, grads_all, outs)]
    grads_left = back(PAIRS, 0, 1, [grad_last], last_out[None, None], (grads_pair[0][0],))
    come_o, come_1, come_2, *come_p = behind((come_o, come_1, come_2, *come_p), grads_left[0])
    sums_f = [
        added(keep[k], come[k]).astype(BF16)
        for keep, come in ((keep_1, come_1), (keep_2, come_2))
        for k in range(2)
    ]
    near_p, far_p = (
        sum((come[away].astype(F32) for come in come_p), proj_0[away].astype(F32)).astype(BF16)
        for away in range(2)
    )
    near_o, far_o = (added(out_keep[away], come_o[away]).astype(BF16) for away in range(2))
    come_f = [turn(sums_f[k], "tensor", -steps_away[k]) for k in range(1, tensors)]
    come_p, come_o = swap(far_p, "fsdp", 1), swap(far_o, "fsdp", 1)
    grads_pair.append(back(1, 1, 2, grads_all, outs, (*sums_f[1:], far_p, far_o, grads_left[0])))
    come_p, *come_f = behind((come_p, *come_f), grads_pair[1][0])
    near_f, far_f = (
        sum((come[away].astype(F32) for come in come_f), sums_f[0][away].astype(F32)).astype(BF16)
        for away in range(2)
    )
    sum_p = added(near_p, come_p).astype(BF16)
    ordered = [entry[part] for part in range(3) for entry in (*grads_pair, grads_left)]
    vectors = jnp.concatenate([sums2, jnp.zeros((tensors, hidden_units), F32)], axis=0)
    for k, distance in enumerate(steps_away):
        vectors = lax.dynamic_update_slice(
            vectors, grad_fc_bias[k], (4 + (tensor - distance) % tensors, 0)
        )
    vectors = jnp.pad(vectors, ((0, 0), (0, padded - width)))
    prompt_grad, cont_grad, sum_qkv, sum_out, late = tail(
        ordered,
        w_own,
        normed,
        rows_own,
        grad_hidden,
        open_vectors,
        vectors,
        near_o,
        come_o,
        prompt_rows,
        (far_f, sum_p),
    )
    come_f, come_p = behind((swap(far_f, "fsdp", 1), swap(sum_p, "ctx", 2)), late)
    sum_f, sum_p = added(near_f, come_f).astype(BF16), added(sum_p, come_p).astype(BF16)
    prompt_grad, cont_grad, sum_qkv, sum_out = behind(
        (prompt_grad, cont_grad, sum_qkv, sum_out), sum_f, sum_p
    )
    by_away = [sum_f] + [swap(sum_f, "ctx", away) for away in range(1, count)]
    halves_f = [
        jnp.concatenate(in_order(by_away[i], by_away[i ^ 2], chip), axis=0) for i in range(2)
    ]
    own_fc = jnp.concatenate(in_order(*halves_f, core), axis=0).astype(F32)
    own_proj = jnp.concatenate(in_order(sum_p, swap(sum_p, "ctx", 1), core), axis=0).astype(F32).T

    fc_bias_sum = lax.dynamic_index_in_dim(late, 12 + tensor, 0, False)[:hidden_units]
    return (
        layer_out[:prompt_rows][None],
        layer_out[prompt_rows:][None],
        prompt_grad,
        cont_grad,
        late[0, :width],
        late[1, :width],
        sum_qkv.astype(F32),
        late[2:4, :width],
        sum_out.astype(F32),
        late[8, :width],
        late[9, :width],
        late[10, :width],
        own_fc,
        fc_bias_sum,
        own_proj,
        late[11, :width],
    )


def solution(mesh):
    placed = (
        P(("fsdp", "tensor"), "ctx", None),
        P(("fsdp", "tensor"), "ctx", None),
        P(("fsdp", "tensor"), None),
        P(),
        P(),
        P("fsdp", None),
        P(),
        P("fsdp", None),
        P(),
        P(),
        P(),
        P("fsdp", "tensor"),
        P("tensor"),
        P("tensor", "fsdp"),
        P(),
        P(("fsdp", "tensor"), "ctx", None),
        P(("fsdp", "tensor"), "ctx", None),
    )
    by_heads = HEADS // mesh.shape["ctx"] == PAIRS * 2 and HEADS % mesh.shape["ctx"] == 1
    return jax.shard_map(
        local_heads if by_heads else local_rows,
        mesh=mesh,
        in_specs=placed,
        out_specs=(
            P(("fsdp", "tensor"), "ctx", None),
            P(("fsdp", "tensor"), "ctx", None),
            P(("fsdp", "tensor"), "ctx", None),
            P(("fsdp", "tensor"), "ctx", None),
            P(),
            P(),
            P("fsdp", None),
            P(),
            P("fsdp", None),
            P(),
            P(),
            P(),
            P("fsdp", "tensor"),
            P("tensor"),
            P("tensor", "fsdp"),
            P(),
        ),
        check_vma=False,
    )
```
